32 devices in a mesh: dp: 4 (over z), context: 4 (over x, core), experts: 2 (over y).
Axes of the slice: x: 2, y: 2, z: 4, core: 2. Of those that a mesh axis runs over, the one named last changes fastest.
Arguments:
- block_input: bfloat16 [16, 1024, 1024], P('dp', ('context', 'experts')), may hold values from -6 to 6
- teacher: bfloat16 [16, 1024, 1024], P('dp', ('context', 'experts')), may hold values from -6 to 6
- lengths: int32 [16], replicated, may hold values from 128 to 1024, as said below
- routes: int32 [16, 1024, 8], P('dp', ('context', 'experts')), may hold values from 0 to 31, all different within a row; in each aligned block of 128 rows (0 to 127, 128 to 255, ..., all dimensions but the last counted through in order) at most 40 rows name the same one
- w_query: bfloat16 [1024, 1024], replicated, may hold values from -0.1875 to 0.1875
- w_key: bfloat16 [1024, 512], replicated, may hold values from -0.1875 to 0.1875
- w_value: bfloat16 [1024, 512], replicated, may hold values from -0.1875 to 0.1875
- w_out: bfloat16 [1024, 1024], replicated, may hold values from -1.5 to 1.5
- query_gain: float32 [64], replicated, may hold values from 0.1 to 1.9
- key_gain: float32 [64], replicated, may hold values from 0.1 to 1.9
- attn_gain: float32 [1024], replicated, may hold values from 0.1 to 1.9
- ffn_gain: float32 [1024], replicated, may hold values from 0.1 to 1.9
- w_router: bfloat16 [1024, 32], replicated, may hold values from -0.09375 to 0.09375
- w_gate: bfloat16 [32, 1024, 512], P(('context', 'experts')), may hold values from -0.1875 to 0.1875
- w_up: bfloat16 [32, 1024, 512], P(('context', 'experts')), may hold values from -0.1875 to 0.1875
- w_down: bfloat16 [32, 512, 1024], P(('context', 'experts')), may hold values from -1 to 1
Outputs:
- loss_mean: float32 [], replicated
- block_output: bfloat16 [16, 1024, 1024], P('dp', ('context', 'experts'))
- input_grad: float32 [16, 1024, 1024], P('dp', ('context', 'experts'))
- query_w_grad: float32 [1024, 1024], replicated
- key_w_grad: float32 [1024, 512], replicated
- value_w_grad: float32 [1024, 512], replicated
- out_w_grad: float32 [1024, 1024], replicated
- query_gain_grad: float32 [64], replicated
- key_gain_grad: float32 [64], replicated
- attn_gain_grad: float32 [1024], replicated
- ffn_gain_grad: float32 [1024], replicated
- router_grad: float32 [1024, 32], replicated
- gate_w_grad: float32 [32, 1024, 512], P(('context', 'experts'))
- up_w_grad: float32 [32, 1024, 512], P(('context', 'experts'))
- down_w_grad: float32 [32, 512, 1024], P(('context', 'experts'))
The draws below stay inside these ranges and needn't reach their ends.
Inputs may be any that keep to these rules, and one draw needn't show every extreme that they name: `lengths`: in each aligned group of 4 slots (those of one index of dp) one slot, drawn from the seed, has length 1024. `routes`: each position names 8 different experts; among the 128 positions of one slot that one device holds, no expert is named more than 40 times.
All inputs are finite; a program needn't handle non-finite values.
Results may differ from the reference program's by a relative error of at most 0.017.
Values may be sent and summed in bfloat16 or wider, within the bound.
A program may use at most 384 MiB of HBM per device.

```python
import math
import jax
import jax.numpy as jnp
import numpy as np
from jax import lax

D = 1024
QUERY_HEADS = 16
KEY_VALUE_HEADS = 8
HEAD_DIM = 64
EXPERTS = 32
EFF = 512
TOP = 8
SLOT_DEV = 128
SLOTS = 4
SLOT_POSITIONS = 1024
SLOT_TOTAL = 16
MOST = 40


def draw_lengths(key, part):
    key = jax.random.fold_in(key, 11)
    first_key, second_key = jax.random.split(key)
    groups = SLOT_TOTAL // SLOTS
    shorter = jax.random.randint(first_key, (groups, SLOTS), SLOT_POSITIONS // 8, SLOT_POSITIONS + 1)
    chosen = jax.random.randint(second_key, (groups, 1), 0, SLOTS)
    picked = jnp.arange(SLOTS, dtype=jnp.int32)[None, :] == chosen
    return jnp.where(picked, SLOT_POSITIONS, shorter).reshape(-1).astype(jnp.int32)


def steps_of(key, dims, cuts, least, high):
    loudness, own = 1.0, jax.random.fold_in(key, 6)
    for axis_at, blocks in cuts:
        steps = jnp.exp(jax.random.uniform(jax.random.fold_in(own, axis_at), (blocks,), jnp.float32, least / len(cuts), high / len(cuts)))
        loudness = loudness * jnp.repeat(steps, dims[axis_at] // blocks).reshape([-1 if axis == axis_at else 1 for axis in range(len(dims))])
    return loudness


def deal_out(key, own, number, rows, number_of, top, bound, lean):
    ranking = jax.random.permutation(key, number_of)
    heavy_load, ordinary = load_shares(number_of, rows * top, bound, lean, True), load_shares(number_of, rows * top, bound, lean, False)
    places = jnp.arange(number_of)

    def named(sizes, turn):
        used = int((sizes > 0).sum())
        fixed = max(1, used // 4)
        shifted = fixed + (places - fixed + turn * (used - fixed)) % max(1, number_of - fixed)
        return jnp.zeros((number_of,), jnp.int32).at[ranking[jnp.where(places < fixed, places, shifted)]].set(jnp.asarray(sizes, jnp.int32))

    sizes = jnp.where(number % 4 == 0, named(heavy_load, number // 4), named(ordinary, number - number // 4 - 1))
    mixed = jax.random.permutation(jax.random.fold_in(own, 3), number_of)
    giver, receiver = mixed[0:number_of // 2 * 2:2], mixed[1:number_of // 2 * 2:2]
    room = jnp.minimum(sizes[giver] - 1, bound - sizes[receiver]) // 2
    room = jnp.where((giver == ranking[0]) | (receiver == ranking[0]) | (sizes[receiver] == 0), 0, jnp.maximum(room, 0))
    shifted = jax.random.randint(jax.random.fold_in(own, 4), (number_of // 2,), 0, 1 << 20) % (room + 1)
    sizes = sizes.at[giver].add(-shifted).at[receiver].add(shifted)
    members = jnp.searchsorted(jnp.cumsum(sizes), jnp.arange(rows * top), side="right").astype(jnp.int32)
    listing = members.reshape(top, rows).T
    listing = listing[jax.random.permutation(jax.random.fold_in(own, 1), rows)]
    turn = jax.random.randint(jax.random.fold_in(own, 2), (rows, 1), 0, top)
    return jnp.take_along_axis(listing, (jnp.arange(top)[None, :] + turn) % top, axis=1)


def load_shares(count, total, reach, skew, full):
    weights = [(1 << 20) // math.isqrt(grade ** skew) + 1 for grade in range(1, count + 1)]
    largest = reach if full else min(reach, max(-(-total // count), total * weights[0] // sum(weights)))
    least = 1 if total - largest >= count - 1 else 0
    given, surplus = [largest] + [least] * (count - 1), total - largest - least * (count - 1)
    while surplus > 0:
        movable = [i for i in range(1, count) if given[i] < largest] or [i for i in range(1, count) if given[i] < reach]
        mass, remaining = sum([weights[i] for i in movable]), surplus
        for i in movable:
            addition = min(reach - given[i], max(1, remaining * weights[i] // mass), surplus)
            given[i] = given[i] + addition
            surplus = surplus - addition
    return np.array(given)


def scatter_about(key, dims, spread, most, cuts=(), held_as=jnp.bfloat16):
    values = jax.random.normal(key, dims, jnp.float32) * spread
    if len(cuts) > 0:
        values = steps_of(key, dims, cuts, -0.22, 0.18) * values
    return jnp.clip(values, min=-most, max=most).astype(held_as)


def setup_inputs(seed: int = 0) -> dict:
    splits = jax.random.split(jax.random.key(seed), 17)
    block_input = scatter_about(splits[0], (SLOT_TOTAL, SLOT_POSITIONS, D), 1.0, 6.0, ((0, 4), (1, 8)))
    teacher = scatter_about(splits[1], (SLOT_TOTAL, SLOT_POSITIONS, D), 1.0, 6.0, ((0, 4), (1, 8)))
    lengths = draw_lengths(jax.random.fold_in(splits[16], 71), 0)
    routes_keys = jax.random.split(jax.random.fold_in(splits[3], 1), SLOT_TOTAL * SLOT_POSITIONS // SLOT_DEV)
    routes_turns = jax.random.permutation(jax.random.fold_in(splits[3], 3), SLOT_TOTAL * SLOT_POSITIONS // SLOT_DEV)
    routes = jax.vmap(lambda own, number: deal_out(jax.random.fold_in(splits[3], 2), own, number, SLOT_DEV, EXPERTS, TOP, MOST, 1))(routes_keys, routes_turns).reshape((SLOT_TOTAL, SLOT_POSITIONS, TOP))
    w_query = scatter_about(splits[4], (D, QUERY_HEADS * HEAD_DIM), D ** -0.5, 0.1875)
    w_key = scatter_about(splits[5], (D, KEY_VALUE_HEADS * HEAD_DIM), D ** -0.5, 0.1875)
    w_value = scatter_about(splits[6], (D, KEY_VALUE_HEADS * HEAD_DIM), D ** -0.5, 0.1875)
    w_out = scatter_about(splits[7], (QUERY_HEADS * HEAD_DIM, D), (QUERY_HEADS * HEAD_DIM // 64) ** -0.5, 1.5)
    query_gain = jnp.clip(1.0 + 0.18 * jax.random.normal(splits[8], (HEAD_DIM,), jnp.float32), 0.1, 1.9)
    key_gain = jnp.clip(1.0 + 0.18 * jax.random.normal(splits[9], (HEAD_DIM,), jnp.float32), 0.1, 1.9)
    attn_gain = jnp.clip(1.0 + 0.18 * jax.random.normal(splits[10], (D,), jnp.float32), 0.1, 1.9)
    ffn_gain = jnp.clip(1.0 + 0.18 * jax.random.normal(splits[11], (D,), jnp.float32), 0.1, 1.9)
    w_router = scatter_about(splits[12], (D, EXPERTS), (4 * D) ** -0.5, 0.09375)
    w_gate = scatter_about(splits[13], (EXPERTS, D, EFF), D ** -0.5, 0.1875, ((0, 8),))
    w_up = scatter_about(splits[14], (EXPERTS, D, EFF), D ** -0.5, 0.1875, ((0, 8),))
    w_down = scatter_about(splits[15], (EXPERTS, EFF, D), (EFF // 16) ** -0.5, 1.0, ((0, 8),))
    return {"block_input": block_input, "teacher": teacher, "lengths": lengths, "routes": routes, "w_query": w_query, "w_key": w_key, "w_value": w_value, "w_out": w_out, "query_gain": query_gain, "key_gain": key_gain, "attn_gain": attn_gain, "ffn_gain": ffn_gain, "w_router": w_router, "w_gate": w_gate, "w_up": w_up, "w_down": w_down}


EPSILON = 1e-06
MASKED = -1e+30
EXACT_ARITHMETIC = lax.Precision.HIGHEST

@jax.custom_vjp
def narrow_number_format(v):
    return lax.optimization_barrier(v.astype(jnp.bfloat16)).astype(jnp.float32)

@jax.custom_vjp
def narrow_format_result(v):
    return v

def low_keep(v):
    return (narrow_number_format(v), None)

def low_pass(kept, grad):
    return (grad,)

def back_keep(v):
    return (v, None)

def back_low(kept, grad):
    return (narrow_number_format(grad),)
narrow_number_format.defvjp(low_keep, low_pass)
narrow_format_result.defvjp(back_keep, back_low)

def rms_scale(tensor, gain):
    return tensor * lax.rsqrt(lax.optimization_barrier(jnp.mean(tensor * tensor, axis=-1, keepdims=True)) + EPSILON) * gain

def rotary(tensor, cosine, sine_part):
    half_width = tensor.shape[-1] // 2
    former = tensor[..., :half_width]
    latter = tensor[..., half_width:]
    return jnp.concatenate([former * cosine - latter * sine_part, latter * cosine + former * sine_part], axis=-1)

def angles(positions, head_size):
    half_width = head_size // 2
    inverse = 10000.0 ** (-(jnp.arange(half_width, dtype=jnp.float32) * 2.0 / head_size))
    turned = positions.astype(jnp.float32)[:, None] * inverse[None, :]
    return (jnp.cos(turned)[None, :, None, :], jnp.sin(turned)[None, :, None, :])

def attend(entry):
    query_rows, key_rows, value_projected, slot_length = entry
    row_span = query_rows.shape[0]
    grouped = query_rows.reshape(row_span, KEY_VALUE_HEADS, QUERY_HEADS // KEY_VALUE_HEADS, HEAD_DIM)
    raw_scores = narrow_format_result(jnp.einsum('qagd,kad->agqk', grouped, key_rows, precision=EXACT_ARITHMETIC))
    places = jnp.arange(row_span, dtype=jnp.int32)
    allowed = (places[None, :] <= places[:, None]) & (places[None, :] < slot_length)
    scores = jnp.where(allowed, raw_scores * 0.125, MASKED)
    weights_soft = narrow_number_format(jax.nn.softmax(scores, axis=-1))
    mixed_heads = jnp.einsum('agqk,kad->qagd', weights_soft, value_projected, precision=EXACT_ARITHMETIC)
    return mixed_heads.reshape(row_span, QUERY_HEADS * HEAD_DIM)

def apply_specialists(token_rows, gate_flat, route_order, counts, offsets, w_gate, w_up, w_down):
    total_routes = gate_flat.shape[0]
    row_span = token_rows.shape[0] // SLOT_DEV * MOST

    def one_expert(entry):
        expert, gate_weight, up_weight, down_weight = entry
        places = jnp.arange(row_span, dtype=jnp.int32)
        picked = route_order[jnp.minimum(offsets[expert] + places, total_routes - 1)]
        live_rows = (places < counts[expert]).astype(jnp.float32)
        token_index = (picked // TOP).astype(jnp.int32)
        inputs = narrow_format_result(token_rows[token_index])
        gate_part = narrow_format_result(jnp.einsum('rd,df->rf', inputs, gate_weight, precision=EXACT_ARITHMETIC))
        up_part = narrow_format_result(jnp.einsum('rd,df->rf', inputs, up_weight, precision=EXACT_ARITHMETIC))
        hidden = narrow_number_format(jax.nn.silu(gate_part) * up_part)
        result = narrow_number_format(narrow_format_result(jnp.einsum('rf,fd->rd', hidden, down_weight, precision=EXACT_ARITHMETIC)))
        return (token_index, (gate_flat[picked] * live_rows)[:, None] * result)
    token_index, parts = lax.map(jax.checkpoint(one_expert), (jnp.arange(EXPERTS, dtype=jnp.int32), w_gate, w_up, w_down))
    return jnp.zeros_like(token_rows).at[token_index.reshape(-1)].add(parts.reshape(-1, token_rows.shape[1]))

def reference(block_input, teacher, lengths, routes, w_query, w_key, w_value, w_out, query_gain, key_gain, attn_gain, ffn_gain, w_router, w_gate, w_up, w_down):
    places = jnp.arange(SLOT_POSITIONS, dtype=jnp.int32)
    valid_mask = (places[None, :] < lengths[:, None]).astype(jnp.float32)
    cosine, sine_part = angles(places, HEAD_DIM)
    route_flat = routes.reshape(-1)
    route_order = jnp.argsort(route_flat, stable=True).astype(jnp.int32)
    counts = lax.optimization_barrier(jnp.sum((route_flat[:, None] == jnp.arange(EXPERTS, dtype=jnp.int32)[None, :]).astype(jnp.int32), axis=0))
    offsets = (jnp.cumsum(counts) - counts).astype(jnp.int32)
    target = teacher.astype(jnp.float32)

    def forward(inputs, query_matrix, key_matrix, value_matrix, final_projection_weight, qg, kg, ag, fg, router_matrix, wg, wu, wd):
        first_normed_input = narrow_number_format(rms_scale(inputs, ag))
        query_unrotated = narrow_format_result(jnp.einsum('pzc,co->pzo', first_normed_input, query_matrix, precision=EXACT_ARITHMETIC)).reshape(SLOT_TOTAL, SLOT_POSITIONS, QUERY_HEADS, HEAD_DIM)
        key_unrotated = narrow_format_result(jnp.einsum('pzc,co->pzo', first_normed_input, key_matrix, precision=EXACT_ARITHMETIC)).reshape(SLOT_TOTAL, SLOT_POSITIONS, KEY_VALUE_HEADS, HEAD_DIM)
        value_projected = narrow_number_format(narrow_format_result(jnp.einsum('pzc,co->pzo', first_normed_input, value_matrix, precision=EXACT_ARITHMETIC))).reshape(SLOT_TOTAL, SLOT_POSITIONS, KEY_VALUE_HEADS, HEAD_DIM)
        query_rows = narrow_number_format(narrow_format_result(rotary(rms_scale(query_unrotated, qg), cosine, sine_part)))
        key_rows = narrow_number_format(narrow_format_result(rotary(rms_scale(key_unrotated, kg), cosine, sine_part)))
        joined_group_vectors = lax.map(jax.checkpoint(attend), (query_rows, key_rows, value_projected, lengths))
        context_mixture = narrow_format_result(jnp.einsum('gxd,dz->gxz', narrow_number_format(narrow_format_result(joined_group_vectors)), final_projection_weight, precision=EXACT_ARITHMETIC))
        after_attn = inputs + valid_mask[..., None] * context_mixture
        second_normed_input = narrow_number_format(rms_scale(after_attn, fg))
        router_logits = narrow_format_result(jnp.einsum('pgb,bf->pgf', second_normed_input, router_matrix, precision=EXACT_ARITHMETIC))
        chosen = jnp.take_along_axis(router_logits, routes, axis=-1)
        gates = jax.nn.softmax(chosen, axis=-1) * valid_mask[..., None]
        expert_mix = apply_specialists(second_normed_input.reshape(-1, D), gates.reshape(-1), route_order, counts, offsets, wg, wu, wd)
        output = after_attn + expert_mix.reshape(after_attn.shape)
        difference = output - target
        loss_sum = jnp.sum(valid_mask[..., None] * difference * difference)
        return (output, loss_sum)
    floats = (block_input.astype(jnp.float32), w_query.astype(jnp.float32), w_key.astype(jnp.float32), w_value.astype(jnp.float32), w_out.astype(jnp.float32), query_gain.astype(jnp.float32), key_gain.astype(jnp.float32), attn_gain.astype(jnp.float32), ffn_gain.astype(jnp.float32), w_router.astype(jnp.float32), w_gate.astype(jnp.float32), w_up.astype(jnp.float32), w_down.astype(jnp.float32))
    (output, loss_sum), pull = jax.vjp(forward, *floats)
    count_all = jnp.sum(lengths).astype(loss_sum.dtype)
    grads = pull((jnp.zeros_like(output), (SLOT_TOTAL * SLOT_POSITIONS / (2.0 * count_all)).astype(loss_sum.dtype)))
    loss_mean = loss_sum / (count_all * D)
    return (loss_mean, output.astype(jnp.bfloat16), grads[0], grads[1], grads[2], grads[3], grads[4], grads[5], grads[6], grads[7], grads[8], grads[9], grads[10], grads[11], grads[12])
```

```python
import functools
import math

import jax
import jax.numpy as jnp
from jax import lax
from jax.experimental import pallas as pl
from jax.experimental.pallas import tpu as pltpu
from jax.sharding import PartitionSpec as P

EPSILON = 1e-06
MOST = 40
PAIR = 2 * MOST
LANES = 128
HEAD = 64
SCALE = 0.125
EXP2_SCALE = 0.125 * math.log2(math.e)
MIB = 2**20
MESH = pl.DeviceIdType.MESH
F32 = jnp.float32
BF16 = jnp.bfloat16


def dot(a, b):
    return lax.dot_general(a, b, (((1,), (0,)), ((), ())), preferred_element_type=F32)


def dot_nt(a, b):
    return lax.dot_general(a, b, (((1,), (1,)), ((), ())), preferred_element_type=F32)


def dot_tn(a, b):
    return lax.dot_general(a, b, (((0,), (0,)), ((), ())), preferred_element_type=F32)


def lane_of(shape):
    return lax.broadcasted_iota(jnp.int32, shape, len(shape) - 1)


def row_of(shape):
    return lax.broadcasted_iota(jnp.int32, shape, len(shape) - 2)


def swap_halves(tile):
    low = lax.rem(lane_of(tile.shape), HEAD) < HEAD // 2
    return jnp.where(low, pltpu.roll(tile, LANES - HEAD // 2, 1), pltpu.roll(tile, HEAD // 2, 1))


def head_mean(tile):
    low = lane_of(tile.shape) < HEAD
    first = jnp.sum(jnp.where(low, tile, 0.0), axis=-1, keepdims=True)
    second = jnp.sum(jnp.where(low, 0.0, tile), axis=-1, keepdims=True)
    return jnp.where(low, first, second) * (1.0 / HEAD)


def rope_forward(raw, gain, cosine, sine):
    normed = raw * lax.rsqrt(head_mean(raw * raw) + EPSILON) * gain
    return normed * cosine + swap_halves(normed) * sine


def rope_backward(grad, raw, gain, cosine, sine):
    inverse = lax.rsqrt(head_mean(raw * raw) + EPSILON)
    unit = raw * inverse
    normed_grad = grad * cosine - swap_halves(grad) * sine
    gain_grad = jnp.sum(normed_grad * unit, axis=0, keepdims=True)
    unit_grad = normed_grad * gain
    return inverse * (unit_grad - unit * head_mean(unit_grad * unit)), gain_grad


def rms_parts(rows):
    inverse = lax.rsqrt(jnp.mean(rows * rows, axis=-1, keepdims=True) + EPSILON)
    return rows * inverse, inverse


def rms_backward(grad, rows, gain):
    unit, inverse = rms_parts(rows)
    gain_grad = jnp.sum(grad * unit, axis=0, keepdims=True)
    unit_grad = grad * gain
    back = inverse * (unit_grad - unit * jnp.mean(unit_grad * unit, axis=-1, keepdims=True))
    return back, gain_grad


def stack_heads(tile, masked):
    first, second = tile[:, :LANES].astype(F32), tile[:, LANES:].astype(F32)
    parts = [first, pltpu.roll(first, HEAD, 1), pltpu.roll(second, HEAD, 1), second]
    if masked:
        low = lane_of(first.shape) < HEAD
        parts = [jnp.where(low, part, 0.0) for part in parts[:2]] + [
            jnp.where(low, 0.0, part) for part in parts[2:]
        ]
    return jnp.concatenate(parts, axis=0)


def unstack_heads(rows):
    count = rows.shape[0] // 4
    one, two, three, four = (rows[k * count : (k + 1) * count] for k in range(4))
    low = lane_of(one.shape) < HEAD
    return jnp.concatenate(
        [
            jnp.where(low, one, pltpu.roll(two, HEAD, 1)),
            jnp.where(low, pltpu.roll(three, HEAD, 1), four),
        ],
        axis=1,
    )


def project_kernel(
    x_ref, gain_ref, wq_ref, wk_ref, wv_ref, qg_ref, kg_ref, cos_ref, sin_ref,
    h_ref, q_ref, kv_ref, qraw_ref, kraw_ref,
):
    slots, rows, width = x_ref.shape
    x = x_ref[...].astype(F32).reshape(slots * rows, width)
    unit, unused = rms_parts(x)
    normed = (unit * gain_ref[...]).astype(BF16)
    h_ref[...] = normed.reshape(slots, rows, width)
    cosine = jnp.concatenate([cos_ref[...]] * slots, axis=0)
    sine = jnp.concatenate([sin_ref[...]] * slots, axis=0)
    q_raw = dot(normed, wq_ref[...])
    qraw_ref[...] = q_raw.reshape(qraw_ref.shape)
    for tile in range(q_raw.shape[1] // LANES):
        lanes = slice(tile * LANES, (tile + 1) * LANES)
        turned = rope_forward(q_raw[:, lanes], qg_ref[...], cosine, sine)
        q_ref[:, :, lanes] = turned.astype(BF16).reshape(slots, rows, LANES)
    k_raw = dot(normed, wk_ref[...])
    kraw_ref[...] = k_raw.reshape(kraw_ref.shape)
    value = dot(normed, wv_ref[...]).astype(BF16)
    for tile in range(k_raw.shape[1] // LANES):
        lanes = slice(tile * LANES, (tile + 1) * LANES)
        turned = rope_forward(k_raw[:, lanes], kg_ref[...], cosine, sine)
        at = 2 * tile * LANES
        kv_ref[:, :, at : at + LANES] = turned.astype(BF16).reshape(slots, rows, LANES)
        kv_ref[:, :, at + LANES : at + 2 * LANES] = value[:, lanes].reshape(slots, rows, LANES)


def project(x, attn_gain, w_query, w_key, w_value, qg, kg, cosine, sine):
    slots, rows, width = x.shape
    step = 2
    block = lambda lanes: pl.BlockSpec((step, rows, lanes), lambda i: (i, 0, 0))
    whole = lambda a: pl.BlockSpec(a.shape, lambda i: (0,) * a.ndim)
    qw, kw = w_query.shape[1], w_key.shape[1]
    return pl.pallas_call(
        project_kernel,
        grid=(slots // step,),
        out_shape=(
            jax.ShapeDtypeStruct((slots, rows, width), BF16),
            jax.ShapeDtypeStruct((slots, rows, qw), BF16),
            jax.ShapeDtypeStruct((slots, rows, 2 * kw), BF16),
            jax.ShapeDtypeStruct((slots, rows, qw), F32),
            jax.ShapeDtypeStruct((slots, rows, kw), F32),
        ),
        in_specs=[block(width)] + [whole(a) for a in (attn_gain, w_query, w_key, w_value, qg, kg, cosine, sine)],
        out_specs=(block(width), block(qw), block(2 * kw), block(qw), block(kw)),
        compiler_params=pltpu.CompilerParams(vmem_limit_bytes=56 * MIB),
        name="project",
    )(x, attn_gain, w_query, w_key, w_value, qg, kg, cosine, sine)


def attend_kernel(
    sc_ref, q_ref, kv_ref, x_ref, wo_ref, fg_ref, wr_ref, routes_ref,
    mixed_ref, invl_ref, after_ref, xg_ref, soft_ref, acc,
):
    slot, tile = pl.program_id(0), pl.program_id(1)
    slots, tiles = pl.num_programs(0), pl.num_programs(1)
    rows = q_ref.shape[1]
    here = sc_ref[slots]
    length = sc_ref[slot]
    live = here * rows < length
    chunk = 2 * rows
    chunks = (here + 2) // 2

    @pl.when(tile == 0)
    def _():
        acc[...] = jnp.zeros_like(acc)

    @pl.when(live)
    def _():
        q4 = stack_heads(q_ref[0], True).astype(BF16)

        def step(index, carry, masked):
            mass, total = carry
            pair = kv_ref[pl.ds(2 * index, 2), 0]
            keys = pair[:, :, :LANES].reshape(chunk, LANES)
            values = pair[:, :, LANES:].reshape(chunk, LANES)
            weight = jnp.exp2(dot_nt(q4, keys) * EXP2_SCALE)
            if masked:
                at = lax.rem(row_of(weight.shape), rows) + here * rows
                weight = jnp.where(lane_of(weight.shape) + index * chunk <= at, weight, 0.0)
            for part in range(chunk // LANES):
                mass = mass + weight[:, part * LANES : (part + 1) * LANES]
            return mass, total + dot(weight.astype(BF16), values)

        blank = jnp.zeros((4 * rows, LANES), F32)
        carry = lax.fori_loop(0, chunks - 1, lambda i, c: step(i, c, False), (blank, blank))
        mass, total = step(chunks - 1, carry, True)
        inverse = 1.0 / jnp.sum(mass, axis=-1, keepdims=True)
        mixed = unstack_heads(total * inverse).astype(BF16)
        mixed_ref[0] = mixed
        invl_ref[0] = unstack_heads(jnp.broadcast_to(inverse, total.shape))
        acc[...] += dot(mixed, wo_ref[...])

    @pl.when(jnp.logical_not(live))
    def _():
        mixed_ref[...] = jnp.zeros_like(mixed_ref)
        invl_ref[...] = jnp.zeros_like(invl_ref)

    @pl.when(tile == tiles - 1)
    def _():
        width = x_ref.shape[2]
        valid = (row_of((rows, 1)) + here * rows < length).astype(F32)
        after = x_ref[0].astype(F32) + valid * acc[...]
        after_ref[0] = after
        unit, unused = rms_parts(after)
        normed = (unit * fg_ref[...]).astype(BF16)
        xg_ref[0, :, :width] = normed
        logits = dot(normed, wr_ref[...])
        lanes = lane_of(logits.shape)
        routes = routes_ref[0]
        chosen = lanes == routes[:, 0:1]
        for k in range(1, routes.shape[1]):
            chosen = chosen | (lanes == routes[:, k : k + 1])
        top = jnp.max(jnp.where(chosen, logits, -1e30), axis=-1, keepdims=True)
        weight = jnp.where(chosen, jnp.exp(jnp.minimum(logits - top, 0.0)), 0.0)
        soft = weight / jnp.sum(weight, axis=-1, keepdims=True)
        soft_ref[0] = soft
        gates = soft * valid
        high = gates.astype(BF16).astype(F32)
        half = logits.shape[1] // 2
        xg_ref[0, :, width:] = (high + pltpu.roll(gates - high, half, 1)).astype(BF16)


def attend(scalars, q, kv, x, w_out, ffn_gain, router, routes):
    slots, rows, width = x.shape
    group = kv.shape[0]
    qw = q.shape[2]
    tiles = qw // 256
    row = lambda lanes: pl.BlockSpec((1, rows, lanes), lambda s, b, sc: (s, 0, 0))
    tile = pl.BlockSpec((1, rows, 256), lambda s, b, sc: (s, 0, b))
    return pl.pallas_call(
        attend_kernel,
        grid_spec=pltpu.PrefetchScalarGridSpec(
            num_scalar_prefetch=1,
            grid=(slots, tiles),
            in_specs=[
                tile,
                pl.BlockSpec((group, 1, rows, 256), lambda s, b, sc: (0, s, 0, b)),
                row(width),
                pl.BlockSpec((256, width), lambda s, b, sc: (b, 0)),
                pl.BlockSpec(ffn_gain.shape, lambda s, b, sc: (0, 0)),
                pl.BlockSpec(router.shape, lambda s, b, sc: (0, 0)),
                row(routes.shape[2]),
            ],
            out_specs=(tile, tile, row(width), row(width + LANES), row(LANES)),
            scratch_shapes=[pltpu.VMEM((rows, width), F32)],
        ),
        out_shape=(
            jax.ShapeDtypeStruct((slots, rows, qw), BF16),
            jax.ShapeDtypeStruct((slots, rows, qw), F32),
            jax.ShapeDtypeStruct((slots, rows, width), F32),
            jax.ShapeDtypeStruct((slots, rows, width + LANES), BF16),
            jax.ShapeDtypeStruct((slots, rows, LANES), F32),
        ),
        compiler_params=pltpu.CompilerParams(vmem_limit_bytes=56 * MIB),
        name="attend",
    )(scalars, q, kv, x, w_out, ffn_gain, router, routes)


def row_gates(picked, first, owned):
    lanes = lane_of(picked.shape)
    expert = row_of(picked.shape) // PAIR + first
    half = picked.shape[1] // 2
    mine = (lanes == expert) | (lanes == expert + half)
    return jnp.sum(jnp.where(mine, picked, 0.0), axis=-1, keepdims=True)


def experts_forward_kernel(
    sc_ref, xg_ref, wg_ref, wu_ref, wd_ref, pick_ref, xe_ref, gp_ref, up_ref, hid_ref, part_ref, gates, ybuf
):
    sources, unused, rows, wide = xg_ref.shape
    owned, width, eff = wg_ref.shape
    pairs = sources // 2
    double = 2 * rows
    first = sc_ref[pl.num_programs(0)] * owned
    tokens = xg_ref[...].reshape(sources * rows, wide)
    slab = tokens[:, width:]
    chosen = (lane_of((8, LANES)) == row_of((8, LANES)) + first).astype(BF16)
    routed = dot_nt(chosen, slab) > 0.0
    before = row_of((double, double))
    after = lane_of((double, double))
    count = ((before < after) & (before // rows == after // rows)).astype(BF16)
    place = lax.broadcasted_iota(jnp.int32, (PAIR, double), 0)
    offset = (lane_of((8, double)) // rows) * MOST
    for p in range(pairs):
        mask = routed[:, p * double : (p + 1) * double]
        rank = dot(mask.astype(F32).astype(BF16), count).astype(jnp.int32) + offset
        rank = jnp.where(mask, rank, -1)
        pick = jnp.concatenate(
            [(place == rank[e : e + 1, :]).astype(F32).astype(BF16) for e in range(owned)], axis=0
        )
        pick_ref[0, p] = pick
        block = tokens[p * double : (p + 1) * double]
        picked = dot(pick, block[:, :width]).astype(BF16)
        scale = row_gates(dot(pick, block[:, width:]), first, owned)
        for e in range(owned):
            xe_ref[0, e, p * PAIR : (p + 1) * PAIR] = picked[e * PAIR : (e + 1) * PAIR]
            gates[e, p * PAIR : (p + 1) * PAIR] = jnp.broadcast_to(
                scale[e * PAIR : (e + 1) * PAIR], (PAIR, LANES)
            )

    def one(e, carry):
        rows_in = xe_ref[0, e]
        gate_part = dot(rows_in, wg_ref[e])
        up_part = dot(rows_in, wu_ref[e])
        gp_ref[0, e] = gate_part
        up_ref[0, e] = up_part
        hidden = (gate_part * jax.nn.sigmoid(gate_part) * up_part).astype(BF16)
        hid_ref[0, e] = hidden
        result = (dot(hidden, wd_ref[e]) * gates[e][:, 0:1]).astype(BF16)
        for p in range(pairs):
            ybuf[p, e] = result[p * PAIR : (p + 1) * PAIR]
        return carry

    lax.fori_loop(0, owned, one, 0)
    for p in range(pairs):
        back = dot_tn(pick_ref[0, p], ybuf[p].reshape(owned * PAIR, width))
        part_ref[2 * p : 2 * p + 2, 0] = back.astype(BF16).reshape(2, rows, width)


def step_spec(shape):
    return pl.BlockSpec((1,) + shape, lambda s, j, sc: (s * pl.num_programs(1) + j,) + (0,) * len(shape))


def resident(array):
    return pl.BlockSpec(array.shape, lambda s, j, sc: (0,) * array.ndim, pipeline_mode=pl.Buffered(1))


def experts_forward(scalars, tokens, w_gate, w_up, w_down):
    group, slots, rows, wide = tokens.shape
    owned, width, eff = w_gate.shape
    sources = 8
    parts = group // sources
    pairs = sources // 2
    steps = slots * parts
    held = pairs * PAIR
    source = lambda lanes: pl.BlockSpec((sources, 1, rows, lanes), lambda s, j, sc: (j, s, 0, 0))
    saved = [
        ((pairs, owned * PAIR, 2 * rows), BF16),
        ((owned, held, width), BF16),
        ((owned, held, eff), F32),
        ((owned, held, eff), F32),
        ((owned, held, eff), BF16),
    ]
    return pl.pallas_call(
        experts_forward_kernel,
        grid_spec=pltpu.PrefetchScalarGridSpec(
            num_scalar_prefetch=1,
            grid=(slots, parts),
            in_specs=[source(wide), resident(w_gate), resident(w_up), resident(w_down)],
            out_specs=tuple(step_spec(shape) for shape, unused in saved) + (source(width),),
            scratch_shapes=[
                pltpu.VMEM((owned, held, LANES), F32),
                pltpu.VMEM((pairs, owned, PAIR, width), BF16),
            ],
        ),
        out_shape=tuple(jax.ShapeDtypeStruct((steps,) + shape, kind) for shape, kind in saved)
        + (jax.ShapeDtypeStruct((group, slots, rows, width), BF16),),
        compiler_params=pltpu.CompilerParams(vmem_limit_bytes=60 * MIB),
        name="experts_forward",
    )(scalars, tokens, w_gate, w_up, w_down)


def experts_backward_kernel(
    sc_ref, dy_ref, slab_ref, pick_ref, gp_ref, up_ref, hid_ref, wg_ref, wu_ref, wd_ref,
    part_ref, dyw_ref, gg_ref, ug_ref, gates, dye, dxb,
):
    sources, unused, rows, width = dy_ref.shape
    owned = wg_ref.shape[0]
    pairs = sources // 2
    double = 2 * rows
    first = sc_ref[pl.num_programs(0)] * owned
    for p in range(pairs):
        pick = pick_ref[0, p]
        picked = dot(pick, dy_ref[2 * p : 2 * p + 2].reshape(double, width)).astype(BF16)
        scale = row_gates(dot(pick, slab_ref[2 * p : 2 * p + 2].reshape(double, LANES)), first, owned)
        for e in range(owned):
            dye[e, p * PAIR : (p + 1) * PAIR] = picked[e * PAIR : (e + 1) * PAIR]
            gates[e, p * PAIR : (p + 1) * PAIR] = jnp.broadcast_to(
                scale[e * PAIR : (e + 1) * PAIR], (PAIR, LANES)
            )

    def one(e, carry):
        grad_rows = dye[e]
        scale = gates[e][:, 0:1]
        plain = dot_nt(grad_rows, wd_ref[e])
        gate_part, up_part = gp_ref[0, e], up_ref[0, e]
        soft_grad = jnp.sum(plain * hid_ref[0, e].astype(F32), axis=-1, keepdims=True)
        hidden_grad = plain * scale
        sigma = jax.nn.sigmoid(gate_part)
        gate_grad = (hidden_grad * up_part * sigma * (1.0 + gate_part * (1.0 - sigma))).astype(BF16)
        up_grad = (hidden_grad * gate_part * sigma).astype(BF16)
        gg_ref[0, e] = gate_grad
        ug_ref[0, e] = up_grad
        dyw_ref[0, e] = (grad_rows.astype(F32) * scale).astype(BF16)
        input_grad = (dot_nt(gate_grad, wg_ref[e]) + dot_nt(up_grad, wu_ref[e])).astype(BF16)
        lanes = lane_of((pairs * PAIR, LANES))
        high = soft_grad.astype(BF16).astype(F32)
        spot = jnp.where(
            lanes == first + e, high, jnp.where(lanes == first + e + LANES // 2, soft_grad - high, 0.0)
        ).astype(BF16)
        for p in range(pairs):
            dxb[p, e, :, :width] = input_grad[p * PAIR : (p + 1) * PAIR]
            dxb[p, e, :, width:] = spot[p * PAIR : (p + 1) * PAIR]
        return carry

    lax.fori_loop(0, owned, one, 0)
    for p in range(pairs):
        back = dot_tn(pick_ref[0, p], dxb[p].reshape(owned * PAIR, width + LANES))
        part_ref[2 * p : 2 * p + 2, 0] = back.astype(BF16).reshape(2, rows, width + LANES)


def experts_backward(scalars, grads, tokens, pick, gate_part, up_part, hidden, w_gate, w_up, w_down):
    group, slots, rows, width = grads.shape
    owned, unused, eff = w_gate.shape
    sources = 8
    parts = group // sources
    pairs = sources // 2
    steps = slots * parts
    held = pairs * PAIR
    source = lambda lanes, at: pl.BlockSpec((sources, 1, rows, lanes), lambda s, j, sc: (j, s, 0, at))
    return pl.pallas_call(
        experts_backward_kernel,
        grid_spec=pltpu.PrefetchScalarGridSpec(
            num_scalar_prefetch=1,
            grid=(slots, parts),
            in_specs=[
                source(width, 0),
                source(LANES, width // LANES),
                step_spec((pairs, owned * PAIR, 2 * rows)),
                step_spec((owned, held, eff)),
                step_spec((owned, held, eff)),
                step_spec((owned, held, eff)),
                resident(w_gate), resident(w_up), resident(w_down),
            ],
            out_specs=(
                source(width + LANES, 0),
                step_spec((owned, held, width)),
                step_spec((owned, held, eff)),
                step_spec((owned, held, eff)),
            ),
            scratch_shapes=[
                pltpu.VMEM((owned, held, LANES), F32),
                pltpu.VMEM((owned, held, width), BF16),
                pltpu.VMEM((pairs, owned, PAIR, width + LANES), BF16),
            ],
        ),
        out_shape=(
            jax.ShapeDtypeStruct((group, slots, rows, width + LANES), BF16),
            jax.ShapeDtypeStruct((steps, owned, held, width), BF16),
            jax.ShapeDtypeStruct((steps, owned, held, eff), BF16),
            jax.ShapeDtypeStruct((steps, owned, held, eff), BF16),
        ),
        compiler_params=pltpu.CompilerParams(vmem_limit_bytes=62 * MIB),
        name="experts_backward",
    )(scalars, grads, tokens, pick, gate_part, up_part, hidden, w_gate, w_up, w_down)


def expert_weights_kernel(xe_ref, gg_ref, ug_ref, hid_ref, dyw_ref, dg_ref, du_ref, dd_ref, ag, au, ad):
    step = pl.program_id(1)
    flat = lambda ref: ref[:, 0].reshape(ref.shape[0] * ref.shape[2], ref.shape[3])
    for acc, left, right in ((ad, hid_ref, dyw_ref), (ag, xe_ref, gg_ref), (au, xe_ref, ug_ref)):
        part = dot_tn(flat(left), flat(right))

        @pl.when(step == 0)
        def _():
            acc[...] = part

        @pl.when(step > 0)
        def _():
            acc[...] += part

    @pl.when(step == pl.num_programs(1) - 1)
    def _():
        dg_ref[0] = ag[...].astype(BF16)
        du_ref[0] = au[...].astype(BF16)
        dd_ref[0] = ad[...].astype(BF16)


def expert_weights(xe, gate_grad, up_grad, hidden, weighted):
    steps, owned, held, width = xe.shape
    eff = hidden.shape[3]
    each = 4
    block = lambda lanes: pl.BlockSpec((each, 1, held, lanes), lambda e, i: (i, e, 0, 0))
    out = lambda a, b: pl.BlockSpec((1, a, b), lambda e, i: (e, 0, 0))
    return pl.pallas_call(
        expert_weights_kernel,
        grid=(owned, steps // each),
        in_specs=[block(width), block(eff), block(eff), block(eff), block(width)],
        out_specs=(out(width, eff), out(width, eff), out(eff, width)),
        out_shape=(
            jax.ShapeDtypeStruct((owned, width, eff), BF16),
            jax.ShapeDtypeStruct((owned, width, eff), BF16),
            jax.ShapeDtypeStruct((owned, eff, width), BF16),
        ),
        scratch_shapes=[pltpu.VMEM((width, eff), F32), pltpu.VMEM((width, eff), F32), pltpu.VMEM((eff, width), F32)],
        compiler_params=pltpu.CompilerParams(vmem_limit_bytes=56 * MIB),
        name="expert_weights",
    )(xe, gate_grad, up_grad, hidden, weighted)


def attend_backward_kernel(
    sc_ref, q_ref, kv_ref, mixed_ref, invl_ref, dx_ref, soft_ref, og_ref, after_ref, fg_ref, wr_ref, wo_ref,
    dq_ref, dkv_ref, ag_ref, at_ref, lg_ref, fgg_ref, mg_s,
):
    slot, tile = pl.program_id(0), pl.program_id(1)
    slots, tiles = pl.num_programs(0), pl.num_programs(1)
    rows = q_ref.shape[1]
    here = sc_ref[slots]
    length = sc_ref[slot]
    live = here * rows < length
    chunk = 2 * rows
    chunks = (here + 2) // 2
    width = og_ref.shape[2]

    @pl.when(tile == 0)
    def _():
        valid = (row_of((rows, 1)) + here * rows < length).astype(F32)
        slab = dx_ref[0, :, width:].astype(F32)
        half = slab.shape[1] // 2
        soft = soft_ref[0]
        soft_grad = jnp.where(lane_of(slab.shape) < half, slab + pltpu.roll(slab, half, 1), 0.0)
        chosen = soft * (soft_grad - jnp.sum(soft * soft_grad, axis=-1, keepdims=True))
        logit_grad = chosen.astype(BF16)
        lg_ref[0] = logit_grad
        normed_grad = dx_ref[0, :, :width].astype(F32) + dot_nt(logit_grad, wr_ref[...])
        back, gain_grad = rms_backward(normed_grad, after_ref[0], fg_ref[...])

        @pl.when(slot == 0)
        def _():
            fgg_ref[...] = gain_grad

        @pl.when(slot > 0)
        def _():
            fgg_ref[...] += gain_grad

        after_grad = og_ref[0] + back
        ag_ref[0] = after_grad
        attn_grad = (valid * after_grad).astype(BF16)
        at_ref[0] = attn_grad
        mixed_grad = dot_nt(attn_grad, wo_ref[...]).astype(BF16)
        for t in range(mg_s.shape[0]):
            mg_s[t] = mixed_grad[:, t * 256 : (t + 1) * 256]

    dkv_ref[...] = jnp.zeros_like(dkv_ref)

    @pl.when(live)
    def _():
        q4 = stack_heads(q_ref[0], True).astype(BF16)
        do4_f = stack_heads(mg_s[tile].astype(F32) * invl_ref[0], True)
        do4 = do4_f.astype(BF16)
        product = do4_f * stack_heads(mixed_ref[0], False)
        delta = lax.dot_general(
            jnp.ones((8, LANES), F32), product, (((1,), (1,)), ((), ())),
            preferred_element_type=F32, precision=lax.Precision.HIGHEST,
        )[0:1]

        def step(index, total, masked):
            pair = kv_ref[pl.ds(2 * index, 2), 0]
            keys = pair[:, :, :LANES].reshape(chunk, LANES)
            values = pair[:, :, LANES:].reshape(chunk, LANES)
            weight = jnp.exp2(dot_nt(keys, q4) * EXP2_SCALE)
            if masked:
                at = lax.rem(lane_of(weight.shape), rows) + here * rows
                weight = jnp.where(row_of(weight.shape) + index * chunk <= at, weight, 0.0)
            pressure = dot_nt(values, do4)
            score_grad = (weight * (pressure - delta) * SCALE).astype(BF16)
            key_grad = dot(score_grad, q4)
            value_grad = dot(weight.astype(BF16), do4)
            dkv_ref[pl.ds(2 * index, 2), 0, :, :LANES] = key_grad.astype(BF16).reshape(2, rows, LANES)
            dkv_ref[pl.ds(2 * index, 2), 0, :, LANES:] = value_grad.astype(BF16).reshape(2, rows, LANES)
            return total + dot_tn(score_grad, keys)

        total = lax.fori_loop(
            0, chunks - 1, lambda i, c: step(i, c, False), jnp.zeros((4 * rows, LANES), F32)
        )
        total = step(chunks - 1, total, True)
        dq_ref[0] = unstack_heads(total).astype(BF16)

    @pl.when(jnp.logical_not(live))
    def _():
        dq_ref[...] = jnp.zeros_like(dq_ref)


def attend_backward(scalars, q, kv, mixed, invl, dx, soft, out_grad, after, ffn_gain, router, w_out):
    slots, rows, width = out_grad.shape
    group = kv.shape[0]
    qw = q.shape[2]
    tiles = qw // 256
    row = lambda lanes: pl.BlockSpec((1, rows, lanes), lambda s, b, sc: (s, 0, 0))
    tile = pl.BlockSpec((1, rows, 256), lambda s, b, sc: (s, 0, b))
    group_tile = pl.BlockSpec((group, 1, rows, 256), lambda s, b, sc: (0, s, 0, b))
    whole = lambda a: pl.BlockSpec(a.shape, lambda s, b, sc: (0, 0))
    return pl.pallas_call(
        attend_backward_kernel,
        grid_spec=pltpu.PrefetchScalarGridSpec(
            num_scalar_prefetch=1,
            grid=(slots, tiles),
            in_specs=[
                tile, group_tile, tile, tile, row(width + LANES), row(LANES), row(width), row(width),
                whole(ffn_gain), whole(router), whole(w_out),
            ],
            out_specs=(
                tile, group_tile, row(width), row(width), row(LANES),
                pl.BlockSpec((1, width), lambda s, b, sc: (0, 0)),
            ),
            scratch_shapes=[pltpu.VMEM((tiles, rows, 256), BF16)],
        ),
        out_shape=(
            jax.ShapeDtypeStruct((slots, rows, qw), BF16),
            jax.ShapeDtypeStruct(kv.shape, BF16),
            jax.ShapeDtypeStruct((slots, rows, width), F32),
            jax.ShapeDtypeStruct((slots, rows, width), BF16),
            jax.ShapeDtypeStruct((slots, rows, LANES), BF16),
            jax.ShapeDtypeStruct((1, width), F32),
        ),
        compiler_params=pltpu.CompilerParams(vmem_limit_bytes=56 * MIB),
        name="attend_backward",
    )(scalars, q, kv, mixed, invl, dx, soft, out_grad, after, ffn_gain, router, w_out)


def finish_kernel(
    dq_ref, dkv_ref, qraw_ref, kraw_ref, x_ref, ag_ref, cos_ref, sin_ref, gain_ref, qg_ref, kg_ref,
    wq_ref, wk_ref, wv_ref, h_ref, mixed_ref, at_ref, n2_ref, lg_ref,
    ig_ref, dense_ref, rt_ref, qgg_ref, kgg_ref, agg_ref, q_s, k_s, v_s,
):
    slot = pl.program_id(0)
    rows = x_ref.shape[1]
    cosine, sine = cos_ref[...], sin_ref[...]

    @pl.when(slot == 0)
    def _():
        qgg_ref[...] = jnp.zeros_like(qgg_ref)
        kgg_ref[...] = jnp.zeros_like(kgg_ref)
        agg_ref[...] = jnp.zeros_like(agg_ref)

    here = pl.ds(pl.multiple_of(slot * rows, rows), rows)
    for t in range(dq_ref.shape[2] // LANES):
        lanes = slice(t * LANES, (t + 1) * LANES)
        raw, gain = rope_backward(dq_ref[0, :, lanes].astype(F32), qraw_ref[0, :, lanes], qg_ref[...], cosine, sine)
        q_s[here, lanes] = raw.astype(BF16)
        qgg_ref[...] += gain
    for t in range(kraw_ref.shape[2] // LANES):
        lanes = slice(t * LANES, (t + 1) * LANES)
        at = 2 * t * LANES
        grad = dkv_ref[0, :, at : at + LANES].astype(BF16).astype(F32)
        raw, gain = rope_backward(grad, kraw_ref[0, :, lanes], kg_ref[...], cosine, sine)
        k_s[here, lanes] = raw.astype(BF16)
        kgg_ref[...] += gain
        v_s[here, lanes] = dkv_ref[0, :, at + LANES : at + 2 * LANES].astype(BF16)
    normed_grad = dot_nt(q_s[here], wq_ref[...]) + dot_nt(k_s[here], wk_ref[...]) + dot_nt(v_s[here], wv_ref[...])
    back, gain = rms_backward(normed_grad, x_ref[0].astype(F32), gain_ref[...])
    agg_ref[...] += gain
    ig_ref[0] = ag_ref[0] + back

    @pl.when(slot == pl.num_programs(0) - 1)
    def _():
        flat = lambda ref: ref[...].reshape(ref.shape[0] * ref.shape[1], ref.shape[2])
        shards, unused, shard_rows, width = dense_ref.shape
        h = flat(h_ref)
        half = width // 2

        def put(index, lanes, value):
            dense_ref[:, index, :, lanes] = value.astype(BF16).reshape(shards, shard_rows, value.shape[1])

        put(0, slice(0, width), dot_tn(h, q_s[...]))
        put(1, slice(0, half), dot_tn(h, k_s[...]))
        put(1, slice(half, width), dot_tn(h, v_s[...]))
        put(2, slice(0, width), dot_tn(flat(mixed_ref), flat(at_ref)))
        rt_ref[...] = dot_tn(flat(n2_ref), flat(lg_ref))


def finish(dq, dkv, qraw, kraw, x, after_grad, cosine, sine, attn_gain, qg, kg, wq, wk, wv, h, mixed, attn_grad, n2, lg):
    slots, rows, width = x.shape
    qw, kw = wq.shape[1], wk.shape[1]
    shards = 8
    row = lambda lanes: pl.BlockSpec((1, rows, lanes), lambda s: (s, 0, 0))
    whole = lambda a: pl.BlockSpec(a.shape, lambda s: (0,) * a.ndim)
    lanes_out = pl.BlockSpec((1, LANES), lambda s: (0, 0))
    return pl.pallas_call(
        finish_kernel,
        grid=(slots,),
        in_specs=[row(qw), row(2 * kw), row(qw), row(kw), row(width), row(width)]
        + [whole(a) for a in (cosine, sine, attn_gain, qg, kg, wq, wk, wv, h, mixed, attn_grad)]
        + [pl.BlockSpec((slots, rows, width), lambda s: (0, 0, 0)), whole(lg)],
        out_specs=(
            row(width),
            pl.BlockSpec((shards, 3, width // shards, width), lambda s: (0, 0, 0, 0)),
            pl.BlockSpec((width, LANES), lambda s: (0, 0)),
            lanes_out, lanes_out, pl.BlockSpec((1, width), lambda s: (0, 0)),
        ),
        out_shape=(
            jax.ShapeDtypeStruct((slots, rows, width), F32),
            jax.ShapeDtypeStruct((shards, 3, width // shards, width), BF16),
            jax.ShapeDtypeStruct((width, LANES), F32),
            jax.ShapeDtypeStruct((1, LANES), F32),
            jax.ShapeDtypeStruct((1, LANES), F32),
            jax.ShapeDtypeStruct((1, width), F32),
        ),
        scratch_shapes=[
            pltpu.VMEM((slots * rows, qw), BF16),
            pltpu.VMEM((slots * rows, kw), BF16),
            pltpu.VMEM((slots * rows, kw), BF16),
        ],
        compiler_params=pltpu.CompilerParams(vmem_limit_bytes=60 * MIB),
        name="finish",
    )(dq, dkv, qraw, kraw, x, after_grad, cosine, sine, attn_gain, qg, kg, wq, wk, wv, h, mixed, attn_grad, n2, lg)


def remote(src, dst, ss, rs, dev):
    return pltpu.make_async_remote_copy(src_ref=src, dst_ref=dst, send_sem=ss, recv_sem=rs, device_id=dev, device_id_type=MESH)

def ag_kernel(x_ref, o_ref, lsem, ss, rs):
    z = lax.axis_index("dp"); c = lax.axis_index("context"); y = lax.axis_index("experts")
    cs = c + 1 - 2 * lax.rem(c, 2)
    cx = lax.rem(c + 2, 4)
    yy = 1 - y
    sib, xn, yn = (z, cs, y), (z, cx, y), (z, c, yy)
    me = c * 2 + y
    gx = cx * 2 + y; gy = c * 2 + yy; gd = cx * 2 + yy
    bar = pltpu.get_barrier_semaphore()
    for d in (sib, xn, yn):
        pl.semaphore_signal(bar, inc=1, device_id=d, device_id_type=MESH)
    pl.semaphore_wait(bar, 3)
    n = x_ref.shape[0]
    h = n // 2
    loc = [pltpu.make_async_copy(x_ref.at[s], o_ref.at[me, s], lsem.at[s]) for s in range(n)]
    sx = [remote(x_ref.at[s], o_ref.at[me, s], ss.at[0, s], rs.at[0, s], xn) for s in range(n)]
    sy = [remote(x_ref.at[s], o_ref.at[me, s], ss.at[1, s], rs.at[1, s], yn) for s in range(n)]
    sc = [remote(x_ref.at[s], o_ref.at[me, s], ss.at[2, s], rs.at[2, s], sib) for s in range(n)]
    fx = [remote(o_ref.at[gx, s], o_ref.at[gx, s], ss.at[3, s], rs.at[3, s], sib) for s in range(n)]
    fy = [remote(o_ref.at[gy, s], o_ref.at[gy, s], ss.at[4, s], rs.at[4, s], sib) for s in range(n)]
    fd = [remote(o_ref.at[gd, s], o_ref.at[gd, s], ss.at[5, s], rs.at[5, s], sib) for s in range(n)]
    dg = [remote(o_ref.at[gx, s], o_ref.at[gx, s], ss.at[6, s], rs.at[6, s], yn) if s < h else
          remote(o_ref.at[gy, s], o_ref.at[gy, s], ss.at[6, s], rs.at[6, s], xn) for s in range(n)]
    for i in range(n):
        sx[i].start()
        sy[(i + h) % n].start()
    for s in range(n):
        sc[s].start()
        loc[s].start()
    for i in range(n):
        a = i; b = (i + h) % n
        sx[a].wait_recv()
        if a < h: dg[a].start()
        fx[a].start()
        sy[b].wait_recv()
        if b >= h: dg[b].start()
        fy[b].start()
    for i in range(h):
        for s in (i, i + h):
            dg[s].wait_recv(); fd[s].start()
    for s in range(n):
        sc[s].wait_recv(); fx[s].wait_recv(); fy[s].wait_recv(); fd[s].wait_recv()
        loc[s].wait()
        for k in (sx, sy, sc, fx, fy, fd, dg): k[s].wait_send()

def all_gather(x, cid):
    n = x.shape[0]
    return pl.pallas_call(ag_kernel,
        out_shape=jax.ShapeDtypeStruct((8,) + x.shape, x.dtype),
        in_specs=[pl.BlockSpec(memory_space=pl.ANY)], out_specs=pl.BlockSpec(memory_space=pl.ANY),
        scratch_shapes=[pltpu.SemaphoreType.DMA((n,)), pltpu.SemaphoreType.DMA((7, n)), pltpu.SemaphoreType.DMA((7, n))],
        compiler_params=pltpu.CompilerParams(collective_id=cid, has_side_effects=True), name="ag")(x)

def rs_kernel(p_ref, o_ref, own, other, sb, q, dx, dy, rx, ry, lsem, ss, rs):
    z = lax.axis_index("dp"); c = lax.axis_index("context"); y = lax.axis_index("experts")
    core = lax.rem(c, 2)
    cs = c + 1 - 2 * core
    cx = lax.rem(c + 2, 4)
    yy = 1 - y
    sib, xn, yn = (z, cs, y), (z, cx, y), (z, c, yy)
    bar = pltpu.get_barrier_semaphore()
    for d in (sib, xn, yn):
        pl.semaphore_signal(bar, inc=1, device_id=d, device_id_type=MESH)
    n = p_ref.shape[1]
    h = n // 2
    chips = [(cx, yy), (cx, y), (c, yy), (c, y)]
    idx = [a * 2 + b for a, b in chips]
    oth = [(a + 1 - 2 * core) * 2 + b for a, b in chips]
    ld = [[pltpu.make_async_copy(p_ref.at[idx[k], s], own.at[k, s], lsem.at[k, s]) for s in range(n)] for k in range(4)]
    st = [[remote(p_ref.at[oth[k], s], sb.at[k, s], ss.at[k, s], rs.at[k, s], sib) for s in range(n)] for k in range(4)]
    for k in range(4):
        for s in range(n):
            ld[k][s].start()
    pl.semaphore_wait(bar, 3)
    for k in range(4):
        for s in range(n):
            st[k][s].start()
    dgs = [remote(q.at[0, s], dx.at[s], ss.at[4, s], rs.at[4, s], xn) if s < h else
           remote(q.at[0, s], dy.at[s - h], ss.at[4, s], rs.at[4, s], yn) for s in range(n)]
    tx = [remote(q.at[1, s], rx.at[s], ss.at[5, s], rs.at[5, s], xn) for s in range(n)]
    ty = [remote(q.at[2, s], ry.at[s], ss.at[6, s], rs.at[6, s], yn) for s in range(n)]
    f32 = jnp.float32
    def pair(k, s):
        ld[k][s].wait(); st[k][s].wait_recv()
        return own[k, s].astype(f32) + sb[k, s].astype(f32)
    for i in range(h):
        for s in (i, i + h):
            q[0, s] = pair(0, s).astype(q.dtype); dgs[s].start()
    for i in range(h):
        q[1, i] = pair(1, i).astype(q.dtype); tx[i].start()
        q[2, i + h] = pair(2, i + h).astype(q.dtype); ty[i + h].start()
    for i in range(h):
        a = pair(2, i)
        dgs[i].wait_recv()
        q[2, i] = (a + dx[i].astype(f32)).astype(q.dtype); ty[i].start()
        b = pair(1, i + h)
        dgs[i + h].wait_recv()
        q[1, i + h] = (b + dy[i].astype(f32)).astype(q.dtype); tx[i + h].start()
    for i in range(h):
        for s in (i, i + h):
            a = pair(3, s)
            tx[s].wait_recv(); ty[s].wait_recv()
            o_ref[s] = (a + rx[s].astype(f32) + ry[s].astype(f32)).astype(o_ref.dtype)
    for s in range(n):
        for k in st: k[s].wait_send()
        for k in (dgs, tx, ty): k[s].wait_send()

def reduce_scatter(p, cid, dt):
    _, n, r, w = p.shape
    h = n // 2
    V = pltpu.VMEM
    return pl.pallas_call(rs_kernel,
        out_shape=jax.ShapeDtypeStruct((n, r, w), dt),
        in_specs=[pl.BlockSpec(memory_space=pl.ANY)], out_specs=pl.BlockSpec(memory_space=pltpu.VMEM),
        scratch_shapes=[V((4, n, r, w), p.dtype), V((1, 8, 128), p.dtype), V((4, n, r, w), p.dtype), V((3, n, r, w), p.dtype),
            V((h, r, w), p.dtype), V((h, r, w), p.dtype), V((n, r, w), p.dtype), V((n, r, w), p.dtype),
            pltpu.SemaphoreType.DMA((4, n)), pltpu.SemaphoreType.DMA((7, n)), pltpu.SemaphoreType.DMA((7, n))],
        compiler_params=pltpu.CompilerParams(collective_id=cid, has_side_effects=True, vmem_limit_bytes=60 * 2**20), name="rs")(p)


def plane_gather(rows, fast, number):
    if fast:
        return all_gather(rows, number)
    return lax.all_gather(rows, ("context", "experts"), axis=0, tiled=False)


def plane_scatter(parts, fast, number):
    if fast:
        return reduce_scatter(parts, number, F32)
    return lax.psum_scatter(parts, ("context", "experts"), scatter_dimension=0, tiled=False).astype(F32)


def per_device(
    fast, block_input, teacher, lengths, routes, w_query, w_key, w_value, w_out, query_gain, key_gain,
    attn_gain, ffn_gain, w_router, w_gate, w_up, w_down,
):
    slots, rows, width = block_input.shape
    expert_total = w_router.shape[1]
    group = lax.axis_size(("context", "experts"))
    here = lax.axis_index(("context", "experts"))
    span = rows * group
    slot_lengths = lax.dynamic_slice_in_dim(lengths, lax.axis_index("dp") * slots, slots)
    scalars = jnp.concatenate([slot_lengths, here[None]]).astype(jnp.int32)
    positions = here * rows + jnp.arange(rows, dtype=jnp.int32)
    valid = (positions[None, :] < slot_lengths[:, None]).astype(F32)[..., None]
    count_all = jnp.sum(lengths).astype(F32)
    positions_all = lengths.shape[0] * span

    half = HEAD // 2
    lanes = jnp.arange(LANES, dtype=jnp.int32)
    inverse = 10000.0 ** (-((lanes % half).astype(F32) * 2.0 / HEAD))
    turned = positions.astype(F32)[:, None] * inverse[None, :]
    cosine = jnp.cos(turned)
    sine = jnp.sin(turned) * jnp.where(lanes % HEAD < half, -1.0, 1.0)[None, :]
    qg = jnp.concatenate([query_gain, query_gain])[None, :]
    kg = jnp.concatenate([key_gain, key_gain])[None, :]
    ag, fg = attn_gain[None, :], ffn_gain[None, :]
    router = jnp.pad(w_router, ((0, 0), (0, LANES - expert_total)))

    h, q, kv_local, qraw, kraw = project(block_input, ag, w_query, w_key, w_value, qg, kg, cosine, sine)
    kv = plane_gather(kv_local, fast, 1)
    mixed, invl, after, xg, soft = attend(scalars, q, kv, block_input, w_out, fg, router, routes)
    tokens = plane_gather(xg, fast, 2)
    pick, xe, gate_part, up_part, hidden, part = experts_forward(scalars, tokens, w_gate, w_up, w_down)
    output = after + plane_scatter(part, fast, 3)
    difference = valid * (output - teacher.astype(F32))
    loss_part = jnp.sum(difference * difference)
    out_grad = difference * (positions_all / count_all)
    grads = plane_gather(out_grad.astype(BF16), fast, 4)
    dpart, weighted, gate_grad, up_grad = experts_backward(
        scalars, grads, tokens, pick, gate_part, up_part, hidden, w_gate, w_up, w_down
    )
    expert_grads = lax.psum(expert_weights(xe, gate_grad, up_grad, hidden, weighted), "dp")
    dx = plane_scatter(dpart, fast, 5)
    dq, dkv_parts, after_grad, attn_grad, logit_grad, ffn_gain_grad = attend_backward(
        scalars, q, kv, mixed, invl, dx, soft, out_grad, after, fg, router, w_out
    )
    dkv = plane_scatter(dkv_parts, fast, 6)
    input_grad, dense, router_grad, query_gg, key_gg, attn_gg = finish(
        dq, dkv, qraw, kraw, block_input, after_grad, cosine, sine, ag, qg, kg,
        w_query, w_key, w_value, h, mixed, attn_grad, xg, logit_grad,
    )
    if fast:
        shards, kinds, shard_rows, unused = dense.shape
        shard = reduce_scatter(dense.reshape(shards, 2 * kinds, shard_rows // 2, width), 7, F32)
        shard = lax.psum(shard, "dp").astype(BF16)
        dense = all_gather(shard, 8).reshape(shards, kinds, shard_rows, width)
    else:
        dense = lax.psum(dense, ("dp", "context", "experts"))
    dense = [dense[:, k].reshape(width, width).astype(F32) for k in range(3)]
    small = lax.psum(
        (
            query_gg[0, :HEAD] + query_gg[0, HEAD:], key_gg[0, :HEAD] + key_gg[0, HEAD:], attn_gg[0],
            ffn_gain_grad[0], router_grad[:, :expert_total], loss_part,
        ),
        ("dp", "context", "experts"),
    )
    key_width = w_key.shape[1]
    return (
        small[5] / (count_all * width),
        output.astype(BF16),
        input_grad,
        dense[0],
        dense[1][:, :key_width],
        dense[1][:, key_width:],
        dense[2],
        small[0], small[1], small[2], small[3], small[4],
        expert_grads[0].astype(F32), expert_grads[1].astype(F32), expert_grads[2].astype(F32),
    )


def solution(mesh):
    fast = mesh.shape["context"] == 4 and mesh.shape["experts"] == 2
    rows = P("dp", ("context", "experts"), None)
    owned = P(("context", "experts"), None, None)
    return jax.shard_map(
        functools.partial(per_device, fast),
        mesh=mesh,
        in_specs=(rows, rows, P(), rows) + (P(),) * 9 + (owned,) * 3,
        out_specs=(P(), rows, rows) + (P(),) * 9 + (owned,) * 3,
        check_vma=False,
    )
```

```python
import functools
import math

import jax
import jax.numpy as jnp
from jax import lax
from jax.experimental import pallas as pl
from jax.experimental.pallas import tpu as pltpu
from jax.sharding import PartitionSpec as P

EPSILON = 1e-06
MOST = 40
PAIR = 2 * MOST
LANES = 128
HEAD = 64
SCALE = 0.125
EXP2_SCALE = 0.125 * math.log2(math.e)
MIB = 2**20
MESH = pl.DeviceIdType.MESH
F32 = jnp.float32
BF16 = jnp.bfloat16


def dot(a, b):
    return lax.dot_general(a, b, (((1,), (0,)), ((), ())), preferred_element_type=F32)


def dot_nt(a, b):
    return lax.dot_general(a, b, (((1,), (1,)), ((), ())), preferred_element_type=F32)


def dot_tn(a, b):
    return lax.dot_general(a, b, (((0,), (0,)), ((), ())), preferred_element_type=F32)


def lane_of(shape):
    return lax.broadcasted_iota(jnp.int32, shape, len(shape) - 1)


def row_of(shape):
    return lax.broadcasted_iota(jnp.int32, shape, len(shape) - 2)


def swap_halves(tile):
    low = lax.rem(lane_of(tile.shape), HEAD) < HEAD // 2
    return jnp.where(low, pltpu.roll(tile, LANES - HEAD // 2, 1), pltpu.roll(tile, HEAD // 2, 1))


def head_mean(tile):
    low = lane_of(tile.shape) < HEAD
    first = jnp.sum(jnp.where(low, tile, 0.0), axis=-1, keepdims=True)
    second = jnp.sum(jnp.where(low, 0.0, tile), axis=-1, keepdims=True)
    return jnp.where(low, first, second) * (1.0 / HEAD)


def rope_forward(raw, gain, cosine, sine):
    normed = raw * lax.rsqrt(head_mean(raw * raw) + EPSILON) * gain
    return normed * cosine + swap_halves(normed) * sine


def rope_backward(grad, raw, gain, cosine, sine):
    inverse = lax.rsqrt(head_mean(raw * raw) + EPSILON)
    unit = raw * inverse
    normed_grad = grad * cosine - swap_halves(grad) * sine
    gain_grad = jnp.sum(normed_grad * unit, axis=0, keepdims=True)
    unit_grad = normed_grad * gain
    return inverse * (unit_grad - unit * head_mean(unit_grad * unit)), gain_grad


def rms_parts(rows):
    inverse = lax.rsqrt(jnp.mean(rows * rows, axis=-1, keepdims=True) + EPSILON)
    return rows * inverse, inverse


def rms_backward(grad, rows, gain):
    unit, inverse = rms_parts(rows)
    gain_grad = jnp.sum(grad * unit, axis=0, keepdims=True)
    unit_grad = grad * gain
    back = inverse * (unit_grad - unit * jnp.mean(unit_grad * unit, axis=-1, keepdims=True))
    return back, gain_grad


def stack_heads(tile, masked):
    first, second = tile[:, :LANES].astype(F32), tile[:, LANES:].astype(F32)
    parts = [first, pltpu.roll(first, HEAD, 1), pltpu.roll(second, HEAD, 1), second]
    if masked:
        low = lane_of(first.shape) < HEAD
        parts = [jnp.where(low, part, 0.0) for part in parts[:2]] + [
            jnp.where(low, 0.0, part) for part in parts[2:]
        ]
    return jnp.concatenate(parts, axis=0)


def unstack_heads(rows):
    count = rows.shape[0] // 4
    one, two, three, four = (rows[k * count : (k + 1) * count] for k in range(4))
    low = lane_of(one.shape) < HEAD
    return jnp.concatenate(
        [
            jnp.where(low, one, pltpu.roll(two, HEAD, 1)),
            jnp.where(low, pltpu.roll(three, HEAD, 1), four),
        ],
        axis=1,
    )


def project_kernel(
    x_ref, gain_ref, wq_ref, wk_ref, wv_ref, qg_ref, kg_ref, cos_ref, sin_ref,
    h_ref, q_ref, kv_ref, qraw_ref, kraw_ref,
):
    slots, rows, width = x_ref.shape
    x = x_ref[...].astype(F32).reshape(slots * rows, width)
    unit, unused = rms_parts(x)
    normed = (unit * gain_ref[...]).astype(BF16)
    h_ref[...] = normed.reshape(slots, rows, width)
    cosine = jnp.concatenate([cos_ref[...]] * slots, axis=0)
    sine = jnp.concatenate([sin_ref[...]] * slots, axis=0)
    q_raw = dot(normed, wq_ref[...])
    qraw_ref[...] = q_raw.reshape(qraw_ref.shape)
    for tile in range(q_raw.shape[1] // LANES):
        lanes = slice(tile * LANES, (tile + 1) * LANES)
        turned = rope_forward(q_raw[:, lanes], qg_ref[...], cosine, sine)
        q_ref[:, :, lanes] = turned.astype(BF16).reshape(slots, rows, LANES)
    k_raw = dot(normed, wk_ref[...])
    kraw_ref[...] = k_raw.reshape(kraw_ref.shape)
    value = dot(normed, wv_ref[...]).astype(BF16)
    for tile in range(k_raw.shape[1] // LANES):
        lanes = slice(tile * LANES, (tile + 1) * LANES)
        turned = rope_forward(k_raw[:, lanes], kg_ref[...], cosine, sine)
        at = 2 * tile * LANES
        kv_ref[:, :, at : at + LANES] = turned.astype(BF16).reshape(slots, rows, LANES)
        kv_ref[:, :, at + LANES : at + 2 * LANES] = value[:, lanes].reshape(slots, rows, LANES)


def project(x, attn_gain, w_query, w_key, w_value, qg, kg, cosine, sine):
    slots, rows, width = x.shape
    step = 2
    block = lambda lanes: pl.BlockSpec((step, rows, lanes), lambda i: (i, 0, 0))
    whole = lambda a: pl.BlockSpec(a.shape, lambda i: (0,) * a.ndim)
    qw, kw = w_query.shape[1], w_key.shape[1]
    return pl.pallas_call(
        project_kernel,
        grid=(slots // step,),
        out_shape=(
            jax.ShapeDtypeStruct((slots, rows, width), BF16),
            jax.ShapeDtypeStruct((slots, rows, qw), BF16),
            jax.ShapeDtypeStruct((slots, rows, 2 * kw), BF16),
            jax.ShapeDtypeStruct((slots, rows, qw), F32),
            jax.ShapeDtypeStruct((slots, rows, kw), F32),
        ),
        in_specs=[block(width)] + [whole(a) for a in (attn_gain, w_query, w_key, w_value, qg, kg, cosine, sine)],
        out_specs=(block(width), block(qw), block(2 * kw), block(qw), block(kw)),
        compiler_params=pltpu.CompilerParams(vmem_limit_bytes=56 * MIB),
        name="project",
    )(x, attn_gain, w_query, w_key, w_value, qg, kg, cosine, sine)


def attend_kernel(
    sc_ref, q_ref, kv_ref, x_ref, wo_ref, fg_ref, wr_ref, routes_ref,
    mixed_ref, invl_ref, after_ref, xg_ref, soft_ref, acc,
):
    slot, tile = pl.program_id(0), pl.program_id(1)
    slots, tiles = pl.num_programs(0), pl.num_programs(1)
    rows = q_ref.shape[1]
    here = sc_ref[slots]
    length = sc_ref[slot]
    live = here * rows < length
    chunk = 2 * rows
    chunks = (here + 2) // 2

    @pl.when(tile == 0)
    def _():
        acc[...] = jnp.zeros_like(acc)

    @pl.when(live)
    def _():
        q4 = stack_heads(q_ref[0], True).astype(BF16)

        def step(index, carry, masked):
            mass, total = carry
            pair = kv_ref[pl.ds(2 * index, 2), 0]
            keys = pair[:, :, :LANES].reshape(chunk, LANES)
            values = pair[:, :, LANES:].reshape(chunk, LANES)
            weight = jnp.exp2(dot_nt(q4, keys) * EXP2_SCALE)
            if masked:
                at = lax.rem(row_of(weight.shape), rows) + here * rows
                weight = jnp.where(lane_of(weight.shape) + index * chunk <= at, weight, 0.0)
            for part in range(chunk // LANES):
                mass = mass + weight[:, part * LANES : (part + 1) * LANES]
            return mass, total + dot(weight.astype(BF16), values)

        blank = jnp.zeros((4 * rows, LANES), F32)
        carry = lax.fori_loop(0, chunks - 1, lambda i, c: step(i, c, False), (blank, blank))
        mass, total = step(chunks - 1, carry, True)
        inverse = 1.0 / jnp.sum(mass, axis=-1, keepdims=True)
        mixed = unstack_heads(total * inverse).astype(BF16)
        mixed_ref[0] = mixed
        invl_ref[0] = unstack_heads(jnp.broadcast_to(inverse, total.shape))
        acc[...] += dot(mixed, wo_ref[...])

    @pl.when(jnp.logical_not(live))
    def _():
        mixed_ref[...] = jnp.zeros_like(mixed_ref)
        invl_ref[...] = jnp.zeros_like(invl_ref)

    @pl.when(tile == tiles - 1)
    def _():
        width = x_ref.shape[2]
        valid = (row_of((rows, 1)) + here * rows < length).astype(F32)
        after = x_ref[0].astype(F32) + valid * acc[...]
        after_ref[0] = after
        unit, unused = rms_parts(after)
        normed = (unit * fg_ref[...]).astype(BF16)
        xg_ref[0, :, :width] = normed
        logits = dot(normed, wr_ref[...])
        lanes = lane_of(logits.shape)
        routes = routes_ref[0]
        chosen = lanes == routes[:, 0:1]
        for k in range(1, routes.shape[1]):
            chosen = chosen | (lanes == routes[:, k : k + 1])
        top = jnp.max(jnp.where(chosen, logits, -1e30), axis=-1, keepdims=True)
        weight = jnp.where(chosen, jnp.exp(jnp.minimum(logits - top, 0.0)), 0.0)
        soft = weight / jnp.sum(weight, axis=-1, keepdims=True)
        soft_ref[0] = soft
        gates = soft * valid
        high = gates.astype(BF16).astype(F32)
        half = logits.shape[1] // 2
        xg_ref[0, :, width:] = (high + pltpu.roll(gates - high, half, 1)).astype(BF16)


def attend(scalars, q, kv, x, w_out, ffn_gain, router, routes):
    slots, rows, width = x.shape
    group = kv.shape[0]
    qw = q.shape[2]
    tiles = qw // 256
    row = lambda lanes: pl.BlockSpec((1, rows, lanes), lambda s, b, sc: (s, 0, 0))
    tile = pl.BlockSpec((1, rows, 256), lambda s, b, sc: (s, 0, b))
    return pl.pallas_call(
        attend_kernel,
        grid_spec=pltpu.PrefetchScalarGridSpec(
            num_scalar_prefetch=1,
            grid=(slots, tiles),
            in_specs=[
                tile,
                pl.BlockSpec((group, 1, rows, 256), lambda s, b, sc: (0, s, 0, b)),
                row(width),
                pl.BlockSpec((256, width), lambda s, b, sc: (b, 0)),
                pl.BlockSpec(ffn_gain.shape, lambda s, b, sc: (0, 0)),
                pl.BlockSpec(router.shape, lambda s, b, sc: (0, 0)),
                row(routes.shape[2]),
            ],
            out_specs=(tile, tile, row(width), row(width + LANES), row(LANES)),
            scratch_shapes=[pltpu.VMEM((rows, width), F32)],
        ),
        out_shape=(
            jax.ShapeDtypeStruct((slots, rows, qw), BF16),
            jax.ShapeDtypeStruct((slots, rows, qw), F32),
            jax.ShapeDtypeStruct((slots, rows, width), F32),
            jax.ShapeDtypeStruct((slots, rows, width + LANES), BF16),
            jax.ShapeDtypeStruct((slots, rows, LANES), F32),
        ),
        compiler_params=pltpu.CompilerParams(vmem_limit_bytes=56 * MIB),
        name="attend",
    )(scalars, q, kv, x, w_out, ffn_gain, router, routes)


def row_gates(picked, first, owned):
    lanes = lane_of(picked.shape)
    expert = row_of(picked.shape) // PAIR + first
    half = picked.shape[1] // 2
    mine = (lanes == expert) | (lanes == expert + half)
    return jnp.sum(jnp.where(mine, picked, 0.0), axis=-1, keepdims=True)


def experts_forward_kernel(
    sc_ref, xg_ref, wg_ref, wu_ref, wd_ref, pick_ref, xe_ref, gp_ref, up_ref, hid_ref, part_ref, gates, ybuf
):
    sources, unused, rows, wide = xg_ref.shape
    owned, width, eff = wg_ref.shape
    pairs = sources // 2
    double = 2 * rows
    first = sc_ref[pl.num_programs(0)] * owned
    tokens = xg_ref[...].reshape(sources * rows, wide)
    slab = tokens[:, width:]
    chosen = (lane_of((8, LANES)) == row_of((8, LANES)) + first).astype(BF16)
    routed = dot_nt(chosen, slab) > 0.0
    before = row_of((double, double))
    after = lane_of((double, double))
    count = ((before < after) & (before // rows == after // rows)).astype(BF16)
    place = lax.broadcasted_iota(jnp.int32, (PAIR, double), 0)
    offset = (lane_of((8, double)) // rows) * MOST
    for p in range(pairs):
        mask = routed[:, p * double : (p + 1) * double]
        rank = dot(mask.astype(F32).astype(BF16), count).astype(jnp.int32) + offset
        rank = jnp.where(mask, rank, -1)
        pick = jnp.concatenate(
            [(place == rank[e : e + 1, :]).astype(F32).astype(BF16) for e in range(owned)], axis=0
        )
        pick_ref[0, p] = pick
        block = tokens[p * double : (p + 1) * double]
        picked = dot(pick, block[:, :width]).astype(BF16)
        scale = row_gates(dot(pick, block[:, width:]), first, owned)
        for e in range(owned):
            xe_ref[0, e, p * PAIR : (p + 1) * PAIR] = picked[e * PAIR : (e + 1) * PAIR]
            gates[e, p * PAIR : (p + 1) * PAIR] = jnp.broadcast_to(
                scale[e * PAIR : (e + 1) * PAIR], (PAIR, LANES)
            )

    def one(e, carry):
        rows_in = xe_ref[0, e]
        gate_part = dot(rows_in, wg_ref[e])
        up_part = dot(rows_in, wu_ref[e])
        gp_ref[0, e] = gate_part
        up_ref[0, e] = up_part
        hidden = (gate_part * jax.nn.sigmoid(gate_part) * up_part).astype(BF16)
        hid_ref[0, e] = hidden
        result = (dot(hidden, wd_ref[e]) * gates[e][:, 0:1]).astype(BF16)
        for p in range(pairs):
            ybuf[p, e] = result[p * PAIR : (p + 1) * PAIR]
        return carry

    lax.fori_loop(0, owned, one, 0)
    for p in range(pairs):
        back = dot_tn(pick_ref[0, p], ybuf[p].reshape(owned * PAIR, width))
        part_ref[2 * p : 2 * p + 2, 0] = back.astype(BF16).reshape(2, rows, width)


def step_spec(shape):
    return pl.BlockSpec((1,) + shape, lambda s, j, sc: (s * pl.num_programs(1) + j,) + (0,) * len(shape))


def resident(array):
    return pl.BlockSpec(array.shape, lambda s, j, sc: (0,) * array.ndim, pipeline_mode=pl.Buffered(1))


def experts_forward(scalars, tokens, w_gate, w_up, w_down):
    group, slots, rows, wide = tokens.shape
    owned, width, eff = w_gate.shape
    sources = 8
    parts = group // sources
    pairs = sources // 2
    steps = slots * parts
    held = pairs * PAIR
    source = lambda lanes: pl.BlockSpec((sources, 1, rows, lanes), lambda s, j, sc: (j, s, 0, 0))
    saved = [
        ((pairs, owned * PAIR, 2 * rows), BF16),
        ((owned, held, width), BF16),
        ((owned, held, eff), F32),
        ((owned, held, eff), F32),
        ((owned, held, eff), BF16),
    ]
    return pl.pallas_call(
        experts_forward_kernel,
        grid_spec=pltpu.PrefetchScalarGridSpec(
            num_scalar_prefetch=1,
            grid=(slots, parts),
            in_specs=[source(wide), resident(w_gate), resident(w_up), resident(w_down)],
            out_specs=tuple(step_spec(shape) for shape, unused in saved) + (source(width),),
            scratch_shapes=[
                pltpu.VMEM((owned, held, LANES), F32),
                pltpu.VMEM((pairs, owned, PAIR, width), BF16),
            ],
        ),
        out_shape=tuple(jax.ShapeDtypeStruct((steps,) + shape, kind) for shape, kind in saved)
        + (jax.ShapeDtypeStruct((group, slots, rows, width), BF16),),
        compiler_params=pltpu.CompilerParams(vmem_limit_bytes=60 * MIB),
        name="experts_forward",
    )(scalars, tokens, w_gate, w_up, w_down)


def experts_backward_kernel(
    sc_ref, dy_ref, slab_ref, pick_ref, gp_ref, up_ref, hid_ref, wg_ref, wu_ref, wd_ref,
    part_ref, dyw_ref, gg_ref, ug_ref, gates, dye, dxb,
):
    sources, unused, rows, width = dy_ref.shape
    owned = wg_ref.shape[0]
    pairs = sources // 2
    double = 2 * rows
    first = sc_ref[pl.num_programs(0)] * owned
    for p in range(pairs):
        pick = pick_ref[0, p]
        picked = dot(pick, dy_ref[2 * p : 2 * p + 2].reshape(double, width)).astype(BF16)
        scale = row_gates(dot(pick, slab_ref[2 * p : 2 * p + 2].reshape(double, LANES)), first, owned)
        for e in range(owned):
            dye[e, p * PAIR : (p + 1) * PAIR] = picked[e * PAIR : (e + 1) * PAIR]
            gates[e, p * PAIR : (p + 1) * PAIR] = jnp.broadcast_to(
                scale[e * PAIR : (e + 1) * PAIR], (PAIR, LANES)
            )

    def one(e, carry):
        grad_rows = dye[e]
        scale = gates[e][:, 0:1]
        plain = dot_nt(grad_rows, wd_ref[e])
        gate_part, up_part = gp_ref[0, e], up_ref[0, e]
        soft_grad = jnp.sum(plain * hid_ref[0, e].astype(F32), axis=-1, keepdims=True)
        hidden_grad = plain * scale
        sigma = jax.nn.sigmoid(gate_part)
        gate_grad = (hidden_grad * up_part * sigma * (1.0 + gate_part * (1.0 - sigma))).astype(BF16)
        up_grad = (hidden_grad * gate_part * sigma).astype(BF16)
        gg_ref[0, e] = gate_grad
        ug_ref[0, e] = up_grad
        dyw_ref[0, e] = (grad_rows.astype(F32) * scale).astype(BF16)
        input_grad = (dot_nt(gate_grad, wg_ref[e]) + dot_nt(up_grad, wu_ref[e])).astype(BF16)
        lanes = lane_of((pairs * PAIR, LANES))
        high = soft_grad.astype(BF16).astype(F32)
        spot = jnp.where(
            lanes == first + e, high, jnp.where(lanes == first + e + LANES // 2, soft_grad - high, 0.0)
        ).astype(BF16)
        for p in range(pairs):
            dxb[p, e, :, :width] = input_grad[p * PAIR : (p + 1) * PAIR]
            dxb[p, e, :, width:] = spot[p * PAIR : (p + 1) * PAIR]
        return carry

    lax.fori_loop(0, owned, one, 0)
    for p in range(pairs):
        back = dot_tn(pick_ref[0, p], dxb[p].reshape(owned * PAIR, width + LANES))
        part_ref[2 * p : 2 * p + 2, 0] = back.astype(BF16).reshape(2, rows, width + LANES)


def experts_backward(scalars, grads, tokens, pick, gate_part, up_part, hidden, w_gate, w_up, w_down):
    group, slots, rows, width = grads.shape
    owned, unused, eff = w_gate.shape
    sources = 8
    parts = group // sources
    pairs = sources // 2
    steps = slots * parts
    held = pairs * PAIR
    source = lambda lanes, at: pl.BlockSpec((sources, 1, rows, lanes), lambda s, j, sc: (j, s, 0, at))
    return pl.pallas_call(
        experts_backward_kernel,
        grid_spec=pltpu.PrefetchScalarGridSpec(
            num_scalar_prefetch=1,
            grid=(slots, parts),
            in_specs=[
                source(width, 0),
                source(LANES, width // LANES),
                step_spec((pairs, owned * PAIR, 2 * rows)),
                step_spec((owned, held, eff)),
                step_spec((owned, held, eff)),
                step_spec((owned, held, eff)),
                resident(w_gate), resident(w_up), resident(w_down),
            ],
            out_specs=(
                source(width + LANES, 0),
                step_spec((owned, held, width)),
                step_spec((owned, held, eff)),
                step_spec((owned, held, eff)),
            ),
            scratch_shapes=[
                pltpu.VMEM((owned, held, LANES), F32),
                pltpu.VMEM((owned, held, width), BF16),
                pltpu.VMEM((pairs, owned, PAIR, width + LANES), BF16),
            ],
        ),
        out_shape=(
            jax.ShapeDtypeStruct((group, slots, rows, width + LANES), BF16),
            jax.ShapeDtypeStruct((steps, owned, held, width), BF16),
            jax.ShapeDtypeStruct((steps, owned, held, eff), BF16),
            jax.ShapeDtypeStruct((steps, owned, held, eff), BF16),
        ),
        compiler_params=pltpu.CompilerParams(vmem_limit_bytes=62 * MIB),
        name="experts_backward",
    )(scalars, grads, tokens, pick, gate_part, up_part, hidden, w_gate, w_up, w_down)


def expert_weights_kernel(xe_ref, gg_ref, ug_ref, hid_ref, dyw_ref, dg_ref, du_ref, dd_ref, ag, au, ad):
    step = pl.program_id(1)
    flat = lambda ref: ref[:, 0].reshape(ref.shape[0] * ref.shape[2], ref.shape[3])
    for acc, left, right in ((ad, hid_ref, dyw_ref), (ag, xe_ref, gg_ref), (au, xe_ref, ug_ref)):
        part = dot_tn(flat(left), flat(right))

        @pl.when(step == 0)
        def _():
            acc[...] = part

        @pl.when(step > 0)
        def _():
            acc[...] += part

    @pl.when(step == pl.num_programs(1) - 1)
    def _():
        dg_ref[0] = ag[...].astype(BF16)
        du_ref[0] = au[...].astype(BF16)
        dd_ref[0] = ad[...].astype(BF16)


def expert_weights(xe, gate_grad, up_grad, hidden, weighted):
    steps, owned, held, width = xe.shape
    eff = hidden.shape[3]
    each = 4
    block = lambda lanes: pl.BlockSpec((each, 1, held, lanes), lambda e, i: (i, e, 0, 0))
    out = lambda a, b: pl.BlockSpec((1, a, b), lambda e, i: (e, 0, 0))
    return pl.pallas_call(
        expert_weights_kernel,
        grid=(owned, steps // each),
        in_specs=[block(width), block(eff), block(eff), block(eff), block(width)],
        out_specs=(out(width, eff), out(width, eff), out(eff, width)),
        out_shape=(
            jax.ShapeDtypeStruct((owned, width, eff), BF16),
            jax.ShapeDtypeStruct((owned, width, eff), BF16),
            jax.ShapeDtypeStruct((owned, eff, width), BF16),
        ),
        scratch_shapes=[pltpu.VMEM((width, eff), F32), pltpu.VMEM((width, eff), F32), pltpu.VMEM((eff, width), F32)],
        compiler_params=pltpu.CompilerParams(vmem_limit_bytes=56 * MIB),
        name="expert_weights",
    )(xe, gate_grad, up_grad, hidden, weighted)


def attend_backward_kernel(
    sc_ref, q_ref, kv_ref, mixed_ref, invl_ref, dx_ref, soft_ref, og_ref, after_ref, fg_ref, wr_ref, wo_ref,
    dq_ref, dkv_ref, ag_ref, at_ref, lg_ref, fgg_ref, mg_s,
):
    slot, tile = pl.program_id(0), pl.program_id(1)
    slots, tiles = pl.num_programs(0), pl.num_programs(1)
    rows = q_ref.shape[1]
    here = sc_ref[slots]
    length = sc_ref[slot]
    live = here * rows < length
    chunk = 2 * rows
    chunks = (here + 2) // 2
    width = og_ref.shape[2]

    @pl.when(tile == 0)
    def _():
        valid = (row_of((rows, 1)) + here * rows < length).astype(F32)
        slab = dx_ref[0, :, width:].astype(F32)
        half = slab.shape[1] // 2
        soft = soft_ref[0]
        soft_grad = jnp.where(lane_of(slab.shape) < half, slab + pltpu.roll(slab, half, 1), 0.0)
        chosen = soft * (soft_grad - jnp.sum(soft * soft_grad, axis=-1, keepdims=True))
        logit_grad = chosen.astype(BF16)
        lg_ref[0] = logit_grad
        normed_grad = dx_ref[0, :, :width].astype(F32) + dot_nt(logit_grad, wr_ref[...])
        back, gain_grad = rms_backward(normed_grad, after_ref[0], fg_ref[...])

        @pl.when(slot == 0)
        def _():
            fgg_ref[...] = gain_grad

        @pl.when(slot > 0)
        def _():
            fgg_ref[...] += gain_grad

        after_grad = og_ref[0] + back
        ag_ref[0] = after_grad
        attn_grad = (valid * after_grad).astype(BF16)
        at_ref[0] = attn_grad
        mixed_grad = dot_nt(attn_grad, wo_ref[...]).astype(BF16)
        for t in range(mg_s.shape[0]):
            mg_s[t] = mixed_grad[:, t * 256 : (t + 1) * 256]

    dkv_ref[...] = jnp.zeros_like(dkv_ref)

    @pl.when(live)
    def _():
        q4 = stack_heads(q_ref[0], True).astype(BF16)
        do4_f = stack_heads(mg_s[tile].astype(F32) * invl_ref[0], True)
        do4 = do4_f.astype(BF16)
        product = do4_f * stack_heads(mixed_ref[0], False)
        delta = lax.dot_general(
            jnp.ones((8, LANES), F32), product, (((1,), (1,)), ((), ())),
            preferred_element_type=F32, precision=lax.Precision.HIGHEST,
        )[0:1]

        def step(index, total, masked):
            pair = kv_ref[pl.ds(2 * index, 2), 0]
            keys = pair[:, :, :LANES].reshape(chunk, LANES)
            values = pair[:, :, LANES:].reshape(chunk, LANES)
            weight = jnp.exp2(dot_nt(keys, q4) * EXP2_SCALE)
            if masked:
                at = lax.rem(lane_of(weight.shape), rows) + here * rows
                weight = jnp.where(row_of(weight.shape) + index * chunk <= at, weight, 0.0)
            pressure = dot_nt(values, do4)
            score_grad = (weight * (pressure - delta) * SCALE).astype(BF16)
            key_grad = dot(score_grad, q4)
            value_grad = dot(weight.astype(BF16), do4)
            dkv_ref[pl.ds(2 * index, 2), 0, :, :LANES] = key_grad.astype(BF16).reshape(2, rows, LANES)
            dkv_ref[pl.ds(2 * index, 2), 0, :, LANES:] = value_grad.astype(BF16).reshape(2, rows, LANES)
            return total + dot_tn(score_grad, keys)

        total = lax.fori_loop(
            0, chunks - 1, lambda i, c: step(i, c, False), jnp.zeros((4 * rows, LANES), F32)
        )
        total = step(chunks - 1, total, True)
        dq_ref[0] = unstack_heads(total).astype(BF16)

    @pl.when(jnp.logical_not(live))
    def _():
        dq_ref[...] = jnp.zeros_like(dq_ref)


def attend_backward(scalars, q, kv, mixed, invl, dx, soft, out_grad, after, ffn_gain, router, w_out):
    slots, rows, width = out_grad.shape
    group = kv.shape[0]
    qw = q.shape[2]
    tiles = qw // 256
    row = lambda lanes: pl.BlockSpec((1, rows, lanes), lambda s, b, sc: (s, 0, 0))
    tile = pl.BlockSpec((1, rows, 256), lambda s, b, sc: (s, 0, b))
    group_tile = pl.BlockSpec((group, 1, rows, 256), lambda s, b, sc: (0, s, 0, b))
    whole = lambda a: pl.BlockSpec(a.shape, lambda s, b, sc: (0, 0))
    return pl.pallas_call(
        attend_backward_kernel,
        grid_spec=pltpu.PrefetchScalarGridSpec(
            num_scalar_prefetch=1,
            grid=(slots, tiles),
            in_specs=[
                tile, group_tile, tile, tile, row(width + LANES), row(LANES), row(width), row(width),
                whole(ffn_gain), whole(router), whole(w_out),
            ],
            out_specs=(
                tile, group_tile, row(width), row(width), row(LANES),
                pl.BlockSpec((1, width), lambda s, b, sc: (0, 0)),
            ),
            scratch_shapes=[pltpu.VMEM((tiles, rows, 256), BF16)],
        ),
        out_shape=(
            jax.ShapeDtypeStruct((slots, rows, qw), BF16),
            jax.ShapeDtypeStruct(kv.shape, BF16),
            jax.ShapeDtypeStruct((slots, rows, width), F32),
            jax.ShapeDtypeStruct((slots, rows, width), BF16),
            jax.ShapeDtypeStruct((slots, rows, LANES), BF16),
            jax.ShapeDtypeStruct((1, width), F32),
        ),
        compiler_params=pltpu.CompilerParams(vmem_limit_bytes=56 * MIB),
        name="attend_backward",
    )(scalars, q, kv, mixed, invl, dx, soft, out_grad, after, ffn_gain, router, w_out)


def finish_kernel(
    dq_ref, dkv_ref, qraw_ref, kraw_ref, x_ref, ag_ref, cos_ref, sin_ref, gain_ref, qg_ref, kg_ref,
    wq_ref, wk_ref, wv_ref, h_ref, mixed_ref, at_ref, n2_ref, lg_ref,
    ig_ref, dense_ref, rt_ref, qgg_ref, kgg_ref, agg_ref, q_s, k_s, v_s,
):
    slot = pl.program_id(0)
    rows = x_ref.shape[1]
    cosine, sine = cos_ref[...], sin_ref[...]

    @pl.when(slot == 0)
    def _():
        qgg_ref[...] = jnp.zeros_like(qgg_ref)
        kgg_ref[...] = jnp.zeros_like(kgg_ref)
        agg_ref[...] = jnp.zeros_like(agg_ref)

    here = pl.ds(pl.multiple_of(slot * rows, rows), rows)
    for t in range(dq_ref.shape[2] // LANES):
        lanes = slice(t * LANES, (t + 1) * LANES)
        raw, gain = rope_backward(dq_ref[0, :, lanes].astype(F32), qraw_ref[0, :, lanes], qg_ref[...], cosine, sine)
        q_s[here, lanes] = raw.astype(BF16)
        qgg_ref[...] += gain
    for t in range(kraw_ref.shape[2] // LANES):
        lanes = slice(t * LANES, (t + 1) * LANES)
        at = 2 * t * LANES
        grad = dkv_ref[0, :, at : at + LANES].astype(BF16).astype(F32)
        raw, gain = rope_backward(grad, kraw_ref[0, :, lanes], kg_ref[...], cosine, sine)
        k_s[here, lanes] = raw.astype(BF16)
        kgg_ref[...] += gain
        v_s[here, lanes] = dkv_ref[0, :, at + LANES : at + 2 * LANES].astype(BF16)
    normed_grad = dot_nt(q_s[here], wq_ref[...]) + dot_nt(k_s[here], wk_ref[...]) + dot_nt(v_s[here], wv_ref[...])
    back, gain = rms_backward(normed_grad, x_ref[0].astype(F32), gain_ref[...])
    agg_ref[...] += gain
    ig_ref[0] = ag_ref[0] + back

    @pl.when(slot == pl.num_programs(0) - 1)
    def _():
        flat = lambda ref: ref[...].reshape(ref.shape[0] * ref.shape[1], ref.shape[2])
        shards, unused, shard_rows, width = dense_ref.shape
        h = flat(h_ref)
        half = width // 2

        def put(index, lanes, value):
            dense_ref[:, index, :, lanes] = value.astype(BF16).reshape(shards, shard_rows, value.shape[1])

        put(0, slice(0, width), dot_tn(h, q_s[...]))
        put(1, slice(0, half), dot_tn(h, k_s[...]))
        put(1, slice(half, width), dot_tn(h, v_s[...]))
        put(2, slice(0, width), dot_tn(flat(mixed_ref), flat(at_ref)))
        rt_ref[...] = dot_tn(flat(n2_ref), flat(lg_ref))


def finish(dq, dkv, qraw, kraw, x, after_grad, cosine, sine, attn_gain, qg, kg, wq, wk, wv, h, mixed, attn_grad, n2, lg):
    slots, rows, width = x.shape
    qw, kw = wq.shape[1], wk.shape[1]
    shards = 8
    row = lambda lanes: pl.BlockSpec((1, rows, lanes), lambda s: (s, 0, 0))
    whole = lambda a: pl.BlockSpec(a.shape, lambda s: (0,) * a.ndim)
    lanes_out = pl.BlockSpec((1, LANES), lambda s: (0, 0))
    return pl.pallas_call(
        finish_kernel,
        grid=(slots,),
        in_specs=[row(qw), row(2 * kw), row(qw), row(kw), row(width), row(width)]
        + [whole(a) for a in (cosine, sine, attn_gain, qg, kg, wq, wk, wv, h, mixed, attn_grad)]
        + [pl.BlockSpec((slots, rows, width), lambda s: (0, 0, 0)), whole(lg)],
        out_specs=(
            row(width),
            pl.BlockSpec((shards, 3, width // shards, width), lambda s: (0, 0, 0, 0)),
            pl.BlockSpec((width, LANES), lambda s: (0, 0)),
            lanes_out, lanes_out, pl.BlockSpec((1, width), lambda s: (0, 0)),
        ),
        out_shape=(
            jax.ShapeDtypeStruct((slots, rows, width), F32),
            jax.ShapeDtypeStruct((shards, 3, width // shards, width), BF16),
            jax.ShapeDtypeStruct((width, LANES), F32),
            jax.ShapeDtypeStruct((1, LANES), F32),
            jax.ShapeDtypeStruct((1, LANES), F32),
            jax.ShapeDtypeStruct((1, width), F32),
        ),
        scratch_shapes=[
            pltpu.VMEM((slots * rows, qw), BF16),
            pltpu.VMEM((slots * rows, kw), BF16),
            pltpu.VMEM((slots * rows, kw), BF16),
        ],
        compiler_params=pltpu.CompilerParams(vmem_limit_bytes=60 * MIB),
        name="finish",
    )(dq, dkv, qraw, kraw, x, after_grad, cosine, sine, attn_gain, qg, kg, wq, wk, wv, h, mixed, attn_grad, n2, lg)


def remote(src, dst, ss, rs, dev):
    return pltpu.make_async_remote_copy(src_ref=src, dst_ref=dst, send_sem=ss, recv_sem=rs, device_id=dev, device_id_type=MESH)

def ag_kernel(x_ref, o_ref, lsem, ss, rs):
    z = lax.axis_index("dp"); c = lax.axis_index("context"); y = lax.axis_index("experts")
    cs = c + 1 - 2 * lax.rem(c, 2)
    cx = lax.rem(c + 2, 4)
    yy = 1 - y
    sib, xn, yn = (z, cs, y), (z, cx, y), (z, c, yy)
    me = c * 2 + y
    gx = cx * 2 + y; gy = c * 2 + yy; gd = cx * 2 + yy
    bar = pltpu.get_barrier_semaphore()
    for d in (sib, xn, yn):
        pl.semaphore_signal(bar, inc=1, device_id=d, device_id_type=MESH)
    pl.semaphore_wait(bar, 3)
    n = x_ref.shape[0]
    h = n // 2
    loc = [pltpu.make_async_copy(x_ref.at[s], o_ref.at[me, s], lsem.at[s]) for s in range(n)]
    sx = [remote(x_ref.at[s], o_ref.at[me, s], ss.at[0, s], rs.at[0, s], xn) for s in range(n)]
    sy = [remote(x_ref.at[s], o_ref.at[me, s], ss.at[1, s], rs.at[1, s], yn) for s in range(n)]
    sc = [remote(x_ref.at[s], o_ref.at[me, s], ss.at[2, s], rs.at[2, s], sib) for s in range(n)]
    fx = [remote(o_ref.at[gx, s], o_ref.at[gx, s], ss.at[3, s], rs.at[3, s], sib) for s in range(n)]
    fy = [remote(o_ref.at[gy, s], o_ref.at[gy, s], ss.at[4, s], rs.at[4, s], sib) for s in range(n)]
    fd = [remote(o_ref.at[gd, s], o_ref.at[gd, s], ss.at[5, s], rs.at[5, s], sib) for s in range(n)]
    dg = [remote(o_ref.at[gx, s], o_ref.at[gx, s], ss.at[6, s], rs.at[6, s], yn) if s < h else
          remote(o_ref.at[gy, s], o_ref.at[gy, s], ss.at[6, s], rs.at[6, s], xn) for s in range(n)]
    for i in range(n):
        sx[i].start()
        sy[(i + h) % n].start()
    for s in range(n):
        sc[s].start()
        loc[s].start()
    for i in range(n):
        a = i; b = (i + h) % n
        sx[a].wait_recv()
        if a < h: dg[a].start()
        fx[a].start()
        sy[b].wait_recv()
        if b >= h: dg[b].start()
        fy[b].start()
    for i in range(h):
        for s in (i, i + h):
            dg[s].wait_recv(); fd[s].start()
    for s in range(n):
        sc[s].wait_recv(); fx[s].wait_recv(); fy[s].wait_recv(); fd[s].wait_recv()
        loc[s].wait()
        for k in (sx, sy, sc, fx, fy, fd, dg): k[s].wait_send()

def all_gather(x, cid):
    n = x.shape[0]
    return pl.pallas_call(ag_kernel,
        out_shape=jax.ShapeDtypeStruct((8,) + x.shape, x.dtype),
        in_specs=[pl.BlockSpec(memory_space=pl.ANY)], out_specs=pl.BlockSpec(memory_space=pl.ANY),
        scratch_shapes=[pltpu.SemaphoreType.DMA((n,)), pltpu.SemaphoreType.DMA((7, n)), pltpu.SemaphoreType.DMA((7, n))],
        compiler_params=pltpu.CompilerParams(collective_id=cid, has_side_effects=True), name="ag")(x)

def rs_kernel(p_ref, o_ref, own, other, sb, q, dx, dy, rx, ry, lsem, ss, rs):
    z = lax.axis_index("dp"); c = lax.axis_index("context"); y = lax.axis_index("experts")
    core = lax.rem(c, 2)
    cs = c + 1 - 2 * core
    cx = lax.rem(c + 2, 4)
    yy = 1 - y
    sib, xn, yn = (z, cs, y), (z, cx, y), (z, c, yy)
    bar = pltpu.get_barrier_semaphore()
    for d in (sib, xn, yn):
        pl.semaphore_signal(bar, inc=1, device_id=d, device_id_type=MESH)
    n = p_ref.shape[1]
    h = n // 2
    chips = [(cx, yy), (cx, y), (c, yy), (c, y)]
    idx = [a * 2 + b for a, b in chips]
    oth = [(a + 1 - 2 * core) * 2 + b for a, b in chips]
    ld = [[pltpu.make_async_copy(p_ref.at[idx[k], s], own.at[k, s], lsem.at[k, s]) for s in range(n)] for k in range(4)]
    st = [[remote(p_ref.at[oth[k], s], sb.at[k, s], ss.at[k, s], rs.at[k, s], sib) for s in range(n)] for k in range(4)]
    for k in range(4):
        for s in range(n):
            ld[k][s].start()
    pl.semaphore_wait(bar, 3)
    for k in range(4):
        for s in range(n):
            st[k][s].start()
    dgs = [remote(q.at[0, s], dx.at[s], ss.at[4, s], rs.at[4, s], xn) if s < h else
           remote(q.at[0, s], dy.at[s - h], ss.at[4, s], rs.at[4, s], yn) for s in range(n)]
    tx = [remote(q.at[1, s], rx.at[s], ss.at[5, s], rs.at[5, s], xn) for s in range(n)]
    ty = [remote(q.at[2, s], ry.at[s], ss.at[6, s], rs.at[6, s], yn) for s in range(n)]
    f32 = jnp.float32
    def pair(k, s):
        ld[k][s].wait(); st[k][s].wait_recv()
        return own[k, s].astype(f32) + sb[k, s].astype(f32)
    for i in range(h):
        for s in (i, i + h):
            q[0, s] = pair(0, s).astype(q.dtype); dgs[s].start()
    for i in range(h):
        q[1, i] = pair(1, i).astype(q.dtype); tx[i].start()
        q[2, i + h] = pair(2, i + h).astype(q.dtype); ty[i + h].start()
    for i in range(h):
        a = pair(2, i)
        dgs[i].wait_recv()
        q[2, i] = (a + dx[i].astype(f32)).astype(q.dtype); ty[i].start()
        b = pair(1, i + h)
        dgs[i + h].wait_recv()
        q[1, i + h] = (b + dy[i].astype(f32)).astype(q.dtype); tx[i + h].start()
    for i in range(h):
        for s in (i, i + h):
            a = pair(3, s)
            tx[s].wait_recv(); ty[s].wait_recv()
            o_ref[s] = (a + rx[s].astype(f32) + ry[s].astype(f32)).astype(o_ref.dtype)
    for s in range(n):
        for k in st: k[s].wait_send()
        for k in (dgs, tx, ty): k[s].wait_send()

def reduce_scatter(p, cid, dt):
    _, n, r, w = p.shape
    h = n // 2
    V = pltpu.VMEM
    return pl.pallas_call(rs_kernel,
        out_shape=jax.ShapeDtypeStruct((n, r, w), dt),
        in_specs=[pl.BlockSpec(memory_space=pl.ANY)], out_specs=pl.BlockSpec(memory_space=pltpu.VMEM),
        scratch_shapes=[V((4, n, r, w), p.dtype), V((1, 8, 128), p.dtype), V((4, n, r, w), p.dtype), V((3, n, r, w), p.dtype),
            V((h, r, w), p.dtype), V((h, r, w), p.dtype), V((n, r, w), p.dtype), V((n, r, w), p.dtype),
            pltpu.SemaphoreType.DMA((4, n)), pltpu.SemaphoreType.DMA((7, n)), pltpu.SemaphoreType.DMA((7, n))],
        compiler_params=pltpu.CompilerParams(collective_id=cid, has_side_effects=True, vmem_limit_bytes=60 * 2**20), name="rs")(p)


def add_to(ref, value):
    ref[...] = (ref[...].astype(F32) + value).astype(ref.dtype)


class Plane:
    def __init__(self):
        z, c, y = lax.axis_index("dp"), lax.axis_index("context"), lax.axis_index("experts")
        core = lax.rem(c, 2)
        cx, yy = lax.rem(c + 2, 4), 1 - y
        self.me = c * 2 + y
        self.sib, self.xn, self.yn = (z, c + 1 - 2 * core, y), (z, cx, y), (z, c, yy)
        chips = [(cx, yy), (cx, y), (c, yy), (c, y)]
        self.own = [a * 2 + b for a, b in chips]
        self.other = [(a + 1 - 2 * core) * 2 + b for a, b in chips]
        self.inner_plane = (z == 1) | (z == 2)
        self.outer_plane = (z == 0) | (z == 3)
        self.inner = (1 + z // 2, c, y)
        self.across = (3 - z, c, y)
        self.outer = ((z - 1) * 3, c, y)

    def barrier(self, line):
        bar = pltpu.get_barrier_semaphore()
        tell = lambda who: pl.semaphore_signal(bar, inc=1, device_id=who, device_id_type=MESH)
        for who in (self.sib, self.xn, self.yn):
            tell(who)
        if not line:
            pl.semaphore_wait(bar, 3)
            return

        @pl.when(self.outer_plane)
        def _():
            tell(self.inner)
            pl.semaphore_wait(bar, 4)

        @pl.when(self.inner_plane)
        def _():
            tell(self.across)
            tell(self.outer)
            pl.semaphore_wait(bar, 5)


class Scatter:
    def __init__(self, plane, own, other, buffers, sems):
        self.plane, self.own, self.other = plane, own, other
        self.sb, self.da, self.db, self.rx, self.ry = buffers
        self.sent, self.got = sems
        self.rows = self.sb.shape[2]
        self.top, self.low = pl.ds(0, self.rows // 2), pl.ds(self.rows // 2, self.rows // 2)

    def core(self, k, s):
        return remote(self.other(k, s), self.sb.at[k, s], self.sent.at[k, s], self.got.at[k, s], self.plane.sib)

    def diag(self, s):
        mine = self.own(0, s)
        return (
            remote(mine.at[self.top], self.da.at[s], self.sent.at[4, s], self.got.at[4, s], self.plane.xn),
            remote(mine.at[self.low], self.db.at[s], self.sent.at[5, s], self.got.at[5, s], self.plane.yn),
        )

    def side(self, number, s):
        axis, half = number // 2, (self.top, self.low)[number % 2]
        there = (self.rx, self.ry)[axis]
        who = (self.plane.xn, self.plane.yn)[axis]
        return remote(
            self.own(1 + axis, s).at[half], there.at[s, half], self.sent.at[6 + number, s], self.got.at[6 + number, s], who
        )

    def pair(self, k, s, half):
        return self.own(k, s)[half].astype(F32) + self.sb[k, s, half].astype(F32)

    def start(self, s):
        for k in range(4):
            self.core(k, s).start()

    def first(self, s):
        self.core(0, s).wait_recv()
        mine = self.own(0, s)
        add_to(mine, self.sb[0, s].astype(F32))
        for copy in self.diag(s):
            copy.start()

    def second(self, s):
        self.core(1, s).wait_recv()
        self.own(1, s)[self.top] = self.pair(1, s, self.top).astype(BF16)
        self.side(0, s).start()
        self.core(2, s).wait_recv()
        self.own(2, s)[self.low] = self.pair(2, s, self.low).astype(BF16)
        self.side(3, s).start()

    def third(self, s):
        by_x, by_y = self.diag(s)
        by_x.wait_recv()
        self.own(2, s)[self.top] = (self.pair(2, s, self.top) + self.da[s].astype(F32)).astype(BF16)
        self.side(2, s).start()
        by_y.wait_recv()
        self.own(1, s)[self.low] = (self.pair(1, s, self.low) + self.db[s].astype(F32)).astype(BF16)
        self.side(1, s).start()

    def result(self, s):
        self.core(3, s).wait_recv()
        for number in range(4):
            self.side(number, s).wait_recv()
        return (
            self.own(3, s)[...].astype(F32)
            + self.sb[3, s].astype(F32)
            + self.rx[s].astype(F32)
            + self.ry[s].astype(F32)
        )

    def drain(self, s):
        for k in range(4):
            self.core(k, s).wait_send()
        for copy in self.diag(s):
            copy.wait_send()
        for number in range(4):
            self.side(number, s).wait_send()


class Line:
    ring, back = 4, 2

    def __init__(self, plane, held, first, second, total, buffers, sems):
        self.plane, self.held, self.r1, self.r2, self.total = plane, held, first, second, total
        self.l1, self.va, self.vt = buffers
        self.sent, self.got, self.local = sems
        self.count = held.shape[0]

    def inward(self, i):
        return remote(self.held.at[i], self.r1.at[i], self.sent.at[0, i], self.got.at[0, i], self.plane.inner)

    def across(self, i):
        return remote(self.va.at[i % self.ring], self.r2.at[i], self.sent.at[1, i], self.got.at[1, i], self.plane.across)

    def outward(self, i):
        return remote(self.vt.at[i % self.back], self.total.at[i], self.sent.at[2, i], self.got.at[2, i], self.plane.outer)

    def keep(self, i):
        return pltpu.make_async_copy(self.vt.at[i % self.back], self.total.at[i], self.local.at[i % self.back])

    def load(self, number, i):
        source, there = (
            (self.r1, self.l1.at[i % 2]), (self.held, self.va.at[i % self.ring]), (self.r2, self.vt.at[i % self.back])
        )[number]
        return pltpu.make_async_copy(source.at[i], there, self.local.at[self.ring + 2 * number + i % 2])

    def advance(self, j):
        steps = self.count // 2
        ahead = [2 * j, 2 * j + 1] if j < steps else []
        behind = [2 * j - 2, 2 * j - 1] if j >= 1 else []

        @pl.when(self.plane.inner_plane)
        def _():
            for i in ahead:
                if i >= self.ring:
                    self.across(i - self.ring).wait_send()
                self.load(1, i).start()
            for i in ahead:
                self.inward(i).wait_recv()
                self.load(0, i).start()
            for i in ahead:
                self.load(1, i).wait()
                self.load(0, i).wait()
                add_to(self.va.at[i % self.ring], self.l1[i % 2].astype(F32))
                self.across(i).start()
            for i in behind:
                if i >= self.back:
                    self.outward(i - self.back).wait_send()
                    self.keep(i - self.back).wait()
                self.across(i).wait_recv()
                self.load(2, i).start()
            for i in behind:
                self.load(2, i).wait()
                add_to(self.vt.at[i % self.back], self.va[i % self.ring].astype(F32))
                self.outward(i).start()
                self.keep(i).start()

    def finish(self):
        @pl.when(self.plane.inner_plane)
        def _():
            for i in range(self.count - self.ring, self.count):
                self.across(i).wait_send()
            for i in range(self.count - self.back, self.count):
                self.outward(i).wait_send()
                self.keep(i).wait()

        @pl.when(self.plane.outer_plane)
        def _():
            def one(i, carry):
                self.inward(i).wait_send()
                remote(
                    self.held.at[i], self.total.at[i], self.sent.at[2, i], self.got.at[2, i], self.plane.inner
                ).wait_recv()
                return carry

            lax.fori_loop(0, self.count, one, 0)


HELD_BACK = 14


def tail_kernel(
    sc_ref, dpart, xe, gg, ug, hid, dyw, q_in, kv_in, mixed_in, invl_in, soft_in, og_in, after_in, qraw_in, kraw_in,
    x_in, h_in, n2_in, wo_in, wq_in, wk_in, wv_in, fg_ref, wr_ref, cos_ref, sin_ref, gain_ref, qg_ref, kg_ref, loss_ref,
    total, ig_out, dense_out, small_out, held, r1, r2,
    dx_own, dx_sb, dx_da, dx_db, dx_rx, dx_ry, kv_sb, kv_da, kv_db, kv_rx, kv_ry,
    l1, va, vt, dsh, dr1, dr2, dfin, sm_mine, sm_got,
    sent_dx, got_dx, sent_kv, got_kv, sent_de, got_de, sent_z, got_z, local_z, sent_ag, got_ag, sent_sm, got_sm, local,
):
    plane = Plane()
    slots, rows = x_in.shape[0], x_in.shape[1]
    width = x_in.shape[2]
    group = dpart.shape[0]
    owned = xe.shape[1]
    eff = gg.shape[3]
    each = lambda body, count=slots: lax.fori_loop(0, count, lambda s, c: (body(s), c)[1], 0)
    line = Line(plane, held, r1, r2, total, (l1, va, vt), (sent_z, got_z, local_z))
    scat_dx = Scatter(
        plane, lambda k, s: dx_own.at[k, s], lambda k, s: dpart.at[plane.other[k], s],
        (dx_sb, dx_da, dx_db, dx_rx, dx_ry), (sent_dx, got_dx),
    )
    own_load = lambda k, s: pltpu.make_async_copy(dpart.at[plane.own[k], s], dx_own.at[k, s], local.at[0])
    for k in range(4):
        each(lambda s: own_load(k, s).start())
    plane.barrier(True)
    each(scat_dx.start)

    def expert_phase(xeb, ggb, ugb, hidb, dywb, gb, sems, out_sem):
        def loads(e):
            slot = e % 2
            return [
                pltpu.make_async_copy(source.at[:, e], there.at[slot], sems.at[slot, n])
                for n, (source, there) in enumerate(((xe, xeb), (gg, ggb), (ug, ugb), (hid, hidb), (dyw, dywb)))
            ]

        def store(e):
            return pltpu.make_async_copy(gb.at[e % 2], held.at[pl.ds(6 * e, 6)], out_sem.at[e % 2])

        def send(e):
            store(e).wait()
            todo = [6 * e + n for n in range(6) if 6 * e + n < HELD_BACK]
            if todo:
                @pl.when(plane.outer_plane)
                def _():
                    for i in todo:
                        line.inward(i).start()

        flat = lambda ref, slot: ref[slot].reshape(ref.shape[1] * ref.shape[2], ref.shape[3])
        for copy in loads(0):
            copy.start()
        for e in range(owned):
            slot = e % 2
            if e + 1 < owned:
                for copy in loads(e + 1):
                    copy.start()
            for copy in loads(e):
                copy.wait()
            half = width // 2
            for n, (left, right) in enumerate(((xeb, ggb), (xeb, ugb))):
                part = dot_tn(flat(left, slot), flat(right, slot)).astype(BF16)
                gb[slot, 2 * n] = part[:half]
                gb[slot, 2 * n + 1] = part[half:]
            part = dot_tn(flat(hidb, slot), flat(dywb, slot)).astype(BF16)
            gb[slot, 4] = part[:, :half]
            gb[slot, 5] = part[:, half:]
            store(e).start()
            if e >= 1:
                send(e - 1)
            if e == 1:
                for k in range(4):
                    each(lambda s: own_load(k, s).wait())
                each(scat_dx.first)
            if e == 2:
                each(scat_dx.second)
        send(owned - 1)
        each(scat_dx.third)

    held_rows = (xe.shape[0], xe.shape[2])
    pl.run_scoped(
        expert_phase,
        pltpu.VMEM((2,) + held_rows + (width,), BF16),
        pltpu.VMEM((2,) + held_rows + (eff,), BF16),
        pltpu.VMEM((2,) + held_rows + (eff,), BF16),
        pltpu.VMEM((2,) + held_rows + (eff,), BF16),
        pltpu.VMEM((2,) + held_rows + (width,), BF16),
        pltpu.VMEM((2, 6, eff, width // 2), BF16),
        pltpu.SemaphoreType.DMA((2, 5)),
        pltpu.SemaphoreType.DMA((2,)),
    )
    line.advance(0)
    here = plane.me
    chunk = 2 * rows
    chunks = (here + 2) // 2
    qw = q_in.shape[2]
    kw = kraw_in.shape[2]
    tiles = qw // 256

    def rest(dkv, ag_s, at_s, lg_s, mixed_s, q_s, qgg, kgg, agg, fgg, mg_s):
        scat_kv = Scatter(
            plane, lambda k, s: dkv.at[plane.own[k], s], lambda k, s: dkv.at[plane.other[k], s],
            (kv_sb, kv_da, kv_db, kv_rx, kv_ry), (sent_kv, got_kv),
        )
        for ref in (qgg, kgg, agg, fgg):
            ref[...] = jnp.zeros_like(ref)
        mixed_load = pltpu.make_async_copy(mixed_in, mixed_s, local.at[1])
        mixed_load.start()

        def attention_phase(wo, qb, kvb, invlb, softb, ogb, afterb, qrawb, sems):
            wo_load = pltpu.make_async_copy(wo_in, wo, local.at[2])
            wo_load.start()

            def loads(s):
                slot = lax.rem(s, 2)
                out = [pltpu.make_async_copy(kv_in.at[:, s], kvb.at[slot], sems.at[slot, 0])]
                for n, (source, there) in enumerate(
                    ((q_in, qb), (invl_in, invlb), (soft_in, softb), (og_in, ogb), (after_in, afterb), (qraw_in, qrawb))
                ):
                    out.append(pltpu.make_async_copy(source.at[s], there.at[slot], sems.at[slot, n + 1]))
                return out

            for s in range(2):
                for copy in loads(s):
                    copy.start()
            wo_load.wait()
            mixed_load.wait()

            def one_slot(s):
                slot = lax.rem(s, 2)
                for copy in loads(s):
                    copy.wait()
                dx = scat_dx.result(s)
                valid = (row_of((rows, 1)) + here * rows < sc_ref[s]).astype(F32)
                slab = dx[:, width:]
                half = slab.shape[1] // 2
                soft = softb[slot]
                soft_grad = jnp.where(lane_of(slab.shape) < half, slab + pltpu.roll(slab, half, 1), 0.0)
                chosen = soft * (soft_grad - jnp.sum(soft * soft_grad, axis=-1, keepdims=True))
                logit_grad = chosen.astype(BF16)
                lg_s[s] = logit_grad
                normed_grad = dx[:, :width] + dot_nt(logit_grad, wr_ref[...])
                back, gain_grad = rms_backward(normed_grad, afterb[slot], fg_ref[...])
                fgg[...] += gain_grad
                after_grad = ogb[slot] + back
                ag_s[s] = after_grad
                attn_grad = (valid * after_grad).astype(BF16)
                at_s[s] = attn_grad
                mixed_grad = dot_nt(attn_grad, wo[...]).astype(BF16)
                for t in range(tiles):
                    mg_s[t] = mixed_grad[:, t * 256 : (t + 1) * 256]

                def one_tile(t, carry):
                    lanes = pl.ds(pl.multiple_of(t * 256, 256), 256)
                    key_lanes = pl.ds(pl.multiple_of(t * 256, 256), LANES)
                    value_lanes = pl.ds(pl.multiple_of(t * 256 + LANES, LANES), LANES)
                    q4 = stack_heads(qb[slot, :, lanes], True).astype(BF16)
                    do4_f = stack_heads(mg_s[t].astype(F32) * invlb[slot, :, lanes], True)
                    do4 = do4_f.astype(BF16)
                    product = do4_f * stack_heads(mixed_s[s, :, lanes], False)
                    delta = lax.dot_general(
                        jnp.ones((8, LANES), F32), product, (((1,), (1,)), ((), ())),
                        preferred_element_type=F32, precision=lax.Precision.HIGHEST,
                    )[0:1]

                    def step(index, sum_q, masked):
                        two = pl.ds(2 * index, 2)
                        keys = kvb[slot, two, :, key_lanes].reshape(chunk, LANES)
                        values = kvb[slot, two, :, value_lanes].reshape(chunk, LANES)
                        weight = jnp.exp2(dot_nt(keys, q4) * EXP2_SCALE)
                        if masked:
                            at = lax.rem(lane_of(weight.shape), rows) + here * rows
                            weight = jnp.where(row_of(weight.shape) + index * chunk <= at, weight, 0.0)
                        pressure = dot_nt(values, do4)
                        score_grad = (weight * (pressure - delta) * SCALE).astype(BF16)
                        key_grad = dot(score_grad, q4).astype(BF16)
                        value_grad = dot(weight.astype(BF16), do4).astype(BF16)
                        dkv[two, s, :, key_lanes] = key_grad.reshape(2, rows, LANES)
                        dkv[two, s, :, value_lanes] = value_grad.reshape(2, rows, LANES)
                        return sum_q + dot_tn(score_grad, keys)

                    total_q = lax.fori_loop(
                        0, chunks - 1, lambda i, c: step(i, c, False), jnp.zeros((4 * rows, LANES), F32)
                    )
                    total_q = step(chunks - 1, total_q, True)

                    def blank(index, carry):
                        dkv[pl.ds(2 * index, 2), s, :, lanes] = jnp.zeros((2, rows, 256), BF16)
                        return carry

                    lax.fori_loop(chunks, group // 2, blank, 0)
                    dq = unstack_heads(total_q).astype(BF16).astype(F32)
                    for n in range(2):
                        part = slice(n * LANES, (n + 1) * LANES)
                        here_lanes = pl.ds(pl.multiple_of(t * 256 + n * LANES, LANES), LANES)
                        raw, gain = rope_backward(
                            dq[:, part], qrawb[slot, :, here_lanes], qg_ref[...], cos_ref[...], sin_ref[...]
                        )
                        q_s[s, :, here_lanes] = raw.astype(BF16)
                        qgg[...] += gain
                    return carry

                lax.fori_loop(0, tiles, one_tile, 0)

                @pl.when(s + 2 < slots)
                def _():
                    for copy in loads(s + 2):
                        copy.start()

                scat_kv.start(s)

                @pl.when(s >= 1)
                def _():
                    scat_kv.first(s - 1)
                    scat_kv.second(s - 1)

                @pl.when(s >= 2)
                def _():
                    scat_kv.third(s - 2)

            lax.fori_loop(0, 2, lambda s, c: (one_slot(s), c)[1], 0)
            line.advance(1)
            lax.fori_loop(2, slots, lambda s, c: (one_slot(s), c)[1], 0)
            line.advance(2)

        pl.run_scoped(
            attention_phase,
            pltpu.VMEM(wo_in.shape, BF16),
            pltpu.VMEM((2, rows, qw), BF16),
            pltpu.VMEM((2, group, rows, 2 * kw), BF16),
            pltpu.VMEM((2, rows, qw), F32),
            pltpu.VMEM((2, rows, LANES), F32),
            pltpu.VMEM((2, rows, width), F32),
            pltpu.VMEM((2, rows, width), F32),
            pltpu.VMEM((2, rows, qw), F32),
            pltpu.SemaphoreType.DMA((2, 7)),
        )
        each(scat_dx.drain)

        def last_phase(wq, wk, wv, xb, krawb, hb, n2b, k_s, v_s):
            loads = [
                pltpu.make_async_copy(source, there, local.at[2 + n])
                for n, (source, there) in enumerate(
                    ((wq_in, wq), (wk_in, wk), (wv_in, wv), (x_in, xb), (kraw_in, krawb), (h_in, hb),
                     (n2_in.at[:, :, pl.ds(0, width)], n2b))
                )
            ]
            for copy in loads:
                copy.start()
            scat_kv.first(slots - 1)
            scat_kv.second(slots - 1)
            scat_kv.third(slots - 2)
            flat = lambda ref: ref[...].reshape(slots * rows, ref.shape[2])
            for copy in loads:
                copy.wait()
            shards, shard_rows = group, width // group

            def product(left, right, place):
                def one(n, carry):
                    lanes = pl.ds(pl.multiple_of(n * 256, 256), 256)
                    column = right[:, :, lanes].reshape(slots * rows, 256)
                    place(n, dot_tn(flat(left), column).astype(BF16).reshape(shards, shard_rows, 256))
                    return carry

                lax.fori_loop(0, right.shape[2] // 256, one, 0)

            def aside(k):
                def place(n, value):
                    lanes = pl.ds(pl.multiple_of(n * 256, 256), 256)
                    for shard in range(shards):
                        dx_own[k + shard // slots, shard % slots, :, lanes] = value[shard]

                return place

            product(mixed_s, at_s, aside(0))
            scat_kv.third(slots - 1)
            product(hb, q_s, aside(2))
            router = dot_tn(flat(lg_s), flat(n2b))
            experts = small_out.shape[0] - 8
            sm_mine[0] = jnp.zeros(sm_mine.shape[1:], F32)
            sm_mine[0, :experts] = router[:experts]
            sm_mine[0, experts + 1 : experts + 2] = fgg[...]
            sm_mine[0, experts + 2 : experts + 3, :LANES] = qgg[...]
            sm_mine[0, experts + 4 : experts + 5, :LANES] = loss_ref[...]
            line.advance(3)

            def one_slot(s):
                grads = scat_kv.result(s)
                for t in range(kw // LANES):
                    lanes = slice(t * LANES, (t + 1) * LANES)
                    at = 2 * t * LANES
                    grad = grads[:, at : at + LANES].astype(BF16).astype(F32)
                    raw, gain = rope_backward(grad, krawb[s, :, lanes], kg_ref[...], cos_ref[...], sin_ref[...])
                    k_s[s, :, lanes] = raw.astype(BF16)
                    kgg[...] += gain
                    v_s[s, :, lanes] = grads[:, at + LANES : at + 2 * LANES].astype(BF16)
                normed_grad = dot_nt(q_s[s], wq[...]) + dot_nt(k_s[s], wk[...]) + dot_nt(v_s[s], wv[...])
                back, gain = rms_backward(normed_grad, xb[s].astype(F32), gain_ref[...])
                agg[...] += gain
                ag_s[s] += back
                pltpu.make_async_copy(ag_s.at[s], ig_out.at[s], local.at[0]).start()

            each(one_slot)
            each(scat_kv.drain)
            line.advance(4)
            sm_mine[0, experts : experts + 1] = agg[...]
            sm_mine[0, experts + 3 : experts + 4, :LANES] = kgg[...]
            for shard in range(shards):
                dkv[shard, 2] = dx_own[shard // slots, shard % slots, :, :width]
                dkv[shard, 0] = dx_own[2 + shard // slots, shard % slots, :, :width]

            def beside(first):
                def place(n, value):
                    dkv[:, 1, :, pl.ds(pl.multiple_of(first + n * 256, 256), 256)] = value

                return place

            product(hb, k_s, beside(0))
            product(hb, v_s, beside(kw))

        pl.run_scoped(
            last_phase,
            pltpu.VMEM(wq_in.shape, BF16),
            pltpu.VMEM(wk_in.shape, BF16),
            pltpu.VMEM(wv_in.shape, BF16),
            pltpu.VMEM(x_in.shape, BF16),
            pltpu.VMEM(kraw_in.shape, F32),
            pltpu.VMEM(h_in.shape, BF16),
            pltpu.VMEM((slots, rows, width), BF16),
            pltpu.VMEM((slots, rows, kw), BF16),
            pltpu.VMEM((slots, rows, kw), BF16),
        )
        kinds = 3
        narrow = pl.ds(0, width)
        again = [dx_sb.at[:, :, :, narrow]] + [r.at[:, :, narrow] for r in (dx_da, dx_db, dx_rx, dx_ry)]
        scat_de = Scatter(
            plane, lambda k, s: dkv.at[plane.own[k], s], lambda k, s: dkv.at[plane.other[k], s],
            again, (sent_de, got_de),
        )
        by_kind = lambda body: each(body, kinds)
        by_kind(scat_de.start)
        small = lambda n, who: remote(sm_mine.at[n], sm_got.at[n], sent_sm.at[n], got_sm.at[n], who)

        def small_step(n, who):
            small(n, who).wait_recv()
            sm_mine[n + 1] = sm_mine[n] + sm_got[n]

        small(0, plane.sib).start()
        by_kind(scat_de.first)
        small_step(0, plane.sib)
        small(1, plane.xn).start()
        by_kind(scat_de.second)
        small_step(1, plane.xn)
        small(2, plane.yn).start()
        by_kind(scat_de.third)
        small_step(2, plane.yn)
        line.advance(5)

        def one_kind(s):
            dsh[s] = scat_de.result(s).astype(BF16)

        by_kind(one_kind)
        by_kind(scat_de.drain)
        each(lambda s: pltpu.make_async_copy(ag_s.at[s], ig_out.at[s], local.at[0]).wait())

    pl.run_scoped(
        rest,
        pltpu.VMEM((group, slots, rows, 2 * kw), BF16),
        pltpu.VMEM((slots, rows, width), F32),
        pltpu.VMEM((slots, rows, width), BF16),
        pltpu.VMEM((slots, rows, LANES), BF16),
        pltpu.VMEM((slots, rows, qw), BF16),
        pltpu.VMEM((slots, rows, qw), BF16),
        pltpu.VMEM((1, LANES), F32),
        pltpu.VMEM((1, LANES), F32),
        pltpu.VMEM((1, width), F32),
        pltpu.VMEM((1, width), F32),
        pltpu.VMEM((tiles, rows, 256), BF16),
    )

    small_in = remote(sm_mine.at[3], sm_got.at[3], sent_sm.at[3], got_sm.at[3], plane.inner)
    small_across = remote(sm_mine.at[4], sm_got.at[4], sent_sm.at[4], got_sm.at[4], plane.across)
    small_back = remote(sm_mine.at[5], sm_got.at[5], sent_sm.at[5], got_sm.at[5], plane.outer)
    dense_in = remote(dsh, dr1, sent_sm.at[6], got_sm.at[6], plane.inner)
    dense_across = remote(dsh, dr2, sent_sm.at[7], got_sm.at[7], plane.across)
    dense_back = remote(dfin, dfin, sent_sm.at[8], got_sm.at[8], plane.outer)

    @pl.when(plane.outer_plane)
    def _():
        small_in.start()
        dense_in.start()

        def one(i, carry):
            line.inward(i).start()
            return carry

        lax.fori_loop(HELD_BACK, line.count, one, 0)

    line.advance(6)

    @pl.when(plane.inner_plane)
    def _():
        small_in.wait_recv()
        sm_mine[4] = sm_mine[3] + sm_got[3]
        small_across.start()
        dense_in.wait_recv()
        add_to(dsh, dr1[...].astype(F32))
        dense_across.start()

    line.advance(7)

    @pl.when(plane.inner_plane)
    def _():
        small_across.wait_recv()
        sm_mine[5] = sm_mine[4] + sm_got[4]
        small_back.start()
        dense_across.wait_recv()
        dfin[...] = (dsh[...].astype(F32) + dr2[...].astype(F32)).astype(BF16)
        dense_back.start()
        small_out[...] = sm_mine[5]

    line.advance(8)

    @pl.when(plane.outer_plane)
    def _():
        small_back.wait_recv()
        dense_back.wait_recv()
        small_out[...] = sm_got[5]

    gather = Gather(plane, dfin, dense_out, sent_ag, got_ag, local)
    gather.start()
    line.advance(9)
    gather.forward()
    line.advance(10)
    gather.finish()
    line.advance(11)
    line.advance(12)
    line.finish()
    for n, who in ((0, plane.sib), (1, plane.xn), (2, plane.yn)):
        remote(sm_mine.at[n], sm_got.at[n], sent_sm.at[n], got_sm.at[n], who).wait_send()

    @pl.when(plane.outer_plane)
    def _():
        small_in.wait_send()
        dense_in.wait_send()

    @pl.when(plane.inner_plane)
    def _():
        small_across.wait_send()
        small_back.wait_send()
        dense_across.wait_send()
        dense_back.wait_send()


class Gather:
    def __init__(self, plane, mine, out, sent, got, local):
        self.plane, self.mine, self.out, self.sent, self.got, self.local = plane, mine, out, sent, got, local
        self.n = mine.shape[0]
        rows = mine.shape[1]
        self.halves = (pl.ds(0, rows // 2), pl.ds(rows // 2, rows // 2))
        self.at_x, self.at_y, self.at_d = plane.own[1], plane.own[2], plane.own[0]

    def own(self, number, s):
        who = (self.plane.xn, self.plane.yn, self.plane.sib)[number]
        return remote(self.mine.at[s], self.out.at[self.plane.me, s], self.sent.at[number, s], self.got.at[number, s], who)

    def keep(self, s):
        return pltpu.make_async_copy(self.mine.at[s], self.out.at[self.plane.me, s], self.local.at[s])

    def pass_on(self, number, s):
        at = (self.at_x, self.at_y, self.at_d)[number]
        view = self.out.at[at, s]
        return remote(view, view, self.sent.at[3 + number, s], self.got.at[3 + number, s], self.plane.sib)

    def far(self, number, s):
        at, who = ((self.at_x, self.plane.yn), (self.at_y, self.plane.xn))[number]
        view = self.out.at[at, s, self.halves[number]]
        return remote(view, view, self.sent.at[6 + number, s], self.got.at[6 + number, s], who)

    def start(self):
        for s in range(self.n):
            for number in range(3):
                self.own(number, s).start()
            self.keep(s).start()

    def forward(self):
        for s in range(self.n):
            for number in range(2):
                self.own(number, s).wait_recv()
                self.far(number, s).start()
                self.pass_on(number, s).start()

    def finish(self):
        for s in range(self.n):
            for number in range(2):
                self.far(number, s).wait_recv()
            self.pass_on(2, s).start()
        for s in range(self.n):
            self.keep(s).wait()
            self.own(2, s).wait_recv()
            for number in range(3):
                self.pass_on(number, s).wait_recv()
                self.pass_on(number, s).wait_send()
                self.own(number, s).wait_send()
            for number in range(2):
                self.far(number, s).wait_send()


def tail(
    slot_lengths, dpart, xe, gate_grad, up_grad, hidden, weighted, q, kv, mixed, invl, soft, out_grad, after, qraw, kraw,
    x, h, n2, w_out, w_query, w_key, w_value, ffn_gain, router, cosine, sine, attn_gain, qg, kg, loss, experts, number,
):
    slots, rows, width = x.shape
    group, unused, unused_rows, wide = dpart.shape
    owned, eff = xe.shape[1], gate_grad.shape[3]
    kw = kraw.shape[2]
    chunks = 6 * owned
    piece = (eff, width // 2)
    kinds = 3
    hbm = pl.BlockSpec(memory_space=pl.ANY)
    vmem = pl.BlockSpec(memory_space=pltpu.VMEM)
    smem = pl.BlockSpec(memory_space=pltpu.SMEM)
    V, D = pltpu.VMEM, pltpu.SemaphoreType.DMA
    half = rows // 2

    def landing(n, lanes):
        return [
            V((4, n, rows, lanes), BF16), V((n, half, lanes), BF16), V((n, half, lanes), BF16),
            V((n, rows, lanes), BF16), V((n, rows, lanes), BF16),
        ]

    small_rows = experts + 8
    return pl.pallas_call(
        tail_kernel,
        in_specs=[smem] + [hbm] * 22 + [vmem] * 8,
        out_specs=(hbm, hbm, hbm, vmem, hbm, hbm, hbm),
        out_shape=(
            jax.ShapeDtypeStruct((chunks,) + piece, BF16),
            jax.ShapeDtypeStruct((slots, rows, width), F32),
            jax.ShapeDtypeStruct((group, kinds, width // group, width), BF16),
            jax.ShapeDtypeStruct((small_rows, width), F32),
            jax.ShapeDtypeStruct((chunks,) + piece, BF16),
            jax.ShapeDtypeStruct((chunks,) + piece, BF16),
            jax.ShapeDtypeStruct((chunks,) + piece, BF16),
        ),
        scratch_shapes=[V((4, slots, rows, wide), BF16)]
        + landing(slots, wide) + landing(slots, 2 * kw)
        + [V((2,) + piece, BF16), V((4,) + piece, BF16), V((2,) + piece, BF16)]
        + [V((kinds, rows, width), BF16)] * 4
        + [V((6, small_rows, width), F32)] * 2
        + [D((10, slots))] * 4 + [D((10, kinds))] * 2
        + [D((3, chunks))] * 2 + [D((10,))]
        + [D((8, kinds))] * 2 + [D((9,))] * 2 + [D((9,))],
        compiler_params=pltpu.CompilerParams(collective_id=number, has_side_effects=True, vmem_limit_bytes=63 * MIB),
        name="tail",
    )(
        slot_lengths, dpart, xe, gate_grad, up_grad, hidden, weighted, q, kv, mixed, invl, soft, out_grad, after, qraw,
        kraw, x, h, n2, w_out, w_query, w_key, w_value, ffn_gain, router, cosine, sine, attn_gain, qg, kg, loss,
    )


def plane_gather(rows, fast, number):
    if fast:
        return all_gather(rows, number)
    return lax.all_gather(rows, ("context", "experts"), axis=0, tiled=False)


def plane_scatter(parts, fast, number):
    if fast:
        return reduce_scatter(parts, number, F32)
    return lax.psum_scatter(parts, ("context", "experts"), scatter_dimension=0, tiled=False).astype(F32)


def per_device(
    fast, block_input, teacher, lengths, routes, w_query, w_key, w_value, w_out, query_gain, key_gain,
    attn_gain, ffn_gain, w_router, w_gate, w_up, w_down,
):
    slots, rows, width = block_input.shape
    expert_total = w_router.shape[1]
    group = lax.axis_size(("context", "experts"))
    here = lax.axis_index(("context", "experts"))
    span = rows * group
    slot_lengths = lax.dynamic_slice_in_dim(lengths, lax.axis_index("dp") * slots, slots)
    scalars = jnp.concatenate([slot_lengths, here[None]]).astype(jnp.int32)
    positions = here * rows + jnp.arange(rows, dtype=jnp.int32)
    valid = (positions[None, :] < slot_lengths[:, None]).astype(F32)[..., None]
    count_all = jnp.sum(lengths).astype(F32)
    positions_all = lengths.shape[0] * span

    half = HEAD // 2
    lanes = jnp.arange(LANES, dtype=jnp.int32)
    inverse = 10000.0 ** (-((lanes % half).astype(F32) * 2.0 / HEAD))
    turned = positions.astype(F32)[:, None] * inverse[None, :]
    cosine = jnp.cos(turned)
    sine = jnp.sin(turned) * jnp.where(lanes % HEAD < half, -1.0, 1.0)[None, :]
    qg = jnp.concatenate([query_gain, query_gain])[None, :]
    kg = jnp.concatenate([key_gain, key_gain])[None, :]
    ag, fg = attn_gain[None, :], ffn_gain[None, :]
    router = jnp.pad(w_router, ((0, 0), (0, LANES - expert_total)))

    h, q, kv_local, qraw, kraw = project(block_input, ag, w_query, w_key, w_value, qg, kg, cosine, sine)
    kv = plane_gather(kv_local, fast, 1)
    mixed, invl, after, xg, soft = attend(scalars, q, kv, block_input, w_out, fg, router, routes)
    tokens = plane_gather(xg, fast, 2)
    pick, xe, gate_part, up_part, hidden, part = experts_forward(scalars, tokens, w_gate, w_up, w_down)
    output = after + plane_scatter(part, fast, 3)
    difference = valid * (output - teacher.astype(F32))
    loss_part = jnp.sum(difference * difference)
    out_grad = difference * (positions_all / count_all)
    grads = plane_gather(out_grad.astype(BF16), fast, 4)
    dpart, weighted, gate_grad, up_grad = experts_backward(
        scalars, grads, tokens, pick, gate_part, up_part, hidden, w_gate, w_up, w_down
    )
    if fast:
        eff = w_gate.shape[2]
        owned = w_gate.shape[0]
        total, input_grad, dense, sums = tail(
            slot_lengths, dpart, xe, gate_grad, up_grad, hidden, weighted, q, kv, mixed, invl, soft, out_grad, after,
            qraw, kraw, block_input, h, xg, w_out, w_query, w_key, w_value, fg, router, cosine, sine, ag, qg, kg,
            jnp.broadcast_to(loss_part[None, None], (1, LANES)), expert_total, 5,
        )[:4]
        total = total.reshape(owned, 6, eff, width // 2)
        expert_grads = (
            total[:, 0:2].reshape(owned, width, eff),
            total[:, 2:4].reshape(owned, width, eff),
            jnp.concatenate([total[:, 4], total[:, 5]], axis=2),
        )
        dense = [dense[:, k].reshape(width, width).astype(F32) for k in range(3)]
        tops = sums[expert_total : expert_total + 5]
        small = (
            tops[2, :HEAD] + tops[2, HEAD : 2 * HEAD], tops[3, :HEAD] + tops[3, HEAD : 2 * HEAD], tops[0], tops[1],
            sums[:expert_total].T, tops[4, 0],
        )
    else:
        expert_grads = lax.psum(expert_weights(xe, gate_grad, up_grad, hidden, weighted), "dp")
        dx = plane_scatter(dpart, fast, 5)
        dq, dkv_parts, after_grad, attn_grad, logit_grad, ffn_gain_grad = attend_backward(
            scalars, q, kv, mixed, invl, dx, soft, out_grad, after, fg, router, w_out
        )
        dkv = plane_scatter(dkv_parts, fast, 6)
        input_grad, dense, router_grad, query_gg, key_gg, attn_gg = finish(
            dq, dkv, qraw, kraw, block_input, after_grad, cosine, sine, ag, qg, kg,
            w_query, w_key, w_value, h, mixed, attn_grad, xg, logit_grad,
        )
        dense = lax.psum(dense, ("dp", "context", "experts"))
        dense = [dense[:, k].reshape(width, width).astype(F32) for k in range(3)]
        small = lax.psum(
            (
                query_gg[0, :HEAD] + query_gg[0, HEAD:], key_gg[0, :HEAD] + key_gg[0, HEAD:], attn_gg[0],
                ffn_gain_grad[0], router_grad[:, :expert_total], loss_part,
            ),
            ("dp", "context", "experts"),
        )
    key_width = w_key.shape[1]
    return (
        small[5] / (count_all * width),
        output.astype(BF16),
        input_grad,
        dense[0],
        dense[1][:, :key_width],
        dense[1][:, key_width:],
        dense[2],
        small[0], small[1], small[2], small[3], small[4],
        expert_grads[0].astype(F32), expert_grads[1].astype(F32), expert_grads[2].astype(F32),
    )


def solution(mesh):
    fast = mesh.shape["context"] == 4 and mesh.shape["experts"] == 2
    rows = P("dp", ("context", "experts"), None)
    owned = P(("context", "experts"), None, None)
    return jax.shard_map(
        functools.partial(per_device, fast),
        mesh=mesh,
        in_specs=(rows, rows, P(), rows) + (P(),) * 9 + (owned,) * 3,
        out_specs=(P(), rows, rows) + (P(),) * 9 + (owned,) * 3,
        check_vma=False,
    )
```

```python
import functools
import math

import jax
import jax.numpy as jnp
from jax import lax
from jax.experimental import pallas as pl
from jax.experimental.pallas import tpu as pltpu
from jax.sharding import PartitionSpec as P

EPSILON = 1e-06
MOST = 40
PAIR = 2 * MOST
LANES = 128
HEAD = 64
SCALE = 0.125
EXP2_SCALE = 0.125 * math.log2(math.e)
MIB = 2**20
MESH = pl.DeviceIdType.MESH
F32 = jnp.float32
BF16 = jnp.bfloat16


def dot(a, b):
    return lax.dot_general(a, b, (((1,), (0,)), ((), ())), preferred_element_type=F32)


def dot_nt(a, b):
    return lax.dot_general(a, b, (((1,), (1,)), ((), ())), preferred_element_type=F32)


def dot_tn(a, b):
    return lax.dot_general(a, b, (((0,), (0,)), ((), ())), preferred_element_type=F32)


def lane_of(shape):
    return lax.broadcasted_iota(jnp.int32, shape, len(shape) - 1)


def row_of(shape):
    return lax.broadcasted_iota(jnp.int32, shape, len(shape) - 2)


def swap_halves(tile):
    low = lax.rem(lane_of(tile.shape), HEAD) < HEAD // 2
    return jnp.where(low, pltpu.roll(tile, LANES - HEAD // 2, 1), pltpu.roll(tile, HEAD // 2, 1))


def head_mean(tile):
    low = lane_of(tile.shape) < HEAD
    first = jnp.sum(jnp.where(low, tile, 0.0), axis=-1, keepdims=True)
    second = jnp.sum(jnp.where(low, 0.0, tile), axis=-1, keepdims=True)
    return jnp.where(low, first, second) * (1.0 / HEAD)


def rope_forward(raw, gain, cosine, sine):
    normed = raw * lax.rsqrt(head_mean(raw * raw) + EPSILON) * gain
    return normed * cosine + swap_halves(normed) * sine


def rope_backward(grad, raw, gain, cosine, sine):
    inverse = lax.rsqrt(head_mean(raw * raw) + EPSILON)
    unit = raw * inverse
    normed_grad = grad * cosine - swap_halves(grad) * sine
    gain_grad = jnp.sum(normed_grad * unit, axis=0, keepdims=True)
    unit_grad = normed_grad * gain
    return inverse * (unit_grad - unit * head_mean(unit_grad * unit)), gain_grad


def rms_parts(rows):
    inverse = lax.rsqrt(jnp.mean(rows * rows, axis=-1, keepdims=True) + EPSILON)
    return rows * inverse, inverse


def rms_backward(grad, rows, gain):
    unit, inverse = rms_parts(rows)
    gain_grad = jnp.sum(grad * unit, axis=0, keepdims=True)
    unit_grad = grad * gain
    back = inverse * (unit_grad - unit * jnp.mean(unit_grad * unit, axis=-1, keepdims=True))
    return back, gain_grad


def stack_heads(tile, masked):
    first, second = tile[:, :LANES].astype(F32), tile[:, LANES:].astype(F32)
    parts = [first, pltpu.roll(first, HEAD, 1), pltpu.roll(second, HEAD, 1), second]
    if masked:
        low = lane_of(first.shape) < HEAD
        parts = [jnp.where(low, part, 0.0) for part in parts[:2]] + [
            jnp.where(low, 0.0, part) for part in parts[2:]
        ]
    return jnp.concatenate(parts, axis=0)


def unstack_heads(rows):
    count = rows.shape[0] // 4
    one, two, three, four = (rows[k * count : (k + 1) * count] for k in range(4))
    low = lane_of(one.shape) < HEAD
    return jnp.concatenate(
        [
            jnp.where(low, one, pltpu.roll(two, HEAD, 1)),
            jnp.where(low, pltpu.roll(three, HEAD, 1), four),
        ],
        axis=1,
    )


def project_kernel(
    x_ref, gain_ref, wq_ref, wk_ref, wv_ref, qg_ref, kg_ref, cos_ref, sin_ref,
    h_ref, q_ref, kv_ref, qraw_ref, kraw_ref,
):
    slots, rows, width = x_ref.shape
    x = x_ref[...].astype(F32).reshape(slots * rows, width)
    unit, unused = rms_parts(x)
    normed = (unit * gain_ref[...]).astype(BF16)
    h_ref[...] = normed.reshape(slots, rows, width)
    cosine = jnp.concatenate([cos_ref[...]] * slots, axis=0)
    sine = jnp.concatenate([sin_ref[...]] * slots, axis=0)
    q_raw = dot(normed, wq_ref[...])
    qraw_ref[...] = q_raw.reshape(qraw_ref.shape)
    for tile in range(q_raw.shape[1] // LANES):
        lanes = slice(tile * LANES, (tile + 1) * LANES)
        turned = rope_forward(q_raw[:, lanes], qg_ref[...], cosine, sine)
        q_ref[:, :, lanes] = turned.astype(BF16).reshape(slots, rows, LANES)
    k_raw = dot(normed, wk_ref[...])
    kraw_ref[...] = k_raw.reshape(kraw_ref.shape)
    value = dot(normed, wv_ref[...]).astype(BF16)
    for tile in range(k_raw.shape[1] // LANES):
        lanes = slice(tile * LANES, (tile + 1) * LANES)
        turned = rope_forward(k_raw[:, lanes], kg_ref[...], cosine, sine)
        at = 2 * tile * LANES
        kv_ref[:, :, at : at + LANES] = turned.astype(BF16).reshape(slots, rows, LANES)
        kv_ref[:, :, at + LANES : at + 2 * LANES] = value[:, lanes].reshape(slots, rows, LANES)


def project(x, attn_gain, w_query, w_key, w_value, qg, kg, cosine, sine):
    slots, rows, width = x.shape
    step = 2
    block = lambda lanes: pl.BlockSpec((step, rows, lanes), lambda i: (i, 0, 0))
    whole = lambda a: pl.BlockSpec(a.shape, lambda i: (0,) * a.ndim)
    qw, kw = w_query.shape[1], w_key.shape[1]
    return pl.pallas_call(
        project_kernel,
        grid=(slots // step,),
        out_shape=(
            jax.ShapeDtypeStruct((slots, rows, width), BF16),
            jax.ShapeDtypeStruct((slots, rows, qw), BF16),
            jax.ShapeDtypeStruct((slots, rows, 2 * kw), BF16),
            jax.ShapeDtypeStruct((slots, rows, qw), F32),
            jax.ShapeDtypeStruct((slots, rows, kw), F32),
        ),
        in_specs=[block(width)] + [whole(a) for a in (attn_gain, w_query, w_key, w_value, qg, kg, cosine, sine)],
        out_specs=(block(width), block(qw), block(2 * kw), block(qw), block(kw)),
        compiler_params=pltpu.CompilerParams(vmem_limit_bytes=56 * MIB),
        name="project",
    )(x, attn_gain, w_query, w_key, w_value, qg, kg, cosine, sine)


def attend_kernel(
    sc_ref, q_ref, kv_ref, x_ref, wo_ref, fg_ref, wr_ref, routes_ref,
    mixed_ref, invl_ref, after_ref, xg_ref, soft_ref, acc,
):
    slot, tile = pl.program_id(0), pl.program_id(1)
    slots, tiles = pl.num_programs(0), pl.num_programs(1)
    rows = q_ref.shape[1]
    here = sc_ref[slots]
    length = sc_ref[slot]
    live = here * rows < length
    chunk = 2 * rows
    chunks = (here + 2) // 2

    @pl.when(tile == 0)
    def _():
        acc[...] = jnp.zeros_like(acc)

    @pl.when(live)
    def _():
        q4 = stack_heads(q_ref[0], True).astype(BF16)

        def step(index, carry, masked):
            mass, total = carry
            pair = kv_ref[pl.ds(2 * index, 2), 0]
            keys = pair[:, :, :LANES].reshape(chunk, LANES)
            values = pair[:, :, LANES:].reshape(chunk, LANES)
            weight = jnp.exp2(dot_nt(q4, keys) * EXP2_SCALE)
            if masked:
                at = lax.rem(row_of(weight.shape), rows) + here * rows
                weight = jnp.where(lane_of(weight.shape) + index * chunk <= at, weight, 0.0)
            for part in range(chunk // LANES):
                mass = mass + weight[:, part * LANES : (part + 1) * LANES]
            return mass, total + dot(weight.astype(BF16), values)

        blank = jnp.zeros((4 * rows, LANES), F32)
        carry = lax.fori_loop(0, chunks - 1, lambda i, c: step(i, c, False), (blank, blank))
        mass, total = step(chunks - 1, carry, True)
        inverse = 1.0 / jnp.sum(mass, axis=-1, keepdims=True)
        mixed = unstack_heads(total * inverse).astype(BF16)
        mixed_ref[0] = mixed
        invl_ref[0] = unstack_heads(jnp.broadcast_to(inverse, total.shape))
        acc[...] += dot(mixed, wo_ref[...])

    @pl.when(jnp.logical_not(live))
    def _():
        mixed_ref[...] = jnp.zeros_like(mixed_ref)
        invl_ref[...] = jnp.zeros_like(invl_ref)

    @pl.when(tile == tiles - 1)
    def _():
        width = x_ref.shape[2]
        valid = (row_of((rows, 1)) + here * rows < length).astype(F32)
        after = x_ref[0].astype(F32) + valid * acc[...]
        after_ref[0] = after
        unit, unused = rms_parts(after)
        normed = (unit * fg_ref[...]).astype(BF16)
        xg_ref[0, :, :width] = normed
        logits = dot(normed, wr_ref[...])
        lanes = lane_of(logits.shape)
        routes = routes_ref[0]
        chosen = lanes == routes[:, 0:1]
        for k in range(1, routes.shape[1]):
            chosen = chosen | (lanes == routes[:, k : k + 1])
        top = jnp.max(jnp.where(chosen, logits, -1e30), axis=-1, keepdims=True)
        weight = jnp.where(chosen, jnp.exp(jnp.minimum(logits - top, 0.0)), 0.0)
        soft = weight / jnp.sum(weight, axis=-1, keepdims=True)
        soft_ref[0] = soft
        gates = soft * valid
        high = gates.astype(BF16).astype(F32)
        half = logits.shape[1] // 2
        xg_ref[0, :, width:] = (high + pltpu.roll(gates - high, half, 1)).astype(BF16)


def attend(scalars, q, kv, x, w_out, ffn_gain, router, routes):
    slots, rows, width = x.shape
    group = kv.shape[0]
    qw = q.shape[2]
    tiles = qw // 256
    row = lambda lanes: pl.BlockSpec((1, rows, lanes), lambda s, b, sc: (s, 0, 0))
    tile = pl.BlockSpec((1, rows, 256), lambda s, b, sc: (s, 0, b))
    return pl.pallas_call(
        attend_kernel,
        grid_spec=pltpu.PrefetchScalarGridSpec(
            num_scalar_prefetch=1,
            grid=(slots, tiles),
            in_specs=[
                tile,
                pl.BlockSpec((group, 1, rows, 256), lambda s, b, sc: (0, s, 0, b)),
                row(width),
                pl.BlockSpec((256, width), lambda s, b, sc: (b, 0)),
                pl.BlockSpec(ffn_gain.shape, lambda s, b, sc: (0, 0)),
                pl.BlockSpec(router.shape, lambda s, b, sc: (0, 0)),
                row(routes.shape[2]),
            ],
            out_specs=(tile, tile, row(width), row(width + LANES), row(LANES)),
            scratch_shapes=[pltpu.VMEM((rows, width), F32)],
        ),
        out_shape=(
            jax.ShapeDtypeStruct((slots, rows, qw), BF16),
            jax.ShapeDtypeStruct((slots, rows, qw), F32),
            jax.ShapeDtypeStruct((slots, rows, width), F32),
            jax.ShapeDtypeStruct((slots, rows, width + LANES), BF16),
            jax.ShapeDtypeStruct((slots, rows, LANES), F32),
        ),
        compiler_params=pltpu.CompilerParams(vmem_limit_bytes=56 * MIB),
        name="attend",
    )(scalars, q, kv, x, w_out, ffn_gain, router, routes)


def row_gates(picked, first, owned):
    lanes = lane_of(picked.shape)
    expert = row_of(picked.shape) // PAIR + first
    half = picked.shape[1] // 2
    mine = (lanes == expert) | (lanes == expert + half)
    return jnp.sum(jnp.where(mine, picked, 0.0), axis=-1, keepdims=True)


def experts_forward_kernel(
    sc_ref, xg_ref, wg_ref, wu_ref, wd_ref, pick_ref, xe_ref, gp_ref, up_ref, hid_ref, part_ref, gates, ybuf
):
    sources, unused, rows, wide = xg_ref.shape
    owned, width, eff = wg_ref.shape
    pairs = sources // 2
    double = 2 * rows
    first = sc_ref[pl.num_programs(0)] * owned
    tokens = xg_ref[...].reshape(sources * rows, wide)
    slab = tokens[:, width:]
    chosen = (lane_of((8, LANES)) == row_of((8, LANES)) + first).astype(BF16)
    routed = dot_nt(chosen, slab) > 0.0
    before = row_of((double, double))
    after = lane_of((double, double))
    count = ((before < after) & (before // rows == after // rows)).astype(BF16)
    place = lax.broadcasted_iota(jnp.int32, (PAIR, double), 0)
    offset = (lane_of((8, double)) // rows) * MOST
    for p in range(pairs):
        mask = routed[:, p * double : (p + 1) * double]
        rank = dot(mask.astype(F32).astype(BF16), count).astype(jnp.int32) + offset
        rank = jnp.where(mask, rank, -1)
        pick = jnp.concatenate(
            [(place == rank[e : e + 1, :]).astype(F32).astype(BF16) for e in range(owned)], axis=0
        )
        pick_ref[0, p] = pick
        block = tokens[p * double : (p + 1) * double]
        picked = dot(pick, block[:, :width]).astype(BF16)
        scale = row_gates(dot(pick, block[:, width:]), first, owned)
        for e in range(owned):
            xe_ref[0, e, p * PAIR : (p + 1) * PAIR] = picked[e * PAIR : (e + 1) * PAIR]
            gates[e, p * PAIR : (p + 1) * PAIR] = jnp.broadcast_to(
                scale[e * PAIR : (e + 1) * PAIR], (PAIR, LANES)
            )

    def one(e, carry):
        rows_in = xe_ref[0, e]
        gate_part = dot(rows_in, wg_ref[e])
        up_part = dot(rows_in, wu_ref[e])
        gp_ref[0, e] = gate_part
        up_ref[0, e] = up_part
        hidden = (gate_part * jax.nn.sigmoid(gate_part) * up_part).astype(BF16)
        hid_ref[0, e] = hidden
        result = (dot(hidden, wd_ref[e]) * gates[e][:, 0:1]).astype(BF16)
        for p in range(pairs):
            ybuf[p, e] = result[p * PAIR : (p + 1) * PAIR]
        return carry

    lax.fori_loop(0, owned, one, 0)
    for p in range(pairs):
        back = dot_tn(pick_ref[0, p], ybuf[p].reshape(owned * PAIR, width))
        part_ref[2 * p : 2 * p + 2, 0] = back.astype(BF16).reshape(2, rows, width)


def step_spec(shape):
    return pl.BlockSpec((1,) + shape, lambda s, j, sc: (s * pl.num_programs(1) + j,) + (0,) * len(shape))


def resident(array):
    return pl.BlockSpec(array.shape, lambda s, j, sc: (0,) * array.ndim, pipeline_mode=pl.Buffered(1))


def experts_forward(scalars, tokens, w_gate, w_up, w_down):
    group, slots, rows, wide = tokens.shape
    owned, width, eff = w_gate.shape
    sources = 8
    parts = group // sources
    pairs = sources // 2
    steps = slots * parts
    held = pairs * PAIR
    source = lambda lanes: pl.BlockSpec((sources, 1, rows, lanes), lambda s, j, sc: (j, s, 0, 0))
    saved = [
        ((pairs, owned * PAIR, 2 * rows), BF16),
        ((owned, held, width), BF16),
        ((owned, held, eff), F32),
        ((owned, held, eff), F32),
        ((owned, held, eff), BF16),
    ]
    return pl.pallas_call(
        experts_forward_kernel,
        grid_spec=pltpu.PrefetchScalarGridSpec(
            num_scalar_prefetch=1,
            grid=(slots, parts),
            in_specs=[source(wide), resident(w_gate), resident(w_up), resident(w_down)],
            out_specs=tuple(step_spec(shape) for shape, unused in saved) + (source(width),),
            scratch_shapes=[
                pltpu.VMEM((owned, held, LANES), F32),
                pltpu.VMEM((pairs, owned, PAIR, width), BF16),
            ],
        ),
        out_shape=tuple(jax.ShapeDtypeStruct((steps,) + shape, kind) for shape, kind in saved)
        + (jax.ShapeDtypeStruct((group, slots, rows, width), BF16),),
        compiler_params=pltpu.CompilerParams(vmem_limit_bytes=60 * MIB),
        name="experts_forward",
    )(scalars, tokens, w_gate, w_up, w_down)


def experts_backward_kernel(
    sc_ref, dy_ref, slab_ref, pick_ref, gp_ref, up_ref, hid_ref, wg_ref, wu_ref, wd_ref,
    part_ref, dyw_ref, gg_ref, ug_ref, gates, dye, dxb,
):
    sources, unused, rows, width = dy_ref.shape
    owned = wg_ref.shape[0]
    pairs = sources // 2
    double = 2 * rows
    first = sc_ref[pl.num_programs(0)] * owned
    for p in range(pairs):
        pick = pick_ref[0, p]
        picked = dot(pick, dy_ref[2 * p : 2 * p + 2].reshape(double, width)).astype(BF16)
        scale = row_gates(dot(pick, slab_ref[2 * p : 2 * p + 2].reshape(double, LANES)), first, owned)
        for e in range(owned):
            dye[e, p * PAIR : (p + 1) * PAIR] = picked[e * PAIR : (e + 1) * PAIR]
            gates[e, p * PAIR : (p + 1) * PAIR] = jnp.broadcast_to(
                scale[e * PAIR : (e + 1) * PAIR], (PAIR, LANES)
            )

    def one(e, carry):
        grad_rows = dye[e]
        scale = gates[e][:, 0:1]
        plain = dot_nt(grad_rows, wd_ref[e])
        gate_part, up_part = gp_ref[0, e], up_ref[0, e]
        soft_grad = jnp.sum(plain * hid_ref[0, e].astype(F32), axis=-1, keepdims=True)
        hidden_grad = plain * scale
        sigma = jax.nn.sigmoid(gate_part)
        gate_grad = (hidden_grad * up_part * sigma * (1.0 + gate_part * (1.0 - sigma))).astype(BF16)
        up_grad = (hidden_grad * gate_part * sigma).astype(BF16)
        gg_ref[0, e] = gate_grad
        ug_ref[0, e] = up_grad
        dyw_ref[0, e] = (grad_rows.astype(F32) * scale).astype(BF16)
        input_grad = (dot_nt(gate_grad, wg_ref[e]) + dot_nt(up_grad, wu_ref[e])).astype(BF16)
        lanes = lane_of((pairs * PAIR, LANES))
        high = soft_grad.astype(BF16).astype(F32)
        spot = jnp.where(
            lanes == first + e, high, jnp.where(lanes == first + e + LANES // 2, soft_grad - high, 0.0)
        ).astype(BF16)
        for p in range(pairs):
            dxb[p, e, :, :width] = input_grad[p * PAIR : (p + 1) * PAIR]
            dxb[p, e, :, width:] = spot[p * PAIR : (p + 1) * PAIR]
        return carry

    lax.fori_loop(0, owned, one, 0)
    for p in range(pairs):
        back = dot_tn(pick_ref[0, p], dxb[p].reshape(owned * PAIR, width + LANES))
        part_ref[2 * p : 2 * p + 2, 0] = back.astype(BF16).reshape(2, rows, width + LANES)


def experts_backward(scalars, grads, tokens, pick, gate_part, up_part, hidden, w_gate, w_up, w_down):
    group, slots, rows, width = grads.shape
    owned, unused, eff = w_gate.shape
    sources = 8
    parts = group // sources
    pairs = sources // 2
    steps = slots * parts
    held = pairs * PAIR
    source = lambda lanes, at: pl.BlockSpec((sources, 1, rows, lanes), lambda s, j, sc: (j, s, 0, at))
    return pl.pallas_call(
        experts_backward_kernel,
        grid_spec=pltpu.PrefetchScalarGridSpec(
            num_scalar_prefetch=1,
            grid=(slots, parts),
            in_specs=[
                source(width, 0),
                source(LANES, width // LANES),
                step_spec((pairs, owned * PAIR, 2 * rows)),
                step_spec((owned, held, eff)),
                step_spec((owned, held, eff)),
                step_spec((owned, held, eff)),
                resident(w_gate), resident(w_up), resident(w_down),
            ],
            out_specs=(
                source(width + LANES, 0),
                step_spec((owned, held, width)),
                step_spec((owned, held, eff)),
                step_spec((owned, held, eff)),
            ),
            scratch_shapes=[
                pltpu.VMEM((owned, held, LANES), F32),
                pltpu.VMEM((owned, held, width), BF16),
                pltpu.VMEM((pairs, owned, PAIR, width + LANES), BF16),
            ],
        ),
        out_shape=(
            jax.ShapeDtypeStruct((group, slots, rows, width + LANES), BF16),
            jax.ShapeDtypeStruct((steps, owned, held, width), BF16),
            jax.ShapeDtypeStruct((steps, owned, held, eff), BF16),
            jax.ShapeDtypeStruct((steps, owned, held, eff), BF16),
        ),
        compiler_params=pltpu.CompilerParams(vmem_limit_bytes=62 * MIB),
        name="experts_backward",
    )(scalars, grads, tokens, pick, gate_part, up_part, hidden, w_gate, w_up, w_down)


def expert_weights_kernel(xe_ref, gg_ref, ug_ref, hid_ref, dyw_ref, dg_ref, du_ref, dd_ref, ag, au, ad):
    step = pl.program_id(1)
    flat = lambda ref: ref[:, 0].reshape(ref.shape[0] * ref.shape[2], ref.shape[3])
    for acc, left, right in ((ad, hid_ref, dyw_ref), (ag, xe_ref, gg_ref), (au, xe_ref, ug_ref)):
        part = dot_tn(flat(left), flat(right))

        @pl.when(step == 0)
        def _():
            acc[...] = part

        @pl.when(step > 0)
        def _():
            acc[...] += part

    @pl.when(step == pl.num_programs(1) - 1)
    def _():
        dg_ref[0] = ag[...].astype(BF16)
        du_ref[0] = au[...].astype(BF16)
        dd_ref[0] = ad[...].astype(BF16)


def expert_weights(xe, gate_grad, up_grad, hidden, weighted):
    steps, owned, held, width = xe.shape
    eff = hidden.shape[3]
    each = 4
    block = lambda lanes: pl.BlockSpec((each, 1, held, lanes), lambda e, i: (i, e, 0, 0))
    out = lambda a, b: pl.BlockSpec((1, a, b), lambda e, i: (e, 0, 0))
    return pl.pallas_call(
        expert_weights_kernel,
        grid=(owned, steps // each),
        in_specs=[block(width), block(eff), block(eff), block(eff), block(width)],
        out_specs=(out(width, eff), out(width, eff), out(eff, width)),
        out_shape=(
            jax.ShapeDtypeStruct((owned, width, eff), BF16),
            jax.ShapeDtypeStruct((owned, width, eff), BF16),
            jax.ShapeDtypeStruct((owned, eff, width), BF16),
        ),
        scratch_shapes=[pltpu.VMEM((width, eff), F32), pltpu.VMEM((width, eff), F32), pltpu.VMEM((eff, width), F32)],
        compiler_params=pltpu.CompilerParams(vmem_limit_bytes=56 * MIB),
        name="expert_weights",
    )(xe, gate_grad, up_grad, hidden, weighted)


def attend_backward_kernel(
    sc_ref, q_ref, kv_ref, mixed_ref, invl_ref, dx_ref, soft_ref, og_ref, after_ref, fg_ref, wr_ref, wo_ref,
    dq_ref, dkv_ref, ag_ref, at_ref, lg_ref, fgg_ref, mg_s,
):
    slot, tile = pl.program_id(0), pl.program_id(1)
    slots, tiles = pl.num_programs(0), pl.num_programs(1)
    rows = q_ref.shape[1]
    here = sc_ref[slots]
    length = sc_ref[slot]
    live = here * rows < length
    chunk = 2 * rows
    chunks = (here + 2) // 2
    width = og_ref.shape[2]

    @pl.when(tile == 0)
    def _():
        valid = (row_of((rows, 1)) + here * rows < length).astype(F32)
        slab = dx_ref[0, :, width:].astype(F32)
        half = slab.shape[1] // 2
        soft = soft_ref[0]
        soft_grad = jnp.where(lane_of(slab.shape) < half, slab + pltpu.roll(slab, half, 1), 0.0)
        chosen = soft * (soft_grad - jnp.sum(soft * soft_grad, axis=-1, keepdims=True))
        logit_grad = chosen.astype(BF16)
        lg_ref[0] = logit_grad
        normed_grad = dx_ref[0, :, :width].astype(F32) + dot_nt(logit_grad, wr_ref[...])
        back, gain_grad = rms_backward(normed_grad, after_ref[0], fg_ref[...])

        @pl.when(slot == 0)
        def _():
            fgg_ref[...] = gain_grad

        @pl.when(slot > 0)
        def _():
            fgg_ref[...] += gain_grad

        after_grad = og_ref[0] + back
        ag_ref[0] = after_grad
        attn_grad = (valid * after_grad).astype(BF16)
        at_ref[0] = attn_grad
        mixed_grad = dot_nt(attn_grad, wo_ref[...]).astype(BF16)
        for t in range(mg_s.shape[0]):
            mg_s[t] = mixed_grad[:, t * 256 : (t + 1) * 256]

    dkv_ref[...] = jnp.zeros_like(dkv_ref)

    @pl.when(live)
    def _():
        q4 = stack_heads(q_ref[0], True).astype(BF16)
        do4_f = stack_heads(mg_s[tile].astype(F32) * invl_ref[0], True)
        do4 = do4_f.astype(BF16)
        product = do4_f * stack_heads(mixed_ref[0], False)
        delta = lax.dot_general(
            jnp.ones((8, LANES), F32), product, (((1,), (1,)), ((), ())),
            preferred_element_type=F32, precision=lax.Precision.HIGHEST,
        )[0:1]

        def step(index, total, masked):
            pair = kv_ref[pl.ds(2 * index, 2), 0]
            keys = pair[:, :, :LANES].reshape(chunk, LANES)
            values = pair[:, :, LANES:].reshape(chunk, LANES)
            weight = jnp.exp2(dot_nt(keys, q4) * EXP2_SCALE)
            if masked:
                at = lax.rem(lane_of(weight.shape), rows) + here * rows
                weight = jnp.where(row_of(weight.shape) + index * chunk <= at, weight, 0.0)
            pressure = dot_nt(values, do4)
            score_grad = (weight * (pressure - delta) * SCALE).astype(BF16)
            key_grad = dot(score_grad, q4)
            value_grad = dot(weight.astype(BF16), do4)
            dkv_ref[pl.ds(2 * index, 2), 0, :, :LANES] = key_grad.astype(BF16).reshape(2, rows, LANES)
            dkv_ref[pl.ds(2 * index, 2), 0, :, LANES:] = value_grad.astype(BF16).reshape(2, rows, LANES)
            return total + dot_tn(score_grad, keys)

        total = lax.fori_loop(
            0, chunks - 1, lambda i, c: step(i, c, False), jnp.zeros((4 * rows, LANES), F32)
        )
        total = step(chunks - 1, total, True)
        dq_ref[0] = unstack_heads(total).astype(BF16)

    @pl.when(jnp.logical_not(live))
    def _():
        dq_ref[...] = jnp.zeros_like(dq_ref)


def attend_backward(scalars, q, kv, mixed, invl, dx, soft, out_grad, after, ffn_gain, router, w_out):
    slots, rows, width = out_grad.shape
    group = kv.shape[0]
    qw = q.shape[2]
    tiles = qw // 256
    row = lambda lanes: pl.BlockSpec((1, rows, lanes), lambda s, b, sc: (s, 0, 0))
    tile = pl.BlockSpec((1, rows, 256), lambda s, b, sc: (s, 0, b))
    group_tile = pl.BlockSpec((group, 1, rows, 256), lambda s, b, sc: (0, s, 0, b))
    whole = lambda a: pl.BlockSpec(a.shape, lambda s, b, sc: (0, 0))
    return pl.pallas_call(
        attend_backward_kernel,
        grid_spec=pltpu.PrefetchScalarGridSpec(
            num_scalar_prefetch=1,
            grid=(slots, tiles),
            in_specs=[
                tile, group_tile, tile, tile, row(width + LANES), row(LANES), row(width), row(width),
                whole(ffn_gain), whole(router), whole(w_out),
            ],
            out_specs=(
                tile, group_tile, row(width), row(width), row(LANES),
                pl.BlockSpec((1, width), lambda s, b, sc: (0, 0)),
            ),
            scratch_shapes=[pltpu.VMEM((tiles, rows, 256), BF16)],
        ),
        out_shape=(
            jax.ShapeDtypeStruct((slots, rows, qw), BF16),
            jax.ShapeDtypeStruct(kv.shape, BF16),
            jax.ShapeDtypeStruct((slots, rows, width), F32),
            jax.ShapeDtypeStruct((slots, rows, width), BF16),
            jax.ShapeDtypeStruct((slots, rows, LANES), BF16),
            jax.ShapeDtypeStruct((1, width), F32),
        ),
        compiler_params=pltpu.CompilerParams(vmem_limit_bytes=56 * MIB),
        name="attend_backward",
    )(scalars, q, kv, mixed, invl, dx, soft, out_grad, after, ffn_gain, router, w_out)


def finish_kernel(
    dq_ref, dkv_ref, qraw_ref, kraw_ref, x_ref, ag_ref, cos_ref, sin_ref, gain_ref, qg_ref, kg_ref,
    wq_ref, wk_ref, wv_ref, h_ref, mixed_ref, at_ref, n2_ref, lg_ref,
    ig_ref, dense_ref, rt_ref, qgg_ref, kgg_ref, agg_ref, q_s, k_s, v_s,
):
    slot = pl.program_id(0)
    rows = x_ref.shape[1]
    cosine, sine = cos_ref[...], sin_ref[...]

    @pl.when(slot == 0)
    def _():
        qgg_ref[...] = jnp.zeros_like(qgg_ref)
        kgg_ref[...] = jnp.zeros_like(kgg_ref)
        agg_ref[...] = jnp.zeros_like(agg_ref)

    here = pl.ds(pl.multiple_of(slot * rows, rows), rows)
    for t in range(dq_ref.shape[2] // LANES):
        lanes = slice(t * LANES, (t + 1) * LANES)
        raw, gain = rope_backward(dq_ref[0, :, lanes].astype(F32), qraw_ref[0, :, lanes], qg_ref[...], cosine, sine)
        q_s[here, lanes] = raw.astype(BF16)
        qgg_ref[...] += gain
    for t in range(kraw_ref.shape[2] // LANES):
        lanes = slice(t * LANES, (t + 1) * LANES)
        at = 2 * t * LANES
        grad = dkv_ref[0, :, at : at + LANES].astype(BF16).astype(F32)
        raw, gain = rope_backward(grad, kraw_ref[0, :, lanes], kg_ref[...], cosine, sine)
        k_s[here, lanes] = raw.astype(BF16)
        kgg_ref[...] += gain
        v_s[here, lanes] = dkv_ref[0, :, at + LANES : at + 2 * LANES].astype(BF16)
    normed_grad = dot_nt(q_s[here], wq_ref[...]) + dot_nt(k_s[here], wk_ref[...]) + dot_nt(v_s[here], wv_ref[...])
    back, gain = rms_backward(normed_grad, x_ref[0].astype(F32), gain_ref[...])
    agg_ref[...] += gain
    ig_ref[0] = ag_ref[0] + back

    @pl.when(slot == pl.num_programs(0) - 1)
    def _():
        flat = lambda ref: ref[...].reshape(ref.shape[0] * ref.shape[1], ref.shape[2])
        shards, unused, shard_rows, width = dense_ref.shape
        h = flat(h_ref)
        half = width // 2

        def put(index, lanes, value):
            dense_ref[:, index, :, lanes] = value.astype(BF16).reshape(shards, shard_rows, value.shape[1])

        put(0, slice(0, width), dot_tn(h, q_s[...]))
        put(1, slice(0, half), dot_tn(h, k_s[...]))
        put(1, slice(half, width), dot_tn(h, v_s[...]))
        put(2, slice(0, width), dot_tn(flat(mixed_ref), flat(at_ref)))
        rt_ref[...] = dot_tn(flat(n2_ref), flat(lg_ref))


def finish(dq, dkv, qraw, kraw, x, after_grad, cosine, sine, attn_gain, qg, kg, wq, wk, wv, h, mixed, attn_grad, n2, lg):
    slots, rows, width = x.shape
    qw, kw = wq.shape[1], wk.shape[1]
    shards = 8
    row = lambda lanes: pl.BlockSpec((1, rows, lanes), lambda s: (s, 0, 0))
    whole = lambda a: pl.BlockSpec(a.shape, lambda s: (0,) * a.ndim)
    lanes_out = pl.BlockSpec((1, LANES), lambda s: (0, 0))
    return pl.pallas_call(
        finish_kernel,
        grid=(slots,),
        in_specs=[row(qw), row(2 * kw), row(qw), row(kw), row(width), row(width)]
        + [whole(a) for a in (cosine, sine, attn_gain, qg, kg, wq, wk, wv, h, mixed, attn_grad)]
        + [pl.BlockSpec((slots, rows, width), lambda s: (0, 0, 0)), whole(lg)],
        out_specs=(
            row(width),
            pl.BlockSpec((shards, 3, width // shards, width), lambda s: (0, 0, 0, 0)),
            pl.BlockSpec((width, LANES), lambda s: (0, 0)),
            lanes_out, lanes_out, pl.BlockSpec((1, width), lambda s: (0, 0)),
        ),
        out_shape=(
            jax.ShapeDtypeStruct((slots, rows, width), F32),
            jax.ShapeDtypeStruct((shards, 3, width // shards, width), BF16),
            jax.ShapeDtypeStruct((width, LANES), F32),
            jax.ShapeDtypeStruct((1, LANES), F32),
            jax.ShapeDtypeStruct((1, LANES), F32),
            jax.ShapeDtypeStruct((1, width), F32),
        ),
        scratch_shapes=[
            pltpu.VMEM((slots * rows, qw), BF16),
            pltpu.VMEM((slots * rows, kw), BF16),
            pltpu.VMEM((slots * rows, kw), BF16),
        ],
        compiler_params=pltpu.CompilerParams(vmem_limit_bytes=60 * MIB),
        name="finish",
    )(dq, dkv, qraw, kraw, x, after_grad, cosine, sine, attn_gain, qg, kg, wq, wk, wv, h, mixed, attn_grad, n2, lg)


def remote(src, dst, ss, rs, dev):
    return pltpu.make_async_remote_copy(src_ref=src, dst_ref=dst, send_sem=ss, recv_sem=rs, device_id=dev, device_id_type=MESH)


class Slots:
    def __init__(self, plane, mine, out, sent, got, local):
        self.plane, self.mine, self.out, self.sent, self.got, self.local = plane, mine, out, sent, got, local
        rows = mine.shape[1]
        self.halves = (pl.ds(0, rows // 2), pl.ds(rows // 2, rows // 2))
        self.at = (plane.own[1], plane.own[2], plane.own[0])

    def own(self, number, s):
        who = (self.plane.xn, self.plane.yn, self.plane.sib)[number]
        return remote(self.mine.at[s], self.out.at[self.plane.me, s], self.sent.at[number, s], self.got.at[number, s], who)

    def keep(self, s):
        return pltpu.make_async_copy(self.mine.at[s], self.out.at[self.plane.me, s], self.local.at[s])

    def pass_on(self, number, s):
        view = self.out.at[self.at[number], s]
        return remote(view, view, self.sent.at[3 + number, s], self.got.at[3 + number, s], self.plane.sib)

    def far(self, number, s):
        at, who = ((self.at[0], self.plane.yn), (self.at[1], self.plane.xn))[number]
        view = self.out.at[at, s, self.halves[number]]
        return remote(view, view, self.sent.at[6 + number, s], self.got.at[6 + number, s], who)

    def start(self, s):
        for number in range(3):
            self.own(number, s).start()
        self.keep(s).start()

    def forward(self, s):
        for number in range(2):
            self.own(number, s).wait_recv()
            self.far(number, s).start()
            self.pass_on(number, s).start()

    def settle(self, s):
        for number in range(2):
            self.far(number, s).wait_recv()
        self.pass_on(2, s).start()

    def arrive(self, s):
        self.keep(s).wait()
        self.own(2, s).wait_recv()
        for number in range(3):
            self.pass_on(number, s).wait_recv()

    def drain(self, s):
        for number in range(3):
            self.own(number, s).wait_send()
            self.pass_on(number, s).wait_send()
        for number in range(2):
            self.far(number, s).wait_send()


def front_kernel(
    sc_ref, x_in, teacher_in, routes_ref, wq_in, wk_in, wv_in, wo_in, wg_in, wu_in, wd_in,
    gain_ref, fg_ref, qg_ref, kg_ref, cos_ref, sin_ref, wr_ref, scale_ref,
    h_out, q_out, qraw_out, kraw_out, kv_out, mixed_out, invl_out, after_out, soft_out, tokens_out,
    pick_out, xe_out, gp_out, up_out, hid_out, y_out, og_out, loss_out, grads_out,
    sb, da, db, rx, ry, parts, wg, wu, wd, after_s, xg_s, dy_s,
    sent_kv, got_kv, loc_kv, sent_xg, got_xg, loc_xg, sent_dy, got_dy, loc_dy, sent_rs, got_rs, wsem, local,
):
    plane = Plane()
    slots, rows, width = x_in.shape
    group = kv_out.shape[0]
    qw, kw = wq_in.shape[1], wk_in.shape[1]
    tiles = qw // 256
    here = plane.me
    owned = wg_in.shape[0]
    first = here * owned
    wide = xg_s.shape[2]
    each = lambda body, start=0, stop=slots: lax.fori_loop(start, stop, lambda s, c: (body(s), c)[1], 0)
    row_gather = Slots(plane, xg_s, tokens_out, sent_xg, got_xg, loc_xg)
    grad_gather = Slots(plane, dy_s, grads_out, sent_dy, got_dy, loc_dy)
    scatter = Scatter(
        plane, lambda k, s: parts.at[plane.own[k], s], lambda k, s: parts.at[plane.other[k], s],
        (sb, da, db, rx, ry), (sent_rs, got_rs),
    )
    expert_loads = [
        pltpu.make_async_copy(source, there, wsem.at[n])
        for n, (source, there) in enumerate(((wg_in, wg), (wu_in, wu), (wd_in, wd)))
    ]

    def first_phase(wq, wk, wv, wo, xb, kvl, q_s, h_s, qraw_s, kraw_s, kvb, mixed_s, invl_s, soft_s, acc, sems, out_sems):
        loads = [
            pltpu.make_async_copy(source, there, sems.at[n])
            for n, (source, there) in enumerate(((x_in, xb), (wk_in, wk), (wv_in, wv), (wq_in, wq), (wo_in, wo)))
        ]
        for copy in loads:
            copy.start()
        for copy in expert_loads:
            copy.start()
        kv_gather = Slots(plane, kvl, kv_out, sent_kv, got_kv, loc_kv)
        plane.barrier(False)
        for copy in loads[:4]:
            copy.wait()

        def project_two(s):
            two = pl.ds(s, 2)
            x = xb[two].astype(F32).reshape(2 * rows, width)
            unit, unused = rms_parts(x)
            normed = (unit * gain_ref[...]).astype(BF16)
            h_s[two] = normed.reshape(2, rows, width)
            cosine = jnp.concatenate([cos_ref[...]] * 2, axis=0)
            sine = jnp.concatenate([sin_ref[...]] * 2, axis=0)
            k_raw = dot(normed, wk[...])
            kraw_s[two] = k_raw.reshape(2, rows, kw)
            value = dot(normed, wv[...]).astype(BF16)
            for tile in range(kw // LANES):
                lanes = slice(tile * LANES, (tile + 1) * LANES)
                turned = rope_forward(k_raw[:, lanes], kg_ref[...], cosine, sine)
                at = 2 * tile * LANES
                kvl[two, :, at : at + LANES] = turned.astype(BF16).reshape(2, rows, LANES)
                kvl[two, :, at + LANES : at + 2 * LANES] = value[:, lanes].reshape(2, rows, LANES)
            kv_gather.start(s)
            kv_gather.start(s + 1)
            q_raw = dot(normed, wq[...])
            qraw_s[two] = q_raw.reshape(2, rows, qw)
            for tile in range(qw // LANES):
                lanes = slice(tile * LANES, (tile + 1) * LANES)
                turned = rope_forward(q_raw[:, lanes], qg_ref[...], cosine, sine)
                q_s[two, :, lanes] = turned.astype(BF16).reshape(2, rows, LANES)

        lax.fori_loop(0, slots // 2, lambda n, c: (project_two(2 * n), c)[1], 0)
        keeps = [
            pltpu.make_async_copy(source, there, out_sems.at[n])
            for n, (source, there) in enumerate(((h_s, h_out), (q_s, q_out), (qraw_s, qraw_out), (kraw_s, kraw_out)))
        ]
        for copy in keeps:
            copy.start()
        kv_gather.forward(0)
        kv_gather.forward(1)
        kv_gather.settle(0)
        loads[4].wait()

        def attend_slot(s):
            load = pltpu.make_async_copy(kv_out.at[:, s], kvb, sems.at[5])
            load.start()
            load.wait()
            chunk = 2 * rows
            chunks = (here + 2) // 2
            acc[...] = jnp.zeros_like(acc)

            def one_tile(t, carry):
                lanes = pl.ds(pl.multiple_of(t * 256, 256), 256)
                key_lanes = pl.ds(pl.multiple_of(t * 256, 256), LANES)
                value_lanes = pl.ds(pl.multiple_of(t * 256 + LANES, LANES), LANES)
                q4 = stack_heads(q_s[s, :, lanes], True).astype(BF16)

                def step(index, carry, masked):
                    mass, total = carry
                    two = pl.ds(2 * index, 2)
                    keys = kvb[two, :, key_lanes].reshape(chunk, LANES)
                    values = kvb[two, :, value_lanes].reshape(chunk, LANES)
                    weight = jnp.exp2(dot_nt(q4, keys) * EXP2_SCALE)
                    if masked:
                        at = lax.rem(row_of(weight.shape), rows) + here * rows
                        weight = jnp.where(lane_of(weight.shape) + index * chunk <= at, weight, 0.0)
                    for part in range(chunk // LANES):
                        mass = mass + weight[:, part * LANES : (part + 1) * LANES]
                    return mass, total + dot(weight.astype(BF16), values)

                blank = jnp.zeros((4 * rows, LANES), F32)
                state = lax.fori_loop(0, chunks - 1, lambda i, c: step(i, c, False), (blank, blank))
                mass, total = step(chunks - 1, state, True)
                inverse = 1.0 / jnp.sum(mass, axis=-1, keepdims=True)
                mixed = unstack_heads(total * inverse).astype(BF16)
                mixed_s[s, :, lanes] = mixed
                invl_s[s, :, lanes] = unstack_heads(jnp.broadcast_to(inverse, total.shape))
                acc[...] += dot(mixed, wo[pl.ds(pl.multiple_of(t * 256, 256), 256)])
                return carry

            lax.fori_loop(0, tiles, one_tile, 0)
            valid = (row_of((rows, 1)) + here * rows < sc_ref[s]).astype(F32)
            after = xb[s].astype(F32) + valid * acc[...]
            after_s[s] = after
            unit, unused = rms_parts(after)
            normed = (unit * fg_ref[...]).astype(BF16)
            xg_s[s, :, :width] = normed
            logits = dot(normed, wr_ref[...])
            lanes = lane_of(logits.shape)
            routes = routes_ref[s]
            chosen = lanes == routes[:, 0:1]
            for k in range(1, routes.shape[1]):
                chosen = chosen | (lanes == routes[:, k : k + 1])
            top = jnp.max(jnp.where(chosen, logits, -1e30), axis=-1, keepdims=True)
            weight = jnp.where(chosen, jnp.exp(jnp.minimum(logits - top, 0.0)), 0.0)
            soft = weight / jnp.sum(weight, axis=-1, keepdims=True)
            soft_s[s] = soft
            gates = soft * valid
            high = gates.astype(BF16).astype(F32)
            xg_s[s, :, width:] = (high + pltpu.roll(gates - high, LANES // 2, 1)).astype(BF16)

        def one(t):
            kv_gather.arrive(t)
            attend_slot(t)
            row_gather.start(t)

            @pl.when(t <= slots - 3)
            def _():
                kv_gather.forward(t + 2)

            @pl.when(t <= slots - 2)
            def _():
                kv_gather.settle(t + 1)

            @pl.when(t >= 1)
            def _():
                row_gather.forward(t - 1)

            @pl.when(t >= 2)
            def _():
                row_gather.settle(t - 2)

        each(one)
        keeps += [
            pltpu.make_async_copy(source, there, out_sems.at[4 + n])
            for n, (source, there) in enumerate(
                ((mixed_s, mixed_out), (invl_s, invl_out), (after_s, after_out), (soft_s, soft_out))
            )
        ]
        for copy in keeps[4:]:
            copy.start()
        each(kv_gather.drain)
        for copy in keeps:
            copy.wait()

    V, D = pltpu.VMEM, pltpu.SemaphoreType.DMA
    full = lambda lanes, kind: V((slots, rows, lanes), kind)
    pl.run_scoped(
        first_phase,
        V(wq_in.shape, BF16), V(wk_in.shape, BF16), V(wv_in.shape, BF16), V(wo_in.shape, BF16),
        full(width, BF16), full(2 * kw, BF16), full(qw, BF16), full(width, BF16), full(qw, F32), full(kw, F32),
        V((group, rows, 2 * kw), BF16), full(qw, BF16), full(qw, F32), full(LANES, F32), V((rows, width), F32),
        D((6,)), D((8,)),
    )
    sources, double, pairs, held = group, 2 * rows, group // 2, group // 2 * PAIR

    def second_phase(tok, pick_s, xe_s, gp_s, up_s, hid_s, gates, ybuf, teach, y_s, og_s, sems, out_sems):
        teacher_load = pltpu.make_async_copy(teacher_in, teach, sems.at[1])
        teacher_load.start()
        for copy in expert_loads:
            copy.wait()
        teacher_load.wait()
        loss_out[...] = jnp.zeros_like(loss_out)
        keeps = lambda s: [
            pltpu.make_async_copy(source, there.at[s], out_sems.at[n])
            for n, (source, there) in enumerate(
                ((pick_s, pick_out), (xe_s, xe_out), (gp_s, gp_out), (up_s, up_out), (hid_s, hid_out))
            )
        ]

        def experts_slot(s, between):
            load = pltpu.make_async_copy(tokens_out.at[:, s], tok, sems.at[0])
            load.start()

            @pl.when(s >= 1)
            def _():
                for copy in keeps(s - 1):
                    copy.wait()

            load.wait()
            slab = tok[:, :, width:].reshape(sources * rows, LANES)
            chosen = (lane_of((8, LANES)) == row_of((8, LANES)) + first).astype(BF16)
            routed = dot_nt(chosen, slab) > 0.0
            before, after = row_of((double, double)), lane_of((double, double))
            count = ((before < after) & (before // rows == after // rows)).astype(BF16)
            place = lax.broadcasted_iota(jnp.int32, (PAIR, double), 0)
            offset = (lane_of((8, double)) // rows) * MOST
            for p in range(pairs):
                mask = routed[:, p * double : (p + 1) * double]
                rank = dot(mask.astype(F32).astype(BF16), count).astype(jnp.int32) + offset
                rank = jnp.where(mask, rank, -1)
                pick = jnp.concatenate(
                    [(place == rank[e : e + 1, :]).astype(F32).astype(BF16) for e in range(owned)], axis=0
                )
                pick_s[p] = pick
                picked = dot(pick, tok[2 * p : 2 * p + 2, :, :width].reshape(double, width)).astype(BF16)
                scale = row_gates(dot(pick, slab[p * double : (p + 1) * double]), first, owned)
                for e in range(owned):
                    xe_s[e, p * PAIR : (p + 1) * PAIR] = picked[e * PAIR : (e + 1) * PAIR]
                    gates[e, p * PAIR : (p + 1) * PAIR] = jnp.broadcast_to(
                        scale[e * PAIR : (e + 1) * PAIR], (PAIR, LANES)
                    )

            def one_expert(e, carry):
                rows_in = xe_s[e]
                gate_part = dot(rows_in, wg[e])
                up_part = dot(rows_in, wu[e])
                gp_s[e] = gate_part
                up_s[e] = up_part
                hidden = (gate_part * jax.nn.sigmoid(gate_part) * up_part).astype(BF16)
                hid_s[e] = hidden
                result = (dot(hidden, wd[e]) * gates[e][:, 0:1]).astype(BF16)
                for p in range(pairs):
                    ybuf[p, e] = result[p * PAIR : (p + 1) * PAIR]
                return carry

            lax.fori_loop(0, owned // 2, one_expert, 0)
            between()
            lax.fori_loop(owned // 2, owned, one_expert, 0)
            for p in range(pairs):
                back = dot_tn(pick_s[p], ybuf[p].reshape(owned * PAIR, width))
                parts[2 * p : 2 * p + 2, s] = back.astype(BF16).reshape(2, rows, width)
            for copy in keeps(s):
                copy.start()

        def loss_slot(s):
            output = after_s[s] + scatter.result(s)
            y_s[s] = output.astype(BF16)
            valid = (row_of((rows, 1)) + here * rows < sc_ref[s]).astype(F32)
            difference = valid * (output - teach[s].astype(F32))
            square = jnp.sum(difference * difference, axis=0, keepdims=True)
            loss_out[...] += square
            grad = difference * scale_ref[0]
            og_s[s] = grad
            dy_s[s] = grad.astype(BF16)
            grad_gather.start(s)

        def one(t):
            row_gather.arrive(t)

            def between():
                @pl.when(t == 0)
                def _():
                    row_gather.settle(slots - 2)
                    row_gather.forward(slots - 1)

                @pl.when(t == 1)
                def _():
                    row_gather.settle(slots - 1)

                @pl.when(t >= 1)
                def _():
                    scatter.first(t - 1)
                    scatter.second(t - 1)

                @pl.when(t == slots - 1)
                def _():
                    grad_gather.forward(0)

            experts_slot(t, between)
            scatter.start(t)

            @pl.when(t >= 1)
            def _():
                scatter.third(t - 1)

            @pl.when(t >= 2)
            def _():
                loss_slot(t - 2)

        each(one)
        last = slots - 1
        scatter.first(last)
        scatter.second(last)
        loss_slot(last - 1)
        grad_gather.settle(0)
        grad_gather.forward(1)
        scatter.third(last)
        grad_gather.settle(1)
        loss_slot(last)
        outs = [
            pltpu.make_async_copy(source, there, sems.at[n]) for n, (source, there) in enumerate(((y_s, y_out), (og_s, og_out)))
        ]
        for copy in outs:
            copy.start()
        for s in range(2, slots):
            grad_gather.forward(s)
            grad_gather.settle(s)
        each(grad_gather.arrive)
        each(grad_gather.drain)
        each(row_gather.drain)
        each(scatter.drain)
        for copy in keeps(last) + outs:
            copy.wait()

    eff = wg_in.shape[2]
    pl.run_scoped(
        second_phase,
        V((group, rows, wide), BF16), V((pairs, owned * PAIR, double), BF16), V((owned, held, width), BF16),
        V((owned, held, eff), F32), V((owned, held, eff), F32), V((owned, held, eff), BF16), V((owned, held, LANES), F32),
        V((pairs, owned, PAIR, width), BF16), full(width, BF16), full(width, BF16), full(width, F32), D((2,)), D((5,)),
    )


def front(
    slot_lengths, x, teacher, routes, w_query, w_key, w_value, w_out, w_gate, w_up, w_down,
    attn_gain, ffn_gain, qg, kg, cosine, sine, router, scale, group, number,
):
    slots, rows, width = x.shape
    qw, kw = w_query.shape[1], w_key.shape[1]
    owned, unused, eff = w_gate.shape
    wide = width + LANES
    pairs = group // 2
    held = pairs * PAIR
    hbm = pl.BlockSpec(memory_space=pl.ANY)
    vmem = pl.BlockSpec(memory_space=pltpu.VMEM)
    smem = pl.BlockSpec(memory_space=pltpu.SMEM)
    V, D = pltpu.VMEM, pltpu.SemaphoreType.DMA
    half = rows // 2
    mine = lambda lanes, kind: jax.ShapeDtypeStruct((slots, rows, lanes), kind)
    all_of = lambda lanes: jax.ShapeDtypeStruct((group, slots, rows, lanes), BF16)
    saved = lambda *dims: jax.ShapeDtypeStruct((slots,) + dims, BF16)
    outs = (
        mine(width, BF16), mine(qw, BF16), mine(qw, F32), mine(kw, F32), all_of(2 * kw), mine(qw, BF16), mine(qw, F32),
        mine(width, F32), mine(LANES, F32), all_of(wide),
        saved(pairs, owned * PAIR, 2 * rows), saved(owned, held, width),
        jax.ShapeDtypeStruct((slots, owned, held, eff), F32), jax.ShapeDtypeStruct((slots, owned, held, eff), F32),
        saved(owned, held, eff), mine(width, BF16), mine(width, F32), jax.ShapeDtypeStruct((1, width), F32), all_of(width),
    )
    return pl.pallas_call(
        front_kernel,
        in_specs=[smem, hbm, hbm, vmem] + [hbm] * 7 + [vmem] * 7 + [smem],
        out_specs=(hbm,) * 17 + (vmem, hbm),
        out_shape=outs,
        scratch_shapes=[
            V((4, slots, rows, width), BF16), V((slots, half, width), BF16), V((slots, half, width), BF16),
            V((slots, rows, width), BF16), V((slots, rows, width), BF16),
            V((group, slots, rows, width), BF16),
            V(w_gate.shape, BF16), V(w_up.shape, BF16), V(w_down.shape, BF16),
            V((slots, rows, width), F32), V((slots, rows, wide), BF16), V((slots, rows, width), BF16),
        ]
        + [D((8, slots)), D((8, slots)), D((slots,))] * 3
        + [D((10, slots)), D((10, slots)), D((3,)), D((1,))],
        compiler_params=pltpu.CompilerParams(collective_id=number, has_side_effects=True, vmem_limit_bytes=63 * MIB),
        name="front",
    )(
        slot_lengths, x, teacher, routes, w_query, w_key, w_value, w_out, w_gate, w_up, w_down,
        attn_gain, ffn_gain, qg, kg, cosine, sine, router, scale,
    )


def add_to(ref, value):
    ref[...] = (ref[...].astype(F32) + value).astype(ref.dtype)


class Plane:
    def __init__(self):
        z, c, y = lax.axis_index("dp"), lax.axis_index("context"), lax.axis_index("experts")
        core = lax.rem(c, 2)
        cx, yy = lax.rem(c + 2, 4), 1 - y
        self.me = c * 2 + y
        self.sib, self.xn, self.yn = (z, c + 1 - 2 * core, y), (z, cx, y), (z, c, yy)
        chips = [(cx, yy), (cx, y), (c, yy), (c, y)]
        self.own = [a * 2 + b for a, b in chips]
        self.other = [(a + 1 - 2 * core) * 2 + b for a, b in chips]
        self.inner_plane = (z == 1) | (z == 2)
        self.outer_plane = (z == 0) | (z == 3)
        self.inner = (1 + z // 2, c, y)
        self.across = (3 - z, c, y)
        self.outer = ((z - 1) * 3, c, y)

    def barrier(self, line):
        bar = pltpu.get_barrier_semaphore()
        tell = lambda who: pl.semaphore_signal(bar, inc=1, device_id=who, device_id_type=MESH)
        for who in (self.sib, self.xn, self.yn):
            tell(who)
        if not line:
            pl.semaphore_wait(bar, 3)
            return

        @pl.when(self.outer_plane)
        def _():
            tell(self.inner)
            pl.semaphore_wait(bar, 4)

        @pl.when(self.inner_plane)
        def _():
            tell(self.across)
            tell(self.outer)
            pl.semaphore_wait(bar, 5)


class Scatter:
    def __init__(self, plane, own, other, buffers, sems):
        self.plane, self.own, self.other = plane, own, other
        self.sb, self.da, self.db, self.rx, self.ry = buffers
        self.sent, self.got = sems
        self.rows = self.sb.shape[2]
        self.top, self.low = pl.ds(0, self.rows // 2), pl.ds(self.rows // 2, self.rows // 2)

    def core(self, k, s):
        return remote(self.other(k, s), self.sb.at[k, s], self.sent.at[k, s], self.got.at[k, s], self.plane.sib)

    def diag(self, s):
        mine = self.own(0, s)
        return (
            remote(mine.at[self.top], self.da.at[s], self.sent.at[4, s], self.got.at[4, s], self.plane.xn),
            remote(mine.at[self.low], self.db.at[s], self.sent.at[5, s], self.got.at[5, s], self.plane.yn),
        )

    def side(self, number, s):
        axis, half = number // 2, (self.top, self.low)[number % 2]
        there = (self.rx, self.ry)[axis]
        who = (self.plane.xn, self.plane.yn)[axis]
        return remote(
            self.own(1 + axis, s).at[half], there.at[s, half], self.sent.at[6 + number, s], self.got.at[6 + number, s], who
        )

    def pair(self, k, s, half):
        return self.own(k, s)[half].astype(F32) + self.sb[k, s, half].astype(F32)

    def start(self, s):
        for k in range(4):
            self.core(k, s).start()

    def first(self, s):
        self.core(0, s).wait_recv()
        mine = self.own(0, s)
        add_to(mine, self.sb[0, s].astype(F32))
        for copy in self.diag(s):
            copy.start()

    def second(self, s):
        self.core(1, s).wait_recv()
        self.own(1, s)[self.top] = self.pair(1, s, self.top).astype(BF16)
        self.side(0, s).start()
        self.core(2, s).wait_recv()
        self.own(2, s)[self.low] = self.pair(2, s, self.low).astype(BF16)
        self.side(3, s).start()

    def third(self, s):
        by_x, by_y = self.diag(s)
        by_x.wait_recv()
        self.own(2, s)[self.top] = (self.pair(2, s, self.top) + self.da[s].astype(F32)).astype(BF16)
        self.side(2, s).start()
        by_y.wait_recv()
        self.own(1, s)[self.low] = (self.pair(1, s, self.low) + self.db[s].astype(F32)).astype(BF16)
        self.side(1, s).start()

    def result(self, s):
        self.core(3, s).wait_recv()
        for number in range(4):
            self.side(number, s).wait_recv()
        return (
            self.own(3, s)[...].astype(F32)
            + self.sb[3, s].astype(F32)
            + self.rx[s].astype(F32)
            + self.ry[s].astype(F32)
        )

    def drain(self, s):
        for k in range(4):
            self.core(k, s).wait_send()
        for copy in self.diag(s):
            copy.wait_send()
        for number in range(4):
            self.side(number, s).wait_send()


class Line:
    ring, back = 4, 2

    def __init__(self, plane, held, first, second, total, buffers, sems):
        self.plane, self.held, self.r1, self.r2, self.total = plane, held, first, second, total
        self.l1, self.va, self.vt = buffers
        self.sent, self.got, self.local = sems
        self.count = held.shape[0]

    def inward(self, i):
        return remote(self.held.at[i], self.r1.at[i], self.sent.at[0, i], self.got.at[0, i], self.plane.inner)

    def across(self, i):
        return remote(self.va.at[i % self.ring], self.r2.at[i], self.sent.at[1, i], self.got.at[1, i], self.plane.across)

    def outward(self, i):
        return remote(self.vt.at[i % self.back], self.total.at[i], self.sent.at[2, i], self.got.at[2, i], self.plane.outer)

    def keep(self, i):
        return pltpu.make_async_copy(self.vt.at[i % self.back], self.total.at[i], self.local.at[i % self.back])

    def load(self, number, i):
        source, there = (
            (self.r1, self.l1.at[i % 2]), (self.held, self.va.at[i % self.ring]), (self.r2, self.vt.at[i % self.back])
        )[number]
        return pltpu.make_async_copy(source.at[i], there, self.local.at[self.ring + 2 * number + i % 2])

    def when(self, fact, body):
        if isinstance(fact, bool):
            if fact:
                body()
        else:
            pl.when(fact)(body)

    def take(self, i):
        def wait():
            self.across(i - self.ring).wait_send()

        self.when(i >= self.ring, wait)
        self.load(1, i).start()
        self.inward(i).wait_recv()
        self.load(0, i).start()

    def give(self, i):
        self.load(1, i).wait()
        self.load(0, i).wait()
        add_to(self.va.at[i % self.ring], self.l1[i % 2].astype(F32))
        self.across(i).start()

    def fetch(self, i):
        def wait():
            self.outward(i - self.back).wait_send()
            self.keep(i - self.back).wait()

        self.when(i >= self.back, wait)
        self.across(i).wait_recv()
        self.load(2, i).start()

    def settle(self, i):
        self.load(2, i).wait()
        add_to(self.vt.at[i % self.back], self.va[i % self.ring].astype(F32))
        self.outward(i).start()
        self.keep(i).start()

    def move(self, i, lag=2):
        @pl.when(self.plane.inner_plane)
        def _():
            self.take(i)
            self.when(i >= lag, lambda: self.fetch(i - lag))
            self.give(i)
            self.when(i >= lag, lambda: self.settle(i - lag))

    def wind_up(self, start):
        @pl.when(self.plane.inner_plane)
        def _():
            for i in range(start, self.count + 1):
                if i < self.count:
                    self.take(i)
                    self.give(i)
                for n in ([start - 2] if i == start else []) + [i - 1]:
                    self.fetch(n)
                    self.settle(n)

    def finish(self):
        @pl.when(self.plane.inner_plane)
        def _():
            for i in range(self.count - self.ring, self.count):
                self.across(i).wait_send()
            for i in range(self.count - self.back, self.count):
                self.outward(i).wait_send()
                self.keep(i).wait()

        @pl.when(self.plane.outer_plane)
        def _():
            def one(i, carry):
                self.inward(i).wait_send()
                remote(
                    self.held.at[i], self.total.at[i], self.sent.at[2, i], self.got.at[2, i], self.plane.inner
                ).wait_recv()
                return carry

            lax.fori_loop(0, self.count, one, 0)


HELD_BACK = 14


def tail_kernel(
    sc_ref, dpart, xe, gg, ug, hid, dyw, q_in, kv_in, mixed_in, invl_in, soft_in, og_in, after_in, qraw_in, kraw_in,
    x_in, h_in, n2_in, wo_in, wq_in, wk_in, wv_in, fg_ref, wr_ref, cos_ref, sin_ref, gain_ref, qg_ref, kg_ref, loss_ref,
    total, ig_out, dense_out, small_out, held, r1, r2,
    dx_own, dx_sb, dx_da, dx_db, dx_rx, dx_ry, kv_sb, kv_da, kv_db, kv_rx, kv_ry,
    l1, va, vt, dsh, dr1, dr2, dfin, sm_mine, sm_got,
    sent_dx, got_dx, sent_kv, got_kv, sent_de, got_de, sent_z, got_z, local_z, sent_ag, got_ag, sent_sm, got_sm, local,
):
    plane = Plane()
    slots, rows = x_in.shape[0], x_in.shape[1]
    width = x_in.shape[2]
    group = dpart.shape[0]
    kinds = dsh.shape[0]
    owned = xe.shape[1]
    eff = gg.shape[3]
    each = lambda body, count=slots: lax.fori_loop(0, count, lambda s, c: (body(s), c)[1], 0)
    line = Line(plane, held, r1, r2, total, (l1, va, vt), (sent_z, got_z, local_z))
    scat_dx = Scatter(
        plane, lambda k, s: dx_own.at[k, s], lambda k, s: dpart.at[plane.other[k], s],
        (dx_sb, dx_da, dx_db, dx_rx, dx_ry), (sent_dx, got_dx),
    )
    own_load = lambda k, s: pltpu.make_async_copy(dpart.at[plane.own[k], s], dx_own.at[k, s], local.at[0])
    for k in range(4):
        each(lambda s: own_load(k, s).start())
    def expert_phase(xeb, ggb, ugb, hidb, dywb, gb, sems, out_sem):
        def loads(e):
            slot = e % 2
            return [
                pltpu.make_async_copy(source.at[:, e], there.at[slot], sems.at[slot, n])
                for n, (source, there) in enumerate(((xe, xeb), (gg, ggb), (ug, ugb), (hid, hidb), (dyw, dywb)))
            ]

        def store(number):
            return pltpu.make_async_copy(gb.at[number % 4], held.at[pl.ds(2 * number, 2)], out_sem.at[number % 4])

        def send(number):
            store(number).wait()
            todo = [2 * number + n for n in range(2) if 2 * number + n < HELD_BACK]
            if todo:
                @pl.when(plane.outer_plane)
                def _():
                    for i in todo:
                        line.inward(i).start()

        flat = lambda ref, slot: ref[slot].reshape(ref.shape[1] * ref.shape[2], ref.shape[3])
        half = width // 2
        for copy in loads(0):
            copy.start()
        plane.barrier(True)
        each(scat_dx.start)
        for e in range(owned):
            slot = e % 2
            if e + 1 < owned:
                for copy in loads(e + 1):
                    copy.start()
            for copy in loads(e):
                copy.wait()
            for n, (left, right) in enumerate(((xeb, ggb), (xeb, ugb), (hidb, dywb))):
                number = 3 * e + n
                part = dot_tn(flat(left, slot), flat(right, slot)).astype(BF16)
                gb[number % 4, 0] = part[:half] if n < 2 else part[:, :half]
                gb[number % 4, 1] = part[half:] if n < 2 else part[:, half:]
                store(number).start()
                if number >= 1:
                    send(number - 1)
            if e == 1:
                for k in range(4):
                    each(lambda s: own_load(k, s).wait())
                each(scat_dx.first)
            if e == 2:
                each(scat_dx.second)
                line.move(0)
        send(3 * owned - 1)
        line.move(1)
        each(scat_dx.third)

    held_rows = (xe.shape[0], xe.shape[2])
    pl.run_scoped(
        expert_phase,
        pltpu.VMEM((2,) + held_rows + (width,), BF16),
        pltpu.VMEM((2,) + held_rows + (eff,), BF16),
        pltpu.VMEM((2,) + held_rows + (eff,), BF16),
        pltpu.VMEM((2,) + held_rows + (eff,), BF16),
        pltpu.VMEM((2,) + held_rows + (width,), BF16),
        pltpu.VMEM((4, 2, eff, width // 2), BF16),
        pltpu.SemaphoreType.DMA((2, 5)),
        pltpu.SemaphoreType.DMA((4,)),
    )
    line.move(2)
    here = plane.me
    chunk = 2 * rows
    chunks = (here + 2) // 2
    qw = q_in.shape[2]
    kw = kraw_in.shape[2]
    tiles = qw // 256

    def rest(dkv, ag_s, at_s, lg_s, mixed_s, q_s, qgg, kgg, agg, fgg, mg_s):
        scat_kv = Scatter(
            plane, lambda k, s: dkv.at[plane.own[k], s], lambda k, s: dkv.at[plane.other[k], s],
            (kv_sb, kv_da, kv_db, kv_rx, kv_ry), (sent_kv, got_kv),
        )
        for ref in (qgg, kgg, agg, fgg):
            ref[...] = jnp.zeros_like(ref)
        mixed_load = pltpu.make_async_copy(mixed_in, mixed_s, local.at[1])
        mixed_load.start()

        def attention_phase(wo, qb, kvb, invlb, softb, ogb, afterb, qrawb, sems):
            wo_load = pltpu.make_async_copy(wo_in, wo, local.at[2])
            wo_load.start()

            def loads(s):
                slot = lax.rem(s, 2)
                out = [pltpu.make_async_copy(kv_in.at[:, s], kvb.at[slot], sems.at[slot, 0])]
                for n, (source, there) in enumerate(
                    ((q_in, qb), (invl_in, invlb), (soft_in, softb), (og_in, ogb), (after_in, afterb), (qraw_in, qrawb))
                ):
                    out.append(pltpu.make_async_copy(source.at[s], there.at[slot], sems.at[slot, n + 1]))
                return out

            for s in range(2):
                for copy in loads(s):
                    copy.start()
            wo_load.wait()
            mixed_load.wait()

            def one_slot(s):
                slot = lax.rem(s, 2)
                for copy in loads(s):
                    copy.wait()
                dx = scat_dx.result(s)
                valid = (row_of((rows, 1)) + here * rows < sc_ref[s]).astype(F32)
                slab = dx[:, width:]
                half = slab.shape[1] // 2
                soft = softb[slot]
                soft_grad = jnp.where(lane_of(slab.shape) < half, slab + pltpu.roll(slab, half, 1), 0.0)
                chosen = soft * (soft_grad - jnp.sum(soft * soft_grad, axis=-1, keepdims=True))
                logit_grad = chosen.astype(BF16)
                lg_s[s] = logit_grad
                normed_grad = dx[:, :width] + dot_nt(logit_grad, wr_ref[...])
                back, gain_grad = rms_backward(normed_grad, afterb[slot], fg_ref[...])
                fgg[...] += gain_grad
                after_grad = ogb[slot] + back
                ag_s[s] = after_grad
                attn_grad = (valid * after_grad).astype(BF16)
                at_s[s] = attn_grad
                mixed_grad = dot_nt(attn_grad, wo[...]).astype(BF16)
                for t in range(tiles):
                    mg_s[t] = mixed_grad[:, t * 256 : (t + 1) * 256]

                def one_tile(t, carry):
                    lanes = pl.ds(pl.multiple_of(t * 256, 256), 256)
                    key_lanes = pl.ds(pl.multiple_of(t * 256, 256), LANES)
                    value_lanes = pl.ds(pl.multiple_of(t * 256 + LANES, LANES), LANES)
                    q4 = stack_heads(qb[slot, :, lanes], True).astype(BF16)
                    do4_f = stack_heads(mg_s[t].astype(F32) * invlb[slot, :, lanes], True)
                    do4 = do4_f.astype(BF16)
                    product = do4_f * stack_heads(mixed_s[s, :, lanes], False)
                    delta = lax.dot_general(
                        jnp.ones((8, LANES), F32), product, (((1,), (1,)), ((), ())),
                        preferred_element_type=F32, precision=lax.Precision.HIGHEST,
                    )[0:1]

                    def step(index, sum_q, masked):
                        two = pl.ds(2 * index, 2)
                        keys = kvb[slot, two, :, key_lanes].reshape(chunk, LANES)
                        values = kvb[slot, two, :, value_lanes].reshape(chunk, LANES)
                        weight = jnp.exp2(dot_nt(keys, q4) * EXP2_SCALE)
                        if masked:
                            at = lax.rem(lane_of(weight.shape), rows) + here * rows
                            weight = jnp.where(row_of(weight.shape) + index * chunk <= at, weight, 0.0)
                        pressure = dot_nt(values, do4)
                        score_grad = (weight * (pressure - delta) * SCALE).astype(BF16)
                        key_grad = dot(score_grad, q4).astype(BF16)
                        value_grad = dot(weight.astype(BF16), do4).astype(BF16)
                        dkv[two, s, :, key_lanes] = key_grad.reshape(2, rows, LANES)
                        dkv[two, s, :, value_lanes] = value_grad.reshape(2, rows, LANES)
                        return sum_q + dot_tn(score_grad, keys)

                    total_q = lax.fori_loop(
                        0, chunks - 1, lambda i, c: step(i, c, False), jnp.zeros((4 * rows, LANES), F32)
                    )
                    total_q = step(chunks - 1, total_q, True)

                    def blank(index, carry):
                        dkv[pl.ds(2 * index, 2), s, :, lanes] = jnp.zeros((2, rows, 256), BF16)
                        return carry

                    lax.fori_loop(chunks, group // 2, blank, 0)
                    dq = unstack_heads(total_q).astype(BF16).astype(F32)
                    for n in range(2):
                        part = slice(n * LANES, (n + 1) * LANES)
                        here_lanes = pl.ds(pl.multiple_of(t * 256 + n * LANES, LANES), LANES)
                        raw, gain = rope_backward(
                            dq[:, part], qrawb[slot, :, here_lanes], qg_ref[...], cos_ref[...], sin_ref[...]
                        )
                        q_s[s, :, here_lanes] = raw.astype(BF16)
                        qgg[...] += gain
                    return carry

                lax.fori_loop(0, tiles, one_tile, 0)

                @pl.when(s + 2 < slots)
                def _():
                    for copy in loads(s + 2):
                        copy.start()

                scat_kv.start(s)

                @pl.when(s >= 1)
                def _():
                    scat_kv.first(s - 1)
                    scat_kv.second(s - 1)

                @pl.when(s >= 2)
                def _():
                    scat_kv.third(s - 2)

            def slot_and_move(s):
                one_slot(s)
                line.move(s + 3)

            each(slot_and_move)

        pl.run_scoped(
            attention_phase,
            pltpu.VMEM(wo_in.shape, BF16),
            pltpu.VMEM((2, rows, qw), BF16),
            pltpu.VMEM((2, group, rows, 2 * kw), BF16),
            pltpu.VMEM((2, rows, qw), F32),
            pltpu.VMEM((2, rows, LANES), F32),
            pltpu.VMEM((2, rows, width), F32),
            pltpu.VMEM((2, rows, width), F32),
            pltpu.VMEM((2, rows, qw), F32),
            pltpu.SemaphoreType.DMA((2, 7)),
        )
        each(scat_dx.drain)

        def last_phase(wq, wk, wv, xb, krawb, hb, n2b, k_s, v_s):
            loads = [
                pltpu.make_async_copy(source, there, local.at[2 + n])
                for n, (source, there) in enumerate(
                    ((wq_in, wq), (wk_in, wk), (wv_in, wv), (x_in, xb), (kraw_in, krawb), (h_in, hb),
                     (n2_in.at[plane.me, :, :, pl.ds(0, width)], n2b))
                )
            ]
            for copy in loads:
                copy.start()
            scat_kv.first(slots - 1)
            scat_kv.second(slots - 1)
            scat_kv.third(slots - 2)
            line.move(slots + 3)
            flat = lambda ref: ref[...].reshape(slots * rows, ref.shape[2])
            for copy in loads:
                copy.wait()
            shards, shard_rows = group, width // group

            def product(left, right, place):
                def one(n, carry):
                    lanes = pl.ds(pl.multiple_of(n * 256, 256), 256)
                    column = right[:, :, lanes].reshape(slots * rows, 256)
                    place(n, dot_tn(flat(left), column).astype(BF16).reshape(shards, shard_rows, 256))
                    return carry

                lax.fori_loop(0, right.shape[2] // 256, one, 0)

            def aside(k):
                def place(n, value):
                    lanes = pl.ds(pl.multiple_of(n * 256, 256), 256)
                    for shard in range(shards):
                        dx_own[k + shard // slots, shard % slots, :, lanes] = value[shard]

                return place

            product(mixed_s, at_s, aside(0))
            scat_kv.third(slots - 1)
            line.move(slots + 4)
            product(hb, q_s, aside(2))
            router = dot_tn(flat(lg_s), flat(n2b))
            experts = small_out.shape[0] - 8
            sm_mine[0] = jnp.zeros(sm_mine.shape[1:], F32)
            sm_mine[0, :experts] = router[:experts]
            sm_mine[0, experts + 1 : experts + 2] = fgg[...]
            sm_mine[0, experts + 2 : experts + 3, :LANES] = qgg[...]
            sm_mine[0, experts + 4 : experts + 5] = loss_ref[...]
            line.move(slots + 5)

            def one_slot(s):
                grads = scat_kv.result(s)
                for t in range(kw // LANES):
                    lanes = slice(t * LANES, (t + 1) * LANES)
                    at = 2 * t * LANES
                    grad = grads[:, at : at + LANES].astype(BF16).astype(F32)
                    raw, gain = rope_backward(grad, krawb[s, :, lanes], kg_ref[...], cos_ref[...], sin_ref[...])
                    k_s[s, :, lanes] = raw.astype(BF16)
                    kgg[...] += gain
                    v_s[s, :, lanes] = grads[:, at + LANES : at + 2 * LANES].astype(BF16)
                normed_grad = dot_nt(q_s[s], wq[...]) + dot_nt(k_s[s], wk[...]) + dot_nt(v_s[s], wv[...])
                back, gain = rms_backward(normed_grad, xb[s].astype(F32), gain_ref[...])
                agg[...] += gain
                ag_s[s] += back
                pltpu.make_async_copy(ag_s.at[s], ig_out.at[s], local.at[0]).start()

            each(one_slot)
            each(scat_kv.drain)
            line.move(slots + 6)
            sm_mine[0, experts : experts + 1] = agg[...]
            sm_mine[0, experts + 3 : experts + 4, :LANES] = kgg[...]
            for shard in range(shards):
                dkv[shard, 2] = dx_own[shard // slots, shard % slots, :, :width]
                dkv[shard, 0] = dx_own[2 + shard // slots, shard % slots, :, :width]

            def beside(first):
                def place(n, value):
                    dkv[:, 1, :, pl.ds(pl.multiple_of(first + n * 256, 256), 256)] = value

                return place

            product(hb, k_s, beside(0))
            product(hb, v_s, beside(kw))
            line.move(slots + 7)

        pl.run_scoped(
            last_phase,
            pltpu.VMEM(wq_in.shape, BF16),
            pltpu.VMEM(wk_in.shape, BF16),
            pltpu.VMEM(wv_in.shape, BF16),
            pltpu.VMEM(x_in.shape, BF16),
            pltpu.VMEM(kraw_in.shape, F32),
            pltpu.VMEM(h_in.shape, BF16),
            pltpu.VMEM((slots, rows, width), BF16),
            pltpu.VMEM((slots, rows, kw), BF16),
            pltpu.VMEM((slots, rows, kw), BF16),
        )
        narrow = pl.ds(0, width)
        again = [dx_sb.at[:, :, :, narrow]] + [r.at[:, :, narrow] for r in (dx_da, dx_db, dx_rx, dx_ry)]
        scat_de = Scatter(
            plane, lambda k, s: dkv.at[plane.own[k], s], lambda k, s: dkv.at[plane.other[k], s],
            again, (sent_de, got_de),
        )
        by_kind = lambda body: each(body, kinds)
        by_kind(scat_de.start)
        small = lambda n, who: remote(sm_mine.at[n], sm_got.at[n], sent_sm.at[n], got_sm.at[n], who)

        def small_step(n, who):
            small(n, who).wait_recv()
            sm_mine[n + 1] = sm_mine[n] + sm_got[n]

        small(0, plane.sib).start()
        by_kind(scat_de.first)
        small_step(0, plane.sib)
        small(1, plane.xn).start()
        by_kind(scat_de.second)
        small_step(1, plane.xn)
        small(2, plane.yn).start()
        by_kind(scat_de.third)
        small_step(2, plane.yn)
        line.move(slots + 8)

        def one_kind(s):
            dsh[s] = scat_de.result(s).astype(BF16)

        by_kind(one_kind)
        by_kind(scat_de.drain)
        line.move(slots + 9)
        each(lambda s: pltpu.make_async_copy(ag_s.at[s], ig_out.at[s], local.at[0]).wait())

    pl.run_scoped(
        rest,
        pltpu.VMEM((group, slots, rows, 2 * kw), BF16),
        pltpu.VMEM((slots, rows, width), F32),
        pltpu.VMEM((slots, rows, width), BF16),
        pltpu.VMEM((slots, rows, LANES), BF16),
        pltpu.VMEM((slots, rows, qw), BF16),
        pltpu.VMEM((slots, rows, qw), BF16),
        pltpu.VMEM((1, LANES), F32),
        pltpu.VMEM((1, LANES), F32),
        pltpu.VMEM((1, width), F32),
        pltpu.VMEM((1, width), F32),
        pltpu.VMEM((tiles, rows, 256), BF16),
    )

    small_in = remote(sm_mine.at[3], sm_got.at[3], sent_sm.at[3], got_sm.at[3], plane.inner)
    small_across = remote(sm_mine.at[4], sm_got.at[4], sent_sm.at[4], got_sm.at[4], plane.across)
    small_back = remote(sm_mine.at[5], sm_got.at[5], sent_sm.at[5], got_sm.at[5], plane.outer)
    dense_in = remote(dsh, dr1, sent_sm.at[6], got_sm.at[6], plane.inner)
    dense_across = remote(dsh, dr2, sent_sm.at[7], got_sm.at[7], plane.across)
    dense_back = remote(dfin, dfin, sent_sm.at[8], got_sm.at[8], plane.outer)

    @pl.when(plane.outer_plane)
    def _():
        small_in.start()
        dense_in.start()

        def one(i, carry):
            line.inward(i).start()
            return carry

        lax.fori_loop(HELD_BACK, line.count, one, 0)

    @pl.when(plane.inner_plane)
    def _():
        small_in.wait_recv()
        sm_mine[4] = sm_mine[3] + sm_got[3]
        small_across.start()
        dense_in.wait_recv()
        add_to(dsh, dr1[...].astype(F32))
        dense_across.start()

    line.move(14)

    @pl.when(plane.inner_plane)
    def _():
        small_across.wait_recv()
        sm_mine[5] = sm_mine[4] + sm_got[4]
        small_back.start()
        small_out[...] = sm_mine[5]

    line.move(15)

    @pl.when(plane.inner_plane)
    def _():
        dense_across.wait_recv()
        dfin[...] = (dsh[...].astype(F32) + dr2[...].astype(F32)).astype(BF16)
        dense_back.start()

    @pl.when(plane.outer_plane)
    def _():
        small_back.wait_recv()
        small_out[...] = sm_got[5]
        dense_back.wait_recv()

    gather = Slots(plane, dfin, dense_out, sent_ag, got_ag, local)
    for s in range(kinds):
        gather.start(s)
    line.move(16)
    for s in range(kinds):
        gather.forward(s)
    line.move(17)
    for s in range(kinds):
        gather.settle(s)
    line.move(18)
    for s in range(kinds):
        gather.arrive(s)
        gather.drain(s)
    line.wind_up(19)
    line.finish()
    for n, who in ((0, plane.sib), (1, plane.xn), (2, plane.yn)):
        remote(sm_mine.at[n], sm_got.at[n], sent_sm.at[n], got_sm.at[n], who).wait_send()

    @pl.when(plane.outer_plane)
    def _():
        small_in.wait_send()
        dense_in.wait_send()

    @pl.when(plane.inner_plane)
    def _():
        small_across.wait_send()
        small_back.wait_send()
        dense_across.wait_send()
        dense_back.wait_send()


def tail(
    slot_lengths, dpart, xe, gate_grad, up_grad, hidden, weighted, q, kv, mixed, invl, soft, out_grad, after, qraw, kraw,
    x, h, n2, w_out, w_query, w_key, w_value, ffn_gain, router, cosine, sine, attn_gain, qg, kg, loss, experts, number,
):
    slots, rows, width = x.shape
    group, unused, unused_rows, wide = dpart.shape
    owned, eff = xe.shape[1], gate_grad.shape[3]
    kw = kraw.shape[2]
    chunks = 6 * owned
    piece = (eff, width // 2)
    kinds = 3
    hbm = pl.BlockSpec(memory_space=pl.ANY)
    vmem = pl.BlockSpec(memory_space=pltpu.VMEM)
    smem = pl.BlockSpec(memory_space=pltpu.SMEM)
    V, D = pltpu.VMEM, pltpu.SemaphoreType.DMA
    half = rows // 2

    def landing(n, lanes):
        return [
            V((4, n, rows, lanes), BF16), V((n, half, lanes), BF16), V((n, half, lanes), BF16),
            V((n, rows, lanes), BF16), V((n, rows, lanes), BF16),
        ]

    small_rows = experts + 8
    return pl.pallas_call(
        tail_kernel,
        in_specs=[smem] + [hbm] * 22 + [vmem] * 8,
        out_specs=(hbm, hbm, hbm, vmem, hbm, hbm, hbm),
        out_shape=(
            jax.ShapeDtypeStruct((chunks,) + piece, BF16),
            jax.ShapeDtypeStruct((slots, rows, width), F32),
            jax.ShapeDtypeStruct((group, kinds, width // group, width), BF16),
            jax.ShapeDtypeStruct((small_rows, width), F32),
            jax.ShapeDtypeStruct((chunks,) + piece, BF16),
            jax.ShapeDtypeStruct((chunks,) + piece, BF16),
            jax.ShapeDtypeStruct((chunks,) + piece, BF16),
        ),
        scratch_shapes=[V((4, slots, rows, wide), BF16)]
        + landing(slots, wide) + landing(slots, 2 * kw)
        + [V((2,) + piece, BF16), V((4,) + piece, BF16), V((2,) + piece, BF16)]
        + [V((kinds, rows, width), BF16)] * 4
        + [V((6, small_rows, width), F32)] * 2
        + [D((10, slots))] * 4 + [D((10, kinds))] * 2
        + [D((3, chunks))] * 2 + [D((10,))]
        + [D((8, kinds))] * 2 + [D((9,))] * 2 + [D((9,))],
        compiler_params=pltpu.CompilerParams(collective_id=number, has_side_effects=True, vmem_limit_bytes=63 * MIB),
        name="tail",
    )(
        slot_lengths, dpart, xe, gate_grad, up_grad, hidden, weighted, q, kv, mixed, invl, soft, out_grad, after, qraw,
        kraw, x, h, n2, w_out, w_query, w_key, w_value, ffn_gain, router, cosine, sine, attn_gain, qg, kg, loss,
    )


def plane_gather(rows):
    return lax.all_gather(rows, ("context", "experts"), axis=0, tiled=False)


def plane_scatter(parts):
    return lax.psum_scatter(parts, ("context", "experts"), scatter_dimension=0, tiled=False).astype(F32)


def unpack_kernel(gate_ref, up_ref, down_ref, dense_ref, dg_ref, du_ref, dd_ref, dq_ref, dk_ref, dv_ref, do_ref):
    dg_ref[0] = gate_ref[0].astype(F32)
    du_ref[0] = up_ref[0].astype(F32)
    dd_ref[0] = down_ref[0].astype(F32)
    half = dk_ref.shape[1]
    dq_ref[...] = dense_ref[0, 0].astype(F32)
    dk_ref[...] = dense_ref[0, 1, :, :half].astype(F32)
    dv_ref[...] = dense_ref[0, 1, :, half:].astype(F32)
    do_ref[...] = dense_ref[0, 2].astype(F32)


def unpack(total, dense, key_width):
    chunks, eff, half = total.shape
    shards, kinds, shard_rows, width = dense.shape
    owned = chunks // 6
    steps = 2 * owned
    piece = lambda kind: pl.BlockSpec((1, eff, half), lambda i: (i // 2 * 6 + 2 * kind + i % 2, 0, 0))
    row = lambda lanes: pl.BlockSpec((shard_rows * shards // steps, lanes), lambda i: (i, 0))
    shape = lambda *dims: jax.ShapeDtypeStruct(dims, F32)
    return pl.pallas_call(
        unpack_kernel,
        grid=(steps,),
        in_specs=[piece(0), piece(1), piece(2), pl.BlockSpec((1, kinds, shard_rows, width), lambda i: (i, 0, 0, 0))],
        out_specs=(
            pl.BlockSpec((1, eff, half), lambda i: (i // 2, i % 2, 0)),
            pl.BlockSpec((1, eff, half), lambda i: (i // 2, i % 2, 0)),
            pl.BlockSpec((1, eff, half), lambda i: (i // 2, 0, i % 2)),
            row(width), row(key_width), row(key_width), row(width),
        ),
        out_shape=(
            shape(owned, width, eff), shape(owned, width, eff), shape(owned, eff, width),
            shape(width, width), shape(width, key_width), shape(width, key_width), shape(width, width),
        ),
        compiler_params=pltpu.CompilerParams(vmem_limit_bytes=48 * MIB),
        name="unpack",
    )(total, total, total, dense)


def per_device(
    fast, block_input, teacher, lengths, routes, w_query, w_key, w_value, w_out, query_gain, key_gain,
    attn_gain, ffn_gain, w_router, w_gate, w_up, w_down,
):
    slots, rows, width = block_input.shape
    expert_total = w_router.shape[1]
    group = lax.axis_size(("context", "experts"))
    here = lax.axis_index(("context", "experts"))
    span = rows * group
    slot_lengths = lax.dynamic_slice_in_dim(lengths, lax.axis_index("dp") * slots, slots)
    scalars = jnp.concatenate([slot_lengths, here[None]]).astype(jnp.int32)
    positions = here * rows + jnp.arange(rows, dtype=jnp.int32)
    valid = (positions[None, :] < slot_lengths[:, None]).astype(F32)[..., None]
    count_all = jnp.sum(lengths).astype(F32)
    positions_all = lengths.shape[0] * span

    half = HEAD // 2
    lanes = jnp.arange(LANES, dtype=jnp.int32)
    inverse = 10000.0 ** (-((lanes % half).astype(F32) * 2.0 / HEAD))
    turned = positions.astype(F32)[:, None] * inverse[None, :]
    cosine = jnp.cos(turned)
    sine = jnp.sin(turned) * jnp.where(lanes % HEAD < half, -1.0, 1.0)[None, :]
    qg = jnp.concatenate([query_gain, query_gain])[None, :]
    kg = jnp.concatenate([key_gain, key_gain])[None, :]
    ag, fg = attn_gain[None, :], ffn_gain[None, :]
    router = jnp.pad(w_router, ((0, 0), (0, LANES - expert_total)))

    if fast:
        scale = (positions_all / count_all)[None]
        (
            h, q, qraw, kraw, kv, mixed, invl, after, soft, tokens, pick, xe, gate_part, up_part, hidden,
            block_output, out_grad, loss_row, grads,
        ) = front(
            slot_lengths, block_input, teacher, routes, w_query, w_key, w_value, w_out, w_gate, w_up, w_down,
            ag, fg, qg, kg, cosine, sine, router, scale, group, 1,
        )
        dpart, weighted, gate_grad, up_grad = experts_backward(
            scalars, grads, tokens, pick, gate_part, up_part, hidden, w_gate, w_up, w_down
        )
        total, input_grad, dense, sums = tail(
            slot_lengths, dpart, xe, gate_grad, up_grad, hidden, weighted, q, kv, mixed, invl, soft, out_grad, after,
            qraw, kraw, block_input, h, tokens, w_out, w_query, w_key, w_value, fg, router, cosine, sine, ag, qg, kg,
            loss_row, expert_total, 2,
        )[:4]
        unpacked = unpack(total, dense, w_key.shape[1])
        expert_grads, dense = unpacked[:3], unpacked[3:]
        tops = sums[expert_total : expert_total + 5]
        small = (
            tops[2, :HEAD] + tops[2, HEAD : 2 * HEAD], tops[3, :HEAD] + tops[3, HEAD : 2 * HEAD], tops[0], tops[1],
            sums[:expert_total].T, jnp.sum(tops[4]),
        )
    else:
        h, q, kv_local, qraw, kraw = project(block_input, ag, w_query, w_key, w_value, qg, kg, cosine, sine)
        kv = plane_gather(kv_local)
        mixed, invl, after, xg, soft = attend(scalars, q, kv, block_input, w_out, fg, router, routes)
        tokens = plane_gather(xg)
        pick, xe, gate_part, up_part, hidden, part = experts_forward(scalars, tokens, w_gate, w_up, w_down)
        output = after + plane_scatter(part)
        difference = valid * (output - teacher.astype(F32))
        loss_part = jnp.sum(difference * difference)
        out_grad = difference * (positions_all / count_all)
        grads = plane_gather(out_grad.astype(BF16))
        dpart, weighted, gate_grad, up_grad = experts_backward(
            scalars, grads, tokens, pick, gate_part, up_part, hidden, w_gate, w_up, w_down
        )
        expert_grads = lax.psum(expert_weights(xe, gate_grad, up_grad, hidden, weighted), "dp")
        dx = plane_scatter(dpart)
        dq, dkv_parts, after_grad, attn_grad, logit_grad, ffn_gain_grad = attend_backward(
            scalars, q, kv, mixed, invl, dx, soft, out_grad, after, fg, router, w_out
        )
        dkv = plane_scatter(dkv_parts)
        input_grad, dense, router_grad, query_gg, key_gg, attn_gg = finish(
            dq, dkv, qraw, kraw, block_input, after_grad, cosine, sine, ag, qg, kg,
            w_query, w_key, w_value, h, mixed, attn_grad, xg, logit_grad,
        )
        dense = lax.psum(dense, ("dp", "context", "experts"))
        dense = [dense[:, k].reshape(width, width).astype(F32) for k in range(3)]
        small = lax.psum(
            (
                query_gg[0, :HEAD] + query_gg[0, HEAD:], key_gg[0, :HEAD] + key_gg[0, HEAD:], attn_gg[0],
                ffn_gain_grad[0], router_grad[:, :expert_total], loss_part,
            ),
            ("dp", "context", "experts"),
        )
        key_width = w_key.shape[1]
        expert_grads = [grad.astype(F32) for grad in expert_grads]
        dense = [dense[0], dense[1][:, :key_width], dense[1][:, key_width:], dense[2]]
        block_output = output.astype(BF16)
    return (
        small[5] / (count_all * width), block_output, input_grad, dense[0], dense[1], dense[2], dense[3],
        small[0], small[1], small[2], small[3], small[4], expert_grads[0], expert_grads[1], expert_grads[2],
    )


def solution(mesh):
    fast = mesh.shape["context"] == 4 and mesh.shape["experts"] == 2
    rows = P("dp", ("context", "experts"), None)
    owned = P(("context", "experts"), None, None)
    return jax.shard_map(
        functools.partial(per_device, fast),
        mesh=mesh,
        in_specs=(rows, rows, P(), rows) + (P(),) * 9 + (owned,) * 3,
        out_specs=(P(), rows, rows) + (P(),) * 9 + (owned,) * 3,
        check_vma=False,
    )
```

```python
import functools
import math

import jax
import jax.numpy as jnp
from jax import lax
from jax.experimental import pallas as pl
from jax.experimental.pallas import tpu as pltpu
from jax.sharding import PartitionSpec as P

EPSILON = 1e-06
MOST = 40
PAIR = 2 * MOST
LANES = 128
HEAD = 64
SCALE = 0.125
EXP2_SCALE = 0.125 * math.log2(math.e)
MIB = 2**20
MESH = pl.DeviceIdType.MESH
F32 = jnp.float32
BF16 = jnp.bfloat16


def dot(a, b):
    return lax.dot_general(a, b, (((1,), (0,)), ((), ())), preferred_element_type=F32)


def dot_nt(a, b):
    return lax.dot_general(a, b, (((1,), (1,)), ((), ())), preferred_element_type=F32)


def dot_tn(a, b):
    return lax.dot_general(a, b, (((0,), (0,)), ((), ())), preferred_element_type=F32)


def lane_of(shape):
    return lax.broadcasted_iota(jnp.int32, shape, len(shape) - 1)


def row_of(shape):
    return lax.broadcasted_iota(jnp.int32, shape, len(shape) - 2)


def swap_halves(tile):
    low = lax.rem(lane_of(tile.shape), HEAD) < HEAD // 2
    return jnp.where(low, pltpu.roll(tile, LANES - HEAD // 2, 1), pltpu.roll(tile, HEAD // 2, 1))


def head_mean(tile):
    low = lane_of(tile.shape) < HEAD
    first = jnp.sum(jnp.where(low, tile, 0.0), axis=-1, keepdims=True)
    second = jnp.sum(jnp.where(low, 0.0, tile), axis=-1, keepdims=True)
    return jnp.where(low, first, second) * (1.0 / HEAD)


def rope_forward(raw, gain, cosine, sine):
    normed = raw * lax.rsqrt(head_mean(raw * raw) + EPSILON) * gain
    return normed * cosine + swap_halves(normed) * sine


def rope_backward(grad, raw, gain, cosine, sine):
    inverse = lax.rsqrt(head_mean(raw * raw) + EPSILON)
    unit = raw * inverse
    normed_grad = grad * cosine - swap_halves(grad) * sine
    gain_grad = jnp.sum(normed_grad * unit, axis=0, keepdims=True)
    unit_grad = normed_grad * gain
    return inverse * (unit_grad - unit * head_mean(unit_grad * unit)), gain_grad


def rms_parts(rows):
    inverse = lax.rsqrt(jnp.mean(rows * rows, axis=-1, keepdims=True) + EPSILON)
    return rows * inverse, inverse


def rms_backward(grad, rows, gain):
    unit, inverse = rms_parts(rows)
    gain_grad = jnp.sum(grad * unit, axis=0, keepdims=True)
    unit_grad = grad * gain
    back = inverse * (unit_grad - unit * jnp.mean(unit_grad * unit, axis=-1, keepdims=True))
    return back, gain_grad


def stack_heads(tile, masked):
    first, second = tile[:, :LANES].astype(F32), tile[:, LANES:].astype(F32)
    parts = [first, pltpu.roll(first, HEAD, 1), pltpu.roll(second, HEAD, 1), second]
    if masked:
        low = lane_of(first.shape) < HEAD
        parts = [jnp.where(low, part, 0.0) for part in parts[:2]] + [
            jnp.where(low, 0.0, part) for part in parts[2:]
        ]
    return jnp.concatenate(parts, axis=0)


def unstack_heads(rows):
    count = rows.shape[0] // 4
    one, two, three, four = (rows[k * count : (k + 1) * count] for k in range(4))
    low = lane_of(one.shape) < HEAD
    return jnp.concatenate(
        [
            jnp.where(low, one, pltpu.roll(two, HEAD, 1)),
            jnp.where(low, pltpu.roll(three, HEAD, 1), four),
        ],
        axis=1,
    )


def project_kernel(
    x_ref, gain_ref, wq_ref, wk_ref, wv_ref, qg_ref, kg_ref, cos_ref, sin_ref,
    h_ref, q_ref, kv_ref, qraw_ref, kraw_ref,
):
    slots, rows, width = x_ref.shape
    x = x_ref[...].astype(F32).reshape(slots * rows, width)
    unit, unused = rms_parts(x)
    normed = (unit * gain_ref[...]).astype(BF16)
    h_ref[...] = normed.reshape(slots, rows, width)
    cosine = jnp.concatenate([cos_ref[...]] * slots, axis=0)
    sine = jnp.concatenate([sin_ref[...]] * slots, axis=0)
    q_raw = dot(normed, wq_ref[...])
    qraw_ref[...] = q_raw.reshape(qraw_ref.shape)
    for tile in range(q_raw.shape[1] // LANES):
        lanes = slice(tile * LANES, (tile + 1) * LANES)
        turned = rope_forward(q_raw[:, lanes], qg_ref[...], cosine, sine)
        q_ref[:, :, lanes] = turned.astype(BF16).reshape(slots, rows, LANES)
    k_raw = dot(normed, wk_ref[...])
    kraw_ref[...] = k_raw.reshape(kraw_ref.shape)
    value = dot(normed, wv_ref[...]).astype(BF16)
    for tile in range(k_raw.shape[1] // LANES):
        lanes = slice(tile * LANES, (tile + 1) * LANES)
        turned = rope_forward(k_raw[:, lanes], kg_ref[...], cosine, sine)
        at = 2 * tile * LANES
        kv_ref[:, :, at : at + LANES] = turned.astype(BF16).reshape(slots, rows, LANES)
        kv_ref[:, :, at + LANES : at + 2 * LANES] = value[:, lanes].reshape(slots, rows, LANES)


def project(x, attn_gain, w_query, w_key, w_value, qg, kg, cosine, sine):
    slots, rows, width = x.shape
    step = 2
    block = lambda lanes: pl.BlockSpec((step, rows, lanes), lambda i: (i, 0, 0))
    whole = lambda a: pl.BlockSpec(a.shape, lambda i: (0,) * a.ndim)
    qw, kw = w_query.shape[1], w_key.shape[1]
    return pl.pallas_call(
        project_kernel,
        grid=(slots // step,),
        out_shape=(
            jax.ShapeDtypeStruct((slots, rows, width), BF16),
            jax.ShapeDtypeStruct((slots, rows, qw), BF16),
            jax.ShapeDtypeStruct((slots, rows, 2 * kw), BF16),
            jax.ShapeDtypeStruct((slots, rows, qw), F32),
            jax.ShapeDtypeStruct((slots, rows, kw), F32),
        ),
        in_specs=[block(width)] + [whole(a) for a in (attn_gain, w_query, w_key, w_value, qg, kg, cosine, sine)],
        out_specs=(block(width), block(qw), block(2 * kw), block(qw), block(kw)),
        compiler_params=pltpu.CompilerParams(vmem_limit_bytes=56 * MIB),
        name="project",
    )(x, attn_gain, w_query, w_key, w_value, qg, kg, cosine, sine)


def attend_kernel(
    sc_ref, q_ref, kv_ref, x_ref, wo_ref, fg_ref, wr_ref, routes_ref,
    mixed_ref, invl_ref, after_ref, xg_ref, soft_ref, acc,
):
    slot, tile = pl.program_id(0), pl.program_id(1)
    slots, tiles = pl.num_programs(0), pl.num_programs(1)
    rows = q_ref.shape[1]
    here = sc_ref[slots]
    length = sc_ref[slot]
    live = here * rows < length
    chunk = 2 * rows
    chunks = (here + 2) // 2

    @pl.when(tile == 0)
    def _():
        acc[...] = jnp.zeros_like(acc)

    @pl.when(live)
    def _():
        q4 = stack_heads(q_ref[0], True).astype(BF16)

        def step(index, carry, masked):
            mass, total = carry
            pair = kv_ref[pl.ds(2 * index, 2), 0]
            keys = pair[:, :, :LANES].reshape(chunk, LANES)
            values = pair[:, :, LANES:].reshape(chunk, LANES)
            weight = jnp.exp2(dot_nt(q4, keys) * EXP2_SCALE)
            if masked:
                at = lax.rem(row_of(weight.shape), rows) + here * rows
                weight = jnp.where(lane_of(weight.shape) + index * chunk <= at, weight, 0.0)
            for part in range(chunk // LANES):
                mass = mass + weight[:, part * LANES : (part + 1) * LANES]
            return mass, total + dot(weight.astype(BF16), values)

        blank = jnp.zeros((4 * rows, LANES), F32)
        carry = lax.fori_loop(0, chunks - 1, lambda i, c: step(i, c, False), (blank, blank))
        mass, total = step(chunks - 1, carry, True)
        inverse = 1.0 / jnp.sum(mass, axis=-1, keepdims=True)
        mixed = unstack_heads(total * inverse).astype(BF16)
        mixed_ref[0] = mixed
        invl_ref[0] = unstack_heads(jnp.broadcast_to(inverse, total.shape))
        acc[...] += dot(mixed, wo_ref[...])

    @pl.when(jnp.logical_not(live))
    def _():
        mixed_ref[...] = jnp.zeros_like(mixed_ref)
        invl_ref[...] = jnp.zeros_like(invl_ref)

    @pl.when(tile == tiles - 1)
    def _():
        width = x_ref.shape[2]
        valid = (row_of((rows, 1)) + here * rows < length).astype(F32)
        after = x_ref[0].astype(F32) + valid * acc[...]
        after_ref[0] = after
        unit, unused = rms_parts(after)
        normed = (unit * fg_ref[...]).astype(BF16)
        xg_ref[0, :, :width] = normed
        logits = dot(normed, wr_ref[...])
        lanes = lane_of(logits.shape)
        routes = routes_ref[0]
        chosen = lanes == routes[:, 0:1]
        for k in range(1, routes.shape[1]):
            chosen = chosen | (lanes == routes[:, k : k + 1])
        top = jnp.max(jnp.where(chosen, logits, -1e30), axis=-1, keepdims=True)
        weight = jnp.where(chosen, jnp.exp(jnp.minimum(logits - top, 0.0)), 0.0)
        soft = weight / jnp.sum(weight, axis=-1, keepdims=True)
        soft_ref[0] = soft
        gates = soft * valid
        high = gates.astype(BF16).astype(F32)
        half = logits.shape[1] // 2
        xg_ref[0, :, width:] = (high + pltpu.roll(gates - high, half, 1)).astype(BF16)


def attend(scalars, q, kv, x, w_out, ffn_gain, router, routes):
    slots, rows, width = x.shape
    group = kv.shape[0]
    qw = q.shape[2]
    tiles = qw // 256
    row = lambda lanes: pl.BlockSpec((1, rows, lanes), lambda s, b, sc: (s, 0, 0))
    tile = pl.BlockSpec((1, rows, 256), lambda s, b, sc: (s, 0, b))
    return pl.pallas_call(
        attend_kernel,
        grid_spec=pltpu.PrefetchScalarGridSpec(
            num_scalar_prefetch=1,
            grid=(slots, tiles),
            in_specs=[
                tile,
                pl.BlockSpec((group, 1, rows, 256), lambda s, b, sc: (0, s, 0, b)),
                row(width),
                pl.BlockSpec((256, width), lambda s, b, sc: (b, 0)),
                pl.BlockSpec(ffn_gain.shape, lambda s, b, sc: (0, 0)),
                pl.BlockSpec(router.shape, lambda s, b, sc: (0, 0)),
                row(routes.shape[2]),
            ],
            out_specs=(tile, tile, row(width), row(width + LANES), row(LANES)),
            scratch_shapes=[pltpu.VMEM((rows, width), F32)],
        ),
        out_shape=(
            jax.ShapeDtypeStruct((slots, rows, qw), BF16),
            jax.ShapeDtypeStruct((slots, rows, qw), F32),
            jax.ShapeDtypeStruct((slots, rows, width), F32),
            jax.ShapeDtypeStruct((slots, rows, width + LANES), BF16),
            jax.ShapeDtypeStruct((slots, rows, LANES), F32),
        ),
        compiler_params=pltpu.CompilerParams(vmem_limit_bytes=56 * MIB),
        name="attend",
    )(scalars, q, kv, x, w_out, ffn_gain, router, routes)


def row_gates(picked, first, owned):
    lanes = lane_of(picked.shape)
    expert = row_of(picked.shape) // PAIR + first
    half = picked.shape[1] // 2
    mine = (lanes == expert) | (lanes == expert + half)
    return jnp.sum(jnp.where(mine, picked, 0.0), axis=-1, keepdims=True)


def experts_forward_kernel(
    sc_ref, xg_ref, wg_ref, wu_ref, wd_ref, pick_ref, xe_ref, gp_ref, up_ref, hid_ref, part_ref, gates, ybuf
):
    sources, unused, rows, wide = xg_ref.shape
    owned, width, eff = wg_ref.shape
    pairs = sources // 2
    double = 2 * rows
    first = sc_ref[pl.num_programs(0)] * owned
    tokens = xg_ref[...].reshape(sources * rows, wide)
    slab = tokens[:, width:]
    chosen = (lane_of((8, LANES)) == row_of((8, LANES)) + first).astype(BF16)
    routed = dot_nt(chosen, slab) > 0.0
    before = row_of((double, double))
    after = lane_of((double, double))
    count = ((before < after) & (before // rows == after // rows)).astype(BF16)
    place = lax.broadcasted_iota(jnp.int32, (PAIR, double), 0)
    offset = (lane_of((8, double)) // rows) * MOST
    for p in range(pairs):
        mask = routed[:, p * double : (p + 1) * double]
        rank = dot(mask.astype(F32).astype(BF16), count).astype(jnp.int32) + offset
        rank = jnp.where(mask, rank, -1)
        pick = jnp.concatenate(
            [(place == rank[e : e + 1, :]).astype(F32).astype(BF16) for e in range(owned)], axis=0
        )
        pick_ref[0, p] = pick
        block = tokens[p * double : (p + 1) * double]
        picked = dot(pick, block[:, :width]).astype(BF16)
        scale = row_gates(dot(pick, block[:, width:]), first, owned)
        for e in range(owned):
            xe_ref[0, e, p * PAIR : (p + 1) * PAIR] = picked[e * PAIR : (e + 1) * PAIR]
            gates[e, p * PAIR : (p + 1) * PAIR] = jnp.broadcast_to(
                scale[e * PAIR : (e + 1) * PAIR], (PAIR, LANES)
            )

    def one(e, carry):
        rows_in = xe_ref[0, e]
        gate_part = dot(rows_in, wg_ref[e])
        up_part = dot(rows_in, wu_ref[e])
        gp_ref[0, e] = gate_part
        up_ref[0, e] = up_part
        hidden = (gate_part * jax.nn.sigmoid(gate_part) * up_part).astype(BF16)
        hid_ref[0, e] = hidden
        result = (dot(hidden, wd_ref[e]) * gates[e][:, 0:1]).astype(BF16)
        for p in range(pairs):
            ybuf[p, e] = result[p * PAIR : (p + 1) * PAIR]
        return carry

    lax.fori_loop(0, owned, one, 0)
    for p in range(pairs):
        back = dot_tn(pick_ref[0, p], ybuf[p].reshape(owned * PAIR, width))
        part_ref[2 * p : 2 * p + 2, 0] = back.astype(BF16).reshape(2, rows, width)


def step_spec(shape):
    return pl.BlockSpec((1,) + shape, lambda s, j, sc: (s * pl.num_programs(1) + j,) + (0,) * len(shape))


def resident(array):
    return pl.BlockSpec(array.shape, lambda s, j, sc: (0,) * array.ndim, pipeline_mode=pl.Buffered(1))


def experts_forward(scalars, tokens, w_gate, w_up, w_down):
    group, slots, rows, wide = tokens.shape
    owned, width, eff = w_gate.shape
    sources = 8
    parts = group // sources
    pairs = sources // 2
    steps = slots * parts
    held = pairs * PAIR
    source = lambda lanes: pl.BlockSpec((sources, 1, rows, lanes), lambda s, j, sc: (j, s, 0, 0))
    saved = [
        ((pairs, owned * PAIR, 2 * rows), BF16),
        ((owned, held, width), BF16),
        ((owned, held, eff), F32),
        ((owned, held, eff), F32),
        ((owned, held, eff), BF16),
    ]
    return pl.pallas_call(
        experts_forward_kernel,
        grid_spec=pltpu.PrefetchScalarGridSpec(
            num_scalar_prefetch=1,
            grid=(slots, parts),
            in_specs=[source(wide), resident(w_gate), resident(w_up), resident(w_down)],
            out_specs=tuple(step_spec(shape) for shape, unused in saved) + (source(width),),
            scratch_shapes=[
                pltpu.VMEM((owned, held, LANES), F32),
                pltpu.VMEM((pairs, owned, PAIR, width), BF16),
            ],
        ),
        out_shape=tuple(jax.ShapeDtypeStruct((steps,) + shape, kind) for shape, kind in saved)
        + (jax.ShapeDtypeStruct((group, slots, rows, width), BF16),),
        compiler_params=pltpu.CompilerParams(vmem_limit_bytes=60 * MIB),
        name="experts_forward",
    )(scalars, tokens, w_gate, w_up, w_down)


def experts_backward_kernel(
    sc_ref, dy_ref, slab_ref, pick_ref, gp_ref, up_ref, hid_ref, wg_ref, wu_ref, wd_ref,
    part_ref, dyw_ref, gg_ref, ug_ref, gates, dye, dxb,
):
    sources, unused, rows, width = dy_ref.shape
    owned = wg_ref.shape[0]
    pairs = sources // 2
    double = 2 * rows
    first = sc_ref[pl.num_programs(0)] * owned
    for p in range(pairs):
        pick = pick_ref[0, p]
        picked = dot(pick, dy_ref[2 * p : 2 * p + 2].reshape(double, width)).astype(BF16)
        scale = row_gates(dot(pick, slab_ref[2 * p : 2 * p + 2].reshape(double, LANES)), first, owned)
        for e in range(owned):
            dye[e, p * PAIR : (p + 1) * PAIR] = picked[e * PAIR : (e + 1) * PAIR]
            gates[e, p * PAIR : (p + 1) * PAIR] = jnp.broadcast_to(
                scale[e * PAIR : (e + 1) * PAIR], (PAIR, LANES)
            )

    def one(e, carry):
        grad_rows = dye[e]
        scale = gates[e][:, 0:1]
        plain = dot_nt(grad_rows, wd_ref[e])
        gate_part, up_part = gp_ref[0, e], up_ref[0, e]
        soft_grad = jnp.sum(plain * hid_ref[0, e].astype(F32), axis=-1, keepdims=True)
        hidden_grad = plain * scale
        sigma = jax.nn.sigmoid(gate_part)
        gate_grad = (hidden_grad * up_part * sigma * (1.0 + gate_part * (1.0 - sigma))).astype(BF16)
        up_grad = (hidden_grad * gate_part * sigma).astype(BF16)
        gg_ref[0, e] = gate_grad
        ug_ref[0, e] = up_grad
        dyw_ref[0, e] = (grad_rows.astype(F32) * scale).astype(BF16)
        input_grad = (dot_nt(gate_grad, wg_ref[e]) + dot_nt(up_grad, wu_ref[e])).astype(BF16)
        lanes = lane_of((pairs * PAIR, LANES))
        high = soft_grad.astype(BF16).astype(F32)
        spot = jnp.where(
            lanes == first + e, high, jnp.where(lanes == first + e + LANES // 2, soft_grad - high, 0.0)
        ).astype(BF16)
        for p in range(pairs):
            dxb[p, e, :, :width] = input_grad[p * PAIR : (p + 1) * PAIR]
            dxb[p, e, :, width:] = spot[p * PAIR : (p + 1) * PAIR]
        return carry

    lax.fori_loop(0, owned, one, 0)
    for p in range(pairs):
        back = dot_tn(pick_ref[0, p], dxb[p].reshape(owned * PAIR, width + LANES))
        part_ref[2 * p : 2 * p + 2, 0] = back.astype(BF16).reshape(2, rows, width + LANES)


def experts_backward(scalars, grads, tokens, pick, gate_part, up_part, hidden, w_gate, w_up, w_down):
    group, slots, rows, width = grads.shape
    owned, unused, eff = w_gate.shape
    sources = 8
    parts = group // sources
    pairs = sources // 2
    steps = slots * parts
    held = pairs * PAIR
    source = lambda lanes, at: pl.BlockSpec((sources, 1, rows, lanes), lambda s, j, sc: (j, s, 0, at))
    return pl.pallas_call(
        experts_backward_kernel,
        grid_spec=pltpu.PrefetchScalarGridSpec(
            num_scalar_prefetch=1,
            grid=(slots, parts),
            in_specs=[
                source(width, 0),
                source(LANES, width // LANES),
                step_spec((pairs, owned * PAIR, 2 * rows)),
                step_spec((owned, held, eff)),
                step_spec((owned, held, eff)),
                step_spec((owned, held, eff)),
                resident(w_gate), resident(w_up), resident(w_down),
            ],
            out_specs=(
                source(width + LANES, 0),
                step_spec((owned, held, width)),
                step_spec((owned, held, eff)),
                step_spec((owned, held, eff)),
            ),
            scratch_shapes=[
                pltpu.VMEM((owned, held, LANES), F32),
                pltpu.VMEM((owned, held, width), BF16),
                pltpu.VMEM((pairs, owned, PAIR, width + LANES), BF16),
            ],
        ),
        out_shape=(
            jax.ShapeDtypeStruct((group, slots, rows, width + LANES), BF16),
            jax.ShapeDtypeStruct((steps, owned, held, width), BF16),
            jax.ShapeDtypeStruct((steps, owned, held, eff), BF16),
            jax.ShapeDtypeStruct((steps, owned, held, eff), BF16),
        ),
        compiler_params=pltpu.CompilerParams(vmem_limit_bytes=62 * MIB),
        name="experts_backward",
    )(scalars, grads, tokens, pick, gate_part, up_part, hidden, w_gate, w_up, w_down)


def expert_weights_kernel(xe_ref, gg_ref, ug_ref, hid_ref, dyw_ref, dg_ref, du_ref, dd_ref, ag, au, ad):
    step = pl.program_id(1)
    flat = lambda ref: ref[:, 0].reshape(ref.shape[0] * ref.shape[2], ref.shape[3])
    for acc, left, right in ((ad, hid_ref, dyw_ref), (ag, xe_ref, gg_ref), (au, xe_ref, ug_ref)):
        part = dot_tn(flat(left), flat(right))

        @pl.when(step == 0)
        def _():
            acc[...] = part

        @pl.when(step > 0)
        def _():
            acc[...] += part

    @pl.when(step == pl.num_programs(1) - 1)
    def _():
        dg_ref[0] = ag[...].astype(BF16)
        du_ref[0] = au[...].astype(BF16)
        dd_ref[0] = ad[...].astype(BF16)


def expert_weights(xe, gate_grad, up_grad, hidden, weighted):
    steps, owned, held, width = xe.shape
    eff = hidden.shape[3]
    each = 4
    block = lambda lanes: pl.BlockSpec((each, 1, held, lanes), lambda e, i: (i, e, 0, 0))
    out = lambda a, b: pl.BlockSpec((1, a, b), lambda e, i: (e, 0, 0))
    return pl.pallas_call(
        expert_weights_kernel,
        grid=(owned, steps // each),
        in_specs=[block(width), block(eff), block(eff), block(eff), block(width)],
        out_specs=(out(width, eff), out(width, eff), out(eff, width)),
        out_shape=(
            jax.ShapeDtypeStruct((owned, width, eff), BF16),
            jax.ShapeDtypeStruct((owned, width, eff), BF16),
            jax.ShapeDtypeStruct((owned, eff, width), BF16),
        ),
        scratch_shapes=[pltpu.VMEM((width, eff), F32), pltpu.VMEM((width, eff), F32), pltpu.VMEM((eff, width), F32)],
        compiler_params=pltpu.CompilerParams(vmem_limit_bytes=56 * MIB),
        name="expert_weights",
    )(xe, gate_grad, up_grad, hidden, weighted)


def attend_backward_kernel(
    sc_ref, q_ref, kv_ref, mixed_ref, invl_ref, dx_ref, soft_ref, og_ref, after_ref, fg_ref, wr_ref, wo_ref,
    dq_ref, dkv_ref, ag_ref, at_ref, lg_ref, fgg_ref, mg_s,
):
    slot, tile = pl.program_id(0), pl.program_id(1)
    slots, tiles = pl.num_programs(0), pl.num_programs(1)
    rows = q_ref.shape[1]
    here = sc_ref[slots]
    length = sc_ref[slot]
    live = here * rows < length
    chunk = 2 * rows
    chunks = (here + 2) // 2
    width = og_ref.shape[2]

    @pl.when(tile == 0)
    def _():
        valid = (row_of((rows, 1)) + here * rows < length).astype(F32)
        slab = dx_ref[0, :, width:].astype(F32)
        half = slab.shape[1] // 2
        soft = soft_ref[0]
        soft_grad = jnp.where(lane_of(slab.shape) < half, slab + pltpu.roll(slab, half, 1), 0.0)
        chosen = soft * (soft_grad - jnp.sum(soft * soft_grad, axis=-1, keepdims=True))
        logit_grad = chosen.astype(BF16)
        lg_ref[0] = logit_grad
        normed_grad = dx_ref[0, :, :width].astype(F32) + dot_nt(logit_grad, wr_ref[...])
        back, gain_grad = rms_backward(normed_grad, after_ref[0], fg_ref[...])

        @pl.when(slot == 0)
        def _():
            fgg_ref[...] = gain_grad

        @pl.when(slot > 0)
        def _():
            fgg_ref[...] += gain_grad

        after_grad = og_ref[0] + back
        ag_ref[0] = after_grad
        attn_grad = (valid * after_grad).astype(BF16)
        at_ref[0] = attn_grad
        mixed_grad = dot_nt(attn_grad, wo_ref[...]).astype(BF16)
        for t in range(mg_s.shape[0]):
            mg_s[t] = mixed_grad[:, t * 256 : (t + 1) * 256]

    dkv_ref[...] = jnp.zeros_like(dkv_ref)

    @pl.when(live)
    def _():
        q4 = stack_heads(q_ref[0], True).astype(BF16)
        do4_f = stack_heads(mg_s[tile].astype(F32) * invl_ref[0], True)
        do4 = do4_f.astype(BF16)
        product = do4_f * stack_heads(mixed_ref[0], False)
        delta = lax.dot_general(
            jnp.ones((8, LANES), F32), product, (((1,), (1,)), ((), ())),
            preferred_element_type=F32, precision=lax.Precision.HIGHEST,
        )[0:1]

        def step(index, total, masked):
            pair = kv_ref[pl.ds(2 * index, 2), 0]
            keys = pair[:, :, :LANES].reshape(chunk, LANES)
            values = pair[:, :, LANES:].reshape(chunk, LANES)
            weight = jnp.exp2(dot_nt(keys, q4) * EXP2_SCALE)
            if masked:
                at = lax.rem(lane_of(weight.shape), rows) + here * rows
                weight = jnp.where(row_of(weight.shape) + index * chunk <= at, weight, 0.0)
            pressure = dot_nt(values, do4)
            score_grad = (weight * (pressure - delta) * SCALE).astype(BF16)
            key_grad = dot(score_grad, q4)
            value_grad = dot(weight.astype(BF16), do4)
            dkv_ref[pl.ds(2 * index, 2), 0, :, :LANES] = key_grad.astype(BF16).reshape(2, rows, LANES)
            dkv_ref[pl.ds(2 * index, 2), 0, :, LANES:] = value_grad.astype(BF16).reshape(2, rows, LANES)
            return total + dot_tn(score_grad, keys)

        total = lax.fori_loop(
            0, chunks - 1, lambda i, c: step(i, c, False), jnp.zeros((4 * rows, LANES), F32)
        )
        total = step(chunks - 1, total, True)
        dq_ref[0] = unstack_heads(total).astype(BF16)

    @pl.when(jnp.logical_not(live))
    def _():
        dq_ref[...] = jnp.zeros_like(dq_ref)


def attend_backward(scalars, q, kv, mixed, invl, dx, soft, out_grad, after, ffn_gain, router, w_out):
    slots, rows, width = out_grad.shape
    group = kv.shape[0]
    qw = q.shape[2]
    tiles = qw // 256
    row = lambda lanes: pl.BlockSpec((1, rows, lanes), lambda s, b, sc: (s, 0, 0))
    tile = pl.BlockSpec((1, rows, 256), lambda s, b, sc: (s, 0, b))
    group_tile = pl.BlockSpec((group, 1, rows, 256), lambda s, b, sc: (0, s, 0, b))
    whole = lambda a: pl.BlockSpec(a.shape, lambda s, b, sc: (0, 0))
    return pl.pallas_call(
        attend_backward_kernel,
        grid_spec=pltpu.PrefetchScalarGridSpec(
            num_scalar_prefetch=1,
            grid=(slots, tiles),
            in_specs=[
                tile, group_tile, tile, tile, row(width + LANES), row(LANES), row(width), row(width),
                whole(ffn_gain), whole(router), whole(w_out),
            ],
            out_specs=(
                tile, group_tile, row(width), row(width), row(LANES),
                pl.BlockSpec((1, width), lambda s, b, sc: (0, 0)),
            ),
            scratch_shapes=[pltpu.VMEM((tiles, rows, 256), BF16)],
        ),
        out_shape=(
            jax.ShapeDtypeStruct((slots, rows, qw), BF16),
            jax.ShapeDtypeStruct(kv.shape, BF16),
            jax.ShapeDtypeStruct((slots, rows, width), F32),
            jax.ShapeDtypeStruct((slots, rows, width), BF16),
            jax.ShapeDtypeStruct((slots, rows, LANES), BF16),
            jax.ShapeDtypeStruct((1, width), F32),
        ),
        compiler_params=pltpu.CompilerParams(vmem_limit_bytes=56 * MIB),
        name="attend_backward",
    )(scalars, q, kv, mixed, invl, dx, soft, out_grad, after, ffn_gain, router, w_out)


def finish_kernel(
    dq_ref, dkv_ref, qraw_ref, kraw_ref, x_ref, ag_ref, cos_ref, sin_ref, gain_ref, qg_ref, kg_ref,
    wq_ref, wk_ref, wv_ref, h_ref, mixed_ref, at_ref, n2_ref, lg_ref,
    ig_ref, dense_ref, rt_ref, qgg_ref, kgg_ref, agg_ref, q_s, k_s, v_s,
):
    slot = pl.program_id(0)
    rows = x_ref.shape[1]
    cosine, sine = cos_ref[...], sin_ref[...]

    @pl.when(slot == 0)
    def _():
        qgg_ref[...] = jnp.zeros_like(qgg_ref)
        kgg_ref[...] = jnp.zeros_like(kgg_ref)
        agg_ref[...] = jnp.zeros_like(agg_ref)

    here = pl.ds(pl.multiple_of(slot * rows, rows), rows)
    for t in range(dq_ref.shape[2] // LANES):
        lanes = slice(t * LANES, (t + 1) * LANES)
        raw, gain = rope_backward(dq_ref[0, :, lanes].astype(F32), qraw_ref[0, :, lanes], qg_ref[...], cosine, sine)
        q_s[here, lanes] = raw.astype(BF16)
        qgg_ref[...] += gain
    for t in range(kraw_ref.shape[2] // LANES):
        lanes = slice(t * LANES, (t + 1) * LANES)
        at = 2 * t * LANES
        grad = dkv_ref[0, :, at : at + LANES].astype(BF16).astype(F32)
        raw, gain = rope_backward(grad, kraw_ref[0, :, lanes], kg_ref[...], cosine, sine)
        k_s[here, lanes] = raw.astype(BF16)
        kgg_ref[...] += gain
        v_s[here, lanes] = dkv_ref[0, :, at + LANES : at + 2 * LANES].astype(BF16)
    normed_grad = dot_nt(q_s[here], wq_ref[...]) + dot_nt(k_s[here], wk_ref[...]) + dot_nt(v_s[here], wv_ref[...])
    back, gain = rms_backward(normed_grad, x_ref[0].astype(F32), gain_ref[...])
    agg_ref[...] += gain
    ig_ref[0] = ag_ref[0] + back

    @pl.when(slot == pl.num_programs(0) - 1)
    def _():
        flat = lambda ref: ref[...].reshape(ref.shape[0] * ref.shape[1], ref.shape[2])
        shards, unused, shard_rows, width = dense_ref.shape
        h = flat(h_ref)
        half = width // 2

        def put(index, lanes, value):
            dense_ref[:, index, :, lanes] = value.astype(BF16).reshape(shards, shard_rows, value.shape[1])

        put(0, slice(0, width), dot_tn(h, q_s[...]))
        put(1, slice(0, half), dot_tn(h, k_s[...]))
        put(1, slice(half, width), dot_tn(h, v_s[...]))
        put(2, slice(0, width), dot_tn(flat(mixed_ref), flat(at_ref)))
        rt_ref[...] = dot_tn(flat(n2_ref), flat(lg_ref))


def finish(dq, dkv, qraw, kraw, x, after_grad, cosine, sine, attn_gain, qg, kg, wq, wk, wv, h, mixed, attn_grad, n2, lg):
    slots, rows, width = x.shape
    qw, kw = wq.shape[1], wk.shape[1]
    shards = 8
    row = lambda lanes: pl.BlockSpec((1, rows, lanes), lambda s: (s, 0, 0))
    whole = lambda a: pl.BlockSpec(a.shape, lambda s: (0,) * a.ndim)
    lanes_out = pl.BlockSpec((1, LANES), lambda s: (0, 0))
    return pl.pallas_call(
        finish_kernel,
        grid=(slots,),
        in_specs=[row(qw), row(2 * kw), row(qw), row(kw), row(width), row(width)]
        + [whole(a) for a in (cosine, sine, attn_gain, qg, kg, wq, wk, wv, h, mixed, attn_grad)]
        + [pl.BlockSpec((slots, rows, width), lambda s: (0, 0, 0)), whole(lg)],
        out_specs=(
            row(width),
            pl.BlockSpec((shards, 3, width // shards, width), lambda s: (0, 0, 0, 0)),
            pl.BlockSpec((width, LANES), lambda s: (0, 0)),
            lanes_out, lanes_out, pl.BlockSpec((1, width), lambda s: (0, 0)),
        ),
        out_shape=(
            jax.ShapeDtypeStruct((slots, rows, width), F32),
            jax.ShapeDtypeStruct((shards, 3, width // shards, width), BF16),
            jax.ShapeDtypeStruct((width, LANES), F32),
            jax.ShapeDtypeStruct((1, LANES), F32),
            jax.ShapeDtypeStruct((1, LANES), F32),
            jax.ShapeDtypeStruct((1, width), F32),
        ),
        scratch_shapes=[
            pltpu.VMEM((slots * rows, qw), BF16),
            pltpu.VMEM((slots * rows, kw), BF16),
            pltpu.VMEM((slots * rows, kw), BF16),
        ],
        compiler_params=pltpu.CompilerParams(vmem_limit_bytes=60 * MIB),
        name="finish",
    )(dq, dkv, qraw, kraw, x, after_grad, cosine, sine, attn_gain, qg, kg, wq, wk, wv, h, mixed, attn_grad, n2, lg)


def remote(src, dst, ss, rs, dev):
    return pltpu.make_async_remote_copy(src_ref=src, dst_ref=dst, send_sem=ss, recv_sem=rs, device_id=dev, device_id_type=MESH)


class Slots:
    def __init__(self, plane, mine, out, sent, got, local):
        self.plane, self.mine, self.out, self.sent, self.got, self.local = plane, mine, out, sent, got, local
        rows = mine.shape[1]
        self.halves = (pl.ds(0, rows // 2), pl.ds(rows // 2, rows // 2))
        self.at = (plane.own[1], plane.own[2], plane.own[0])

    def own(self, number, s):
        who = (self.plane.xn, self.plane.yn, self.plane.sib)[number]
        return remote(self.mine.at[s], self.out.at[self.plane.me, s], self.sent.at[number, s], self.got.at[number, s], who)

    def keep(self, s):
        return pltpu.make_async_copy(self.mine.at[s], self.out.at[self.plane.me, s], self.local.at[s])

    def pass_on(self, number, s):
        view = self.out.at[self.at[number], s]
        return remote(view, view, self.sent.at[3 + number, s], self.got.at[3 + number, s], self.plane.sib)

    def far(self, number, s):
        at, who = ((self.at[0], self.plane.yn), (self.at[1], self.plane.xn))[number]
        view = self.out.at[at, s, self.halves[number]]
        return remote(view, view, self.sent.at[6 + number, s], self.got.at[6 + number, s], who)

    def start(self, s):
        for number in range(3):
            self.own(number, s).start()
        self.keep(s).start()

    def forward(self, s):
        for number in range(2):
            self.own(number, s).wait_recv()
            self.far(number, s).start()
            self.pass_on(number, s).start()

    def settle(self, s):
        for number in range(2):
            self.far(number, s).wait_recv()
        self.pass_on(2, s).start()

    def arrive(self, s):
        self.keep(s).wait()
        self.own(2, s).wait_recv()
        for number in range(3):
            self.pass_on(number, s).wait_recv()

    def drain(self, s):
        for number in range(3):
            self.own(number, s).wait_send()
            self.pass_on(number, s).wait_send()
        for number in range(2):
            self.far(number, s).wait_send()


def front_kernel(
    sc_ref, x_in, teacher_in, routes_ref, wq_in, wk_in, wv_in, wo_in, wg_in, wu_in, wd_in,
    gain_ref, fg_ref, qg_ref, kg_ref, cos_ref, sin_ref, wr_ref, scale_ref,
    h_out, q_out, qraw_out, kraw_out, kv_out, mixed_out, invl_out, after_out, soft_out, tokens_out,
    pick_out, xe_out, gp_out, up_out, hid_out, y_out, og_out, loss_out, grads_out, dpart_out, dyw_out, gg_out, ug_out,
    sb, da, db, rx, ry, parts, wg, wu, wd, after_s, xg_s, dy_s,
    sent_kv, got_kv, loc_kv, sent_xg, got_xg, loc_xg, sent_dy, got_dy, loc_dy, sent_rs, got_rs, wsem, local,
):
    plane = Plane()
    slots, rows, width = x_in.shape
    group = kv_out.shape[0]
    qw, kw = wq_in.shape[1], wk_in.shape[1]
    tiles = qw // 256
    here = plane.me
    owned = wg_in.shape[0]
    first = here * owned
    wide = xg_s.shape[2]
    each = lambda body, start=0, stop=slots: lax.fori_loop(start, stop, lambda s, c: (body(s), c)[1], 0)
    row_gather = Slots(plane, xg_s, tokens_out, sent_xg, got_xg, loc_xg)
    grad_gather = Slots(plane, dy_s, grads_out, sent_dy, got_dy, loc_dy)
    scatter = Scatter(
        plane, lambda k, s: parts.at[plane.own[k], s], lambda k, s: parts.at[plane.other[k], s],
        (sb, da, db, rx, ry), (sent_rs, got_rs),
    )
    expert_loads = [
        pltpu.make_async_copy(source, there, wsem.at[n])
        for n, (source, there) in enumerate(((wg_in, wg), (wu_in, wu), (wd_in, wd)))
    ]

    def first_phase(wq, wk, wv, wo, xb, kvl, q_s, h_s, qraw_s, kraw_s, kvb, mixed_s, invl_s, soft_s, acc, sems, out_sems):
        loads = [
            pltpu.make_async_copy(source, there, sems.at[n])
            for n, (source, there) in enumerate(((x_in, xb), (wk_in, wk), (wv_in, wv), (wq_in, wq), (wo_in, wo)))
        ]
        for copy in loads:
            copy.start()
        for copy in expert_loads:
            copy.start()
        kv_gather = Slots(plane, kvl, kv_out, sent_kv, got_kv, loc_kv)
        plane.barrier(False)
        for copy in loads[:4]:
            copy.wait()

        def project_two(s):
            two = pl.ds(s, 2)
            x = xb[two].astype(F32).reshape(2 * rows, width)
            unit, unused = rms_parts(x)
            normed = (unit * gain_ref[...]).astype(BF16)
            h_s[two] = normed.reshape(2, rows, width)
            cosine = jnp.concatenate([cos_ref[...]] * 2, axis=0)
            sine = jnp.concatenate([sin_ref[...]] * 2, axis=0)
            k_raw = dot(normed, wk[...])
            kraw_s[two] = k_raw.reshape(2, rows, kw)
            value = dot(normed, wv[...]).astype(BF16)
            for tile in range(kw // LANES):
                lanes = slice(tile * LANES, (tile + 1) * LANES)
                turned = rope_forward(k_raw[:, lanes], kg_ref[...], cosine, sine)
                at = 2 * tile * LANES
                kvl[two, :, at : at + LANES] = turned.astype(BF16).reshape(2, rows, LANES)
                kvl[two, :, at + LANES : at + 2 * LANES] = value[:, lanes].reshape(2, rows, LANES)

            @pl.when(s == 0)
            def _():
                kv_gather.start(0)
                kv_gather.start(1)

            q_raw = dot(normed, wq[...])
            qraw_s[two] = q_raw.reshape(2, rows, qw)
            for tile in range(qw // LANES):
                lanes = slice(tile * LANES, (tile + 1) * LANES)
                turned = rope_forward(q_raw[:, lanes], qg_ref[...], cosine, sine)
                q_s[two, :, lanes] = turned.astype(BF16).reshape(2, rows, LANES)

        lax.fori_loop(0, slots // 2, lambda n, c: (project_two(2 * n), c)[1], 0)
        keeps = [
            pltpu.make_async_copy(source, there, out_sems.at[n])
            for n, (source, there) in enumerate(((h_s, h_out), (q_s, q_out), (qraw_s, qraw_out), (kraw_s, kraw_out)))
        ]
        for copy in keeps:
            copy.start()
        kv_gather.forward(0)
        kv_gather.start(2)
        kv_gather.forward(1)
        kv_gather.settle(0)
        kv_gather.start(3)
        loads[4].wait()

        def attend_slot(s):
            load = pltpu.make_async_copy(kv_out.at[:, s], kvb, sems.at[5])
            load.start()
            load.wait()
            chunk = 2 * rows
            chunks = (here + 2) // 2
            acc[...] = jnp.zeros_like(acc)

            def one_tile(t, carry):
                lanes = pl.ds(pl.multiple_of(t * 256, 256), 256)
                key_lanes = pl.ds(pl.multiple_of(t * 256, 256), LANES)
                value_lanes = pl.ds(pl.multiple_of(t * 256 + LANES, LANES), LANES)
                q4 = stack_heads(q_s[s, :, lanes], True).astype(BF16)

                def step(index, carry, masked):
                    mass, total = carry
                    two = pl.ds(2 * index, 2)
                    keys = kvb[two, :, key_lanes].reshape(chunk, LANES)
                    values = kvb[two, :, value_lanes].reshape(chunk, LANES)
                    weight = jnp.exp2(dot_nt(q4, keys) * EXP2_SCALE)
                    if masked:
                        at = lax.rem(row_of(weight.shape), rows) + here * rows
                        weight = jnp.where(lane_of(weight.shape) + index * chunk <= at, weight, 0.0)
                    for part in range(chunk // LANES):
                        mass = mass + weight[:, part * LANES : (part + 1) * LANES]
                    return mass, total + dot(weight.astype(BF16), values)

                blank = jnp.zeros((4 * rows, LANES), F32)
                state = lax.fori_loop(0, chunks - 1, lambda i, c: step(i, c, False), (blank, blank))
                mass, total = step(chunks - 1, state, True)
                inverse = 1.0 / jnp.sum(mass, axis=-1, keepdims=True)
                mixed = unstack_heads(total * inverse).astype(BF16)
                mixed_s[s, :, lanes] = mixed
                invl_s[s, :, lanes] = unstack_heads(jnp.broadcast_to(inverse, total.shape))
                acc[...] += dot(mixed, wo[pl.ds(pl.multiple_of(t * 256, 256), 256)])
                return carry

            lax.fori_loop(0, tiles, one_tile, 0)
            valid = (row_of((rows, 1)) + here * rows < sc_ref[s]).astype(F32)
            after = xb[s].astype(F32) + valid * acc[...]
            after_s[s] = after
            unit, unused = rms_parts(after)
            normed = (unit * fg_ref[...]).astype(BF16)
            xg_s[s, :, :width] = normed
            logits = dot(normed, wr_ref[...])
            lanes = lane_of(logits.shape)
            routes = routes_ref[s]
            chosen = lanes == routes[:, 0:1]
            for k in range(1, routes.shape[1]):
                chosen = chosen | (lanes == routes[:, k : k + 1])
            top = jnp.max(jnp.where(chosen, logits, -1e30), axis=-1, keepdims=True)
            weight = jnp.where(chosen, jnp.exp(jnp.minimum(logits - top, 0.0)), 0.0)
            soft = weight / jnp.sum(weight, axis=-1, keepdims=True)
            soft_s[s] = soft
            gates = soft * valid
            high = gates.astype(BF16).astype(F32)
            xg_s[s, :, width:] = (high + pltpu.roll(gates - high, LANES // 2, 1)).astype(BF16)

        def one(t):
            kv_gather.arrive(t)
            attend_slot(t)
            row_gather.start(t)

            @pl.when(t <= slots - 3)
            def _():
                kv_gather.forward(t + 2)

            @pl.when(t <= slots - 2)
            def _():
                kv_gather.settle(t + 1)

            @pl.when(t >= 1)
            def _():
                row_gather.forward(t - 1)

            @pl.when(t >= 2)
            def _():
                row_gather.settle(t - 2)

        each(one)
        keeps += [
            pltpu.make_async_copy(source, there, out_sems.at[4 + n])
            for n, (source, there) in enumerate(
                ((mixed_s, mixed_out), (invl_s, invl_out), (after_s, after_out), (soft_s, soft_out))
            )
        ]
        for copy in keeps[4:]:
            copy.start()
        each(kv_gather.drain)
        for copy in keeps:
            copy.wait()

    V, D = pltpu.VMEM, pltpu.SemaphoreType.DMA
    full = lambda lanes, kind: V((slots, rows, lanes), kind)
    pl.run_scoped(
        first_phase,
        V(wq_in.shape, BF16), V(wk_in.shape, BF16), V(wv_in.shape, BF16), V(wo_in.shape, BF16),
        full(width, BF16), full(2 * kw, BF16), full(qw, BF16), full(width, BF16), full(qw, F32), full(kw, F32),
        V((group, rows, 2 * kw), BF16), full(qw, BF16), full(qw, F32), full(LANES, F32), V((rows, width), F32),
        D((6,)), D((8,)),
    )
    sources, double, pairs, held = group, 2 * rows, group // 2, group // 2 * PAIR

    eff = wg_in.shape[2]

    def late_phases(teach, y_s, og_s, late_sems):
        teacher_load = pltpu.make_async_copy(teacher_in, teach, late_sems.at[0])
        teacher_load.start()
        loss_out[...] = jnp.zeros_like(loss_out)
        outs = lambda s: [
            pltpu.make_async_copy(source.at[lax.rem(s, 2)], there.at[s], late_sems.at[1 + 2 * n + lax.rem(s, 2)])
            for n, (source, there) in enumerate(((y_s, y_out), (og_s, og_out)))
        ]

        def loss_slot(s):
            slot = lax.rem(s, 2)

            def wait():
                for copy in outs(s - 2):
                    copy.wait()

            if isinstance(s, int):
                if s >= 2:
                    wait()
            else:
                pl.when(s >= 2)(wait)
            output = after_s[s] + scatter.result(s)
            y_s[slot] = output.astype(BF16)
            valid = (row_of((rows, 1)) + here * rows < sc_ref[s]).astype(F32)
            difference = valid * (output - teach[s].astype(F32))
            loss_out[...] += jnp.sum(difference * difference, axis=0, keepdims=True)
            grad = difference * scale_ref[0]
            og_s[slot] = grad
            dy_s[s] = grad.astype(BF16)
            for copy in outs(s):
                copy.start()
            grad_gather.start(s)

        teacher_load.wait()

        def second_phase(tok, pick_s, xe_s, gp_s, up_s, hid_s, gates, ybuf, sems, out_sems):
            for copy in expert_loads:
                copy.wait()
            keeps = lambda s: [
                pltpu.make_async_copy(source, there.at[s], out_sems.at[n])
                for n, (source, there) in enumerate(
                    ((pick_s, pick_out), (xe_s, xe_out), (gp_s, gp_out), (up_s, up_out), (hid_s, hid_out))
                )
            ]

            def experts_slot(s, between):
                load = pltpu.make_async_copy(tokens_out.at[:, s], tok, sems.at[0])
                load.start()

                @pl.when(s >= 1)
                def _():
                    for copy in keeps(s - 1):
                        copy.wait()

                load.wait()
                slab = tok[:, :, width:].reshape(sources * rows, LANES)
                chosen = (lane_of((8, LANES)) == row_of((8, LANES)) + first).astype(BF16)
                routed = dot_nt(chosen, slab) > 0.0
                before, after = row_of((double, double)), lane_of((double, double))
                count = ((before < after) & (before // rows == after // rows)).astype(BF16)
                place = lax.broadcasted_iota(jnp.int32, (PAIR, double), 0)
                offset = (lane_of((8, double)) // rows) * MOST
                for p in range(pairs):
                    mask = routed[:, p * double : (p + 1) * double]
                    rank = dot(mask.astype(F32).astype(BF16), count).astype(jnp.int32) + offset
                    rank = jnp.where(mask, rank, -1)
                    pick = jnp.concatenate(
                        [(place == rank[e : e + 1, :]).astype(F32).astype(BF16) for e in range(owned)], axis=0
                    )
                    pick_s[p] = pick
                    picked = dot(pick, tok[2 * p : 2 * p + 2, :, :width].reshape(double, width)).astype(BF16)
                    scale = row_gates(dot(pick, slab[p * double : (p + 1) * double]), first, owned)
                    for e in range(owned):
                        xe_s[e, p * PAIR : (p + 1) * PAIR] = picked[e * PAIR : (e + 1) * PAIR]
                        gates[e, p * PAIR : (p + 1) * PAIR] = jnp.broadcast_to(
                            scale[e * PAIR : (e + 1) * PAIR], (PAIR, LANES)
                        )

                def one_expert(e, carry):
                    rows_in = xe_s[e]
                    gate_part = dot(rows_in, wg[e])
                    up_part = dot(rows_in, wu[e])
                    gp_s[e] = gate_part.astype(BF16)
                    up_s[e] = up_part.astype(BF16)
                    hidden = (gate_part * jax.nn.sigmoid(gate_part) * up_part).astype(BF16)
                    hid_s[e] = hidden
                    result = (dot(hidden, wd[e]) * gates[e][:, 0:1]).astype(BF16)
                    for p in range(pairs):
                        ybuf[p, e] = result[p * PAIR : (p + 1) * PAIR]
                    return carry

                for e in range(owned // 2):
                    one_expert(e, 0)
                between()
                for e in range(owned // 2, owned):
                    one_expert(e, 0)
                for p in range(pairs):
                    back = dot_tn(pick_s[p], ybuf[p].reshape(owned * PAIR, width))
                    parts[2 * p : 2 * p + 2, s] = back.astype(BF16).reshape(2, rows, width)
                for copy in keeps(s):
                    copy.start()

            def one(t):
                row_gather.arrive(t)

                def between():
                    @pl.when(t == 0)
                    def _():
                        row_gather.settle(slots - 2)
                        row_gather.forward(slots - 1)

                    @pl.when(t == 1)
                    def _():
                        row_gather.settle(slots - 1)

                    @pl.when(t >= 1)
                    def _():
                        scatter.first(t - 1)
                        scatter.second(t - 1)

                    @pl.when(t == slots - 1)
                    def _():
                        grad_gather.forward(0)

                experts_slot(t, between)
                scatter.start(t)

                @pl.when(t >= 1)
                def _():
                    scatter.third(t - 1)

                @pl.when(t >= 2)
                def _():
                    loss_slot(t - 2)

            each(one)
            each(row_gather.drain)
            for copy in keeps(slots - 1):
                copy.wait()

        pl.run_scoped(
            second_phase,
            V((group, rows, wide), BF16), V((pairs, owned * PAIR, double), BF16), V((owned, held, width), BF16),
            V((owned, held, eff), BF16), V((owned, held, eff), BF16), V((owned, held, eff), BF16), V((owned, held, LANES), F32),
            V((pairs, owned, PAIR, width), BF16), D((2,)), D((5,)),
        )

        def third_phase(dyb, slabb, pickb, gpb, upb, hidb, gates, dye, dxb, dp_s, dyw_s, gg_s, ug_s, sems, out_sems):
            saved = lambda s: [
                pltpu.make_async_copy(source, there, sems.at[n])
                for n, (source, there) in enumerate(
                    ((tokens_out.at[:, s, :, pl.ds(width, LANES)], slabb), (pick_out.at[s], pickb), (gp_out.at[s], gpb),
                     (up_out.at[s], upb), (hid_out.at[s], hidb))
                )
            ]
            keeps = lambda s: [
                pltpu.make_async_copy(source, there, out_sems.at[n])
                for n, (source, there) in enumerate(
                    ((dp_s, dpart_out.at[:, s]), (dyw_s, dyw_out.at[s]), (gg_s, gg_out.at[s]), (ug_s, ug_out.at[s]))
                )
            ]
            for copy in saved(0):
                copy.start()
            last = slots - 1
            scatter.first(last)
            scatter.second(last)
            loss_slot(last - 1)
            grad_gather.settle(0)
            grad_gather.forward(1)

            def one(s):
                grad_gather.arrive(s)
                load = pltpu.make_async_copy(grads_out.at[:, s], dyb, sems.at[5])
                load.start()

                @pl.when(s >= 1)
                def _():
                    for copy in keeps(s - 1):
                        copy.wait()

                for copy in saved(s):
                    copy.wait()
                load.wait()
                for p in range(pairs):
                    pick = pickb[p]
                    picked = dot(pick, dyb[2 * p : 2 * p + 2].reshape(double, width)).astype(BF16)
                    scale = row_gates(dot(pick, slabb[2 * p : 2 * p + 2].reshape(double, LANES)), first, owned)
                    for e in range(owned):
                        dye[e, p * PAIR : (p + 1) * PAIR] = picked[e * PAIR : (e + 1) * PAIR]
                        gates[e, p * PAIR : (p + 1) * PAIR] = jnp.broadcast_to(
                            scale[e * PAIR : (e + 1) * PAIR], (PAIR, LANES)
                        )

                def one_expert(e, carry):
                    grad_rows = dye[e]
                    scale = gates[e][:, 0:1]
                    plain = dot_nt(grad_rows, wd[e])
                    gate_part, up_part = gpb[e].astype(F32), upb[e].astype(F32)
                    soft_grad = jnp.sum(plain * hidb[e].astype(F32), axis=-1, keepdims=True)
                    hidden_grad = plain * scale
                    sigma = jax.nn.sigmoid(gate_part)
                    gate_grad = (hidden_grad * up_part * sigma * (1.0 + gate_part * (1.0 - sigma))).astype(BF16)
                    up_grad = (hidden_grad * gate_part * sigma).astype(BF16)
                    gg_s[e] = gate_grad
                    ug_s[e] = up_grad
                    dyw_s[e] = (grad_rows.astype(F32) * scale).astype(BF16)
                    input_grad = (dot_nt(gate_grad, wg[e]) + dot_nt(up_grad, wu[e])).astype(BF16)
                    lanes = lane_of((held, LANES))
                    high = soft_grad.astype(BF16).astype(F32)
                    spot = jnp.where(
                        lanes == first + e, high, jnp.where(lanes == first + e + LANES // 2, soft_grad - high, 0.0)
                    ).astype(BF16)
                    for p in range(pairs):
                        dxb[p, e, :, :width] = input_grad[p * PAIR : (p + 1) * PAIR]
                        dxb[p, e, :, width:] = spot[p * PAIR : (p + 1) * PAIR]
                    return carry

                for e in range(owned // 2):
                    one_expert(e, 0)

                @pl.when(s == 0)
                def _():
                    scatter.third(last)
                    grad_gather.settle(1)
                    grad_gather.forward(2)

                @pl.when(s == 1)
                def _():
                    grad_gather.settle(2)
                    grad_gather.forward(3)

                @pl.when(s == 2)
                def _():
                    grad_gather.settle(3)

                for e in range(owned // 2, owned):
                    one_expert(e, 0)
                for p in range(pairs):
                    back = dot_tn(pickb[p], dxb[p].reshape(owned * PAIR, wide))
                    dp_s[2 * p : 2 * p + 2] = back.astype(BF16).reshape(2, rows, wide)
                for copy in keeps(s):
                    copy.start()

                @pl.when(s + 1 < slots)
                def _():
                    for copy in saved(s + 1):
                        copy.start()

                @pl.when(s == 0)
                def _():
                    loss_slot(last)

            each(one)
            each(scatter.drain)
            each(grad_gather.drain)
            for copy in keeps(slots - 1):
                copy.wait()

        pl.run_scoped(
            third_phase,
            V((group, rows, width), BF16), V((group, rows, LANES), BF16), V((pairs, owned * PAIR, double), BF16),
            V((owned, held, eff), BF16), V((owned, held, eff), BF16), V((owned, held, eff), BF16), V((owned, held, LANES), F32),
            V((owned, held, width), BF16), V((pairs, owned, PAIR, wide), BF16), V((group, rows, wide), BF16),
            V((owned, held, width), BF16), V((owned, held, eff), BF16), V((owned, held, eff), BF16), D((6,)), D((4,)),
        )
        for s in range(slots - 2, slots):
            for copy in outs(s):
                copy.wait()

    pl.run_scoped(
        late_phases, full(width, BF16), V((2, rows, width), BF16), V((2, rows, width), F32), D((5,)),
    )


def front(
    slot_lengths, x, teacher, routes, w_query, w_key, w_value, w_out, w_gate, w_up, w_down,
    attn_gain, ffn_gain, qg, kg, cosine, sine, router, scale, group, number,
):
    slots, rows, width = x.shape
    qw, kw = w_query.shape[1], w_key.shape[1]
    owned, unused, eff = w_gate.shape
    wide = width + LANES
    pairs = group // 2
    held = pairs * PAIR
    hbm = pl.BlockSpec(memory_space=pl.ANY)
    vmem = pl.BlockSpec(memory_space=pltpu.VMEM)
    smem = pl.BlockSpec(memory_space=pltpu.SMEM)
    V, D = pltpu.VMEM, pltpu.SemaphoreType.DMA
    half = rows // 2
    mine = lambda lanes, kind: jax.ShapeDtypeStruct((slots, rows, lanes), kind)
    all_of = lambda lanes: jax.ShapeDtypeStruct((group, slots, rows, lanes), BF16)
    saved = lambda *dims: jax.ShapeDtypeStruct((slots,) + dims, BF16)
    outs = (
        mine(width, BF16), mine(qw, BF16), mine(qw, F32), mine(kw, F32), all_of(2 * kw), mine(qw, BF16), mine(qw, F32),
        mine(width, F32), mine(LANES, F32), all_of(wide),
        saved(pairs, owned * PAIR, 2 * rows), saved(owned, held, width),
        saved(owned, held, eff), saved(owned, held, eff), saved(owned, held, eff), mine(width, BF16), mine(width, F32), jax.ShapeDtypeStruct((1, width), F32), all_of(width),
        all_of(wide), saved(owned, held, width), saved(owned, held, eff), saved(owned, held, eff),
    )
    return pl.pallas_call(
        front_kernel,
        in_specs=[smem, hbm, hbm, vmem] + [hbm] * 7 + [vmem] * 7 + [smem],
        out_specs=(hbm,) * 17 + (vmem,) + (hbm,) * 5,
        out_shape=outs,
        scratch_shapes=[
            V((4, slots, rows, width), BF16), V((slots, half, width), BF16), V((slots, half, width), BF16),
            V((slots, rows, width), BF16), V((slots, rows, width), BF16),
            V((group, slots, rows, width), BF16),
            V(w_gate.shape, BF16), V(w_up.shape, BF16), V(w_down.shape, BF16),
            V((slots, rows, width), F32), V((slots, rows, wide), BF16), V((slots, rows, width), BF16),
        ]
        + [D((8, slots)), D((8, slots)), D((slots,))] * 3
        + [D((10, slots)), D((10, slots)), D((3,)), D((1,))],
        compiler_params=pltpu.CompilerParams(collective_id=number, has_side_effects=True, vmem_limit_bytes=63 * MIB),
        name="front",
    )(
        slot_lengths, x, teacher, routes, w_query, w_key, w_value, w_out, w_gate, w_up, w_down,
        attn_gain, ffn_gain, qg, kg, cosine, sine, router, scale,
    )


def add_to(ref, value):
    ref[...] = (ref[...].astype(F32) + value).astype(ref.dtype)


class Plane:
    def __init__(self):
        z, c, y = lax.axis_index("dp"), lax.axis_index("context"), lax.axis_index("experts")
        core = lax.rem(c, 2)
        cx, yy = lax.rem(c + 2, 4), 1 - y
        self.me = c * 2 + y
        self.sib, self.xn, self.yn = (z, c + 1 - 2 * core, y), (z, cx, y), (z, c, yy)
        chips = [(cx, yy), (cx, y), (c, yy), (c, y)]
        self.own = [a * 2 + b for a, b in chips]
        self.other = [(a + 1 - 2 * core) * 2 + b for a, b in chips]
        self.inner_plane = (z == 1) | (z == 2)
        self.outer_plane = (z == 0) | (z == 3)
        self.inner = (1 + z // 2, c, y)
        self.across = (3 - z, c, y)
        self.outer = ((z - 1) * 3, c, y)

    def barrier(self, line):
        bar = pltpu.get_barrier_semaphore()
        tell = lambda who: pl.semaphore_signal(bar, inc=1, device_id=who, device_id_type=MESH)
        for who in (self.sib, self.xn, self.yn):
            tell(who)
        if not line:
            pl.semaphore_wait(bar, 3)
            return

        @pl.when(self.outer_plane)
        def _():
            tell(self.inner)
            pl.semaphore_wait(bar, 4)

        @pl.when(self.inner_plane)
        def _():
            tell(self.across)
            tell(self.outer)
            pl.semaphore_wait(bar, 5)


class Scatter:
    def __init__(self, plane, own, other, buffers, sems):
        self.plane, self.own, self.other = plane, own, other
        self.sb, self.da, self.db, self.rx, self.ry = buffers
        self.sent, self.got = sems
        self.rows = self.sb.shape[2]
        self.top, self.low = pl.ds(0, self.rows // 2), pl.ds(self.rows // 2, self.rows // 2)

    def core(self, k, s):
        return remote(self.other(k, s), self.sb.at[k, s], self.sent.at[k, s], self.got.at[k, s], self.plane.sib)

    def diag(self, s):
        mine = self.own(0, s)
        return (
            remote(mine.at[self.top], self.da.at[s], self.sent.at[4, s], self.got.at[4, s], self.plane.xn),
            remote(mine.at[self.low], self.db.at[s], self.sent.at[5, s], self.got.at[5, s], self.plane.yn),
        )

    def side(self, number, s):
        axis, half = number // 2, (self.top, self.low)[number % 2]
        there = (self.rx, self.ry)[axis]
        who = (self.plane.xn, self.plane.yn)[axis]
        return remote(
            self.own(1 + axis, s).at[half], there.at[s, half], self.sent.at[6 + number, s], self.got.at[6 + number, s], who
        )

    def pair(self, k, s, half):
        return self.own(k, s)[half].astype(F32) + self.sb[k, s, half].astype(F32)

    def start(self, s):
        for k in range(4):
            self.core(k, s).start()

    def first(self, s):
        self.core(0, s).wait_recv()
        mine = self.own(0, s)
        add_to(mine, self.sb[0, s].astype(F32))
        for copy in self.diag(s):
            copy.start()

    def second(self, s):
        self.core(1, s).wait_recv()
        self.own(1, s)[self.top] = self.pair(1, s, self.top).astype(BF16)
        self.side(0, s).start()
        self.core(2, s).wait_recv()
        self.own(2, s)[self.low] = self.pair(2, s, self.low).astype(BF16)
        self.side(3, s).start()

    def third(self, s):
        by_x, by_y = self.diag(s)
        by_x.wait_recv()
        self.own(2, s)[self.top] = (self.pair(2, s, self.top) + self.da[s].astype(F32)).astype(BF16)
        self.side(2, s).start()
        by_y.wait_recv()
        self.own(1, s)[self.low] = (self.pair(1, s, self.low) + self.db[s].astype(F32)).astype(BF16)
        self.side(1, s).start()

    def result(self, s):
        self.core(3, s).wait_recv()
        for number in range(4):
            self.side(number, s).wait_recv()
        return (
            self.own(3, s)[...].astype(F32)
            + self.sb[3, s].astype(F32)
            + self.rx[s].astype(F32)
            + self.ry[s].astype(F32)
        )

    def drain(self, s):
        for k in range(4):
            self.core(k, s).wait_send()
        for copy in self.diag(s):
            copy.wait_send()
        for number in range(4):
            self.side(number, s).wait_send()


class Line:
    ring, back = 4, 2

    def __init__(self, plane, held, first, second, total, buffers, sems):
        self.plane, self.held, self.r1, self.r2, self.total = plane, held, first, second, total
        self.l1, self.va, self.vt = buffers
        self.sent, self.got, self.local = sems
        self.count = held.shape[0]

    def inward(self, i):
        return remote(self.held.at[i], self.r1.at[i], self.sent.at[0, i], self.got.at[0, i], self.plane.inner)

    def across(self, i):
        return remote(self.va.at[i % self.ring], self.r2.at[i], self.sent.at[1, i], self.got.at[1, i], self.plane.across)

    def outward(self, i):
        return remote(self.vt.at[i % self.back], self.total.at[i], self.sent.at[2, i], self.got.at[2, i], self.plane.outer)

    def keep(self, i):
        return pltpu.make_async_copy(self.vt.at[i % self.back], self.total.at[i], self.local.at[i % self.back])

    def load(self, number, i):
        source, there = (
            (self.r1, self.l1.at[i % 2]), (self.held, self.va.at[i % self.ring]), (self.r2, self.vt.at[i % self.back])
        )[number]
        return pltpu.make_async_copy(source.at[i], there, self.local.at[self.ring + 2 * number + i % 2])

    def when(self, fact, body):
        if isinstance(fact, bool):
            if fact:
                body()
        else:
            pl.when(fact)(body)

    def take(self, i):
        def wait():
            self.across(i - self.ring).wait_send()

        self.when(i >= self.ring, wait)
        self.load(1, i).start()
        self.inward(i).wait_recv()
        self.load(0, i).start()

    def give(self, i):
        self.load(1, i).wait()
        self.load(0, i).wait()
        add_to(self.va.at[i % self.ring], self.l1[i % 2].astype(F32))
        self.across(i).start()

    def fetch(self, i):
        def wait():
            self.outward(i - self.back).wait_send()
            self.keep(i - self.back).wait()

        self.when(i >= self.back, wait)
        self.across(i).wait_recv()
        self.load(2, i).start()

    def settle(self, i):
        self.load(2, i).wait()
        add_to(self.vt.at[i % self.back], self.va[i % self.ring].astype(F32))
        self.outward(i).start()
        self.keep(i).start()

    def move(self, i, lag=2):
        @pl.when(self.plane.inner_plane)
        def _():
            self.take(i)
            self.when(i >= lag, lambda: self.fetch(i - lag))
            self.give(i)
            self.when(i >= lag, lambda: self.settle(i - lag))

    def wind_up(self, start):
        @pl.when(self.plane.inner_plane)
        def _():
            for i in range(start, self.count + 1):
                if i < self.count:
                    self.take(i)
                    self.give(i)
                for n in ([start - 2] if i == start else []) + [i - 1]:
                    self.fetch(n)
                    self.settle(n)

    def finish(self):
        @pl.when(self.plane.inner_plane)
        def _():
            for i in range(self.count - self.ring, self.count):
                self.across(i).wait_send()
            for i in range(self.count - self.back, self.count):
                self.outward(i).wait_send()
                self.keep(i).wait()

        @pl.when(self.plane.outer_plane)
        def _():
            def one(i, carry):
                self.inward(i).wait_send()
                remote(
                    self.held.at[i], self.total.at[i], self.sent.at[2, i], self.got.at[2, i], self.plane.inner
                ).wait_recv()
                return carry

            lax.fori_loop(0, self.count, one, 0)


HELD_BACK = 14


def tail_kernel(
    sc_ref, dpart, xe, gg, ug, hid, dyw, q_in, kv_in, mixed_in, invl_in, soft_in, og_in, after_in, qraw_in, kraw_in,
    x_in, h_in, n2_in, wo_in, wq_in, wk_in, wv_in, fg_ref, wr_ref, cos_ref, sin_ref, gain_ref, qg_ref, kg_ref, loss_ref,
    total, ig_out, dense_out, small_out, held, r1, r2,
    dx_own, dx_sb, dx_da, dx_db, dx_rx, dx_ry, kv_sb, kv_da, kv_db, kv_rx, kv_ry,
    l1, va, vt, dsh, dr1, dr2, dfin, sm_mine, sm_got,
    sent_dx, got_dx, sent_kv, got_kv, sent_de, got_de, sent_z, got_z, local_z, sent_ag, got_ag, sent_sm, got_sm, local,
):
    plane = Plane()
    slots, rows = x_in.shape[0], x_in.shape[1]
    width = x_in.shape[2]
    group = dpart.shape[0]
    kinds = dsh.shape[0]
    owned = xe.shape[1]
    eff = gg.shape[3]
    each = lambda body, count=slots: lax.fori_loop(0, count, lambda s, c: (body(s), c)[1], 0)
    line = Line(plane, held, r1, r2, total, (l1, va, vt), (sent_z, got_z, local_z))
    scat_dx = Scatter(
        plane, lambda k, s: dx_own.at[k, s], lambda k, s: dpart.at[plane.other[k], s],
        (dx_sb, dx_da, dx_db, dx_rx, dx_ry), (sent_dx, got_dx),
    )
    own_load = lambda k, s: pltpu.make_async_copy(dpart.at[plane.own[k], s], dx_own.at[k, s], local.at[0])
    for k in range(4):
        each(lambda s: own_load(k, s).start())
    def expert_phase(xeb, ggb, ugb, hidb, dywb, gb, sems, out_sem):
        def loads(e):
            slot = e % 2
            return [
                pltpu.make_async_copy(source.at[:, e], there.at[slot], sems.at[slot, n])
                for n, (source, there) in enumerate(((xe, xeb), (gg, ggb), (ug, ugb), (hid, hidb), (dyw, dywb)))
            ]

        def store(number):
            return pltpu.make_async_copy(gb.at[number % 4], held.at[pl.ds(2 * number, 2)], out_sem.at[number % 4])

        def send(number):
            store(number).wait()
            todo = [2 * number + n for n in range(2) if 2 * number + n < HELD_BACK]
            if todo:
                @pl.when(plane.outer_plane)
                def _():
                    for i in todo:
                        line.inward(i).start()

        flat = lambda ref, slot: ref[slot].reshape(ref.shape[1] * ref.shape[2], ref.shape[3])
        half = width // 2
        for copy in loads(0):
            copy.start()
        plane.barrier(True)
        each(scat_dx.start)
        for e in range(owned):
            slot = e % 2
            if e + 1 < owned:
                for copy in loads(e + 1):
                    copy.start()
            for copy in loads(e):
                copy.wait()
            for n, (left, right) in enumerate(((xeb, ggb), (xeb, ugb), (hidb, dywb))):
                number = 3 * e + n
                part = dot_tn(flat(left, slot), flat(right, slot)).astype(BF16)
                gb[number % 4, 0] = part[:half] if n < 2 else part[:, :half]
                gb[number % 4, 1] = part[half:] if n < 2 else part[:, half:]
                store(number).start()
                if number >= 1:
                    send(number - 1)
            if e == 1:
                for k in range(4):
                    each(lambda s: own_load(k, s).wait())
                each(scat_dx.first)
            if e == 2:
                each(scat_dx.second)
                line.move(0)
        send(3 * owned - 1)
        line.move(1)
        each(scat_dx.third)

    held_rows = (xe.shape[0], xe.shape[2])
    pl.run_scoped(
        expert_phase,
        pltpu.VMEM((2,) + held_rows + (width,), BF16),
        pltpu.VMEM((2,) + held_rows + (eff,), BF16),
        pltpu.VMEM((2,) + held_rows + (eff,), BF16),
        pltpu.VMEM((2,) + held_rows + (eff,), BF16),
        pltpu.VMEM((2,) + held_rows + (width,), BF16),
        pltpu.VMEM((4, 2, eff, width // 2), BF16),
        pltpu.SemaphoreType.DMA((2, 5)),
        pltpu.SemaphoreType.DMA((4,)),
    )
    line.move(2)
    here = plane.me
    chunk = 2 * rows
    chunks = (here + 2) // 2
    qw = q_in.shape[2]
    kw = kraw_in.shape[2]
    tiles = qw // 256

    def rest(dkv, ag_s, at_s, lg_s, mixed_s, q_s, qgg, kgg, agg, fgg, mg_s):
        scat_kv = Scatter(
            plane, lambda k, s: dkv.at[plane.own[k], s], lambda k, s: dkv.at[plane.other[k], s],
            (kv_sb, kv_da, kv_db, kv_rx, kv_ry), (sent_kv, got_kv),
        )
        for ref in (qgg, kgg, agg, fgg):
            ref[...] = jnp.zeros_like(ref)
        mixed_load = pltpu.make_async_copy(mixed_in, mixed_s, local.at[1])
        mixed_load.start()

        def attention_phase(wo, qb, kvb, invlb, softb, ogb, afterb, qrawb, sems):
            wo_load = pltpu.make_async_copy(wo_in, wo, local.at[2])
            wo_load.start()

            def loads(s):
                slot = lax.rem(s, 2)
                out = [pltpu.make_async_copy(kv_in.at[:, s], kvb.at[slot], sems.at[slot, 0])]
                for n, (source, there) in enumerate(
                    ((q_in, qb), (invl_in, invlb), (soft_in, softb), (og_in, ogb), (after_in, afterb), (qraw_in, qrawb))
                ):
                    out.append(pltpu.make_async_copy(source.at[s], there.at[slot], sems.at[slot, n + 1]))
                return out

            for s in range(2):
                for copy in loads(s):
                    copy.start()
            wo_load.wait()
            mixed_load.wait()

            def one_slot(s):
                slot = lax.rem(s, 2)
                for copy in loads(s):
                    copy.wait()
                dx = scat_dx.result(s)
                valid = (row_of((rows, 1)) + here * rows < sc_ref[s]).astype(F32)
                slab = dx[:, width:]
                half = slab.shape[1] // 2
                soft = softb[slot]
                soft_grad = jnp.where(lane_of(slab.shape) < half, slab + pltpu.roll(slab, half, 1), 0.0)
                chosen = soft * (soft_grad - jnp.sum(soft * soft_grad, axis=-1, keepdims=True))
                logit_grad = chosen.astype(BF16)
                lg_s[s] = logit_grad
                normed_grad = dx[:, :width] + dot_nt(logit_grad, wr_ref[...])
                back, gain_grad = rms_backward(normed_grad, afterb[slot], fg_ref[...])
                fgg[...] += gain_grad
                after_grad = ogb[slot] + back
                ag_s[s] = after_grad
                attn_grad = (valid * after_grad).astype(BF16)
                at_s[s] = attn_grad
                mixed_grad = dot_nt(attn_grad, wo[...]).astype(BF16)
                for t in range(tiles):
                    mg_s[t] = mixed_grad[:, t * 256 : (t + 1) * 256]

                def one_tile(t, carry):
                    lanes = pl.ds(pl.multiple_of(t * 256, 256), 256)
                    key_lanes = pl.ds(pl.multiple_of(t * 256, 256), LANES)
                    value_lanes = pl.ds(pl.multiple_of(t * 256 + LANES, LANES), LANES)
                    q4 = stack_heads(qb[slot, :, lanes], True).astype(BF16)
                    do4_f = stack_heads(mg_s[t].astype(F32) * invlb[slot, :, lanes], True)
                    do4 = do4_f.astype(BF16)
                    product = do4_f * stack_heads(mixed_s[s, :, lanes], False)
                    delta = lax.dot_general(
                        jnp.ones((8, LANES), F32), product, (((1,), (1,)), ((), ())),
                        preferred_element_type=F32, precision=lax.Precision.HIGHEST,
                    )[0:1]

                    def step(index, sum_q, masked):
                        two = pl.ds(2 * index, 2)
                        keys = kvb[slot, two, :, key_lanes].reshape(chunk, LANES)
                        values = kvb[slot, two, :, value_lanes].reshape(chunk, LANES)
                        weight = jnp.exp2(dot_nt(keys, q4) * EXP2_SCALE)
                        if masked:
                            at = lax.rem(lane_of(weight.shape), rows) + here * rows
                            weight = jnp.where(row_of(weight.shape) + index * chunk <= at, weight, 0.0)
                        pressure = dot_nt(values, do4)
                        score_grad = (weight * (pressure - delta) * SCALE).astype(BF16)
                        key_grad = dot(score_grad, q4).astype(BF16)
                        value_grad = dot(weight.astype(BF16), do4).astype(BF16)
                        dkv[two, s, :, key_lanes] = key_grad.reshape(2, rows, LANES)
                        dkv[two, s, :, value_lanes] = value_grad.reshape(2, rows, LANES)
                        return sum_q + dot_tn(score_grad, keys)

                    total_q = lax.fori_loop(
                        0, chunks - 1, lambda i, c: step(i, c, False), jnp.zeros((4 * rows, LANES), F32)
                    )
                    total_q = step(chunks - 1, total_q, True)

                    def blank(index, carry):
                        dkv[pl.ds(2 * index, 2), s, :, lanes] = jnp.zeros((2, rows, 256), BF16)
                        return carry

                    lax.fori_loop(chunks, group // 2, blank, 0)
                    dq = unstack_heads(total_q).astype(BF16).astype(F32)
                    for n in range(2):
                        part = slice(n * LANES, (n + 1) * LANES)
                        here_lanes = pl.ds(pl.multiple_of(t * 256 + n * LANES, LANES), LANES)
                        raw, gain = rope_backward(
                            dq[:, part], qrawb[slot, :, here_lanes], qg_ref[...], cos_ref[...], sin_ref[...]
                        )
                        q_s[s, :, here_lanes] = raw.astype(BF16)
                        qgg[...] += gain
                    return carry

                lax.fori_loop(0, tiles, one_tile, 0)

                @pl.when(s + 2 < slots)
                def _():
                    for copy in loads(s + 2):
                        copy.start()

                scat_kv.start(s)

                @pl.when(s >= 1)
                def _():
                    scat_kv.first(s - 1)
                    scat_kv.second(s - 1)

                @pl.when(s >= 2)
                def _():
                    scat_kv.third(s - 2)

            def slot_and_move(s):
                one_slot(s)
                ahead = s + 3 + s // 2
                line.move(ahead)

                @pl.when(lax.rem(s, 2) == 1)
                def _():
                    line.move(ahead + 1)

            each(slot_and_move)

        pl.run_scoped(
            attention_phase,
            pltpu.VMEM(wo_in.shape, BF16),
            pltpu.VMEM((2, rows, qw), BF16),
            pltpu.VMEM((2, group, rows, 2 * kw), BF16),
            pltpu.VMEM((2, rows, qw), F32),
            pltpu.VMEM((2, rows, LANES), F32),
            pltpu.VMEM((2, rows, width), F32),
            pltpu.VMEM((2, rows, width), F32),
            pltpu.VMEM((2, rows, qw), F32),
            pltpu.SemaphoreType.DMA((2, 7)),
        )
        each(scat_dx.drain)

        def last_phase(wq, wk, wv, xb, krawb, hb, n2b, k_s, v_s):
            loads = [
                pltpu.make_async_copy(source, there, local.at[2 + n])
                for n, (source, there) in enumerate(
                    ((wq_in, wq), (wk_in, wk), (wv_in, wv), (x_in, xb), (kraw_in, krawb), (h_in, hb),
                     (n2_in.at[plane.me, :, :, pl.ds(0, width)], n2b))
                )
            ]
            for copy in loads:
                copy.start()
            scat_kv.first(slots - 1)
            scat_kv.second(slots - 1)
            scat_kv.third(slots - 2)
            line.move(9)
            flat = lambda ref: ref[...].reshape(slots * rows, ref.shape[2])
            for copy in loads:
                copy.wait()
            shards, shard_rows = group, width // group

            def product(left, right, place):
                def one(n, carry):
                    lanes = pl.ds(pl.multiple_of(n * 256, 256), 256)
                    column = right[:, :, lanes].reshape(slots * rows, 256)
                    place(n, dot_tn(flat(left), column).astype(BF16).reshape(shards, shard_rows, 256))
                    return carry

                lax.fori_loop(0, right.shape[2] // 256, one, 0)

            def aside(k):
                def place(n, value):
                    lanes = pl.ds(pl.multiple_of(n * 256, 256), 256)
                    for shard in range(shards):
                        dx_own[k + shard // slots, shard % slots, :, lanes] = value[shard]

                return place

            product(mixed_s, at_s, aside(0))
            scat_kv.third(slots - 1)
            product(hb, q_s, aside(2))
            line.move(10)
            router = dot_tn(flat(lg_s), flat(n2b))
            experts = small_out.shape[0] - 8
            sm_mine[0] = jnp.zeros(sm_mine.shape[1:], F32)
            sm_mine[0, :experts] = router[:experts]
            sm_mine[0, experts + 1 : experts + 2] = fgg[...]
            sm_mine[0, experts + 2 : experts + 3, :LANES] = qgg[...]
            sm_mine[0, experts + 4 : experts + 5] = loss_ref[...]

            def one_slot(s):
                grads = scat_kv.result(s)
                for t in range(kw // LANES):
                    lanes = slice(t * LANES, (t + 1) * LANES)
                    at = 2 * t * LANES
                    grad = grads[:, at : at + LANES].astype(BF16).astype(F32)
                    raw, gain = rope_backward(grad, krawb[s, :, lanes], kg_ref[...], cos_ref[...], sin_ref[...])
                    k_s[s, :, lanes] = raw.astype(BF16)
                    kgg[...] += gain
                    v_s[s, :, lanes] = grads[:, at + LANES : at + 2 * LANES].astype(BF16)
                normed_grad = dot_nt(q_s[s], wq[...]) + dot_nt(k_s[s], wk[...]) + dot_nt(v_s[s], wv[...])
                back, gain = rms_backward(normed_grad, xb[s].astype(F32), gain_ref[...])
                agg[...] += gain
                ag_s[s] += back
                pltpu.make_async_copy(ag_s.at[s], ig_out.at[s], local.at[0]).start()

            each(one_slot)
            each(scat_kv.drain)
            line.move(11)
            sm_mine[0, experts : experts + 1] = agg[...]
            sm_mine[0, experts + 3 : experts + 4, :LANES] = kgg[...]
            for shard in range(shards):
                dkv[shard, 2] = dx_own[shard // slots, shard % slots, :, :width]
                dkv[shard, 0] = dx_own[2 + shard // slots, shard % slots, :, :width]

            def beside(first):
                def place(n, value):
                    dkv[:, 1, :, pl.ds(pl.multiple_of(first + n * 256, 256), 256)] = value

                return place

            product(hb, k_s, beside(0))
            product(hb, v_s, beside(kw))
            line.move(12)

        pl.run_scoped(
            last_phase,
            pltpu.VMEM(wq_in.shape, BF16),
            pltpu.VMEM(wk_in.shape, BF16),
            pltpu.VMEM(wv_in.shape, BF16),
            pltpu.VMEM(x_in.shape, BF16),
            pltpu.VMEM(kraw_in.shape, F32),
            pltpu.VMEM(h_in.shape, BF16),
            pltpu.VMEM((slots, rows, width), BF16),
            pltpu.VMEM((slots, rows, kw), BF16),
            pltpu.VMEM((slots, rows, kw), BF16),
        )
        narrow = pl.ds(0, width)
        again = [dx_sb.at[:, :, :, narrow]] + [r.at[:, :, narrow] for r in (dx_da, dx_db, dx_rx, dx_ry)]
        scat_de = Scatter(
            plane, lambda k, s: dkv.at[plane.own[k], s], lambda k, s: dkv.at[plane.other[k], s],
            again, (sent_de, got_de),
        )
        by_kind = lambda body: each(body, kinds)
        by_kind(scat_de.start)
        small = lambda n, who: remote(sm_mine.at[n], sm_got.at[n], sent_sm.at[n], got_sm.at[n], who)

        def small_step(n, who):
            small(n, who).wait_recv()
            sm_mine[n + 1] = sm_mine[n] + sm_got[n]

        small(0, plane.sib).start()
        by_kind(scat_de.first)
        small_step(0, plane.sib)
        small(1, plane.xn).start()
        by_kind(scat_de.second)
        small_step(1, plane.xn)
        small(2, plane.yn).start()
        by_kind(scat_de.third)
        small_step(2, plane.yn)
        line.move(13)

        def one_kind(s):
            dsh[s] = scat_de.result(s).astype(BF16)

        by_kind(one_kind)
        by_kind(scat_de.drain)
        each(lambda s: pltpu.make_async_copy(ag_s.at[s], ig_out.at[s], local.at[0]).wait())

    pl.run_scoped(
        rest,
        pltpu.VMEM((group, slots, rows, 2 * kw), BF16),
        pltpu.VMEM((slots, rows, width), F32),
        pltpu.VMEM((slots, rows, width), BF16),
        pltpu.VMEM((slots, rows, LANES), BF16),
        pltpu.VMEM((slots, rows, qw), BF16),
        pltpu.VMEM((slots, rows, qw), BF16),
        pltpu.VMEM((1, LANES), F32),
        pltpu.VMEM((1, LANES), F32),
        pltpu.VMEM((1, width), F32),
        pltpu.VMEM((1, width), F32),
        pltpu.VMEM((tiles, rows, 256), BF16),
    )

    small_in = remote(sm_mine.at[3], sm_got.at[3], sent_sm.at[3], got_sm.at[3], plane.inner)
    small_across = remote(sm_mine.at[4], sm_got.at[4], sent_sm.at[4], got_sm.at[4], plane.across)
    small_back = remote(sm_mine.at[5], sm_got.at[5], sent_sm.at[5], got_sm.at[5], plane.outer)
    dense_in = remote(dsh, dr1, sent_sm.at[6], got_sm.at[6], plane.inner)
    dense_across = remote(dsh, dr2, sent_sm.at[7], got_sm.at[7], plane.across)
    dense_back = remote(dfin, dfin, sent_sm.at[8], got_sm.at[8], plane.outer)

    @pl.when(plane.outer_plane)
    def _():
        small_in.start()
        dense_in.start()

        def one(i, carry):
            line.inward(i).start()
            return carry

        lax.fori_loop(HELD_BACK, line.count, one, 0)

    @pl.when(plane.inner_plane)
    def _():
        small_in.wait_recv()
        sm_mine[4] = sm_mine[3] + sm_got[3]
        small_across.start()
        dense_in.wait_recv()
        add_to(dsh, dr1[...].astype(F32))
        dense_across.start()

    line.move(14)

    @pl.when(plane.inner_plane)
    def _():
        small_across.wait_recv()
        sm_mine[5] = sm_mine[4] + sm_got[4]
        small_back.start()
        small_out[...] = sm_mine[5]

    line.move(15)

    @pl.when(plane.inner_plane)
    def _():
        dense_across.wait_recv()
        dfin[...] = (dsh[...].astype(F32) + dr2[...].astype(F32)).astype(BF16)
        dense_back.start()

    @pl.when(plane.outer_plane)
    def _():
        small_back.wait_recv()
        small_out[...] = sm_got[5]
        dense_back.wait_recv()

    gather = Slots(plane, dfin, dense_out, sent_ag, got_ag, local)
    for s in range(kinds):
        gather.start(s)
    line.move(16)
    for s in range(kinds):
        gather.forward(s)
    line.move(17)
    for s in range(kinds):
        gather.settle(s)
    line.move(18)
    for s in range(kinds):
        gather.arrive(s)
        gather.drain(s)
    line.wind_up(19)
    line.finish()
    for n, who in ((0, plane.sib), (1, plane.xn), (2, plane.yn)):
        remote(sm_mine.at[n], sm_got.at[n], sent_sm.at[n], got_sm.at[n], who).wait_send()

    @pl.when(plane.outer_plane)
    def _():
        small_in.wait_send()
        dense_in.wait_send()

    @pl.when(plane.inner_plane)
    def _():
        small_across.wait_send()
        small_back.wait_send()
        dense_across.wait_send()
        dense_back.wait_send()


def tail(
    slot_lengths, dpart, xe, gate_grad, up_grad, hidden, weighted, q, kv, mixed, invl, soft, out_grad, after, qraw, kraw,
    x, h, n2, w_out, w_query, w_key, w_value, ffn_gain, router, cosine, sine, attn_gain, qg, kg, loss, experts, number,
):
    slots, rows, width = x.shape
    group, unused, unused_rows, wide = dpart.shape
    owned, eff = xe.shape[1], gate_grad.shape[3]
    kw = kraw.shape[2]
    chunks = 6 * owned
    piece = (eff, width // 2)
    kinds = 3
    hbm = pl.BlockSpec(memory_space=pl.ANY)
    vmem = pl.BlockSpec(memory_space=pltpu.VMEM)
    smem = pl.BlockSpec(memory_space=pltpu.SMEM)
    V, D = pltpu.VMEM, pltpu.SemaphoreType.DMA
    half = rows // 2

    def landing(n, lanes):
        return [
            V((4, n, rows, lanes), BF16), V((n, half, lanes), BF16), V((n, half, lanes), BF16),
            V((n, rows, lanes), BF16), V((n, rows, lanes), BF16),
        ]

    small_rows = experts + 8
    return pl.pallas_call(
        tail_kernel,
        in_specs=[smem] + [hbm] * 22 + [vmem] * 8,
        out_specs=(hbm, hbm, hbm, vmem, hbm, hbm, hbm),
        out_shape=(
            jax.ShapeDtypeStruct((chunks,) + piece, BF16),
            jax.ShapeDtypeStruct((slots, rows, width), F32),
            jax.ShapeDtypeStruct((group, kinds, width // group, width), BF16),
            jax.ShapeDtypeStruct((small_rows, width), F32),
            jax.ShapeDtypeStruct((chunks,) + piece, BF16),
            jax.ShapeDtypeStruct((chunks,) + piece, BF16),
            jax.ShapeDtypeStruct((chunks,) + piece, BF16),
        ),
        scratch_shapes=[V((4, slots, rows, wide), BF16)]
        + landing(slots, wide) + landing(slots, 2 * kw)
        + [V((2,) + piece, BF16), V((4,) + piece, BF16), V((2,) + piece, BF16)]
        + [V((kinds, rows, width), BF16)] * 4
        + [V((6, small_rows, width), F32)] * 2
        + [D((10, slots))] * 4 + [D((10, kinds))] * 2
        + [D((3, chunks))] * 2 + [D((10,))]
        + [D((8, kinds))] * 2 + [D((9,))] * 2 + [D((9,))],
        compiler_params=pltpu.CompilerParams(collective_id=number, has_side_effects=True, vmem_limit_bytes=63 * MIB),
        name="tail",
    )(
        slot_lengths, dpart, xe, gate_grad, up_grad, hidden, weighted, q, kv, mixed, invl, soft, out_grad, after, qraw,
        kraw, x, h, n2, w_out, w_query, w_key, w_value, ffn_gain, router, cosine, sine, attn_gain, qg, kg, loss,
    )


def plane_gather(rows):
    return lax.all_gather(rows, ("context", "experts"), axis=0, tiled=False)


def plane_scatter(parts):
    return lax.psum_scatter(parts, ("context", "experts"), scatter_dimension=0, tiled=False).astype(F32)


def unpack_kernel(gate_ref, up_ref, down_ref, dense_ref, dg_ref, du_ref, dd_ref, dq_ref, dk_ref, dv_ref, do_ref):
    dg_ref[0] = gate_ref[0].astype(F32)
    du_ref[0] = up_ref[0].astype(F32)
    dd_ref[0] = down_ref[0].astype(F32)
    half = dk_ref.shape[1]
    dq_ref[...] = dense_ref[0, 0].astype(F32)
    dk_ref[...] = dense_ref[0, 1, :, :half].astype(F32)
    dv_ref[...] = dense_ref[0, 1, :, half:].astype(F32)
    do_ref[...] = dense_ref[0, 2].astype(F32)


def unpack(total, dense, key_width):
    chunks, eff, half = total.shape
    shards, kinds, shard_rows, width = dense.shape
    owned = chunks // 6
    steps = 2 * owned
    piece = lambda kind: pl.BlockSpec((1, eff, half), lambda i: (i // 2 * 6 + 2 * kind + i % 2, 0, 0))
    row = lambda lanes: pl.BlockSpec((shard_rows * shards // steps, lanes), lambda i: (i, 0))
    shape = lambda *dims: jax.ShapeDtypeStruct(dims, F32)
    return pl.pallas_call(
        unpack_kernel,
        grid=(steps,),
        in_specs=[piece(0), piece(1), piece(2), pl.BlockSpec((1, kinds, shard_rows, width), lambda i: (i, 0, 0, 0))],
        out_specs=(
            pl.BlockSpec((1, eff, half), lambda i: (i // 2, i % 2, 0)),
            pl.BlockSpec((1, eff, half), lambda i: (i // 2, i % 2, 0)),
            pl.BlockSpec((1, eff, half), lambda i: (i // 2, 0, i % 2)),
            row(width), row(key_width), row(key_width), row(width),
        ),
        out_shape=(
            shape(owned, width, eff), shape(owned, width, eff), shape(owned, eff, width),
            shape(width, width), shape(width, key_width), shape(width, key_width), shape(width, width),
        ),
        compiler_params=pltpu.CompilerParams(vmem_limit_bytes=48 * MIB),
        name="unpack",
    )(total, total, total, dense)


def per_device(
    fast, block_input, teacher, lengths, routes, w_query, w_key, w_value, w_out, query_gain, key_gain,
    attn_gain, ffn_gain, w_router, w_gate, w_up, w_down,
):
    slots, rows, width = block_input.shape
    expert_total = w_router.shape[1]
    group = lax.axis_size(("context", "experts"))
    here = lax.axis_index(("context", "experts"))
    span = rows * group
    slot_lengths = lax.dynamic_slice_in_dim(lengths, lax.axis_index("dp") * slots, slots)
    scalars = jnp.concatenate([slot_lengths, here[None]]).astype(jnp.int32)
    positions = here * rows + jnp.arange(rows, dtype=jnp.int32)
    valid = (positions[None, :] < slot_lengths[:, None]).astype(F32)[..., None]
    count_all = jnp.sum(lengths).astype(F32)
    positions_all = lengths.shape[0] * span

    half = HEAD // 2
    lanes = jnp.arange(LANES, dtype=jnp.int32)
    inverse = 10000.0 ** (-((lanes % half).astype(F32) * 2.0 / HEAD))
    turned = positions.astype(F32)[:, None] * inverse[None, :]
    cosine = jnp.cos(turned)
    sine = jnp.sin(turned) * jnp.where(lanes % HEAD < half, -1.0, 1.0)[None, :]
    qg = jnp.concatenate([query_gain, query_gain])[None, :]
    kg = jnp.concatenate([key_gain, key_gain])[None, :]
    ag, fg = attn_gain[None, :], ffn_gain[None, :]
    router = jnp.pad(w_router, ((0, 0), (0, LANES - expert_total)))

    if fast:
        scale = (positions_all / count_all)[None]
        (
            h, q, qraw, kraw, kv, mixed, invl, after, soft, tokens, pick, xe, gate_part, up_part, hidden,
            block_output, out_grad, loss_row, unused_grads, dpart, weighted, gate_grad, up_grad,
        ) = front(
            slot_lengths, block_input, teacher, routes, w_query, w_key, w_value, w_out, w_gate, w_up, w_down,
            ag, fg, qg, kg, cosine, sine, router, scale, group, 1,
        )
        total, input_grad, dense, sums = tail(
            slot_lengths, dpart, xe, gate_grad, up_grad, hidden, weighted, q, kv, mixed, invl, soft, out_grad, after,
            qraw, kraw, block_input, h, tokens, w_out, w_query, w_key, w_value, fg, router, cosine, sine, ag, qg, kg,
            loss_row, expert_total, 2,
        )[:4]
        unpacked = unpack(total, dense, w_key.shape[1])
        expert_grads, dense = unpacked[:3], unpacked[3:]
        tops = sums[expert_total : expert_total + 5]
        small = (
            tops[2, :HEAD] + tops[2, HEAD : 2 * HEAD], tops[3, :HEAD] + tops[3, HEAD : 2 * HEAD], tops[0], tops[1],
            sums[:expert_total].T, jnp.sum(tops[4]),
        )
    else:
        h, q, kv_local, qraw, kraw = project(block_input, ag, w_query, w_key, w_value, qg, kg, cosine, sine)
        kv = plane_gather(kv_local)
        mixed, invl, after, xg, soft = attend(scalars, q, kv, block_input, w_out, fg, router, routes)
        tokens = plane_gather(xg)
        pick, xe, gate_part, up_part, hidden, part = experts_forward(scalars, tokens, w_gate, w_up, w_down)
        output = after + plane_scatter(part)
        difference = valid * (output - teacher.astype(F32))
        loss_part = jnp.sum(difference * difference)
        out_grad = difference * (positions_all / count_all)
        grads = plane_gather(out_grad.astype(BF16))
        dpart, weighted, gate_grad, up_grad = experts_backward(
            scalars, grads, tokens, pick, gate_part, up_part, hidden, w_gate, w_up, w_down
        )
        expert_grads = lax.psum(expert_weights(xe, gate_grad, up_grad, hidden, weighted), "dp")
        dx = plane_scatter(dpart)
        dq, dkv_parts, after_grad, attn_grad, logit_grad, ffn_gain_grad = attend_backward(
            scalars, q, kv, mixed, invl, dx, soft, out_grad, after, fg, router, w_out
        )
        dkv = plane_scatter(dkv_parts)
        input_grad, dense, router_grad, query_gg, key_gg, attn_gg = finish(
            dq, dkv, qraw, kraw, block_input, after_grad, cosine, sine, ag, qg, kg,
            w_query, w_key, w_value, h, mixed, attn_grad, xg, logit_grad,
        )
        dense = lax.psum(dense, ("dp", "context", "experts"))
        dense = [dense[:, k].reshape(width, width).astype(F32) for k in range(3)]
        small = lax.psum(
            (
                query_gg[0, :HEAD] + query_gg[0, HEAD:], key_gg[0, :HEAD] + key_gg[0, HEAD:], attn_gg[0],
                ffn_gain_grad[0], router_grad[:, :expert_total], loss_part,
            ),
            ("dp", "context", "experts"),
        )
        key_width = w_key.shape[1]
        expert_grads = [grad.astype(F32) for grad in expert_grads]
        dense = [dense[0], dense[1][:, :key_width], dense[1][:, key_width:], dense[2]]
        block_output = output.astype(BF16)
    return (
        small[5] / (count_all * width), block_output, input_grad, dense[0], dense[1], dense[2], dense[3],
        small[0], small[1], small[2], small[3], small[4], expert_grads[0], expert_grads[1], expert_grads[2],
    )


def solution(mesh):
    fast = mesh.shape["context"] == 4 and mesh.shape["experts"] == 2
    rows = P("dp", ("context", "experts"), None)
    owned = P(("context", "experts"), None, None)
    return jax.shard_map(
        functools.partial(per_device, fast),
        mesh=mesh,
        in_specs=(rows, rows, P(), rows) + (P(),) * 9 + (owned,) * 3,
        out_specs=(P(), rows, rows) + (P(),) * 9 + (owned,) * 3,
        check_vma=False,
    )
```

```python
import functools
import math

import jax
import jax.numpy as jnp
from jax import lax
from jax.experimental import pallas as pl
from jax.experimental.pallas import tpu as pltpu
from jax.sharding import PartitionSpec as P

EPSILON = 1e-06
MOST = 40
PAIR = 2 * MOST
LANES = 128
HEAD = 64
SCALE = 0.125
EXP2_SCALE = 0.125 * math.log2(math.e)
MIB = 2**20
MESH = pl.DeviceIdType.MESH
F32 = jnp.float32
BF16 = jnp.bfloat16


def dot(a, b):
    return lax.dot_general(a, b, (((1,), (0,)), ((), ())), preferred_element_type=F32)


def dot_nt(a, b):
    return lax.dot_general(a, b, (((1,), (1,)), ((), ())), preferred_element_type=F32)


def dot_tn(a, b):
    return lax.dot_general(a, b, (((0,), (0,)), ((), ())), preferred_element_type=F32)


def lane_of(shape):
    return lax.broadcasted_iota(jnp.int32, shape, len(shape) - 1)


def row_of(shape):
    return lax.broadcasted_iota(jnp.int32, shape, len(shape) - 2)


def swap_halves(tile):
    low = lax.rem(lane_of(tile.shape), HEAD) < HEAD // 2
    return jnp.where(low, pltpu.roll(tile, LANES - HEAD // 2, 1), pltpu.roll(tile, HEAD // 2, 1))


def head_mean(tile):
    low = lane_of(tile.shape) < HEAD
    first = jnp.sum(jnp.where(low, tile, 0.0), axis=-1, keepdims=True)
    second = jnp.sum(jnp.where(low, 0.0, tile), axis=-1, keepdims=True)
    return jnp.where(low, first, second) * (1.0 / HEAD)


def rope_forward(raw, gain, cosine, sine):
    normed = raw * lax.rsqrt(head_mean(raw * raw) + EPSILON) * gain
    return normed * cosine + swap_halves(normed) * sine


def rope_backward(grad, raw, gain, cosine, sine):
    inverse = lax.rsqrt(head_mean(raw * raw) + EPSILON)
    unit = raw * inverse
    normed_grad = grad * cosine - swap_halves(grad) * sine
    gain_grad = jnp.sum(normed_grad * unit, axis=0, keepdims=True)
    unit_grad = normed_grad * gain
    return inverse * (unit_grad - unit * head_mean(unit_grad * unit)), gain_grad


def rms_parts(rows):
    inverse = lax.rsqrt(jnp.mean(rows * rows, axis=-1, keepdims=True) + EPSILON)
    return rows * inverse, inverse


def rms_backward(grad, rows, gain):
    unit, inverse = rms_parts(rows)
    gain_grad = jnp.sum(grad * unit, axis=0, keepdims=True)
    unit_grad = grad * gain
    back = inverse * (unit_grad - unit * jnp.mean(unit_grad * unit, axis=-1, keepdims=True))
    return back, gain_grad


def stack_heads(tile, masked):
    first, second = tile[:, :LANES].astype(F32), tile[:, LANES:].astype(F32)
    parts = [first, pltpu.roll(first, HEAD, 1), pltpu.roll(second, HEAD, 1), second]
    if masked:
        low = lane_of(first.shape) < HEAD
        parts = [jnp.where(low, part, 0.0) for part in parts[:2]] + [
            jnp.where(low, 0.0, part) for part in parts[2:]
        ]
    return jnp.concatenate(parts, axis=0)


def unstack_heads(rows):
    count = rows.shape[0] // 4
    one, two, three, four = (rows[k * count : (k + 1) * count] for k in range(4))
    low = lane_of(one.shape) < HEAD
    return jnp.concatenate(
        [
            jnp.where(low, one, pltpu.roll(two, HEAD, 1)),
            jnp.where(low, pltpu.roll(three, HEAD, 1), four),
        ],
        axis=1,
    )


def project_kernel(
    x_ref, gain_ref, wq_ref, wk_ref, wv_ref, qg_ref, kg_ref, cos_ref, sin_ref,
    h_ref, q_ref, kv_ref, qraw_ref, kraw_ref,
):
    slots, rows, width = x_ref.shape
    x = x_ref[...].astype(F32).reshape(slots * rows, width)
    unit, unused = rms_parts(x)
    normed = (unit * gain_ref[...]).astype(BF16)
    h_ref[...] = normed.reshape(slots, rows, width)
    cosine = jnp.concatenate([cos_ref[...]] * slots, axis=0)
    sine = jnp.concatenate([sin_ref[...]] * slots, axis=0)
    q_raw = dot(normed, wq_ref[...])
    qraw_ref[...] = q_raw.reshape(qraw_ref.shape)
    for tile in range(q_raw.shape[1] // LANES):
        lanes = slice(tile * LANES, (tile + 1) * LANES)
        turned = rope_forward(q_raw[:, lanes], qg_ref[...], cosine, sine)
        q_ref[:, :, lanes] = turned.astype(BF16).reshape(slots, rows, LANES)
    k_raw = dot(normed, wk_ref[...])
    kraw_ref[...] = k_raw.reshape(kraw_ref.shape)
    value = dot(normed, wv_ref[...]).astype(BF16)
    for tile in range(k_raw.shape[1] // LANES):
        lanes = slice(tile * LANES, (tile + 1) * LANES)
        turned = rope_forward(k_raw[:, lanes], kg_ref[...], cosine, sine)
        at = 2 * tile * LANES
        kv_ref[:, :, at : at + LANES] = turned.astype(BF16).reshape(slots, rows, LANES)
        kv_ref[:, :, at + LANES : at + 2 * LANES] = value[:, lanes].reshape(slots, rows, LANES)


def project(x, attn_gain, w_query, w_key, w_value, qg, kg, cosine, sine):
    slots, rows, width = x.shape
    step = 2
    block = lambda lanes: pl.BlockSpec((step, rows, lanes), lambda i: (i, 0, 0))
    whole = lambda a: pl.BlockSpec(a.shape, lambda i: (0,) * a.ndim)
    qw, kw = w_query.shape[1], w_key.shape[1]
    return pl.pallas_call(
        project_kernel,
        grid=(slots // step,),
        out_shape=(
            jax.ShapeDtypeStruct((slots, rows, width), BF16),
            jax.ShapeDtypeStruct((slots, rows, qw), BF16),
            jax.ShapeDtypeStruct((slots, rows, 2 * kw), BF16),
            jax.ShapeDtypeStruct((slots, rows, qw), F32),
            jax.ShapeDtypeStruct((slots, rows, kw), F32),
        ),
        in_specs=[block(width)] + [whole(a) for a in (attn_gain, w_query, w_key, w_value, qg, kg, cosine, sine)],
        out_specs=(block(width), block(qw), block(2 * kw), block(qw), block(kw)),
        compiler_params=pltpu.CompilerParams(vmem_limit_bytes=56 * MIB),
        name="project",
    )(x, attn_gain, w_query, w_key, w_value, qg, kg, cosine, sine)


def attend_kernel(
    sc_ref, q_ref, kv_ref, x_ref, wo_ref, fg_ref, wr_ref, routes_ref,
    mixed_ref, invl_ref, after_ref, xg_ref, soft_ref, acc,
):
    slot, tile = pl.program_id(0), pl.program_id(1)
    slots, tiles = pl.num_programs(0), pl.num_programs(1)
    rows = q_ref.shape[1]
    here = sc_ref[slots]
    length = sc_ref[slot]
    live = here * rows < length
    chunk = 2 * rows
    chunks = (here + 2) // 2

    @pl.when(tile == 0)
    def _():
        acc[...] = jnp.zeros_like(acc)

    @pl.when(live)
    def _():
        q4 = stack_heads(q_ref[0], True).astype(BF16)

        def step(index, carry, masked):
            mass, total = carry
            pair = kv_ref[pl.ds(2 * index, 2), 0]
            keys = pair[:, :, :LANES].reshape(chunk, LANES)
            values = pair[:, :, LANES:].reshape(chunk, LANES)
            weight = jnp.exp2(dot_nt(q4, keys) * EXP2_SCALE)
            if masked:
                at = lax.rem(row_of(weight.shape), rows) + here * rows
                weight = jnp.where(lane_of(weight.shape) + index * chunk <= at, weight, 0.0)
            for part in range(chunk // LANES):
                mass = mass + weight[:, part * LANES : (part + 1) * LANES]
            return mass, total + dot(weight.astype(BF16), values)

        blank = jnp.zeros((4 * rows, LANES), F32)
        carry = lax.fori_loop(0, chunks - 1, lambda i, c: step(i, c, False), (blank, blank))
        mass, total = step(chunks - 1, carry, True)
        inverse = 1.0 / jnp.sum(mass, axis=-1, keepdims=True)
        mixed = unstack_heads(total * inverse).astype(BF16)
        mixed_ref[0] = mixed
        invl_ref[0] = unstack_heads(jnp.broadcast_to(inverse, total.shape))
        acc[...] += dot(mixed, wo_ref[...])

    @pl.when(jnp.logical_not(live))
    def _():
        mixed_ref[...] = jnp.zeros_like(mixed_ref)
        invl_ref[...] = jnp.zeros_like(invl_ref)

    @pl.when(tile == tiles - 1)
    def _():
        width = x_ref.shape[2]
        valid = (row_of((rows, 1)) + here * rows < length).astype(F32)
        after = x_ref[0].astype(F32) + valid * acc[...]
        after_ref[0] = after
        unit, unused = rms_parts(after)
        normed = (unit * fg_ref[...]).astype(BF16)
        xg_ref[0, :, :width] = normed
        logits = dot(normed, wr_ref[...])
        lanes = lane_of(logits.shape)
        routes = routes_ref[0]
        chosen = lanes == routes[:, 0:1]
        for k in range(1, routes.shape[1]):
            chosen = chosen | (lanes == routes[:, k : k + 1])
        top = jnp.max(jnp.where(chosen, logits, -1e30), axis=-1, keepdims=True)
        weight = jnp.where(chosen, jnp.exp(jnp.minimum(logits - top, 0.0)), 0.0)
        soft = weight / jnp.sum(weight, axis=-1, keepdims=True)
        soft_ref[0] = soft
        gates = soft * valid
        high = gates.astype(BF16).astype(F32)
        half = logits.shape[1] // 2
        xg_ref[0, :, width:] = (high + pltpu.roll(gates - high, half, 1)).astype(BF16)


def attend(scalars, q, kv, x, w_out, ffn_gain, router, routes):
    slots, rows, width = x.shape
    group = kv.shape[0]
    qw = q.shape[2]
    tiles = qw // 256
    row = lambda lanes: pl.BlockSpec((1, rows, lanes), lambda s, b, sc: (s, 0, 0))
    tile = pl.BlockSpec((1, rows, 256), lambda s, b, sc: (s, 0, b))
    return pl.pallas_call(
        attend_kernel,
        grid_spec=pltpu.PrefetchScalarGridSpec(
            num_scalar_prefetch=1,
            grid=(slots, tiles),
            in_specs=[
                tile,
                pl.BlockSpec((group, 1, rows, 256), lambda s, b, sc: (0, s, 0, b)),
                row(width),
                pl.BlockSpec((256, width), lambda s, b, sc: (b, 0)),
                pl.BlockSpec(ffn_gain.shape, lambda s, b, sc: (0, 0)),
                pl.BlockSpec(router.shape, lambda s, b, sc: (0, 0)),
                row(routes.shape[2]),
            ],
            out_specs=(tile, tile, row(width), row(width + LANES), row(LANES)),
            scratch_shapes=[pltpu.VMEM((rows, width), F32)],
        ),
        out_shape=(
            jax.ShapeDtypeStruct((slots, rows, qw), BF16),
            jax.ShapeDtypeStruct((slots, rows, qw), F32),
            jax.ShapeDtypeStruct((slots, rows, width), F32),
            jax.ShapeDtypeStruct((slots, rows, width + LANES), BF16),
            jax.ShapeDtypeStruct((slots, rows, LANES), F32),
        ),
        compiler_params=pltpu.CompilerParams(vmem_limit_bytes=56 * MIB),
        name="attend",
    )(scalars, q, kv, x, w_out, ffn_gain, router, routes)


def row_gates(picked, first, owned):
    lanes = lane_of(picked.shape)
    expert = row_of(picked.shape) // PAIR + first
    half = picked.shape[1] // 2
    mine = (lanes == expert) | (lanes == expert + half)
    return jnp.sum(jnp.where(mine, picked, 0.0), axis=-1, keepdims=True)


def experts_forward_kernel(
    sc_ref, xg_ref, wg_ref, wu_ref, wd_ref, pick_ref, xe_ref, gp_ref, up_ref, hid_ref, part_ref, gates, ybuf
):
    sources, unused, rows, wide = xg_ref.shape
    owned, width, eff = wg_ref.shape
    pairs = sources // 2
    double = 2 * rows
    first = sc_ref[pl.num_programs(0)] * owned
    tokens = xg_ref[...].reshape(sources * rows, wide)
    slab = tokens[:, width:]
    chosen = (lane_of((8, LANES)) == row_of((8, LANES)) + first).astype(BF16)
    routed = dot_nt(chosen, slab) > 0.0
    before = row_of((double, double))
    after = lane_of((double, double))
    count = ((before < after) & (before // rows == after // rows)).astype(BF16)
    place = lax.broadcasted_iota(jnp.int32, (PAIR, double), 0)
    offset = (lane_of((8, double)) // rows) * MOST
    for p in range(pairs):
        mask = routed[:, p * double : (p + 1) * double]
        rank = dot(mask.astype(F32).astype(BF16), count).astype(jnp.int32) + offset
        rank = jnp.where(mask, rank, -1)
        pick = jnp.concatenate(
            [(place == rank[e : e + 1, :]).astype(F32).astype(BF16) for e in range(owned)], axis=0
        )
        pick_ref[0, p] = pick
        block = tokens[p * double : (p + 1) * double]
        picked = dot(pick, block[:, :width]).astype(BF16)
        scale = row_gates(dot(pick, block[:, width:]), first, owned)
        for e in range(owned):
            xe_ref[0, e, p * PAIR : (p + 1) * PAIR] = picked[e * PAIR : (e + 1) * PAIR]
            gates[e, p * PAIR : (p + 1) * PAIR] = jnp.broadcast_to(
                scale[e * PAIR : (e + 1) * PAIR], (PAIR, LANES)
            )

    def one(e, carry):
        rows_in = xe_ref[0, e]
        gate_part = dot(rows_in, wg_ref[e])
        up_part = dot(rows_in, wu_ref[e])
        gp_ref[0, e] = gate_part
        up_ref[0, e] = up_part
        hidden = (gate_part * jax.nn.sigmoid(gate_part) * up_part).astype(BF16)
        hid_ref[0, e] = hidden
        result = (dot(hidden, wd_ref[e]) * gates[e][:, 0:1]).astype(BF16)
        for p in range(pairs):
            ybuf[p, e] = result[p * PAIR : (p + 1) * PAIR]
        return carry

    lax.fori_loop(0, owned, one, 0)
    for p in range(pairs):
        back = dot_tn(pick_ref[0, p], ybuf[p].reshape(owned * PAIR, width))
        part_ref[2 * p : 2 * p + 2, 0] = back.astype(BF16).reshape(2, rows, width)


def step_spec(shape):
    return pl.BlockSpec((1,) + shape, lambda s, j, sc: (s * pl.num_programs(1) + j,) + (0,) * len(shape))


def resident(array):
    return pl.BlockSpec(array.shape, lambda s, j, sc: (0,) * array.ndim, pipeline_mode=pl.Buffered(1))


def experts_forward(scalars, tokens, w_gate, w_up, w_down):
    group, slots, rows, wide = tokens.shape
    owned, width, eff = w_gate.shape
    sources = 8
    parts = group // sources
    pairs = sources // 2
    steps = slots * parts
    held = pairs * PAIR
    source = lambda lanes: pl.BlockSpec((sources, 1, rows, lanes), lambda s, j, sc: (j, s, 0, 0))
    saved = [
        ((pairs, owned * PAIR, 2 * rows), BF16),
        ((owned, held, width), BF16),
        ((owned, held, eff), F32),
        ((owned, held, eff), F32),
        ((owned, held, eff), BF16),
    ]
    return pl.pallas_call(
        experts_forward_kernel,
        grid_spec=pltpu.PrefetchScalarGridSpec(
            num_scalar_prefetch=1,
            grid=(slots, parts),
            in_specs=[source(wide), resident(w_gate), resident(w_up), resident(w_down)],
            out_specs=tuple(step_spec(shape) for shape, unused in saved) + (source(width),),
            scratch_shapes=[
                pltpu.VMEM((owned, held, LANES), F32),
                pltpu.VMEM((pairs, owned, PAIR, width), BF16),
            ],
        ),
        out_shape=tuple(jax.ShapeDtypeStruct((steps,) + shape, kind) for shape, kind in saved)
        + (jax.ShapeDtypeStruct((group, slots, rows, width), BF16),),
        compiler_params=pltpu.CompilerParams(vmem_limit_bytes=60 * MIB),
        name="experts_forward",
    )(scalars, tokens, w_gate, w_up, w_down)


def experts_backward_kernel(
    sc_ref, dy_ref, slab_ref, pick_ref, gp_ref, up_ref, hid_ref, wg_ref, wu_ref, wd_ref,
    part_ref, dyw_ref, gg_ref, ug_ref, gates, dye, dxb,
):
    sources, unused, rows, width = dy_ref.shape
    owned = wg_ref.shape[0]
    pairs = sources // 2
    double = 2 * rows
    first = sc_ref[pl.num_programs(0)] * owned
    for p in range(pairs):
        pick = pick_ref[0, p]
        picked = dot(pick, dy_ref[2 * p : 2 * p + 2].reshape(double, width)).astype(BF16)
        scale = row_gates(dot(pick, slab_ref[2 * p : 2 * p + 2].reshape(double, LANES)), first, owned)
        for e in range(owned):
            dye[e, p * PAIR : (p + 1) * PAIR] = picked[e * PAIR : (e + 1) * PAIR]
            gates[e, p * PAIR : (p + 1) * PAIR] = jnp.broadcast_to(
                scale[e * PAIR : (e + 1) * PAIR], (PAIR, LANES)
            )

    def one(e, carry):
        grad_rows = dye[e]
        scale = gates[e][:, 0:1]
        plain = dot_nt(grad_rows, wd_ref[e])
        gate_part, up_part = gp_ref[0, e], up_ref[0, e]
        soft_grad = jnp.sum(plain * hid_ref[0, e].astype(F32), axis=-1, keepdims=True)
        hidden_grad = plain * scale
        sigma = jax.nn.sigmoid(gate_part)
        gate_grad = (hidden_grad * up_part * sigma * (1.0 + gate_part * (1.0 - sigma))).astype(BF16)
        up_grad = (hidden_grad * gate_part * sigma).astype(BF16)
        gg_ref[0, e] = gate_grad
        ug_ref[0, e] = up_grad
        dyw_ref[0, e] = (grad_rows.astype(F32) * scale).astype(BF16)
        input_grad = (dot_nt(gate_grad, wg_ref[e]) + dot_nt(up_grad, wu_ref[e])).astype(BF16)
        lanes = lane_of((pairs * PAIR, LANES))
        high = soft_grad.astype(BF16).astype(F32)
        spot = jnp.where(
            lanes == first + e, high, jnp.where(lanes == first + e + LANES // 2, soft_grad - high, 0.0)
        ).astype(BF16)
        for p in range(pairs):
            dxb[p, e, :, :width] = input_grad[p * PAIR : (p + 1) * PAIR]
            dxb[p, e, :, width:] = spot[p * PAIR : (p + 1) * PAIR]
        return carry

    lax.fori_loop(0, owned, one, 0)
    for p in range(pairs):
        back = dot_tn(pick_ref[0, p], dxb[p].reshape(owned * PAIR, width + LANES))
        part_ref[2 * p : 2 * p + 2, 0] = back.astype(BF16).reshape(2, rows, width + LANES)


def experts_backward(scalars, grads, tokens, pick, gate_part, up_part, hidden, w_gate, w_up, w_down):
    group, slots, rows, width = grads.shape
    owned, unused, eff = w_gate.shape
    sources = 8
    parts = group // sources
    pairs = sources // 2
    steps = slots * parts
    held = pairs * PAIR
    source = lambda lanes, at: pl.BlockSpec((sources, 1, rows, lanes), lambda s, j, sc: (j, s, 0, at))
    return pl.pallas_call(
        experts_backward_kernel,
        grid_spec=pltpu.PrefetchScalarGridSpec(
            num_scalar_prefetch=1,
            grid=(slots, parts),
            in_specs=[
                source(width, 0),
                source(LANES, width // LANES),
                step_spec((pairs, owned * PAIR, 2 * rows)),
                step_spec((owned, held, eff)),
                step_spec((owned, held, eff)),
                step_spec((owned, held, eff)),
                resident(w_gate), resident(w_up), resident(w_down),
            ],
            out_specs=(
                source(width + LANES, 0),
                step_spec((owned, held, width)),
                step_spec((owned, held, eff)),
                step_spec((owned, held, eff)),
            ),
            scratch_shapes=[
                pltpu.VMEM((owned, held, LANES), F32),
                pltpu.VMEM((owned, held, width), BF16),
                pltpu.VMEM((pairs, owned, PAIR, width + LANES), BF16),
            ],
        ),
        out_shape=(
            jax.ShapeDtypeStruct((group, slots, rows, width + LANES), BF16),
            jax.ShapeDtypeStruct((steps, owned, held, width), BF16),
            jax.ShapeDtypeStruct((steps, owned, held, eff), BF16),
            jax.ShapeDtypeStruct((steps, owned, held, eff), BF16),
        ),
        compiler_params=pltpu.CompilerParams(vmem_limit_bytes=62 * MIB),
        name="experts_backward",
    )(scalars, grads, tokens, pick, gate_part, up_part, hidden, w_gate, w_up, w_down)


def expert_weights_kernel(xe_ref, gg_ref, ug_ref, hid_ref, dyw_ref, dg_ref, du_ref, dd_ref, ag, au, ad):
    step = pl.program_id(1)
    flat = lambda ref: ref[:, 0].reshape(ref.shape[0] * ref.shape[2], ref.shape[3])
    for acc, left, right in ((ad, hid_ref, dyw_ref), (ag, xe_ref, gg_ref), (au, xe_ref, ug_ref)):
        part = dot_tn(flat(left), flat(right))

        @pl.when(step == 0)
        def _():
            acc[...] = part

        @pl.when(step > 0)
        def _():
            acc[...] += part

    @pl.when(step == pl.num_programs(1) - 1)
    def _():
        dg_ref[0] = ag[...].astype(BF16)
        du_ref[0] = au[...].astype(BF16)
        dd_ref[0] = ad[...].astype(BF16)


def expert_weights(xe, gate_grad, up_grad, hidden, weighted):
    steps, owned, held, width = xe.shape
    eff = hidden.shape[3]
    each = 4
    block = lambda lanes: pl.BlockSpec((each, 1, held, lanes), lambda e, i: (i, e, 0, 0))
    out = lambda a, b: pl.BlockSpec((1, a, b), lambda e, i: (e, 0, 0))
    return pl.pallas_call(
        expert_weights_kernel,
        grid=(owned, steps // each),
        in_specs=[block(width), block(eff), block(eff), block(eff), block(width)],
        out_specs=(out(width, eff), out(width, eff), out(eff, width)),
        out_shape=(
            jax.ShapeDtypeStruct((owned, width, eff), BF16),
            jax.ShapeDtypeStruct((owned, width, eff), BF16),
            jax.ShapeDtypeStruct((owned, eff, width), BF16),
        ),
        scratch_shapes=[pltpu.VMEM((width, eff), F32), pltpu.VMEM((width, eff), F32), pltpu.VMEM((eff, width), F32)],
        compiler_params=pltpu.CompilerParams(vmem_limit_bytes=56 * MIB),
        name="expert_weights",
    )(xe, gate_grad, up_grad, hidden, weighted)


def attend_backward_kernel(
    sc_ref, q_ref, kv_ref, mixed_ref, invl_ref, dx_ref, soft_ref, og_ref, after_ref, fg_ref, wr_ref, wo_ref,
    dq_ref, dkv_ref, ag_ref, at_ref, lg_ref, fgg_ref, mg_s,
):
    slot, tile = pl.program_id(0), pl.program_id(1)
    slots, tiles = pl.num_programs(0), pl.num_programs(1)
    rows = q_ref.shape[1]
    here = sc_ref[slots]
    length = sc_ref[slot]
    live = here * rows < length
    chunk = 2 * rows
    chunks = (here + 2) // 2
    width = og_ref.shape[2]

    @pl.when(tile == 0)
    def _():
        valid = (row_of((rows, 1)) + here * rows < length).astype(F32)
        slab = dx_ref[0, :, width:].astype(F32)
        half = slab.shape[1] // 2
        soft = soft_ref[0]
        soft_grad = jnp.where(lane_of(slab.shape) < half, slab + pltpu.roll(slab, half, 1), 0.0)
        chosen = soft * (soft_grad - jnp.sum(soft * soft_grad, axis=-1, keepdims=True))
        logit_grad = chosen.astype(BF16)
        lg_ref[0] = logit_grad
        normed_grad = dx_ref[0, :, :width].astype(F32) + dot_nt(logit_grad, wr_ref[...])
        back, gain_grad = rms_backward(normed_grad, after_ref[0], fg_ref[...])

        @pl.when(slot == 0)
        def _():
            fgg_ref[...] = gain_grad

        @pl.when(slot > 0)
        def _():
            fgg_ref[...] += gain_grad

        after_grad = og_ref[0] + back
        ag_ref[0] = after_grad
        attn_grad = (valid * after_grad).astype(BF16)
        at_ref[0] = attn_grad
        mixed_grad = dot_nt(attn_grad, wo_ref[...]).astype(BF16)
        for t in range(mg_s.shape[0]):
            mg_s[t] = mixed_grad[:, t * 256 : (t + 1) * 256]

    dkv_ref[...] = jnp.zeros_like(dkv_ref)

    @pl.when(live)
    def _():
        q4 = stack_heads(q_ref[0], True).astype(BF16)
        do4_f = stack_heads(mg_s[tile].astype(F32) * invl_ref[0], True)
        do4 = do4_f.astype(BF16)
        product = do4_f * stack_heads(mixed_ref[0], False)
        delta = lax.dot_general(
            jnp.ones((8, LANES), F32), product, (((1,), (1,)), ((), ())),
            preferred_element_type=F32, precision=lax.Precision.HIGHEST,
        )[0:1]

        def step(index, total, masked):
            pair = kv_ref[pl.ds(2 * index, 2), 0]
            keys = pair[:, :, :LANES].reshape(chunk, LANES)
            values = pair[:, :, LANES:].reshape(chunk, LANES)
            weight = jnp.exp2(dot_nt(keys, q4) * EXP2_SCALE)
            if masked:
                at = lax.rem(lane_of(weight.shape), rows) + here * rows
                weight = jnp.where(row_of(weight.shape) + index * chunk <= at, weight, 0.0)
            pressure = dot_nt(values, do4)
            score_grad = (weight * (pressure - delta) * SCALE).astype(BF16)
            key_grad = dot(score_grad, q4)
            value_grad = dot(weight.astype(BF16), do4)
            dkv_ref[pl.ds(2 * index, 2), 0, :, :LANES] = key_grad.astype(BF16).reshape(2, rows, LANES)
            dkv_ref[pl.ds(2 * index, 2), 0, :, LANES:] = value_grad.astype(BF16).reshape(2, rows, LANES)
            return total + dot_tn(score_grad, keys)

        total = lax.fori_loop(
            0, chunks - 1, lambda i, c: step(i, c, False), jnp.zeros((4 * rows, LANES), F32)
        )
        total = step(chunks - 1, total, True)
        dq_ref[0] = unstack_heads(total).astype(BF16)

    @pl.when(jnp.logical_not(live))
    def _():
        dq_ref[...] = jnp.zeros_like(dq_ref)


def attend_backward(scalars, q, kv, mixed, invl, dx, soft, out_grad, after, ffn_gain, router, w_out):
    slots, rows, width = out_grad.shape
    group = kv.shape[0]
    qw = q.shape[2]
    tiles = qw // 256
    row = lambda lanes: pl.BlockSpec((1, rows, lanes), lambda s, b, sc: (s, 0, 0))
    tile = pl.BlockSpec((1, rows, 256), lambda s, b, sc: (s, 0, b))
    group_tile = pl.BlockSpec((group, 1, rows, 256), lambda s, b, sc: (0, s, 0, b))
    whole = lambda a: pl.BlockSpec(a.shape, lambda s, b, sc: (0, 0))
    return pl.pallas_call(
        attend_backward_kernel,
        grid_spec=pltpu.PrefetchScalarGridSpec(
            num_scalar_prefetch=1,
            grid=(slots, tiles),
            in_specs=[
                tile, group_tile, tile, tile, row(width + LANES), row(LANES), row(width), row(width),
                whole(ffn_gain), whole(router), whole(w_out),
            ],
            out_specs=(
                tile, group_tile, row(width), row(width), row(LANES),
                pl.BlockSpec((1, width), lambda s, b, sc: (0, 0)),
            ),
            scratch_shapes=[pltpu.VMEM((tiles, rows, 256), BF16)],
        ),
        out_shape=(
            jax.ShapeDtypeStruct((slots, rows, qw), BF16),
            jax.ShapeDtypeStruct(kv.shape, BF16),
            jax.ShapeDtypeStruct((slots, rows, width), F32),
            jax.ShapeDtypeStruct((slots, rows, width), BF16),
            jax.ShapeDtypeStruct((slots, rows, LANES), BF16),
            jax.ShapeDtypeStruct((1, width), F32),
        ),
        compiler_params=pltpu.CompilerParams(vmem_limit_bytes=56 * MIB),
        name="attend_backward",
    )(scalars, q, kv, mixed, invl, dx, soft, out_grad, after, ffn_gain, router, w_out)


def finish_kernel(
    dq_ref, dkv_ref, qraw_ref, kraw_ref, x_ref, ag_ref, cos_ref, sin_ref, gain_ref, qg_ref, kg_ref,
    wq_ref, wk_ref, wv_ref, h_ref, mixed_ref, at_ref, n2_ref, lg_ref,
    ig_ref, dense_ref, rt_ref, qgg_ref, kgg_ref, agg_ref, q_s, k_s, v_s,
):
    slot = pl.program_id(0)
    rows = x_ref.shape[1]
    cosine, sine = cos_ref[...], sin_ref[...]

    @pl.when(slot == 0)
    def _():
        qgg_ref[...] = jnp.zeros_like(qgg_ref)
        kgg_ref[...] = jnp.zeros_like(kgg_ref)
        agg_ref[...] = jnp.zeros_like(agg_ref)

    here = pl.ds(pl.multiple_of(slot * rows, rows), rows)
    for t in range(dq_ref.shape[2] // LANES):
        lanes = slice(t * LANES, (t + 1) * LANES)
        raw, gain = rope_backward(dq_ref[0, :, lanes].astype(F32), qraw_ref[0, :, lanes], qg_ref[...], cosine, sine)
        q_s[here, lanes] = raw.astype(BF16)
        qgg_ref[...] += gain
    for t in range(kraw_ref.shape[2] // LANES):
        lanes = slice(t * LANES, (t + 1) * LANES)
        at = 2 * t * LANES
        grad = dkv_ref[0, :, at : at + LANES].astype(BF16).astype(F32)
        raw, gain = rope_backward(grad, kraw_ref[0, :, lanes], kg_ref[...], cosine, sine)
        k_s[here, lanes] = raw.astype(BF16)
        kgg_ref[...] += gain
        v_s[here, lanes] = dkv_ref[0, :, at + LANES : at + 2 * LANES].astype(BF16)
    normed_grad = dot_nt(q_s[here], wq_ref[...]) + dot_nt(k_s[here], wk_ref[...]) + dot_nt(v_s[here], wv_ref[...])
    back, gain = rms_backward(normed_grad, x_ref[0].astype(F32), gain_ref[...])
    agg_ref[...] += gain
    ig_ref[0] = ag_ref[0] + back

    @pl.when(slot == pl.num_programs(0) - 1)
    def _():
        flat = lambda ref: ref[...].reshape(ref.shape[0] * ref.shape[1], ref.shape[2])
        shards, unused, shard_rows, width = dense_ref.shape
        h = flat(h_ref)
        half = width // 2

        def put(index, lanes, value):
            dense_ref[:, index, :, lanes] = value.astype(BF16).reshape(shards, shard_rows, value.shape[1])

        put(0, slice(0, width), dot_tn(h, q_s[...]))
        put(1, slice(0, half), dot_tn(h, k_s[...]))
        put(1, slice(half, width), dot_tn(h, v_s[...]))
        put(2, slice(0, width), dot_tn(flat(mixed_ref), flat(at_ref)))
        rt_ref[...] = dot_tn(flat(n2_ref), flat(lg_ref))


def finish(dq, dkv, qraw, kraw, x, after_grad, cosine, sine, attn_gain, qg, kg, wq, wk, wv, h, mixed, attn_grad, n2, lg):
    slots, rows, width = x.shape
    qw, kw = wq.shape[1], wk.shape[1]
    shards = 8
    row = lambda lanes: pl.BlockSpec((1, rows, lanes), lambda s: (s, 0, 0))
    whole = lambda a: pl.BlockSpec(a.shape, lambda s: (0,) * a.ndim)
    lanes_out = pl.BlockSpec((1, LANES), lambda s: (0, 0))
    return pl.pallas_call(
        finish_kernel,
        grid=(slots,),
        in_specs=[row(qw), row(2 * kw), row(qw), row(kw), row(width), row(width)]
        + [whole(a) for a in (cosine, sine, attn_gain, qg, kg, wq, wk, wv, h, mixed, attn_grad)]
        + [pl.BlockSpec((slots, rows, width), lambda s: (0, 0, 0)), whole(lg)],
        out_specs=(
            row(width),
            pl.BlockSpec((shards, 3, width // shards, width), lambda s: (0, 0, 0, 0)),
            pl.BlockSpec((width, LANES), lambda s: (0, 0)),
            lanes_out, lanes_out, pl.BlockSpec((1, width), lambda s: (0, 0)),
        ),
        out_shape=(
            jax.ShapeDtypeStruct((slots, rows, width), F32),
            jax.ShapeDtypeStruct((shards, 3, width // shards, width), BF16),
            jax.ShapeDtypeStruct((width, LANES), F32),
            jax.ShapeDtypeStruct((1, LANES), F32),
            jax.ShapeDtypeStruct((1, LANES), F32),
            jax.ShapeDtypeStruct((1, width), F32),
        ),
        scratch_shapes=[
            pltpu.VMEM((slots * rows, qw), BF16),
            pltpu.VMEM((slots * rows, kw), BF16),
            pltpu.VMEM((slots * rows, kw), BF16),
        ],
        compiler_params=pltpu.CompilerParams(vmem_limit_bytes=60 * MIB),
        name="finish",
    )(dq, dkv, qraw, kraw, x, after_grad, cosine, sine, attn_gain, qg, kg, wq, wk, wv, h, mixed, attn_grad, n2, lg)


def remote(src, dst, ss, rs, dev):
    return pltpu.make_async_remote_copy(src_ref=src, dst_ref=dst, send_sem=ss, recv_sem=rs, device_id=dev, device_id_type=MESH)


def padded_rows(rows):
    return jnp.concatenate([rows, jnp.zeros((LANES - rows.shape[0], rows.shape[1]), rows.dtype)], axis=0)


class Slots:
    def __init__(self, plane, mine, out, sent, got, local):
        self.plane, self.mine, self.out, self.sent, self.got, self.local = plane, mine, out, sent, got, local
        rows = mine.shape[1]
        self.halves = (pl.ds(0, rows // 2), pl.ds(rows // 2, rows // 2))
        self.at = (plane.own[1], plane.own[2], plane.own[0])

    def own(self, number, s):
        who = (self.plane.xn, self.plane.yn, self.plane.sib)[number]
        return remote(self.mine.at[s], self.out.at[self.plane.me, s], self.sent.at[number, s], self.got.at[number, s], who)

    def keep(self, s):
        return pltpu.make_async_copy(self.mine.at[s], self.out.at[self.plane.me, s], self.local.at[s])

    def pass_on(self, number, s):
        view = self.out.at[self.at[number], s]
        return remote(view, view, self.sent.at[3 + number, s], self.got.at[3 + number, s], self.plane.sib)

    def far(self, number, s):
        at, who = ((self.at[0], self.plane.yn), (self.at[1], self.plane.xn))[number]
        view = self.out.at[at, s, self.halves[number]]
        return remote(view, view, self.sent.at[6 + number, s], self.got.at[6 + number, s], who)

    def start(self, s):
        for number in range(3):
            self.own(number, s).start()
        self.keep(s).start()

    def forward(self, s):
        for number in range(2):
            self.own(number, s).wait_recv()
            self.far(number, s).start()
            self.pass_on(number, s).start()

    def settle(self, s):
        for number in range(2):
            self.far(number, s).wait_recv()
        self.pass_on(2, s).start()

    def arrive(self, s):
        self.keep(s).wait()
        self.own(2, s).wait_recv()
        for number in range(3):
            self.pass_on(number, s).wait_recv()

    def drain(self, s):
        for number in range(3):
            self.own(number, s).wait_send()
            self.pass_on(number, s).wait_send()
        for number in range(2):
            self.far(number, s).wait_send()


def front_kernel(
    sc_ref, x_in, teacher_in, routes_ref, wq_in, wk_in, wv_in, wo_in, wg_in, wu_in, wd_in,
    gain_ref, fg_ref, qg_ref, kg_ref, cos_ref, sin_ref, wr_ref, scale_ref,
    h_out, q_out, qraw_out, kraw_out, kv_out, mixed_out, invl_out, after_out, soft_out, tokens_out,
    pick_out, xe_out, gp_out, up_out, hid_out, y_out, og_out, loss_out, grads_out, dpart_out, dyw_out, gg_out, ug_out,
    sb, da, db, rx, ry, parts, wg, wu, wd, after_s, xg_s, dy_s,
    sent_kv, got_kv, loc_kv, sent_xg, got_xg, loc_xg, sent_dy, got_dy, loc_dy, sent_rs, got_rs, wsem, local,
):
    plane = Plane()
    slots, rows, width = x_in.shape
    group = kv_out.shape[0]
    qw, kw = wq_in.shape[1], wk_in.shape[1]
    tiles = qw // 256
    here = plane.me
    owned = wg_in.shape[0]
    first = here * owned
    wide = xg_s.shape[2]
    each = lambda body, start=0, stop=slots: lax.fori_loop(start, stop, lambda s, c: (body(s), c)[1], 0)
    row_gather = Slots(plane, xg_s, tokens_out, sent_xg, got_xg, loc_xg)
    grad_gather = Slots(plane, dy_s, grads_out, sent_dy, got_dy, loc_dy)
    scatter = Scatter(
        plane, lambda k, s: parts.at[plane.own[k], s], lambda k, s: parts.at[plane.other[k], s],
        (sb, da, db, rx, ry), (sent_rs, got_rs),
    )
    expert_loads = [
        pltpu.make_async_copy(source, there, wsem.at[n])
        for n, (source, there) in enumerate(((wg_in, wg), (wu_in, wu), (wd_in, wd)))
    ]

    def first_phase(wq, wk, wv, wo, xb, kvl, q_s, h_s, qraw_s, kraw_s, kvb, mixed_s, invl_s, soft_s, acc, sems, out_sems):
        loads = [
            pltpu.make_async_copy(source, there, sems.at[n])
            for n, (source, there) in enumerate(((x_in, xb), (wk_in, wk), (wv_in, wv), (wq_in, wq), (wo_in, wo)))
        ]
        for copy in loads:
            copy.start()
        for copy in expert_loads:
            copy.start()
        kv_gather = Slots(plane, kvl, kv_out, sent_kv, got_kv, loc_kv)
        plane.barrier(False)
        for copy in loads[:4]:
            copy.wait()

        def project_two(s):
            two = pl.ds(s, 2)
            x = xb[two].astype(F32).reshape(2 * rows, width)
            unit, unused = rms_parts(x)
            normed = (unit * gain_ref[...]).astype(BF16)
            h_s[two] = normed.reshape(2, rows, width)
            cosine = jnp.concatenate([cos_ref[...]] * 2, axis=0)
            sine = jnp.concatenate([sin_ref[...]] * 2, axis=0)
            k_raw = dot(normed, wk[...])
            kraw_s[two] = k_raw.reshape(2, rows, kw)
            value = dot(normed, wv[...]).astype(BF16)
            for tile in range(kw // LANES):
                lanes = slice(tile * LANES, (tile + 1) * LANES)
                turned = rope_forward(k_raw[:, lanes], kg_ref[...], cosine, sine)
                at = 2 * tile * LANES
                kvl[two, :, at : at + LANES] = turned.astype(BF16).reshape(2, rows, LANES)
                kvl[two, :, at + LANES : at + 2 * LANES] = value[:, lanes].reshape(2, rows, LANES)

            @pl.when(s == 0)
            def _():
                kv_gather.start(0)
                kv_gather.start(1)

            q_raw = dot(normed, wq[...])
            qraw_s[two] = q_raw.reshape(2, rows, qw)
            for tile in range(qw // LANES):
                lanes = slice(tile * LANES, (tile + 1) * LANES)
                turned = rope_forward(q_raw[:, lanes], qg_ref[...], cosine, sine)
                q_s[two, :, lanes] = turned.astype(BF16).reshape(2, rows, LANES)

        lax.fori_loop(0, slots // 2, lambda n, c: (project_two(2 * n), c)[1], 0)
        keeps = [
            pltpu.make_async_copy(source, there, out_sems.at[n])
            for n, (source, there) in enumerate(((h_s, h_out), (q_s, q_out), (qraw_s, qraw_out), (kraw_s, kraw_out)))
        ]
        for copy in keeps:
            copy.start()
        kv_gather.forward(0)
        kv_gather.start(2)
        kv_gather.forward(1)
        kv_gather.settle(0)
        kv_gather.start(3)
        loads[4].wait()

        def attend_slot(s):
            load = pltpu.make_async_copy(kv_out.at[:, s], kvb, sems.at[5])
            load.start()
            load.wait()
            chunk = 2 * rows
            chunks = (here + 2) // 2
            acc[...] = jnp.zeros_like(acc)

            def one_tile(t, carry):
                lanes = pl.ds(pl.multiple_of(t * 256, 256), 256)
                key_lanes = pl.ds(pl.multiple_of(t * 256, 256), LANES)
                value_lanes = pl.ds(pl.multiple_of(t * 256 + LANES, LANES), LANES)
                q4 = stack_heads(q_s[s, :, lanes], True).astype(BF16)

                def step(index, carry, masked):
                    mass, total = carry
                    two = pl.ds(2 * index, 2)
                    keys = kvb[two, :, key_lanes].reshape(chunk, LANES)
                    values = kvb[two, :, value_lanes].reshape(chunk, LANES)
                    weight = jnp.exp2(dot_nt(q4, keys) * EXP2_SCALE)
                    if masked:
                        at = lax.rem(row_of(weight.shape), rows) + here * rows
                        weight = jnp.where(lane_of(weight.shape) + index * chunk <= at, weight, 0.0)
                    for part in range(chunk // LANES):
                        mass = mass + weight[:, part * LANES : (part + 1) * LANES]
                    return mass, total + dot(weight.astype(BF16), values)

                blank = jnp.zeros((4 * rows, LANES), F32)
                state = lax.fori_loop(0, chunks - 1, lambda i, c: step(i, c, False), (blank, blank))
                mass, total = step(chunks - 1, state, True)
                inverse = 1.0 / jnp.sum(mass, axis=-1, keepdims=True)
                mixed = unstack_heads(total * inverse).astype(BF16)
                mixed_s[s, :, lanes] = mixed
                invl_s[s, :, lanes] = unstack_heads(jnp.broadcast_to(inverse, total.shape))
                acc[...] += dot(mixed, wo[pl.ds(pl.multiple_of(t * 256, 256), 256)])
                return carry

            lax.fori_loop(0, tiles, one_tile, 0)
            valid = (row_of((rows, 1)) + here * rows < sc_ref[s]).astype(F32)
            after = xb[s].astype(F32) + valid * acc[...]
            after_s[s] = after
            unit, unused = rms_parts(after)
            normed = (unit * fg_ref[...]).astype(BF16)
            xg_s[s, :, :width] = normed
            logits = dot_nt(normed, padded_rows(wr_ref[...]))
            lanes = lane_of(logits.shape)
            routes = routes_ref[s].astype(F32).T
            number = lanes.astype(F32)
            chosen = number == routes[:, 0:1]
            for k in range(1, routes.shape[1]):
                chosen = chosen | (number == routes[:, k : k + 1])
            top = jnp.max(jnp.where(chosen, logits, -1e30), axis=-1, keepdims=True)
            weight = jnp.where(chosen, jnp.exp(jnp.minimum(logits - top, 0.0)), 0.0)
            soft = weight / jnp.sum(weight, axis=-1, keepdims=True)
            soft_s[s] = soft
            gates = soft * valid
            high = gates.astype(BF16).astype(F32)
            xg_s[s, :, width:] = (high + pltpu.roll(gates - high, LANES // 2, 1)).astype(BF16)

        def one(t):
            kv_gather.arrive(t)
            attend_slot(t)
            row_gather.start(t)

            @pl.when(t <= slots - 3)
            def _():
                kv_gather.forward(t + 2)

            @pl.when(t <= slots - 2)
            def _():
                kv_gather.settle(t + 1)

            @pl.when(t >= 1)
            def _():
                row_gather.forward(t - 1)

            @pl.when(t >= 2)
            def _():
                row_gather.settle(t - 2)

        each(one)
        keeps += [
            pltpu.make_async_copy(source, there, out_sems.at[4 + n])
            for n, (source, there) in enumerate(
                ((mixed_s, mixed_out), (invl_s, invl_out), (after_s, after_out), (soft_s, soft_out))
            )
        ]
        for copy in keeps[4:]:
            copy.start()
        each(kv_gather.drain)
        for copy in keeps:
            copy.wait()

    V, D = pltpu.VMEM, pltpu.SemaphoreType.DMA
    full = lambda lanes, kind: V((slots, rows, lanes), kind)
    pl.run_scoped(
        first_phase,
        V(wq_in.shape, BF16), V(wk_in.shape, BF16), V(wv_in.shape, BF16), V(wo_in.shape, BF16),
        full(width, BF16), full(2 * kw, BF16), full(qw, BF16), full(width, BF16), full(qw, F32), full(kw, F32),
        V((group, rows, 2 * kw), BF16), full(qw, BF16), full(qw, F32), full(LANES, F32), V((rows, width), F32),
        D((6,)), D((8,)),
    )
    sources, double, pairs, held = group, 2 * rows, group // 2, group // 2 * PAIR

    eff = wg_in.shape[2]

    def late_phases(teach, y_s, og_s, late_sems):
        teacher_load = pltpu.make_async_copy(teacher_in, teach, late_sems.at[0])
        teacher_load.start()
        loss_out[...] = jnp.zeros_like(loss_out)
        outs = lambda s: [
            pltpu.make_async_copy(source.at[lax.rem(s, 2)], there.at[s], late_sems.at[1 + 2 * n + lax.rem(s, 2)])
            for n, (source, there) in enumerate(((y_s, y_out), (og_s, og_out)))
        ]

        def loss_slot(s):
            slot = lax.rem(s, 2)

            def wait():
                for copy in outs(s - 2):
                    copy.wait()

            if isinstance(s, int):
                if s >= 2:
                    wait()
            else:
                pl.when(s >= 2)(wait)
            output = after_s[s] + scatter.result(s)
            y_s[slot] = output.astype(BF16)
            valid = (row_of((rows, 1)) + here * rows < sc_ref[s]).astype(F32)
            difference = valid * (output - teach[s].astype(F32))
            loss_out[...] += jnp.sum(difference * difference, axis=0, keepdims=True)
            grad = difference * scale_ref[0]
            og_s[slot] = grad
            dy_s[s] = grad.astype(BF16)
            for copy in outs(s):
                copy.start()
            grad_gather.start(s)

        teacher_load.wait()

        def second_phase(tok, pick_s, xe_s, gp_s, up_s, hid_s, gates, ybuf, sems, out_sems):
            for copy in expert_loads:
                copy.wait()
            keeps = lambda s: [
                pltpu.make_async_copy(source, there.at[s], out_sems.at[n])
                for n, (source, there) in enumerate(
                    ((pick_s, pick_out), (xe_s, xe_out), (gp_s, gp_out), (up_s, up_out), (hid_s, hid_out))
                )
            ]

            def experts_slot(s, between):
                load = pltpu.make_async_copy(tokens_out.at[:, s], tok, sems.at[0])
                load.start()

                @pl.when(s >= 1)
                def _():
                    for copy in keeps(s - 1):
                        copy.wait()

                load.wait()
                slab = tok[:, :, width:].reshape(sources * rows, LANES)
                chosen = (lane_of((8, LANES)) == row_of((8, LANES)) + first).astype(BF16)
                routed = dot_nt(chosen, slab) > 0.0
                before, after = row_of((double, double)), lane_of((double, double))
                count = ((before < after) & (before // rows == after // rows)).astype(BF16)
                place = lax.broadcasted_iota(jnp.int32, (PAIR, double), 0)
                offset = (lane_of((8, double)) // rows) * MOST
                for p in range(pairs):
                    mask = routed[:, p * double : (p + 1) * double]
                    rank = dot(mask.astype(F32).astype(BF16), count).astype(jnp.int32) + offset
                    rank = jnp.where(mask, rank, -1)
                    pick = jnp.concatenate(
                        [(place == rank[e : e + 1, :]).astype(F32).astype(BF16) for e in range(owned)], axis=0
                    )
                    pick_s[p] = pick
                    picked = dot(pick, tok[2 * p : 2 * p + 2, :, :width].reshape(double, width)).astype(BF16)
                    scale = row_gates(dot(pick, slab[p * double : (p + 1) * double]), first, owned)
                    for e in range(owned):
                        xe_s[e, p * PAIR : (p + 1) * PAIR] = picked[e * PAIR : (e + 1) * PAIR]
                        gates[e, p * PAIR : (p + 1) * PAIR] = jnp.broadcast_to(
                            scale[e * PAIR : (e + 1) * PAIR], (PAIR, LANES)
                        )

                def one_expert(e, carry):
                    rows_in = xe_s[e]
                    gate_part = dot(rows_in, wg[e])
                    up_part = dot(rows_in, wu[e])
                    gp_s[e] = gate_part.astype(BF16)
                    up_s[e] = up_part.astype(BF16)
                    hidden = (gate_part * jax.nn.sigmoid(gate_part) * up_part).astype(BF16)
                    hid_s[e] = hidden
                    result = (dot(hidden, wd[e]) * gates[e][:, 0:1]).astype(BF16)
                    for p in range(pairs):
                        ybuf[p, e] = result[p * PAIR : (p + 1) * PAIR]
                    return carry

                for e in range(owned // 2):
                    one_expert(e, 0)
                between()
                for e in range(owned // 2, owned):
                    one_expert(e, 0)
                for p in range(pairs):
                    back = dot_tn(pick_s[p], ybuf[p].reshape(owned * PAIR, width))
                    parts[2 * p : 2 * p + 2, s] = back.astype(BF16).reshape(2, rows, width)
                for copy in keeps(s):
                    copy.start()

            def one(t):
                row_gather.arrive(t)

                def between():
                    @pl.when(t == 0)
                    def _():
                        row_gather.settle(slots - 2)
                        row_gather.forward(slots - 1)

                    @pl.when(t == 1)
                    def _():
                        row_gather.settle(slots - 1)

                    @pl.when(t >= 1)
                    def _():
                        scatter.first(t - 1)
                        scatter.second(t - 1)

                    @pl.when(t == slots - 1)
                    def _():
                        grad_gather.forward(0)

                experts_slot(t, between)
                scatter.start(t)

                @pl.when(t >= 1)
                def _():
                    scatter.third(t - 1)

                @pl.when(t >= 2)
                def _():
                    loss_slot(t - 2)

            each(one)
            each(row_gather.drain)
            for copy in keeps(slots - 1):
                copy.wait()

        pl.run_scoped(
            second_phase,
            V((group, rows, wide), BF16), V((pairs, owned * PAIR, double), BF16), V((owned, held, width), BF16),
            V((owned, held, eff), BF16), V((owned, held, eff), BF16), V((owned, held, eff), BF16), V((owned, held, LANES), F32),
            V((pairs, owned, PAIR, width), BF16), D((2,)), D((5,)),
        )

        def third_phase(dyb, slabb, pickb, gpb, upb, hidb, gates, dye, dxb, dp_s, dyw_s, gg_s, ug_s, sems, out_sems):
            saved = lambda s: [
                pltpu.make_async_copy(source, there, sems.at[n])
                for n, (source, there) in enumerate(
                    ((tokens_out.at[:, s, :, pl.ds(width, LANES)], slabb), (pick_out.at[s], pickb), (gp_out.at[s], gpb),
                     (up_out.at[s], upb), (hid_out.at[s], hidb))
                )
            ]
            keeps = lambda s: [
                pltpu.make_async_copy(source, there, out_sems.at[n])
                for n, (source, there) in enumerate(
                    ((dp_s, dpart_out.at[:, s]), (dyw_s, dyw_out.at[s]), (gg_s, gg_out.at[s]), (ug_s, ug_out.at[s]))
                )
            ]
            for copy in saved(0):
                copy.start()
            last = slots - 1
            scatter.first(last)
            scatter.second(last)
            loss_slot(last - 1)
            grad_gather.settle(0)
            grad_gather.forward(1)

            def one(s):
                grad_gather.arrive(s)
                load = pltpu.make_async_copy(grads_out.at[:, s], dyb, sems.at[5])
                load.start()

                @pl.when(s >= 1)
                def _():
                    for copy in keeps(s - 1):
                        copy.wait()

                for copy in saved(s):
                    copy.wait()
                load.wait()
                for p in range(pairs):
                    pick = pickb[p]
                    picked = dot(pick, dyb[2 * p : 2 * p + 2].reshape(double, width)).astype(BF16)
                    scale = row_gates(dot(pick, slabb[2 * p : 2 * p + 2].reshape(double, LANES)), first, owned)
                    for e in range(owned):
                        dye[e, p * PAIR : (p + 1) * PAIR] = picked[e * PAIR : (e + 1) * PAIR]
                        gates[e, p * PAIR : (p + 1) * PAIR] = jnp.broadcast_to(
                            scale[e * PAIR : (e + 1) * PAIR], (PAIR, LANES)
                        )

                def one_expert(e, carry):
                    grad_rows = dye[e]
                    scale = gates[e][:, 0:1]
                    plain = dot_nt(grad_rows, wd[e])
                    gate_part, up_part = gpb[e].astype(F32), upb[e].astype(F32)
                    soft_grad = jnp.sum(plain * hidb[e].astype(F32), axis=-1, keepdims=True)
                    hidden_grad = plain * scale
                    sigma = jax.nn.sigmoid(gate_part)
                    gate_grad = (hidden_grad * up_part * sigma * (1.0 + gate_part * (1.0 - sigma))).astype(BF16)
                    up_grad = (hidden_grad * gate_part * sigma).astype(BF16)
                    gg_s[e] = gate_grad
                    ug_s[e] = up_grad
                    dyw_s[e] = (grad_rows.astype(F32) * scale).astype(BF16)
                    input_grad = (dot_nt(gate_grad, wg[e]) + dot_nt(up_grad, wu[e])).astype(BF16)
                    lanes = lane_of((held, LANES))
                    high = soft_grad.astype(BF16).astype(F32)
                    spot = jnp.where(
                        lanes == first + e, high, jnp.where(lanes == first + e + LANES // 2, soft_grad - high, 0.0)
                    ).astype(BF16)
                    for p in range(pairs):
                        dxb[p, e, :, :width] = input_grad[p * PAIR : (p + 1) * PAIR]
                        dxb[p, e, :, width:] = spot[p * PAIR : (p + 1) * PAIR]
                    return carry

                for e in range(owned // 2):
                    one_expert(e, 0)

                @pl.when(s == 0)
                def _():
                    scatter.third(last)
                    grad_gather.settle(1)
                    grad_gather.forward(2)

                @pl.when(s == 1)
                def _():
                    grad_gather.settle(2)
                    grad_gather.forward(3)

                @pl.when(s == 2)
                def _():
                    grad_gather.settle(3)

                for e in range(owned // 2, owned):
                    one_expert(e, 0)
                for p in range(pairs):
                    back = dot_tn(pickb[p], dxb[p].reshape(owned * PAIR, wide))
                    dp_s[2 * p : 2 * p + 2] = back.astype(BF16).reshape(2, rows, wide)
                for copy in keeps(s):
                    copy.start()

                @pl.when(s + 1 < slots)
                def _():
                    for copy in saved(s + 1):
                        copy.start()

                @pl.when(s == 0)
                def _():
                    loss_slot(last)

            each(one)
            each(scatter.drain)
            each(grad_gather.drain)
            for copy in keeps(slots - 1):
                copy.wait()

        pl.run_scoped(
            third_phase,
            V((group, rows, width), BF16), V((group, rows, LANES), BF16), V((pairs, owned * PAIR, double), BF16),
            V((owned, held, eff), BF16), V((owned, held, eff), BF16), V((owned, held, eff), BF16), V((owned, held, LANES), F32),
            V((owned, held, width), BF16), V((pairs, owned, PAIR, wide), BF16), V((group, rows, wide), BF16),
            V((owned, held, width), BF16), V((owned, held, eff), BF16), V((owned, held, eff), BF16), D((6,)), D((4,)),
        )
        for s in range(slots - 2, slots):
            for copy in outs(s):
                copy.wait()

    pl.run_scoped(
        late_phases, full(width, BF16), V((2, rows, width), BF16), V((2, rows, width), F32), D((5,)),
    )


def front(
    slot_lengths, x, teacher, routes, w_query, w_key, w_value, w_out, w_gate, w_up, w_down,
    attn_gain, ffn_gain, qg, kg, cosine, sine, router, scale, group, number,
):
    slots, rows, width = x.shape
    qw, kw = w_query.shape[1], w_key.shape[1]
    owned, unused, eff = w_gate.shape
    wide = width + LANES
    pairs = group // 2
    held = pairs * PAIR
    hbm = pl.BlockSpec(memory_space=pl.ANY)
    vmem = pl.BlockSpec(memory_space=pltpu.VMEM)
    smem = pl.BlockSpec(memory_space=pltpu.SMEM)
    V, D = pltpu.VMEM, pltpu.SemaphoreType.DMA
    half = rows // 2
    mine = lambda lanes, kind: jax.ShapeDtypeStruct((slots, rows, lanes), kind)
    all_of = lambda lanes: jax.ShapeDtypeStruct((group, slots, rows, lanes), BF16)
    saved = lambda *dims: jax.ShapeDtypeStruct((slots,) + dims, BF16)
    outs = (
        mine(width, BF16), mine(qw, BF16), mine(qw, F32), mine(kw, F32), all_of(2 * kw), mine(qw, BF16), mine(qw, F32),
        mine(width, F32), mine(LANES, F32), all_of(wide),
        saved(pairs, owned * PAIR, 2 * rows), saved(owned, held, width),
        saved(owned, held, eff), saved(owned, held, eff), saved(owned, held, eff), mine(width, BF16), mine(width, F32), jax.ShapeDtypeStruct((1, width), F32), all_of(width),
        all_of(wide), saved(owned, held, width), saved(owned, held, eff), saved(owned, held, eff),
    )
    return pl.pallas_call(
        front_kernel,
        in_specs=[smem, hbm, hbm, vmem] + [hbm] * 7 + [vmem] * 7 + [smem],
        out_specs=(hbm,) * 17 + (vmem,) + (hbm,) * 5,
        out_shape=outs,
        scratch_shapes=[
            V((4, slots, rows, width), BF16), V((slots, half, width), BF16), V((slots, half, width), BF16),
            V((slots, rows, width), BF16), V((slots, rows, width), BF16),
            V((group, slots, rows, width), BF16),
            V(w_gate.shape, BF16), V(w_up.shape, BF16), V(w_down.shape, BF16),
            V((slots, rows, width), F32), V((slots, rows, wide), BF16), V((slots, rows, width), BF16),
        ]
        + [D((8, slots)), D((8, slots)), D((slots,))] * 3
        + [D((10, slots)), D((10, slots)), D((3,)), D((1,))],
        compiler_params=pltpu.CompilerParams(collective_id=number, has_side_effects=True, vmem_limit_bytes=63 * MIB),
        name="front",
    )(
        slot_lengths, x, teacher, routes, w_query, w_key, w_value, w_out, w_gate, w_up, w_down,
        attn_gain, ffn_gain, qg, kg, cosine, sine, router, scale,
    )


def add_to(ref, value):
    ref[...] = (ref[...].astype(F32) + value).astype(ref.dtype)


class Plane:
    def __init__(self):
        z, c, y = lax.axis_index("dp"), lax.axis_index("context"), lax.axis_index("experts")
        core = lax.rem(c, 2)
        cx, yy = lax.rem(c + 2, 4), 1 - y
        self.me = c * 2 + y
        self.sib, self.xn, self.yn = (z, c + 1 - 2 * core, y), (z, cx, y), (z, c, yy)
        chips = [(cx, yy), (cx, y), (c, yy), (c, y)]
        self.own = [a * 2 + b for a, b in chips]
        self.other = [(a + 1 - 2 * core) * 2 + b for a, b in chips]
        self.inner_plane = (z == 1) | (z == 2)
        self.outer_plane = (z == 0) | (z == 3)
        self.inner = (1 + z // 2, c, y)
        self.across = (3 - z, c, y)
        self.outer = ((z - 1) * 3, c, y)

    def barrier(self, line):
        bar = pltpu.get_barrier_semaphore()
        tell = lambda who: pl.semaphore_signal(bar, inc=1, device_id=who, device_id_type=MESH)
        for who in (self.sib, self.xn, self.yn):
            tell(who)
        if not line:
            pl.semaphore_wait(bar, 3)
            return

        @pl.when(self.outer_plane)
        def _():
            tell(self.inner)
            pl.semaphore_wait(bar, 4)

        @pl.when(self.inner_plane)
        def _():
            tell(self.across)
            tell(self.outer)
            pl.semaphore_wait(bar, 5)


class Scatter:
    def __init__(self, plane, own, other, buffers, sems):
        self.plane, self.own, self.other = plane, own, other
        self.sb, self.da, self.db, self.rx, self.ry = buffers
        self.sent, self.got = sems
        self.rows = self.sb.shape[2]
        self.top, self.low = pl.ds(0, self.rows // 2), pl.ds(self.rows // 2, self.rows // 2)

    def core(self, k, s):
        return remote(self.other(k, s), self.sb.at[k, s], self.sent.at[k, s], self.got.at[k, s], self.plane.sib)

    def diag(self, s):
        mine = self.own(0, s)
        return (
            remote(mine.at[self.top], self.da.at[s], self.sent.at[4, s], self.got.at[4, s], self.plane.xn),
            remote(mine.at[self.low], self.db.at[s], self.sent.at[5, s], self.got.at[5, s], self.plane.yn),
        )

    def side(self, number, s):
        axis, half = number // 2, (self.top, self.low)[number % 2]
        there = (self.rx, self.ry)[axis]
        who = (self.plane.xn, self.plane.yn)[axis]
        return remote(
            self.own(1 + axis, s).at[half], there.at[s, half], self.sent.at[6 + number, s], self.got.at[6 + number, s], who
        )

    def pair(self, k, s, half):
        return self.own(k, s)[half].astype(F32) + self.sb[k, s, half].astype(F32)

    def start(self, s):
        for k in range(4):
            self.core(k, s).start()

    def first(self, s):
        self.core(0, s).wait_recv()
        mine = self.own(0, s)
        add_to(mine, self.sb[0, s].astype(F32))
        for copy in self.diag(s):
            copy.start()

    def second(self, s):
        self.core(1, s).wait_recv()
        self.own(1, s)[self.top] = self.pair(1, s, self.top).astype(BF16)
        self.side(0, s).start()
        self.core(2, s).wait_recv()
        self.own(2, s)[self.low] = self.pair(2, s, self.low).astype(BF16)
        self.side(3, s).start()

    def third(self, s):
        by_x, by_y = self.diag(s)
        by_x.wait_recv()
        self.own(2, s)[self.top] = (self.pair(2, s, self.top) + self.da[s].astype(F32)).astype(BF16)
        self.side(2, s).start()
        by_y.wait_recv()
        self.own(1, s)[self.low] = (self.pair(1, s, self.low) + self.db[s].astype(F32)).astype(BF16)
        self.side(1, s).start()

    def result(self, s):
        self.core(3, s).wait_recv()
        for number in range(4):
            self.side(number, s).wait_recv()
        return (
            self.own(3, s)[...].astype(F32)
            + self.sb[3, s].astype(F32)
            + self.rx[s].astype(F32)
            + self.ry[s].astype(F32)
        )

    def drain(self, s):
        for k in range(4):
            self.core(k, s).wait_send()
        for copy in self.diag(s):
            copy.wait_send()
        for number in range(4):
            self.side(number, s).wait_send()


class Line:
    ring, back = 4, 2

    def __init__(self, plane, held, first, second, total, buffers, sems):
        self.plane, self.held, self.r1, self.r2, self.total = plane, held, first, second, total
        self.l1, self.va, self.vt = buffers
        self.sent, self.got, self.local = sems
        self.count = held.shape[0]

    def inward(self, i):
        return remote(self.held.at[i], self.r1.at[i], self.sent.at[0, i], self.got.at[0, i], self.plane.inner)

    def across(self, i):
        return remote(self.va.at[i % self.ring], self.r2.at[i], self.sent.at[1, i], self.got.at[1, i], self.plane.across)

    def outward(self, i):
        return remote(self.vt.at[i % self.back], self.total.at[i], self.sent.at[2, i], self.got.at[2, i], self.plane.outer)

    def keep(self, i):
        return pltpu.make_async_copy(self.vt.at[i % self.back], self.total.at[i], self.local.at[i % self.back])

    def load(self, number, i):
        source, there = (
            (self.r1, self.l1.at[i % 2]), (self.held, self.va.at[i % self.ring]), (self.r2, self.vt.at[i % self.back])
        )[number]
        return pltpu.make_async_copy(source.at[i], there, self.local.at[self.ring + 2 * number + i % 2])

    def when(self, fact, body):
        if isinstance(fact, bool):
            if fact:
                body()
        else:
            pl.when(fact)(body)

    def take(self, i):
        def wait():
            self.across(i - self.ring).wait_send()

        self.when(i >= self.ring, wait)
        self.load(1, i).start()
        self.inward(i).wait_recv()
        self.load(0, i).start()

    def give(self, i):
        self.load(1, i).wait()
        self.load(0, i).wait()
        add_to(self.va.at[i % self.ring], self.l1[i % 2].astype(F32))
        self.across(i).start()

    def fetch(self, i):
        def wait():
            self.outward(i - self.back).wait_send()
            self.keep(i - self.back).wait()

        self.when(i >= self.back, wait)
        self.across(i).wait_recv()
        self.load(2, i).start()

    def settle(self, i):
        self.load(2, i).wait()
        add_to(self.vt.at[i % self.back], self.va[i % self.ring].astype(F32))
        self.outward(i).start()
        self.keep(i).start()

    def move(self, i, lag=2):
        @pl.when(self.plane.inner_plane)
        def _():
            self.take(i)
            self.when(i >= lag, lambda: self.fetch(i - lag))
            self.give(i)
            self.when(i >= lag, lambda: self.settle(i - lag))

    def wind_up(self, start):
        @pl.when(self.plane.inner_plane)
        def _():
            for i in range(start, self.count + 1):
                if i < self.count:
                    self.take(i)
                    self.give(i)
                for n in ([start - 2] if i == start else []) + [i - 1]:
                    self.fetch(n)
                    self.settle(n)

    def finish(self):
        @pl.when(self.plane.inner_plane)
        def _():
            for i in range(self.count - self.ring, self.count):
                self.across(i).wait_send()
            for i in range(self.count - self.back, self.count):
                self.outward(i).wait_send()
                self.keep(i).wait()

        @pl.when(self.plane.outer_plane)
        def _():
            def one(i, carry):
                self.inward(i).wait_send()
                remote(
                    self.held.at[i], self.total.at[i], self.sent.at[2, i], self.got.at[2, i], self.plane.inner
                ).wait_recv()
                return carry

            lax.fori_loop(0, self.count, one, 0)


HELD_BACK = 14


def tail_kernel(
    sc_ref, dpart, xe, gg, ug, hid, dyw, q_in, kv_in, mixed_in, invl_in, soft_in, og_in, after_in, qraw_in, kraw_in,
    x_in, h_in, n2_in, wo_in, wq_in, wk_in, wv_in, fg_ref, wr_ref, cos_ref, sin_ref, gain_ref, qg_ref, kg_ref, loss_ref,
    total, ig_out, dense_out, small_out, held, r1, r2,
    dx_own, dx_sb, dx_da, dx_db, dx_rx, dx_ry, kv_sb, kv_da, kv_db, kv_rx, kv_ry,
    l1, va, vt, dsh, dr1, dr2, dfin, sm_mine, sm_got,
    sent_dx, got_dx, sent_kv, got_kv, sent_de, got_de, sent_z, got_z, local_z, sent_ag, got_ag, sent_sm, got_sm, local,
):
    plane = Plane()
    slots, rows = x_in.shape[0], x_in.shape[1]
    width = x_in.shape[2]
    group = dpart.shape[0]
    kinds = dsh.shape[0]
    owned = xe.shape[1]
    eff = gg.shape[3]
    each = lambda body, count=slots: lax.fori_loop(0, count, lambda s, c: (body(s), c)[1], 0)
    line = Line(plane, held, r1, r2, total, (l1, va, vt), (sent_z, got_z, local_z))
    scat_dx = Scatter(
        plane, lambda k, s: dx_own.at[k, s], lambda k, s: dpart.at[plane.other[k], s],
        (dx_sb, dx_da, dx_db, dx_rx, dx_ry), (sent_dx, got_dx),
    )
    own_load = lambda k, s: pltpu.make_async_copy(dpart.at[plane.own[k], s], dx_own.at[k, s], local.at[0])
    for k in range(4):
        each(lambda s: own_load(k, s).start())
    def expert_phase(xeb, ggb, ugb, hidb, dywb, gb, sems, out_sem):
        def loads(e):
            slot = e % 2
            return [
                pltpu.make_async_copy(source.at[:, e], there.at[slot], sems.at[slot, n])
                for n, (source, there) in enumerate(((xe, xeb), (gg, ggb), (ug, ugb), (hid, hidb), (dyw, dywb)))
            ]

        def store(number):
            return pltpu.make_async_copy(gb.at[number % 4], held.at[pl.ds(2 * number, 2)], out_sem.at[number % 4])

        def send(number):
            store(number).wait()
            todo = [2 * number + n for n in range(2) if 2 * number + n < HELD_BACK]
            if todo:
                @pl.when(plane.outer_plane)
                def _():
                    for i in todo:
                        line.inward(i).start()

        flat = lambda ref, slot: ref[slot].reshape(ref.shape[1] * ref.shape[2], ref.shape[3])
        half = width // 2
        for copy in loads(0):
            copy.start()
        plane.barrier(True)
        each(scat_dx.start)
        for e in range(owned):
            slot = e % 2
            if e + 1 < owned:
                for copy in loads(e + 1):
                    copy.start()
            for copy in loads(e):
                copy.wait()
            for n, (left, right) in enumerate(((xeb, ggb), (xeb, ugb), (hidb, dywb))):
                number = 3 * e + n
                part = dot_tn(flat(left, slot), flat(right, slot)).astype(BF16)
                gb[number % 4, 0] = part[:half] if n < 2 else part[:, :half]
                gb[number % 4, 1] = part[half:] if n < 2 else part[:, half:]
                store(number).start()
                if number >= 1:
                    send(number - 1)
            if e == 1:
                for k in range(4):
                    each(lambda s: own_load(k, s).wait())
                each(scat_dx.first)
            if e == 2:
                each(scat_dx.second)
                line.move(0)
        send(3 * owned - 1)
        line.move(1)
        each(scat_dx.third)

    held_rows = (xe.shape[0], xe.shape[2])
    pl.run_scoped(
        expert_phase,
        pltpu.VMEM((2,) + held_rows + (width,), BF16),
        pltpu.VMEM((2,) + held_rows + (eff,), BF16),
        pltpu.VMEM((2,) + held_rows + (eff,), BF16),
        pltpu.VMEM((2,) + held_rows + (eff,), BF16),
        pltpu.VMEM((2,) + held_rows + (width,), BF16),
        pltpu.VMEM((4, 2, eff, width // 2), BF16),
        pltpu.SemaphoreType.DMA((2, 5)),
        pltpu.SemaphoreType.DMA((4,)),
    )
    line.move(2)
    here = plane.me
    chunk = 2 * rows
    chunks = (here + 2) // 2
    qw = q_in.shape[2]
    kw = kraw_in.shape[2]
    tiles = qw // 256

    def rest(dkv, ag_s, at_s, lg_s, mixed_s, q_s, qgg, kgg, agg, fgg, mg_s):
        scat_kv = Scatter(
            plane, lambda k, s: dkv.at[plane.own[k], s], lambda k, s: dkv.at[plane.other[k], s],
            (kv_sb, kv_da, kv_db, kv_rx, kv_ry), (sent_kv, got_kv),
        )
        for ref in (qgg, kgg, agg, fgg):
            ref[...] = jnp.zeros_like(ref)
        mixed_load = pltpu.make_async_copy(mixed_in, mixed_s, local.at[1])
        mixed_load.start()

        def attention_phase(wo, qb, kvb, invlb, softb, ogb, afterb, qrawb, sems):
            wo_load = pltpu.make_async_copy(wo_in, wo, local.at[2])
            wo_load.start()

            def loads(s):
                slot = lax.rem(s, 2)
                out = [pltpu.make_async_copy(kv_in.at[:, s], kvb.at[slot], sems.at[slot, 0])]
                for n, (source, there) in enumerate(
                    ((q_in, qb), (invl_in, invlb), (soft_in, softb), (og_in, ogb), (after_in, afterb), (qraw_in, qrawb))
                ):
                    out.append(pltpu.make_async_copy(source.at[s], there.at[slot], sems.at[slot, n + 1]))
                return out

            for s in range(2):
                for copy in loads(s):
                    copy.start()
            wo_load.wait()
            mixed_load.wait()

            def one_slot(s):
                slot = lax.rem(s, 2)
                for copy in loads(s):
                    copy.wait()
                dx = scat_dx.result(s)
                valid = (row_of((rows, 1)) + here * rows < sc_ref[s]).astype(F32)
                slab = dx[:, width:]
                half = slab.shape[1] // 2
                soft = softb[slot]
                soft_grad = jnp.where(lane_of(slab.shape) < half, slab + pltpu.roll(slab, half, 1), 0.0)
                chosen = soft * (soft_grad - jnp.sum(soft * soft_grad, axis=-1, keepdims=True))
                logit_grad = chosen.astype(BF16)
                lg_s[s] = logit_grad
                normed_grad = dx[:, :width] + dot(logit_grad, padded_rows(wr_ref[...]))
                back, gain_grad = rms_backward(normed_grad, afterb[slot], fg_ref[...])
                fgg[...] += gain_grad
                after_grad = ogb[slot] + back
                ag_s[s] = after_grad
                attn_grad = (valid * after_grad).astype(BF16)
                at_s[s] = attn_grad
                mixed_grad = dot_nt(attn_grad, wo[...]).astype(BF16)
                for t in range(tiles):
                    mg_s[t] = mixed_grad[:, t * 256 : (t + 1) * 256]

                def one_tile(t, carry):
                    lanes = pl.ds(pl.multiple_of(t * 256, 256), 256)
                    key_lanes = pl.ds(pl.multiple_of(t * 256, 256), LANES)
                    value_lanes = pl.ds(pl.multiple_of(t * 256 + LANES, LANES), LANES)
                    q4 = stack_heads(qb[slot, :, lanes], True).astype(BF16)
                    do4_f = stack_heads(mg_s[t].astype(F32) * invlb[slot, :, lanes], True)
                    do4 = do4_f.astype(BF16)
                    product = do4_f * stack_heads(mixed_s[s, :, lanes], False)
                    delta = lax.dot_general(
                        jnp.ones((8, LANES), F32), product, (((1,), (1,)), ((), ())),
                        preferred_element_type=F32, precision=lax.Precision.HIGHEST,
                    )[0:1]

                    def step(index, sum_q, masked):
                        two = pl.ds(2 * index, 2)
                        keys = kvb[slot, two, :, key_lanes].reshape(chunk, LANES)
                        values = kvb[slot, two, :, value_lanes].reshape(chunk, LANES)
                        weight = jnp.exp2(dot_nt(keys, q4) * EXP2_SCALE)
                        if masked:
                            at = lax.rem(lane_of(weight.shape), rows) + here * rows
                            weight = jnp.where(row_of(weight.shape) + index * chunk <= at, weight, 0.0)
                        pressure = dot_nt(values, do4)
                        score_grad = (weight * (pressure - delta) * SCALE).astype(BF16)
                        key_grad = dot(score_grad, q4).astype(BF16)
                        value_grad = dot(weight.astype(BF16), do4).astype(BF16)
                        dkv[two, s, :, key_lanes] = key_grad.reshape(2, rows, LANES)
                        dkv[two, s, :, value_lanes] = value_grad.reshape(2, rows, LANES)
                        return sum_q + dot_tn(score_grad, keys)

                    total_q = lax.fori_loop(
                        0, chunks - 1, lambda i, c: step(i, c, False), jnp.zeros((4 * rows, LANES), F32)
                    )
                    total_q = step(chunks - 1, total_q, True)

                    def blank(index, carry):
                        dkv[pl.ds(2 * index, 2), s, :, lanes] = jnp.zeros((2, rows, 256), BF16)
                        return carry

                    lax.fori_loop(chunks, group // 2, blank, 0)
                    dq = unstack_heads(total_q).astype(BF16).astype(F32)
                    for n in range(2):
                        part = slice(n * LANES, (n + 1) * LANES)
                        here_lanes = pl.ds(pl.multiple_of(t * 256 + n * LANES, LANES), LANES)
                        raw, gain = rope_backward(
                            dq[:, part], qrawb[slot, :, here_lanes], qg_ref[...], cos_ref[...], sin_ref[...]
                        )
                        q_s[s, :, here_lanes] = raw.astype(BF16)
                        qgg[...] += gain
                    return carry

                lax.fori_loop(0, tiles, one_tile, 0)

                @pl.when(s + 2 < slots)
                def _():
                    for copy in loads(s + 2):
                        copy.start()

                scat_kv.start(s)

                @pl.when(s >= 1)
                def _():
                    scat_kv.first(s - 1)
                    scat_kv.second(s - 1)

                @pl.when(s >= 2)
                def _():
                    scat_kv.third(s - 2)

            def slot_and_move(s):
                one_slot(s)
                ahead = s + 3 + s // 2
                line.move(ahead)

                @pl.when(lax.rem(s, 2) == 1)
                def _():
                    line.move(ahead + 1)

            each(slot_and_move)

        pl.run_scoped(
            attention_phase,
            pltpu.VMEM(wo_in.shape, BF16),
            pltpu.VMEM((2, rows, qw), BF16),
            pltpu.VMEM((2, group, rows, 2 * kw), BF16),
            pltpu.VMEM((2, rows, qw), F32),
            pltpu.VMEM((2, rows, LANES), F32),
            pltpu.VMEM((2, rows, width), F32),
            pltpu.VMEM((2, rows, width), F32),
            pltpu.VMEM((2, rows, qw), F32),
            pltpu.SemaphoreType.DMA((2, 7)),
        )
        each(scat_dx.drain)

        def last_phase(wq, wk, wv, xb, krawb, hb, n2b, k_s, v_s):
            loads = [
                pltpu.make_async_copy(source, there, local.at[2 + n])
                for n, (source, there) in enumerate(
                    ((wq_in, wq), (wk_in, wk), (wv_in, wv), (x_in, xb), (kraw_in, krawb), (h_in, hb),
                     (n2_in.at[plane.me, :, :, pl.ds(0, width)], n2b))
                )
            ]
            for copy in loads:
                copy.start()
            scat_kv.first(slots - 1)
            scat_kv.second(slots - 1)
            scat_kv.third(slots - 2)
            line.move(9)
            flat = lambda ref: ref[...].reshape(slots * rows, ref.shape[2])
            for copy in loads:
                copy.wait()
            shards, shard_rows = group, width // group

            def product(left, right, place):
                def one(n, carry):
                    lanes = pl.ds(pl.multiple_of(n * 256, 256), 256)
                    column = right[:, :, lanes].reshape(slots * rows, 256)
                    place(n, dot_tn(flat(left), column).astype(BF16).reshape(shards, shard_rows, 256))
                    return carry

                lax.fori_loop(0, right.shape[2] // 256, one, 0)

            def aside(k):
                def place(n, value):
                    lanes = pl.ds(pl.multiple_of(n * 256, 256), 256)
                    for shard in range(shards):
                        dx_own[k + shard // slots, shard % slots, :, lanes] = value[shard]

                return place

            product(mixed_s, at_s, aside(0))
            scat_kv.third(slots - 1)
            product(hb, q_s, aside(2))
            line.move(10)
            router = dot_tn(flat(lg_s), flat(n2b))
            experts = small_out.shape[0] - 8
            sm_mine[0] = jnp.zeros(sm_mine.shape[1:], F32)
            sm_mine[0, :experts] = router[:experts]
            sm_mine[0, experts + 1 : experts + 2] = fgg[...]
            sm_mine[0, experts + 2 : experts + 3, :LANES] = qgg[...]
            sm_mine[0, experts + 4 : experts + 5] = loss_ref[...]

            def one_slot(s):
                grads = scat_kv.result(s)
                for t in range(kw // LANES):
                    lanes = slice(t * LANES, (t + 1) * LANES)
                    at = 2 * t * LANES
                    grad = grads[:, at : at + LANES].astype(BF16).astype(F32)
                    raw, gain = rope_backward(grad, krawb[s, :, lanes], kg_ref[...], cos_ref[...], sin_ref[...])
                    k_s[s, :, lanes] = raw.astype(BF16)
                    kgg[...] += gain
                    v_s[s, :, lanes] = grads[:, at + LANES : at + 2 * LANES].astype(BF16)
                normed_grad = dot_nt(q_s[s], wq[...]) + dot_nt(k_s[s], wk[...]) + dot_nt(v_s[s], wv[...])
                back, gain = rms_backward(normed_grad, xb[s].astype(F32), gain_ref[...])
                agg[...] += gain
                ag_s[s] += back
                pltpu.make_async_copy(ag_s.at[s], ig_out.at[s], local.at[0]).start()

            each(one_slot)
            each(scat_kv.drain)
            line.move(11)
            sm_mine[0, experts : experts + 1] = agg[...]
            sm_mine[0, experts + 3 : experts + 4, :LANES] = kgg[...]
            for shard in range(shards):
                dkv[shard, 2] = dx_own[shard // slots, shard % slots, :, :width]
                dkv[shard, 0] = dx_own[2 + shard // slots, shard % slots, :, :width]

            def beside(first):
                def place(n, value):
                    dkv[:, 1, :, pl.ds(pl.multiple_of(first + n * 256, 256), 256)] = value

                return place

            product(hb, k_s, beside(0))
            product(hb, v_s, beside(kw))
            line.move(12)

        pl.run_scoped(
            last_phase,
            pltpu.VMEM(wq_in.shape, BF16),
            pltpu.VMEM(wk_in.shape, BF16),
            pltpu.VMEM(wv_in.shape, BF16),
            pltpu.VMEM(x_in.shape, BF16),
            pltpu.VMEM(kraw_in.shape, F32),
            pltpu.VMEM(h_in.shape, BF16),
            pltpu.VMEM((slots, rows, width), BF16),
            pltpu.VMEM((slots, rows, kw), BF16),
            pltpu.VMEM((slots, rows, kw), BF16),
        )
        narrow = pl.ds(0, width)
        again = [dx_sb.at[:, :, :, narrow]] + [r.at[:, :, narrow] for r in (dx_da, dx_db, dx_rx, dx_ry)]
        scat_de = Scatter(
            plane, lambda k, s: dkv.at[plane.own[k], s], lambda k, s: dkv.at[plane.other[k], s],
            again, (sent_de, got_de),
        )
        by_kind = lambda body: each(body, kinds)
        by_kind(scat_de.start)
        small = lambda n, who: remote(sm_mine.at[n], sm_got.at[n], sent_sm.at[n], got_sm.at[n], who)

        def small_step(n, who):
            small(n, who).wait_recv()
            sm_mine[n + 1] = sm_mine[n] + sm_got[n]

        small(0, plane.sib).start()
        by_kind(scat_de.first)
        small_step(0, plane.sib)
        small(1, plane.xn).start()
        by_kind(scat_de.second)
        small_step(1, plane.xn)
        small(2, plane.yn).start()
        by_kind(scat_de.third)
        small_step(2, plane.yn)
        line.move(13)

        def one_kind(s):
            dsh[s] = scat_de.result(s).astype(BF16)

        by_kind(one_kind)
        by_kind(scat_de.drain)
        each(lambda s: pltpu.make_async_copy(ag_s.at[s], ig_out.at[s], local.at[0]).wait())

    pl.run_scoped(
        rest,
        pltpu.VMEM((group, slots, rows, 2 * kw), BF16),
        pltpu.VMEM((slots, rows, width), F32),
        pltpu.VMEM((slots, rows, width), BF16),
        pltpu.VMEM((slots, rows, LANES), BF16),
        pltpu.VMEM((slots, rows, qw), BF16),
        pltpu.VMEM((slots, rows, qw), BF16),
        pltpu.VMEM((1, LANES), F32),
        pltpu.VMEM((1, LANES), F32),
        pltpu.VMEM((1, width), F32),
        pltpu.VMEM((1, width), F32),
        pltpu.VMEM((tiles, rows, 256), BF16),
    )

    small_in = remote(sm_mine.at[3], sm_got.at[3], sent_sm.at[3], got_sm.at[3], plane.inner)
    small_across = remote(sm_mine.at[4], sm_got.at[4], sent_sm.at[4], got_sm.at[4], plane.across)
    small_back = remote(sm_mine.at[5], sm_got.at[5], sent_sm.at[5], got_sm.at[5], plane.outer)
    dense_in = remote(dsh, dr1, sent_sm.at[6], got_sm.at[6], plane.inner)
    dense_across = remote(dsh, dr2, sent_sm.at[7], got_sm.at[7], plane.across)
    dense_back = remote(dfin, dfin, sent_sm.at[8], got_sm.at[8], plane.outer)

    @pl.when(plane.outer_plane)
    def _():
        small_in.start()
        dense_in.start()

        def one(i, carry):
            line.inward(i).start()
            return carry

        lax.fori_loop(HELD_BACK, line.count, one, 0)

    @pl.when(plane.inner_plane)
    def _():
        small_in.wait_recv()
        sm_mine[4] = sm_mine[3] + sm_got[3]
        small_across.start()
        dense_in.wait_recv()
        add_to(dsh, dr1[...].astype(F32))
        dense_across.start()

    line.move(14)

    @pl.when(plane.inner_plane)
    def _():
        small_across.wait_recv()
        sm_mine[5] = sm_mine[4] + sm_got[4]
        small_back.start()
        small_out[...] = sm_mine[5]

    line.move(15)

    @pl.when(plane.inner_plane)
    def _():
        dense_across.wait_recv()
        dfin[...] = (dsh[...].astype(F32) + dr2[...].astype(F32)).astype(BF16)
        dense_back.start()

    @pl.when(plane.outer_plane)
    def _():
        small_back.wait_recv()
        small_out[...] = sm_got[5]
        dense_back.wait_recv()

    gather = Slots(plane, dfin, dense_out, sent_ag, got_ag, local)
    for s in range(kinds):
        gather.start(s)
    line.move(16)
    for s in range(kinds):
        gather.forward(s)
    line.move(17)
    for s in range(kinds):
        gather.settle(s)
    line.move(18)
    for s in range(kinds):
        gather.arrive(s)
        gather.drain(s)
    line.wind_up(19)
    line.finish()
    for n, who in ((0, plane.sib), (1, plane.xn), (2, plane.yn)):
        remote(sm_mine.at[n], sm_got.at[n], sent_sm.at[n], got_sm.at[n], who).wait_send()

    @pl.when(plane.outer_plane)
    def _():
        small_in.wait_send()
        dense_in.wait_send()

    @pl.when(plane.inner_plane)
    def _():
        small_across.wait_send()
        small_back.wait_send()
        dense_across.wait_send()
        dense_back.wait_send()


def tail(
    slot_lengths, dpart, xe, gate_grad, up_grad, hidden, weighted, q, kv, mixed, invl, soft, out_grad, after, qraw, kraw,
    x, h, n2, w_out, w_query, w_key, w_value, ffn_gain, router, cosine, sine, attn_gain, qg, kg, loss, experts, number,
):
    slots, rows, width = x.shape
    group, unused, unused_rows, wide = dpart.shape
    owned, eff = xe.shape[1], gate_grad.shape[3]
    kw = kraw.shape[2]
    chunks = 6 * owned
    piece = (eff, width // 2)
    kinds = 3
    hbm = pl.BlockSpec(memory_space=pl.ANY)
    vmem = pl.BlockSpec(memory_space=pltpu.VMEM)
    smem = pl.BlockSpec(memory_space=pltpu.SMEM)
    V, D = pltpu.VMEM, pltpu.SemaphoreType.DMA
    half = rows // 2

    def landing(n, lanes):
        return [
            V((4, n, rows, lanes), BF16), V((n, half, lanes), BF16), V((n, half, lanes), BF16),
            V((n, rows, lanes), BF16), V((n, rows, lanes), BF16),
        ]

    small_rows = experts + 8
    return pl.pallas_call(
        tail_kernel,
        in_specs=[smem] + [hbm] * 22 + [vmem] * 8,
        out_specs=(hbm, hbm, hbm, vmem, hbm, hbm, hbm),
        out_shape=(
            jax.ShapeDtypeStruct((chunks,) + piece, BF16),
            jax.ShapeDtypeStruct((slots, rows, width), F32),
            jax.ShapeDtypeStruct((group, kinds, width // group, width), BF16),
            jax.ShapeDtypeStruct((small_rows, width), F32),
            jax.ShapeDtypeStruct((chunks,) + piece, BF16),
            jax.ShapeDtypeStruct((chunks,) + piece, BF16),
            jax.ShapeDtypeStruct((chunks,) + piece, BF16),
        ),
        scratch_shapes=[V((4, slots, rows, wide), BF16)]
        + landing(slots, wide) + landing(slots, 2 * kw)
        + [V((2,) + piece, BF16), V((4,) + piece, BF16), V((2,) + piece, BF16)]
        + [V((kinds, rows, width), BF16)] * 4
        + [V((6, small_rows, width), F32)] * 2
        + [D((10, slots))] * 4 + [D((10, kinds))] * 2
        + [D((3, chunks))] * 2 + [D((10,))]
        + [D((8, kinds))] * 2 + [D((9,))] * 2 + [D((9,))],
        compiler_params=pltpu.CompilerParams(collective_id=number, has_side_effects=True, vmem_limit_bytes=63 * MIB),
        name="tail",
    )(
        slot_lengths, dpart, xe, gate_grad, up_grad, hidden, weighted, q, kv, mixed, invl, soft, out_grad, after, qraw,
        kraw, x, h, n2, w_out, w_query, w_key, w_value, ffn_gain, router, cosine, sine, attn_gain, qg, kg, loss,
    )


def plane_gather(rows):
    return lax.all_gather(rows, ("context", "experts"), axis=0, tiled=False)


def plane_scatter(parts):
    return lax.psum_scatter(parts, ("context", "experts"), scatter_dimension=0, tiled=False).astype(F32)


def unpack_kernel(
    gate_ref, up_ref, down_ref, dense_ref, sums_ref, scale_ref, dg_ref, du_ref, dd_ref, dq_ref, dk_ref, dv_ref, do_ref,
    router_ref, attn_ref, ffn_ref, query_ref, key_ref, loss_ref,
):
    @pl.when(pl.program_id(0) == 0)
    def _():
        experts = router_ref.shape[0]
        line = lambda n: sums_ref[experts + n : experts + n + 1, :]
        router_ref[...] = sums_ref[:experts, :]
        attn_ref[...] = line(0)
        ffn_ref[...] = line(1)
        for ref, n in ((query_ref, 2), (key_ref, 3)):
            tile = line(n)[:, :LANES]
            ref[...] = (tile + pltpu.roll(tile, HEAD, 1))[:, :HEAD]
        loss_ref[...] = jnp.sum(line(4), axis=-1, keepdims=True) * scale_ref[0]

    dg_ref[0] = gate_ref[0].astype(F32)
    du_ref[0] = up_ref[0].astype(F32)
    dd_ref[0] = down_ref[0].astype(F32)
    half = dk_ref.shape[1]
    dq_ref[...] = dense_ref[0, 0].astype(F32)
    dk_ref[...] = dense_ref[0, 1, :, :half].astype(F32)
    dv_ref[...] = dense_ref[0, 1, :, half:].astype(F32)
    do_ref[...] = dense_ref[0, 2].astype(F32)


def unpack(total, dense, sums, scale, key_width):
    chunks, eff, half = total.shape
    shards, kinds, shard_rows, width = dense.shape
    owned = chunks // 6
    steps = 2 * owned
    piece = lambda kind: pl.BlockSpec((1, eff, half), lambda i: (i // 2 * 6 + 2 * kind + i % 2, 0, 0))
    row = lambda lanes: pl.BlockSpec((shard_rows * shards // steps, lanes), lambda i: (i, 0))
    shape = lambda *dims: jax.ShapeDtypeStruct(dims, F32)
    still = lambda *dims: pl.BlockSpec(dims, lambda i: (0, 0))
    experts = sums.shape[0] - 8
    return pl.pallas_call(
        unpack_kernel,
        grid=(steps,),
        in_specs=[piece(0), piece(1), piece(2), pl.BlockSpec((1, kinds, shard_rows, width), lambda i: (i, 0, 0, 0)),
            pl.BlockSpec(sums.shape, lambda i: (0, 0)), pl.BlockSpec(memory_space=pltpu.SMEM),
        ],
        out_specs=(
            pl.BlockSpec((1, eff, half), lambda i: (i // 2, i % 2, 0)),
            pl.BlockSpec((1, eff, half), lambda i: (i // 2, i % 2, 0)),
            pl.BlockSpec((1, eff, half), lambda i: (i // 2, 0, i % 2)),
            row(width), row(key_width), row(key_width), row(width),
            still(experts, width), still(1, width), still(1, width), still(1, HEAD), still(1, HEAD), still(1, 1),
        ),
        out_shape=(
            shape(owned, width, eff), shape(owned, width, eff), shape(owned, eff, width),
            shape(width, width), shape(width, key_width), shape(width, key_width), shape(width, width),
            shape(experts, width), shape(1, width), shape(1, width), shape(1, HEAD), shape(1, HEAD), shape(1, 1),
        ),
        compiler_params=pltpu.CompilerParams(vmem_limit_bytes=48 * MIB),
        name="unpack",
    )(total, total, total, dense, sums, scale)


def per_device(
    fast, block_input, teacher, lengths, routes, w_query, w_key, w_value, w_out, query_gain, key_gain,
    attn_gain, ffn_gain, w_router, w_gate, w_up, w_down,
):
    slots, rows, width = block_input.shape
    expert_total = w_router.shape[1]
    group = lax.axis_size(("context", "experts"))
    here = lax.axis_index(("context", "experts"))
    span = rows * group
    slot_lengths = lax.dynamic_slice_in_dim(lengths, lax.axis_index("dp") * slots, slots)
    scalars = jnp.concatenate([slot_lengths, here[None]]).astype(jnp.int32)
    positions = here * rows + jnp.arange(rows, dtype=jnp.int32)
    valid = (positions[None, :] < slot_lengths[:, None]).astype(F32)[..., None]
    count_all = jnp.sum(lengths).astype(F32)
    positions_all = lengths.shape[0] * span

    half = HEAD // 2
    lanes = jnp.arange(LANES, dtype=jnp.int32)
    inverse = 10000.0 ** (-((lanes % half).astype(F32) * 2.0 / HEAD))
    turned = positions.astype(F32)[:, None] * inverse[None, :]
    cosine = jnp.cos(turned)
    sine = jnp.sin(turned) * jnp.where(lanes % HEAD < half, -1.0, 1.0)[None, :]
    qg = jnp.concatenate([query_gain, query_gain])[None, :]
    kg = jnp.concatenate([key_gain, key_gain])[None, :]
    ag, fg = attn_gain[None, :], ffn_gain[None, :]
    router = jnp.pad(w_router, ((0, 0), (0, LANES - expert_total)))

    if fast:
        scale = (positions_all / count_all)[None]
        (
            h, q, qraw, kraw, kv, mixed, invl, after, soft, tokens, pick, xe, gate_part, up_part, hidden,
            block_output, out_grad, loss_row, unused_grads, dpart, weighted, gate_grad, up_grad,
        ) = front(
            slot_lengths, block_input, teacher, jnp.swapaxes(routes, 1, 2), w_query, w_key, w_value, w_out,
            w_gate, w_up, w_down, ag, fg, qg, kg, cosine, sine, w_router.T, scale, group, 1,
        )
        total, input_grad, dense, sums = tail(
            slot_lengths, dpart, xe, gate_grad, up_grad, hidden, weighted, q, kv, mixed, invl, soft, out_grad, after,
            qraw, kraw, block_input, h, tokens, w_out, w_query, w_key, w_value, fg, w_router.T, cosine, sine, ag, qg, kg,
            loss_row, expert_total, 2,
        )[:4]
        unpacked = unpack(total, dense, sums, (1.0 / (count_all * width))[None], w_key.shape[1])
        expert_grads, dense = unpacked[:3], unpacked[3:7]
        router_grad, attn_gg, ffn_gg, query_gg, key_gg, loss = unpacked[7:]
        small = (query_gg[0], key_gg[0], attn_gg[0], ffn_gg[0], router_grad.T, loss[0, 0])
    else:
        h, q, kv_local, qraw, kraw = project(block_input, ag, w_query, w_key, w_value, qg, kg, cosine, sine)
        kv = plane_gather(kv_local)
        mixed, invl, after, xg, soft = attend(scalars, q, kv, block_input, w_out, fg, router, routes)
        tokens = plane_gather(xg)
        pick, xe, gate_part, up_part, hidden, part = experts_forward(scalars, tokens, w_gate, w_up, w_down)
        output = after + plane_scatter(part)
        difference = valid * (output - teacher.astype(F32))
        loss_part = jnp.sum(difference * difference)
        out_grad = difference * (positions_all / count_all)
        grads = plane_gather(out_grad.astype(BF16))
        dpart, weighted, gate_grad, up_grad = experts_backward(
            scalars, grads, tokens, pick, gate_part, up_part, hidden, w_gate, w_up, w_down
        )
        expert_grads = lax.psum(expert_weights(xe, gate_grad, up_grad, hidden, weighted), "dp")
        dx = plane_scatter(dpart)
        dq, dkv_parts, after_grad, attn_grad, logit_grad, ffn_gain_grad = attend_backward(
            scalars, q, kv, mixed, invl, dx, soft, out_grad, after, fg, router, w_out
        )
        dkv = plane_scatter(dkv_parts)
        input_grad, dense, router_grad, query_gg, key_gg, attn_gg = finish(
            dq, dkv, qraw, kraw, block_input, after_grad, cosine, sine, ag, qg, kg,
            w_query, w_key, w_value, h, mixed, attn_grad, xg, logit_grad,
        )
        dense = lax.psum(dense, ("dp", "context", "experts"))
        dense = [dense[:, k].reshape(width, width).astype(F32) for k in range(3)]
        small = lax.psum(
            (
                query_gg[0, :HEAD] + query_gg[0, HEAD:], key_gg[0, :HEAD] + key_gg[0, HEAD:], attn_gg[0],
                ffn_gain_grad[0], router_grad[:, :expert_total], loss_part,
            ),
            ("dp", "context", "experts"),
        )
        key_width = w_key.shape[1]
        expert_grads = [grad.astype(F32) for grad in expert_grads]
        dense = [dense[0], dense[1][:, :key_width], dense[1][:, key_width:], dense[2]]
        block_output = output.astype(BF16)
        small = small[:5] + (small[5] / (count_all * width),)
    return (
        small[5], block_output, input_grad, dense[0], dense[1], dense[2], dense[3],
        small[0], small[1], small[2], small[3], small[4], expert_grads[0], expert_grads[1], expert_grads[2],
    )


def solution(mesh):
    fast = mesh.shape["context"] == 4 and mesh.shape["experts"] == 2
    rows = P("dp", ("context", "experts"), None)
    owned = P(("context", "experts"), None, None)
    return jax.shard_map(
        functools.partial(per_device, fast),
        mesh=mesh,
        in_specs=(rows, rows, P(), rows) + (P(),) * 9 + (owned,) * 3,
        out_specs=(P(), rows, rows) + (P(),) * 9 + (owned,) * 3,
        check_vma=False,
    )
```
